32 devices in a mesh: img: 8 (over z, x), patch: 4 (over y, core).
Axes of the slice: x: 2, y: 2, z: 4, core: 2. Of those that a mesh axis runs over, the one named last changes fastest.
Arguments:
- latents: bfloat16 [4, 32, 64, 1024], P(None, 'img', 'patch'), may hold values from -6 to 6
- media: bfloat16 [4, 128, 256, 1024], P(None, 'img', 'patch'), may hold values from -6 to 6
- doc_ids: int32 [4, 128], P(None, 'img'), may hold values from 0 to 3, as said below
- w_query: bfloat16 [1024, 512], replicated, may hold values from -0.1875 to 0.1875
- w_keyval: bfloat16 [1024, 1024], replicated, may hold values from -0.1875 to 0.1875
- w_output: bfloat16 [512, 1024], replicated, may hold values from -3 to 3
- w_expand: bfloat16 [1024, 4096], replicated, may hold values from -0.1875 to 0.1875
- w_reduce: bfloat16 [4096, 1024], replicated, may hold values from -0.09375 to 0.09375
- media_gain: float32 [1024], replicated, may hold values from 0.1 to 1.9
- media_shift: float32 [1024], replicated, may hold values from -1.8 to 1.8
- latent_gain: float32 [1024], replicated, may hold values from 0.1 to 1.9
- latent_shift: float32 [1024], replicated, may hold values from -1.8 to 1.8
- ff_gain: float32 [1024], replicated, may hold values from 0.1 to 1.9
- ff_shift: float32 [1024], replicated, may hold values from -1.8 to 1.8
- out_grad: bfloat16 [4, 32, 64, 1024], P(None, 'img', 'patch'), may hold values from -6 to 6
Outputs:
- latents_out: bfloat16 [4, 32, 64, 1024], P(None, 'img', 'patch')
- latents_grad: bfloat16 [4, 32, 64, 1024], P(None, 'img', 'patch')
- media_grad: bfloat16 [4, 128, 256, 1024], P(None, 'img', 'patch')
- w_query_grad: float32 [1024, 512], P('img')
- w_keyval_grad: float32 [1024, 1024], P('img')
- w_output_grad: float32 [512, 1024], P('img')
- w_expand_grad: float32 [1024, 4096], P('img')
- w_reduce_grad: float32 [4096, 1024], P('img')
- media_gain_grad: float32 [1024], P('img')
- media_shift_grad: float32 [1024], P('img')
- latent_gain_grad: float32 [1024], P('img')
- latent_shift_grad: float32 [1024], P('img')
- ff_gain_grad: float32 [1024], P('img')
- ff_shift_grad: float32 [1024], P('img')
The draws below stay inside these ranges and needn't reach their ends.
Inputs may be any that keep to these rules, and one draw needn't show every extreme that they name: `doc_ids`: in each micro-batch, the 16 slots of every aligned img block carry document numbers that never fall, and every number 0 to 3 appears in every block.
All inputs are finite; a program needn't handle non-finite values.
Results may differ from the reference program's by a relative error of at most 0.02.
Values may be sent and summed in bfloat16 or wider, within the bound.
No kernel may reach another device: no remote copies, remote signals or barrier semaphores. Data moves between devices by JAX's collectives and lax.ppermute only.
A program may use at most 256 MiB of HBM per device.

```python
import jax
import jax.numpy as jnp
from jax import lax

D = 1024
HEADS = 8
HEAD_DIM = 64
FF = 4096
LAT = 64
PATCHES = 256
IMG_DEV = 16
DOC_DEV = 4
MICRO = 4
INNER = 512
IMAGES = 128
DOCS = 32


def draw_doc_ids(key, part):
    key = jax.random.fold_in(key, 7)
    first_key, second_key = jax.random.split(key)
    blocks = IMAGES // IMG_DEV
    extra_shape = (MICRO, blocks, IMG_DEV - DOC_DEV)
    first_pick = jax.random.randint(first_key, extra_shape, 0, DOC_DEV)
    second_pick = jax.random.randint(second_key, extra_shape, 0, DOC_DEV)
    extra_ids = jnp.minimum(first_pick, second_pick).astype(jnp.int32)
    every_doc = jnp.broadcast_to(jnp.arange(DOC_DEV, dtype=jnp.int32), (MICRO, blocks, DOC_DEV))
    joined = jnp.sort(jnp.concatenate([every_doc, extra_ids], axis=-1), axis=-1)
    return joined.reshape(MICRO, IMAGES).astype(jnp.int32)


def block_levels(key, dims, pieces, least, high):
    factor_of = 1.0
    for dim, blocks in pieces:
        draws = jax.random.uniform(jax.random.fold_in(jax.random.fold_in(key, 6), dim), (blocks,), jnp.float32, least / len(pieces), high / len(pieces))
        factor_of = factor_of * jnp.repeat(jnp.exp(draws), dims[dim] // blocks).reshape((-1,) + (1,) * (len(dims) - 1 - dim))
    return factor_of


def bell_draw(stream_key, extent, scale, bound, shards=(), held_as=jnp.bfloat16):
    loudness = block_levels(stream_key, extent, shards, -0.22, 0.18) if shards else 1.0
    values = jax.random.normal(stream_key, extent, jnp.float32) * scale * loudness
    return jnp.minimum(jnp.maximum(values, -bound), bound).astype(held_as)


def setup_inputs(seed: int = 0) -> dict:
    key_list = jax.random.split(jax.random.key(seed), 16)
    latents = bell_draw(key_list[0], (MICRO, DOCS, LAT, D), 1.0, 6.0, ((1, 8), (2, 4)))
    media = bell_draw(key_list[1], (MICRO, IMAGES, PATCHES, D), 1.0, 6.0, ((1, 8), (2, 4)))
    doc_ids = draw_doc_ids(jax.random.fold_in(key_list[15], 71), 0)
    w_query = bell_draw(key_list[3], (D, INNER), D ** -0.5, 0.1875)
    w_keyval = bell_draw(key_list[4], (D, 2 * INNER), D ** -0.5, 0.1875)
    w_output = bell_draw(key_list[5], (INNER, D), 4 ** -0.5, 3.0)
    w_expand = bell_draw(key_list[6], (D, FF), D ** -0.5, 0.1875)
    w_reduce = bell_draw(key_list[7], (FF, D), FF ** -0.5, 0.09375)
    media_gain = jnp.clip(1.0 + 0.18 * jax.random.normal(key_list[8], (D,), jnp.float32), 0.1, 1.9)
    media_shift = bell_draw(key_list[9], (D,), 0.3, 1.8, (), jnp.float32)
    latent_gain = jnp.clip(1.0 + 0.18 * jax.random.normal(key_list[10], (D,), jnp.float32), 0.1, 1.9)
    latent_shift = bell_draw(key_list[11], (D,), 0.3, 1.8, (), jnp.float32)
    ff_gain = jnp.clip(1.0 + 0.18 * jax.random.normal(key_list[12], (D,), jnp.float32), 0.1, 1.9)
    ff_shift = bell_draw(key_list[13], (D,), 0.3, 1.8, (), jnp.float32)
    out_grad = bell_draw(key_list[14], (MICRO, DOCS, LAT, D), 1.0, 6.0, ((1, 8), (2, 4)))
    return dict(latents=latents, media=media, doc_ids=doc_ids, w_query=w_query, w_keyval=w_keyval, w_output=w_output, w_expand=w_expand, w_reduce=w_reduce, media_gain=media_gain, media_shift=media_shift, latent_gain=latent_gain, latent_shift=latent_shift, ff_gain=ff_gain, ff_shift=ff_shift, out_grad=out_grad)


@jax.custom_vjp
def low(v):
    return lax.optimization_barrier(v.astype(jnp.bfloat16)).astype(jnp.float32)

@jax.custom_vjp
def low_back(v):
    return v

def low_keep(v):
    return (low(v), None)

def low_pass(kept, grad):
    return (grad,)

def back_keep(v):
    return (v, None)

def back_low(kept, grad):
    return (low(grad),)
low.defvjp(low_keep, low_pass)
low_back.defvjp(back_keep, back_low)
EPS = 1e-05
PRECISE = lax.Precision.HIGHEST

def layer_norm(values, gain_vec, shift_vec):
    center = values - lax.optimization_barrier(jnp.mean(values, axis=-1, keepdims=True))
    spread = lax.optimization_barrier(jnp.mean(center * center, axis=-1, keepdims=True))
    return center * lax.rsqrt(spread + EPS) * gain_vec + shift_vec

def group_forward(params, latent_block, media_block, doc_block):
    w_query, w_keyval, w_output, w_expand, w_reduce, media_gain, media_shift, latent_gain, latent_shift, ff_gain, ff_shift = params
    ln_lat = low(layer_norm(latent_block, latent_gain, latent_shift))
    ln_med = low(layer_norm(media_block, media_gain, media_shift))
    queries = low_back(low(jnp.einsum('ald,de->ale', ln_lat, w_query, precision=PRECISE)))
    kv_med = low_back(low(jnp.einsum('ipd,de->ipe', ln_med, w_keyval, precision=PRECISE)))
    kv_lat = low_back(low(jnp.einsum('ald,de->ale', ln_lat, w_keyval, precision=PRECISE)))
    keyvals = jnp.concatenate([kv_med.reshape(IMG_DEV * PATCHES, 2 * INNER), kv_lat.reshape(DOC_DEV * LAT, 2 * INNER)], axis=0)
    doc_index = jnp.arange(DOC_DEV, dtype=jnp.int32)
    key_doc = jnp.concatenate([jnp.repeat(doc_block.astype(jnp.int32), PATCHES), jnp.repeat(doc_index, LAT)])
    query_doc = jnp.repeat(doc_index, LAT)
    same_doc = query_doc[:, None] == key_doc[None, :]
    query_heads = queries.reshape(DOC_DEV * LAT, HEADS, HEAD_DIM)
    key_heads = keyvals[:, :INNER].reshape(-1, HEADS, HEAD_DIM)
    value_heads = keyvals[:, INNER:].reshape(-1, HEADS, HEAD_DIM)
    scores = low_back(jnp.einsum('ihd,jhd->hij', query_heads, key_heads, precision=PRECISE) * HEAD_DIM ** (-0.5))
    scores = jnp.where(same_doc[None], scores, -1e+30)
    top_score = lax.optimization_barrier(jnp.max(scores, axis=-1, keepdims=True))
    expo = jnp.exp(scores - top_score)
    weights = low(expo / lax.optimization_barrier(jnp.sum(expo, axis=-1, keepdims=True)))
    attended = low_back(low(jnp.einsum('hij,jhd->ihd', weights, value_heads, precision=PRECISE).reshape(DOC_DEV, LAT, INNER)))
    mixed = latent_block + low_back(jnp.einsum('ald,de->ale', attended, w_output, precision=PRECISE))
    ln_ff = low(layer_norm(mixed, ff_gain, ff_shift))
    hidden_pre = low_back(jnp.einsum('ald,df->alf', ln_ff, w_expand, precision=PRECISE))
    hidden_act = low(jax.nn.gelu(hidden_pre, approximate=False))
    return mixed + jnp.einsum('alf,fd->ald', hidden_act, w_reduce, precision=PRECISE)

def forward(latents, media, doc_ids, params):
    latent_groups = latents.reshape(-1, DOC_DEV, LAT, D)
    media_groups = media.reshape(-1, IMG_DEV, PATCHES, D)
    doc_groups = doc_ids.reshape(-1, IMG_DEV)

    def one_group(items):
        return group_forward(params, items[0], items[1], items[2])
    mapped = lax.map(jax.checkpoint(one_group), (latent_groups, media_groups, doc_groups))
    return mapped.reshape(MICRO, DOCS, LAT, D)

def reference(latents, media, doc_ids, w_query, w_keyval, w_output, w_expand, w_reduce, media_gain, media_shift, latent_gain, latent_shift, ff_gain, ff_shift, out_grad):
    floats = tuple((item.astype(jnp.float32) for item in (latents, media, w_query, w_keyval, w_output, w_expand, w_reduce, media_gain, media_shift, latent_gain, latent_shift, ff_gain, ff_shift)))

    def whole(*inputs):
        return forward(inputs[0], inputs[1], doc_ids, inputs[2:])
    result, puller = jax.vjp(whole, *floats)
    grads = puller(out_grad.astype(jnp.float32))
    return (result.astype(jnp.bfloat16), grads[0].astype(jnp.bfloat16), grads[1].astype(jnp.bfloat16), grads[2], grads[3], grads[4], grads[5], grads[6], grads[7], grads[8], grads[9], grads[10], grads[11], grads[12])
```

```python
import functools

import jax
import jax.numpy as jnp
from jax import lax
from jax.experimental import pallas as pl
from jax.experimental.pallas import tpu as pltpu
from jax.sharding import PartitionSpec as P

HEADS = 8
GROUP = 4
EPS = 1e-05
BF = jnp.bfloat16
F32 = jnp.float32
VMEM = 56 * 1024 * 1024


def params(n=1):
    return pltpu.CompilerParams(
        vmem_limit_bytes=VMEM, dimension_semantics=("arbitrary",) * n
    )


def dot(a, b, dims):
    return lax.dot_general(a, b, (dims, ((), ())), preferred_element_type=F32)


NN = ((1,), (0,))
NT = ((1,), (1,))
TN = ((0,), (0,))


def standardize(values):
    center = values - jnp.mean(values, axis=-1, keepdims=True)
    inv = lax.rsqrt(jnp.mean(center * center, axis=-1, keepdims=True) + EPS)
    return center * inv, inv


def norm_back(hat, inv, gain, upstream):
    scaled = upstream * gain
    back = inv * (
        scaled
        - jnp.mean(scaled, axis=-1, keepdims=True)
        - hat * jnp.mean(scaled * hat, axis=-1, keepdims=True)
    )
    return back, upstream * hat


def kv_kernel(media_ref, gain_ref, shift_ref, w_ref, ln_ref, kv_ref):
    rows = media_ref.shape[0]
    step = min(rows, 256)
    for at in range(0, rows, step):
        part = pl.ds(at, step)
        hat, _ = standardize(media_ref[part, :].astype(F32))
        ln = (hat * gain_ref[...] + shift_ref[...]).astype(BF)
        ln_ref[part, :] = ln
        kv_ref[part, :] = dot(ln, w_ref[...], NN).astype(BF)


def kv_call(media, gain, shift, w_keyval):
    rows, width = media.shape
    outs = w_keyval.shape[1]
    block = 512
    return pl.pallas_call(
        kv_kernel,
        grid=(rows // block,),
        in_specs=[
            pl.BlockSpec((block, width), lambda i: (i, 0)),
            pl.BlockSpec((1, width), lambda i: (0, 0)),
            pl.BlockSpec((1, width), lambda i: (0, 0)),
            pl.BlockSpec((width, outs), lambda i: (0, 0)),
        ],
        out_specs=[
            pl.BlockSpec((block, width), lambda i: (i, 0)),
            pl.BlockSpec((block, outs), lambda i: (i, 0)),
        ],
        out_shape=[
            jax.ShapeDtypeStruct((rows, width), BF),
            jax.ShapeDtypeStruct((rows, outs), BF),
        ],
        compiler_params=params(),
        cost_estimate=pl.CostEstimate(
            flops=2 * rows * width * outs,
            bytes_accessed=2 * (2 * rows * width + rows * outs),
            transcendentals=0,
        ),
        name="media_keyval",
    )(media, gain, shift, w_keyval)


def block_mask(head_size, lats):
    rows = GROUP * lats
    cols = GROUP * head_size
    row_head = lax.broadcasted_iota(jnp.int32, (rows, cols), 0) // lats
    col_head = lax.broadcasted_iota(jnp.int32, (rows, cols), 1) // head_size
    return row_head == col_head


def spread_heads(values, mask):
    tiled = jnp.concatenate([values] * GROUP, axis=0)
    return jnp.where(mask, tiled, jnp.zeros_like(tiled))


def gather_heads(full, mask, lats):
    kept = jnp.where(mask, full, 0.0)
    total = kept[:lats]
    for head in range(1, GROUP):
        total = total + kept[head * lats : (head + 1) * lats]
    return total


def attend_kernel(
    doc_ref, q_ref, kv_ref, kvl_ref, o_ref, m_ref, l_ref, bd, score, lat_score, acc, top, tot
):
    docs, lats, inner = q_ref.shape[1:]
    slots, keys = kv_ref.shape[1:3]
    groups = HEADS // GROUP
    span = inner // groups
    micro = pl.program_id(0)
    mask = block_mask(inner // HEADS, lats)
    wide = GROUP * lats
    for d in range(docs):
        for g in range(groups):
            part = q_ref[0, d, :, g * span : (g + 1) * span]
            spread = spread_heads(part, mask)
            bd[d, g] = spread
            lat = dot(kvl_ref[0, d, :, g * span : (g + 1) * span], spread, NT)
            lat_score[d, g] = lat
            top[d, g] = jnp.max(lat, axis=0, keepdims=True)
    for s in range(slots):
        d = doc_ref[micro, s]
        for g in range(groups):
            val = dot(kv_ref[0, s, :, g * span : (g + 1) * span], bd[d, g], NT)
            score[s, g] = val
            top[d, g] = jnp.maximum(top[d, g], jnp.max(val, axis=0, keepdims=True))
    for d in range(docs):
        for g in range(groups):
            expo = jnp.exp(lat_score[d, g] - top[d, g])
            tot[d, g] = jnp.sum(expo, axis=0, keepdims=True)
            val = kvl_ref[0, d, :, inner + g * span : inner + (g + 1) * span]
            acc[d, g] = dot(expo.astype(BF), val, TN)
    for s in range(slots):
        d = doc_ref[micro, s]
        for g in range(groups):
            expo = jnp.exp(score[s, g] - top[d, g])
            tot[d, g] = tot[d, g] + jnp.sum(expo, axis=0, keepdims=True)
            val = kv_ref[0, s, :, inner + g * span : inner + (g + 1) * span]
            acc[d, g] = acc[d, g] + dot(expo.astype(BF), val, TN)
    for d in range(docs):
        for g in range(groups):
            o_ref[0, d, :, g * span : (g + 1) * span] = gather_heads(acc[d, g], mask, lats).astype(
                BF
            )
            m_ref[0, d, :, g * wide : (g + 1) * wide] = top[d, g]
            l_ref[0, d, :, g * wide : (g + 1) * wide] = tot[d, g]


def attend_call(doc_ids, queries, kv_med, kv_lat):
    micro, docs, lats, inner = queries.shape
    slots, keys, both = kv_med.shape[1:]
    lat_rows = kv_lat.shape[2]
    groups = HEADS // GROUP
    span = inner // groups
    wide = GROUP * lats

    def whole(*tail):
        return pl.BlockSpec((1,) + tail, lambda i, ids: (i,) + (0,) * len(tail))

    return pl.pallas_call(
        attend_kernel,
        grid_spec=pltpu.PrefetchScalarGridSpec(
            num_scalar_prefetch=1,
            grid=(micro,),
            in_specs=[
                whole(docs, lats, inner),
                whole(slots, keys, both),
                whole(docs, lat_rows, both),
            ],
            out_specs=[
                whole(docs, lats, inner),
                whole(docs, 1, HEADS * lats),
                whole(docs, 1, HEADS * lats),
            ],
            scratch_shapes=[
                pltpu.VMEM((docs, groups, wide, span), BF),
                pltpu.VMEM((slots, groups, keys, wide), F32),
                pltpu.VMEM((docs, groups, lat_rows, wide), F32),
                pltpu.VMEM((docs, groups, wide, span), F32),
                pltpu.VMEM((docs, groups, 1, wide), F32),
                pltpu.VMEM((docs, groups, 1, wide), F32),
            ],
        ),
        out_shape=[
            jax.ShapeDtypeStruct((micro, docs, lats, inner), BF),
            jax.ShapeDtypeStruct((micro, docs, 1, HEADS * lats), F32),
            jax.ShapeDtypeStruct((micro, docs, 1, HEADS * lats), F32),
        ],
        compiler_params=params(),
        cost_estimate=pl.CostEstimate(
            flops=4 * micro * slots * keys * inner * wide,
            bytes_accessed=micro * slots * keys * both * 2,
            transcendentals=micro * slots * keys * HEADS * lats,
        ),
        name="attend",
    )(doc_ids, queries, kv_med, kv_lat)


def attend_back_kernel(
    doc_ref,
    q_ref,
    go_ref,
    k_ref,
    v_ref,
    kl_ref,
    vl_ref,
    lse_ref,
    dot_ref,
    ln_ref,
    gkv_ref,
    gkvl_ref,
    gq_ref,
    wg_ref,
    bdq,
    bdo,
    acc,
    w_acc,
):
    docs, lats, span = q_ref.shape[1:]
    slots, keys = k_ref.shape[1:3]
    micro = pl.program_id(0)
    mask = block_mask(span // GROUP, lats)

    def pair(key, value, d):
        score = dot(key, bdq[d], NT)
        prob = jnp.exp(score - lse_ref[0, d])
        dprob = dot(value, bdo[d], NT)
        dscore = (prob * (dprob - dot_ref[0, d])).astype(BF)
        grad_key = dot(dscore, bdq[d], NN).astype(BF)
        grad_value = dot(prob.astype(BF), bdo[d], NN).astype(BF)
        grad_query = dot(dscore, key, TN)
        return grad_key, grad_value, grad_query

    for d in range(docs):
        bdq[d] = spread_heads(q_ref[0, d], mask)
        bdo[d] = spread_heads(go_ref[0, d], mask)
    for d in range(docs):
        grad_key, grad_value, grad_query = pair(kl_ref[0, d], vl_ref[0, d], d)
        gkvl_ref[0, d, :, :span] = grad_key
        gkvl_ref[0, d, :, span:] = grad_value
        acc[d] = grad_query
    for s in range(slots):
        d = doc_ref[micro, s]
        grad_key, grad_value, grad_query = pair(k_ref[0, s], v_ref[0, s], d)
        gkv_ref[s * keys : (s + 1) * keys, :span] = grad_key
        gkv_ref[s * keys : (s + 1) * keys, span:] = grad_value
        acc[d] = acc[d] + grad_query
    for d in range(docs):
        gq_ref[0, d] = gather_heads(acc[d], mask, lats).astype(BF)
    part = dot(ln_ref[...], gkv_ref[...], TN)

    @pl.when(micro == 0)
    def _():
        w_acc[...] = part

    @pl.when(micro > 0)
    def _():
        w_acc[...] = w_acc[...] + part

    @pl.when(micro == pl.num_programs(0) - 1)
    def _():
        wg_ref[...] = w_acc[...].astype(BF)


def attend_back_call(group, doc_ids, queries, grad_att, kv_med, kv_lat, lse, row_dot, ln_med):
    micro, docs, lats, inner = queries.shape
    slots, keys, both = kv_med.shape[1:]
    lat_rows = kv_lat.shape[2]
    width = ln_med.shape[1]
    groups = HEADS // GROUP
    span = inner // groups
    wide = GROUP * lats
    rows = slots * keys

    def cols(at, *tail):
        return pl.BlockSpec(
            (1,) + tail, lambda i, ids: (i,) + (0,) * (len(tail) - 1) + (at,)
        )

    return pl.pallas_call(
        attend_back_kernel,
        grid_spec=pltpu.PrefetchScalarGridSpec(
            num_scalar_prefetch=1,
            grid=(micro,),
            in_specs=[
                cols(group, docs, lats, span),
                cols(group, docs, lats, span),
                cols(group, slots, keys, span),
                cols(groups + group, slots, keys, span),
                cols(group, docs, lat_rows, span),
                cols(groups + group, docs, lat_rows, span),
                cols(group, docs, 1, wide),
                cols(group, docs, 1, wide),
                pl.BlockSpec((rows, width), lambda i, ids: (i, 0)),
            ],
            out_specs=[
                pl.BlockSpec((rows, 2 * span), lambda i, ids: (i, 0)),
                cols(0, docs, lat_rows, 2 * span),
                cols(0, docs, lats, span),
                pl.BlockSpec((width, 2 * span), lambda i, ids: (0, 0)),
            ],
            scratch_shapes=[
                pltpu.VMEM((docs, wide, span), BF),
                pltpu.VMEM((docs, wide, span), BF),
                pltpu.VMEM((docs, wide, span), F32),
                pltpu.VMEM((width, 2 * span), F32),
            ],
        ),
        out_shape=[
            jax.ShapeDtypeStruct((micro * rows, 2 * span), BF),
            jax.ShapeDtypeStruct((micro, docs, lat_rows, 2 * span), BF),
            jax.ShapeDtypeStruct((micro, docs, lats, span), BF),
            jax.ShapeDtypeStruct((width, 2 * span), BF),
        ],
        compiler_params=params(),
        cost_estimate=pl.CostEstimate(
            flops=micro * rows * (10 * span * wide + 4 * span * width),
            bytes_accessed=micro * rows * 2 * (width + 4 * span),
            transcendentals=micro * rows * wide,
        ),
        name="attend_back",
    )(doc_ids, queries, grad_att, kv_med, kv_med, kv_lat, kv_lat, lse, row_dot, ln_med)


def media_back_kernel(
    media_ref, ga_ref, gb_ref, wa_ref, wb_ref, gain_ref, out_ref, dg_ref, ds_ref
):
    rows = media_ref.shape[0]
    step = min(rows, 256)

    @pl.when(pl.program_id(0) == 0)
    def _():
        dg_ref[...] = jnp.zeros_like(dg_ref)
        ds_ref[...] = jnp.zeros_like(ds_ref)

    for at in range(0, rows, step):
        part = pl.ds(at, step)
        up = dot(ga_ref[part, :], wa_ref[...], NN) + dot(gb_ref[part, :], wb_ref[...], NN)
        hat, inv = standardize(media_ref[part, :].astype(F32))
        back, gains = norm_back(hat, inv, gain_ref[...], up)
        out_ref[part, :] = back.astype(BF)
        dg_ref[...] += jnp.sum(gains, axis=0, keepdims=True)
        ds_ref[...] += jnp.sum(up, axis=0, keepdims=True)


def media_back_call(media, grad_a, grad_b, w_a, w_b, gain):
    rows, width = media.shape
    half = grad_a.shape[1]
    block = 512
    fixed = lambda i: (0, 0)
    moving = lambda i: (i, 0)
    return pl.pallas_call(
        media_back_kernel,
        grid=(rows // block,),
        in_specs=[
            pl.BlockSpec((block, width), moving),
            pl.BlockSpec((block, half), moving),
            pl.BlockSpec((block, half), moving),
            pl.BlockSpec((half, width), fixed),
            pl.BlockSpec((half, width), fixed),
            pl.BlockSpec((1, width), fixed),
        ],
        out_specs=[
            pl.BlockSpec((block, width), moving),
            pl.BlockSpec((1, width), fixed),
            pl.BlockSpec((1, width), fixed),
        ],
        out_shape=[
            jax.ShapeDtypeStruct((rows, width), BF),
            jax.ShapeDtypeStruct((1, width), F32),
            jax.ShapeDtypeStruct((1, width), F32),
        ],
        compiler_params=params(),
        cost_estimate=pl.CostEstimate(
            flops=4 * rows * half * width,
            bytes_accessed=2 * rows * (2 * width + 2 * half),
            transcendentals=0,
        ),
        name="media_back",
    )(media, grad_a, grad_b, w_a, w_b, gain)


def swap(value, axis, bit):
    size = lax.axis_size(axis)
    return lax.ppermute(value, axis, [(i, i ^ bit) for i in range(size)])


def gather_patch(own):
    far = swap(own, "patch", 2)
    return jnp.stack([own, swap(own, "patch", 1), far, swap(far, "patch", 1)], axis=1)


def add(first, second):
    return (first.astype(F32) + second.astype(F32)).astype(BF)


def scatter_patch(value):
    near = add(value[:, 0::2], swap(value[:, 1::2], "patch", 1))
    return near[:, 0], swap(near[:, 1], "patch", 2)


def scatter_bits(value, axis, bits):
    size = lax.axis_size(axis)
    me = lax.axis_index(axis)
    count = size.bit_length() - 1
    tail = value.shape[1:]
    value = value.reshape((2,) * count + tail)
    done = []
    for bit in bits:
        place = (count - 1 - bit) - sum(1 for b in done if b > bit)
        mine = lax.rem(lax.div(me, 1 << bit), 2)
        keep = lax.dynamic_index_in_dim(value, mine, place, keepdims=False)
        send = lax.dynamic_index_in_dim(value, 1 - mine, place, keepdims=False)
        value = add(keep, swap(send, axis, 1 << bit))
        done.append(bit)
    return value


def gather_rows(own):
    me = lax.axis_index("patch")
    far = swap(own, "patch", 2)
    chunks = jnp.stack([own, swap(own, "patch", 1), far, swap(far, "patch", 1)])
    return jnp.stack(
        [
            lax.dynamic_index_in_dim(chunks, jnp.bitwise_xor(me, j), 0, keepdims=False)
            for j in range(4)
        ]
    )


def reduce_all(value):
    value = jnp.moveaxis(value, 1, 0)
    value = scatter_bits(value, "patch", (0, 1))
    count = lax.axis_size("img").bit_length() - 1
    value = scatter_bits(value, "img", tuple(range(count)))
    whole = gather_rows(value)
    return whole.reshape((-1,) + whole.shape[2:]).astype(F32)


def local(
    latents,
    media,
    doc_ids,
    w_query,
    w_keyval,
    w_output,
    w_expand,
    w_reduce,
    media_gain,
    media_shift,
    latent_gain,
    latent_shift,
    ff_gain,
    ff_shift,
    out_grad,
):
    micro, docs, lat_rows, width = latents.shape
    slots, keys = media.shape[1:3]
    inner = w_query.shape[1]
    ff = w_expand.shape[1]
    head_size = inner // HEADS
    scale = head_size ** (-0.5)
    parts = lax.axis_size("patch")
    imgs = lax.axis_size("img")
    patch_index = lax.axis_index("patch")
    lats = lat_rows * parts
    pairs = micro * docs
    own_rows = pairs * lat_rows
    all_rows = own_rows * parts
    groups = HEADS // GROUP
    span = inner // groups

    def by_owner(flat):
        return flat.reshape((pairs, parts, lat_rows) + flat.shape[1:])

    latents_own = latents.reshape(pairs, lat_rows, width)
    cot_own = out_grad.reshape(pairs, lat_rows, width)
    latents_all = gather_patch(latents_own).reshape(all_rows, width)
    cot_all = gather_patch(cot_own).reshape(all_rows, width)

    ln_med, kv_med = kv_call(
        media.reshape(-1, width), media_gain[None], media_shift[None], w_keyval
    )
    kv_med = kv_med.reshape(micro, slots, keys, 2 * inner)

    lat_hat, lat_inv = standardize(latents_own.reshape(own_rows, width).astype(F32))
    ln_lat = (lat_hat * latent_gain + latent_shift).astype(BF)
    kv_lat = dot(ln_lat, w_keyval, NN).astype(BF).reshape(micro, docs, lat_rows, 2 * inner)
    all_hat, _ = standardize(latents_all.astype(F32))
    ln_all = (all_hat * latent_gain + latent_shift).astype(BF)
    queries = (dot(ln_all, w_query, NN).astype(BF).astype(F32) * scale).astype(BF)
    queries = queries.reshape(micro, docs, lats, inner)

    part_out, top, total = attend_call(doc_ids, queries, kv_med, kv_lat)

    def stats(value):
        return jnp.swapaxes(value.reshape(pairs, HEADS, lats), 1, 2).reshape(
            pairs, parts, lat_rows, HEADS
        )

    def join(first, second):
        out_a, top_a, tot_a = first
        out_b, top_b, tot_b = second
        best = jnp.maximum(top_a, top_b)
        fac_a, fac_b = jnp.exp(top_a - best), jnp.exp(top_b - best)

        def wide(fac, out):
            heads = out.astype(F32).reshape(out.shape[:-1] + (HEADS, head_size))
            return (fac[..., None] * heads).reshape(out.shape)

        return (
            wide(fac_a, out_a) + wide(fac_b, out_b),
            best,
            fac_a * tot_a + fac_b * tot_b,
        )

    mine = (part_out.reshape(pairs, parts, lat_rows, inner), stats(top), stats(total))
    near = tuple(v[:, 0::2] for v in mine)
    sent = swap((mine[0][:, 1::2], jnp.concatenate([v[:, 1::2] for v in mine[1:]], -1)), "patch", 1)
    out_n, top_n, tot_n = join(near, (sent[0], sent[1][..., :HEADS], sent[1][..., HEADS:]))
    out_n = out_n.astype(BF)
    far = swap((out_n[:, ::-1], jnp.concatenate([top_n, tot_n], -1)[:, ::-1]), "patch", 2)
    out_j, top_j, tot_j = join(
        (out_n, top_n, tot_n), (far[0], far[1][..., :HEADS], far[1][..., HEADS:])
    )
    lse_j = top_j + jnp.log(tot_j)
    att_j = (
        out_j.reshape(out_j.shape[:-1] + (HEADS, head_size)) / tot_j[..., None]
    ).reshape(out_j.shape).astype(BF)
    att_o, lse_o = swap((att_j, lse_j), "patch", 1)
    attended = jnp.stack([att_j, att_o], axis=2).reshape(pairs, parts, lat_rows, inner)
    lse = jnp.stack([lse_j, lse_o], axis=2).reshape(pairs, lats, HEADS)
    lse = jnp.swapaxes(lse, 1, 2).reshape(micro, docs, 1, HEADS * lats)
    att_all = attended.reshape(all_rows, inner)

    unit = ff // (imgs * parts)
    w_exp = lax.dynamic_index_in_dim(
        w_expand.reshape(width, imgs, parts, unit), patch_index, 2, keepdims=False
    ).reshape(width, imgs * unit)
    w_red = lax.dynamic_index_in_dim(
        w_reduce.reshape(imgs, parts, unit, width), patch_index, 1, keepdims=False
    ).reshape(imgs * unit, width)
    mixed = latents_all.astype(F32) + dot(att_all, w_output, NN)
    ff_hat, ff_inv = standardize(mixed)
    ln_ff = (ff_hat * ff_gain + ff_shift).astype(BF)
    hidden_pre = dot(ln_ff, w_exp, NN)
    cdf = 0.5 * (1.0 + lax.erf(hidden_pre * (0.5**0.5)))
    slope = cdf + hidden_pre * (0.3989422804014327 * jnp.exp(-0.5 * hidden_pre * hidden_pre))
    hidden_act = (hidden_pre * cdf).astype(BF)
    grad_pre = (dot(cot_all, w_red, NT) * slope).astype(BF)
    up_part = dot(grad_pre, w_exp, NT).astype(BF)
    up_near, up_far = scatter_patch(by_owner(up_part))
    out_part = dot(hidden_act, w_red, NN).astype(BF)
    grad_expand = dot(ln_ff, grad_pre, TN).astype(BF)
    grad_reduce = dot(hidden_act, cot_all, TN).astype(BF)
    out_near, out_far = scatter_patch(by_owner(out_part))

    mixed_own = by_owner(mixed)[:, 0]
    latents_out = (mixed_own + (out_near.astype(F32) + out_far.astype(F32))).astype(BF)
    up = up_near.astype(F32) + up_far.astype(F32)
    norm_grad, ff_gain_part = norm_back(
        by_owner(ff_hat)[:, 0], by_owner(ff_inv)[:, 0], ff_gain, up
    )
    grad_mixed = cot_own.astype(F32) + norm_grad
    grad_branch = grad_mixed.astype(BF).reshape(own_rows, width)
    grad_att_own = dot(grad_branch, w_output, NT).astype(BF).reshape(pairs, lat_rows, inner)
    grad_att = gather_patch(grad_att_own)
    row_dot = jnp.sum(
        (grad_att.astype(F32) * attended.astype(F32)).reshape(
            pairs, lats, HEADS, head_size
        ),
        axis=-1,
    )
    row_dot = jnp.swapaxes(row_dot, 1, 2).reshape(micro, docs, 1, HEADS * lats)
    grad_att = grad_att.reshape(micro, docs, lats, inner)
    grad_output = dot(att_all.reshape(pairs, parts, lat_rows, inner)[:, 0].reshape(own_rows, inner), grad_branch, TN).astype(BF)

    shares = lax.psum_scatter(
        (grad_expand, grad_reduce), "img", scatter_dimension=0, tiled=True
    )

    back = [
        attend_back_call(g, doc_ids, queries, grad_att, kv_med, kv_lat, lse, row_dot, ln_med)
        for g in range(groups)
    ]
    w_keyval_t = w_keyval.T
    w_parts = [
        jnp.concatenate(
            [
                w_keyval_t[g * span : (g + 1) * span],
                w_keyval_t[inner + g * span : inner + (g + 1) * span],
            ]
        )
        for g in range(groups)
    ]
    media_grad, media_gain_part, media_shift_part = media_back_call(
        media.reshape(-1, width), back[0][0], back[1][0], w_parts[0], w_parts[1], media_gain[None]
    )

    gq_part = jnp.concatenate([b[2] for b in back], axis=-1)
    gq_near, gq_far = scatter_patch(gq_part.reshape(pairs, parts, lat_rows, inner))
    grad_q = ((gq_near.astype(F32) + gq_far.astype(F32)) * scale).astype(BF).reshape(own_rows, inner)
    lat_kv = [b[1].reshape(own_rows, 2 * span) for b in back]
    grad_query = dot(ln_lat, grad_q, TN).astype(BF)
    grad_ln_lat = dot(grad_q, w_query, NT)
    for g in range(groups):
        grad_ln_lat = grad_ln_lat + dot(lat_kv[g], w_parts[g], NN)
    latent_back, latent_gain_part = norm_back(lat_hat, lat_inv, latent_gain, grad_ln_lat)
    latents_grad = (grad_mixed.reshape(own_rows, width) + latent_back).astype(BF)

    def split(value):
        return value.reshape((imgs, parts, value.shape[0] // (imgs * parts)) + value.shape[1:])

    keyval_rows = [
        reduce_all(split((b[3].astype(F32) + dot(ln_lat, lat_kv[g], TN)).astype(BF)))
        for g, b in enumerate(back)
    ]
    grad_keyval = jnp.concatenate(
        [rows[:, at * span : (at + 1) * span] for at in range(2) for rows in keyval_rows], axis=1
    )
    out_rows = reduce_all(split(grad_output))
    query_rows = reduce_all(split(grad_query))
    vectors = jnp.stack(
        [
            media_gain_part[0],
            media_shift_part[0],
            jnp.sum(latent_gain_part, axis=0),
            jnp.sum(grad_ln_lat, axis=0),
            jnp.sum(ff_gain_part, axis=(0, 1)),
            jnp.sum(up, axis=(0, 1)),
        ],
        axis=1,
    )
    vectors = lax.psum(lax.psum_scatter(vectors, "img", scatter_dimension=0, tiled=True), "patch")

    expand_rows = gather_rows(shares[0].reshape(-1, imgs, unit))
    expand_rows = jnp.transpose(expand_rows, (1, 2, 0, 3)).reshape(-1, ff).astype(F32)
    reduce_rows = gather_rows(shares[1]).reshape(-1, width).astype(F32)

    return (
        latents_out.reshape(latents.shape),
        latents_grad.reshape(latents.shape),
        media_grad.reshape(media.shape),
        query_rows,
        grad_keyval,
        out_rows,
        expand_rows,
        reduce_rows,
    ) + tuple(vectors[:, i] for i in range(6))


def solution(mesh):
    tokens = P(None, "img", "patch", None)
    return jax.shard_map(
        local,
        mesh=mesh,
        in_specs=(tokens, tokens, P(None, "img")) + (P(),) * 11 + (tokens,),
        out_specs=(tokens,) * 3 + (P("img", None),) * 5 + (P("img"),) * 6,
        check_vma=False,
    )
```

```python
import functools

import jax
import jax.numpy as jnp
from jax import lax
from jax.experimental import pallas as pl
from jax.experimental.pallas import tpu as pltpu
from jax.sharding import PartitionSpec as P

HEADS = 8
GROUP = 4
EPS = 1e-05
CHUNK = 4
FAR = -1e30
BF = jnp.bfloat16
F32 = jnp.float32
VMEM = 56 * 1024 * 1024
ANY = pl.BlockSpec(memory_space=pl.ANY)


def params(n=1):
    return pltpu.CompilerParams(
        vmem_limit_bytes=VMEM, dimension_semantics=("arbitrary",) * n
    )


def cost(us):
    return pl.CostEstimate(flops=int(us * 1.1e9), bytes_accessed=0, transcendentals=0)


def nothing_kernel(*refs):
    pass


def gate(carry, deps):
    return pl.pallas_call(
        nothing_kernel,
        in_specs=[ANY] * (len(carry) + len(deps)),
        out_specs=[ANY] * len(carry),
        out_shape=[jax.ShapeDtypeStruct(c.shape, c.dtype) for c in carry],
        input_output_aliases={i: i for i in range(len(carry))},
        name="gate",
    )(*carry, *deps)


def dot(a, b, dims):
    return lax.dot_general(a, b, (dims, ((), ())), preferred_element_type=F32)


NN = ((1,), (0,))
NT = ((1,), (1,))
TN = ((0,), (0,))


def standardize(values):
    center = values - jnp.mean(values, axis=-1, keepdims=True)
    inv = lax.rsqrt(jnp.mean(center * center, axis=-1, keepdims=True) + EPS)
    return center * inv, inv


def norm_back(hat, inv, gain, upstream):
    scaled = upstream * gain
    back = inv * (
        scaled
        - jnp.mean(scaled, axis=-1, keepdims=True)
        - hat * jnp.mean(scaled * hat, axis=-1, keepdims=True)
    )
    return back, upstream * hat


def kv_kernel(media_ref, gain_ref, shift_ref, w_ref, hat_ref, kv_ref):
    rows = media_ref.shape[0]
    step = min(rows, 256)
    for at in range(0, rows, step):
        part = pl.ds(at, step)
        hat, _ = standardize(media_ref[part, :].astype(F32))
        ln = (hat * gain_ref[...] + shift_ref[...]).astype(BF)
        hat_ref[part, :] = hat.astype(BF)
        kv_ref[part, :] = dot(ln, w_ref[...], NN).astype(BF)


def kv_call(media, gain, shift, w_keyval):
    rows, width = media.shape
    outs = w_keyval.shape[1]
    block = 512
    return pl.pallas_call(
        kv_kernel,
        grid=(rows // block,),
        in_specs=[
            pl.BlockSpec((block, width), lambda i: (i, 0)),
            pl.BlockSpec((1, width), lambda i: (0, 0)),
            pl.BlockSpec((1, width), lambda i: (0, 0)),
            pl.BlockSpec((width, outs), lambda i: (0, 0)),
        ],
        out_specs=[
            pl.BlockSpec((block, width), lambda i: (i, 0)),
            pl.BlockSpec((block, outs), lambda i: (i, 0)),
        ],
        out_shape=[
            jax.ShapeDtypeStruct((rows, width), BF),
            jax.ShapeDtypeStruct((rows, outs), BF),
        ],
        compiler_params=params(),
        cost_estimate=cost(16),
        name="media_keyval",
    )(media, gain, shift, w_keyval)


def block_mask(head_size, lats):
    rows = GROUP * lats
    cols = GROUP * head_size
    row_head = lax.broadcasted_iota(jnp.int32, (rows, cols), 0) // lats
    col_head = lax.broadcasted_iota(jnp.int32, (rows, cols), 1) // head_size
    return row_head == col_head


def spread_heads(values, mask):
    tiled = jnp.concatenate([values] * GROUP, axis=0)
    return jnp.where(mask, tiled, jnp.zeros_like(tiled))


def gather_heads(full, mask, lats):
    kept = jnp.where(mask, full, 0.0)
    total = kept[:lats]
    for head in range(1, GROUP):
        total = total + kept[head * lats : (head + 1) * lats]
    return total


LANES = 128


def terms(value):
    first = value.astype(BF)
    rest = value - first.astype(F32)
    second = rest.astype(BF)
    return first, second, (rest - second.astype(F32)).astype(BF)


def pick(shape, fn):
    row = lax.broadcasted_iota(jnp.int32, shape, 0)
    col = lax.broadcasted_iota(jnp.int32, shape, 1)
    return jnp.where(fn(row, col), 1.0, 0.0).astype(BF)


def holds(lane, head, figure):
    return (lane < 24 * figure + 24) & (lane >= 24 * figure) & (lane % HEADS == head)


def pack_rows(figures):
    rows = jnp.concatenate([t for f in figures for t in terms(f)], axis=0)
    eye = pick((rows.shape[0], LANES), lambda r, c: r == c)
    return dot(rows, eye, TN).astype(BF)


def pack_cols(figures):
    total = None
    for i, figure in enumerate(figures):
        for k, term in enumerate(terms(figure)):
            at = HEADS * (3 * i + k)
            place = pick((LANES, LANES), lambda r, c: (r < HEADS) & (c == r + at))
            part = dot(term, place, NN)
            total = part if total is None else total + part
    return total.astype(BF)


def widen(packed, figure, inner):
    size = inner // HEADS
    return dot(packed, pick((LANES, inner), lambda r, c: holds(r, c // size, figure)), NN)


def narrow(packed, figure):
    return dot(
        packed, pick((LANES, LANES), lambda r, c: (c < HEADS) & holds(r, c, figure)), NN
    )


def doc_rows(ref, d, lat_rows, cols):
    rows = slice(d * lat_rows, (d + 1) * lat_rows)
    return jnp.concatenate([ref[c, rows, cols] for c in range(ref.shape[0])], axis=0)


def doc_spans(doc_ref, micro, docs, slots):
    counts = []
    for d in range(docs):
        total = 0
        for s in range(slots):
            total = total + jnp.where(doc_ref[micro, s] == d, 1, 0)
        counts.append(total)
    first = 0
    spans = []
    for count in counts:
        spans.append((first, count))
        first = first + count
    return spans


def slot_chunk(span, step, slots):
    first, count = span
    low = first + step * CHUNK
    return jnp.minimum(low, slots - CHUNK), low, first + count


def own_rows_of(at, low, high, keys):
    slot = at + lax.broadcasted_iota(jnp.int32, (CHUNK * keys, 1), 0) // keys
    return (slot >= low) & (slot < high)


def steps_of(span):
    return (span[1] + CHUNK - 1) // CHUNK


def attend_kernel(deps, doc_ref, q_ref, kv_ref, kvl_ref, *rest):
    keep_ref, send_ref, bd, score, acc, top, tot = rest[deps:]
    chunks, rows, inner = q_ref.shape
    docs, lat_rows = kvl_ref.shape[1:3]
    lats = chunks * lat_rows
    slots, keys = kv_ref.shape[1:3]
    groups = HEADS // GROUP
    span = inner // groups
    micro = pl.program_id(0)
    mask = block_mask(inner // HEADS, lats)
    cols = [slice(g * span, (g + 1) * span) for g in range(groups)]
    vals = [slice(inner + g * span, inner + (g + 1) * span) for g in range(groups)]
    spans = doc_spans(doc_ref, micro, docs, slots)
    tall = CHUNK * keys

    def load(at, part):
        return kv_ref[0, pl.ds(at, CHUNK), :, part].reshape(tall, span)

    for d in range(docs):
        at, low, high = slot_chunk(spans[d], 0, slots)
        bias = jnp.where(own_rows_of(at, low, high, keys), 0.0, FAR)
        bias = jnp.concatenate([bias, jnp.zeros((lat_rows, 1), F32)], axis=0)
        for g in range(groups):
            spread = spread_heads(doc_rows(q_ref, d, lat_rows, cols[g]), mask)
            bd[d, g] = spread
            key = jnp.concatenate([load(at, cols[g]), kvl_ref[0, d, :, cols[g]]], axis=0)
            val = dot(key, spread, NT) + bias
            score[d, g, 0] = val
            top[d, g] = jnp.max(val, axis=0, keepdims=True)
    for d in range(docs):

        def more(step, carry, d=d):
            at, low, high = slot_chunk(spans[d], step, slots)
            bias = jnp.where(own_rows_of(at, low, high, keys), 0.0, FAR)
            for g in range(groups):
                val = dot(load(at, cols[g]), bd[d, g], NT) + bias
                score[d, g, step, :tall] = val
                top[d, g] = jnp.maximum(top[d, g], jnp.max(val, axis=0, keepdims=True))
            return carry

        lax.fori_loop(1, steps_of(spans[d]), more, 0)
    for d in range(docs):
        at, low, high = slot_chunk(spans[d], 0, slots)
        for g in range(groups):
            expo = jnp.exp(score[d, g, 0] - top[d, g])
            tot[d, g] = jnp.sum(expo, axis=0, keepdims=True)
            val = jnp.concatenate([load(at, vals[g]), kvl_ref[0, d, :, vals[g]]], axis=0)
            acc[d, g] = dot(expo.astype(BF), val, TN)
    for d in range(docs):

        def more_values(step, carry, d=d):
            at, low, high = slot_chunk(spans[d], step, slots)
            for g in range(groups):
                expo = jnp.exp(score[d, g, step, :tall] - top[d, g])
                tot[d, g] = tot[d, g] + jnp.sum(expo, axis=0, keepdims=True)
                acc[d, g] = acc[d, g] + dot(expo.astype(BF), load(at, vals[g]), TN)
            return carry

        lax.fori_loop(1, steps_of(spans[d]), more_values, 0)
    half = chunks // 2
    for d in range(docs):
        rows_d = slice(d * lat_rows, (d + 1) * lat_rows)

        def by_head(ref):
            return jnp.concatenate(
                [
                    ref[d, g][:, h * lats : (h + 1) * lats]
                    for g in range(groups)
                    for h in range(GROUP)
                ],
                axis=0,
            )

        packed = pack_rows([by_head(top), by_head(tot)])
        outs = [gather_heads(acc[d, g], mask, lats).astype(BF) for g in range(groups)]
        for c in range(chunks):
            ref = keep_ref if c < half else send_ref
            part = slice(c * lat_rows, (c + 1) * lat_rows)
            for g in range(groups):
                ref[c % half, rows_d, cols[g]] = outs[g][part]
            ref[c % half, rows_d, inner:] = packed[part]


def attend_call(doc_ids, queries, kv_med, kv_lat, deps):
    chunks, _, inner = queries.shape
    micro, slots, keys, both = kv_med.shape
    docs, lat_rows = kv_lat.shape[1:3]
    lats = chunks * lat_rows
    rows = docs * lat_rows
    groups = HEADS // GROUP
    span = inner // groups
    wide = GROUP * lats
    half = chunks // 2
    longest = (slots - docs + CHUNK) // CHUNK
    out_spec = pl.BlockSpec((half, rows, inner + LANES), lambda i, ids: (0, i, 0))
    out_shape = jax.ShapeDtypeStruct((half, micro * rows, inner + LANES), BF)
    return pl.pallas_call(
        functools.partial(attend_kernel, len(deps)),
        grid_spec=pltpu.PrefetchScalarGridSpec(
            num_scalar_prefetch=1,
            grid=(micro,),
            in_specs=[
                pl.BlockSpec((chunks, rows, inner), lambda i, ids: (0, i, 0)),
                pl.BlockSpec((1, slots, keys, both), lambda i, ids: (i, 0, 0, 0)),
                pl.BlockSpec((1, docs, lat_rows, both), lambda i, ids: (i, 0, 0, 0)),
            ]
            + [ANY] * len(deps),
            out_specs=[out_spec, out_spec],
            scratch_shapes=[
                pltpu.VMEM((docs, groups, wide, span), BF),
                pltpu.VMEM((docs, groups, longest, CHUNK * keys + lat_rows, wide), F32),
                pltpu.VMEM((docs, groups, wide, span), F32),
                pltpu.VMEM((docs, groups, 1, wide), F32),
                pltpu.VMEM((docs, groups, 1, wide), F32),
            ],
        ),
        out_shape=[out_shape, out_shape],
        compiler_params=params(),
        cost_estimate=cost(13),
        name="attend",
    )(doc_ids, queries, kv_med, kv_lat, *deps)


def join_kernel(last, flip, a_ref, b_ref, *rest):
    out_ref = rest[-1]
    inner = a_ref.shape[2] - LANES
    count = a_ref.shape[0]
    for c in range(count):
        first, second = a_ref[c], b_ref[count - 1 - c if flip else c]
        pack_a, pack_b = first[:, inner:], second[:, inner:]
        top_a, top_b = widen(pack_a, 0, inner), widen(pack_b, 0, inner)
        best = jnp.maximum(top_a, top_b)
        fac_a, fac_b = jnp.exp(top_a - best), jnp.exp(top_b - best)
        out = fac_a * first[:, :inner].astype(F32) + fac_b * second[:, :inner].astype(F32)
        if last:
            total = fac_a * widen(pack_a, 1, inner) + fac_b * widen(pack_b, 1, inner)
            out = out / total
        out_ref[c, :, :inner] = out.astype(BF)
        small_a, small_b = narrow(pack_a, 0), narrow(pack_b, 0)
        small = jnp.maximum(small_a, small_b)
        sum_ab = jnp.exp(small_a - small) * narrow(pack_a, 1) + jnp.exp(
            small_b - small
        ) * narrow(pack_b, 1)
        if last:
            lane = lax.broadcasted_iota(jnp.int32, sum_ab.shape, 1)
            lse = jnp.where(lane < HEADS, small + jnp.log(jnp.maximum(sum_ab, 1e-30)), 0.0)
            out_ref[c, :, inner:] = pack_cols([lse])
        else:
            out_ref[c, :, inner:] = pack_cols([small, sum_ab])


def join_call(first, second, last, flip, deps=()):
    count, rows, cols = first.shape
    block = min(rows, 128)
    spec = pl.BlockSpec((count, block, cols), lambda i: (0, i, 0))
    return pl.pallas_call(
        functools.partial(join_kernel, last, flip),
        grid=(rows // block,),
        in_specs=[spec, spec] + [ANY] * len(deps),
        out_specs=spec,
        out_shape=jax.ShapeDtypeStruct(first.shape, BF),
        compiler_params=params(),
        cost_estimate=cost(3.5),
        name="join_last" if last else "join_first",
    )(first, second, *deps)


def ff_kernel(
    lat_ref,
    near_ref,
    far_ref,
    cot_ref,
    wo_ref,
    we_ref,
    wr_ref,
    gain_ref,
    shift_ref,
    mixed_ref,
    ln_ref,
    act_ref,
    gpre_ref,
    up_keep,
    up_send,
    out_keep,
    out_send,
):
    i = pl.program_id(0)
    half = pl.num_programs(0) // 2
    att = jnp.where(i < half, near_ref[0], far_ref[0])
    mixed = lat_ref[0].astype(F32) + dot(att, wo_ref[...], NN)
    hat, _ = standardize(mixed)
    ln = (hat * gain_ref[...] + shift_ref[...]).astype(BF)
    ln_ref[0] = ln
    pre = dot(ln, we_ref[...], NN)
    cdf = 0.5 + 0.5 * lax.erf(pre * (0.5**0.5))
    slope = cdf + pre * (0.3989422804014327 * jnp.exp(-0.5 * pre * pre))
    act = (pre * cdf).astype(BF)
    act_ref[0] = act
    gpre = (dot(cot_ref[0], wr_ref[...], NT) * slope).astype(BF)
    gpre_ref[0] = gpre
    up = dot(gpre, we_ref[...], NT).astype(BF)
    out = dot(act, wr_ref[...], NN).astype(BF)

    @pl.when(i == 0)
    def _():
        mixed_ref[...] = mixed

    @pl.when(i < half)
    def _():
        up_keep[0] = up
        out_keep[0] = out

    @pl.when(i >= half)
    def _():
        up_send[0] = up
        out_send[0] = out


def ff_call(latents, near, far, cot, w_output, w_exp, w_red, gain, shift):
    chunks, rows, width = latents.shape
    inner = w_output.shape[0]
    units = w_exp.shape[1]
    half = chunks // 2

    def chunk(cols):
        return pl.BlockSpec((1, rows, cols), lambda i: (i, 0, 0))

    def first(cols):
        return pl.BlockSpec((1, rows, cols), lambda i: (jnp.minimum(i, half - 1), 0, 0))

    def second(cols):
        return pl.BlockSpec((1, rows, cols), lambda i: (jnp.maximum(i - half, 0), 0, 0))

    def fixed(*shape):
        return pl.BlockSpec(shape, lambda i: (0,) * len(shape))

    def out(count, cols):
        return jax.ShapeDtypeStruct((count, rows, cols), BF)

    return pl.pallas_call(
        ff_kernel,
        grid=(chunks,),
        in_specs=[
            chunk(width),
            first(inner),
            second(inner),
            chunk(width),
            fixed(inner, width),
            fixed(width, units),
            fixed(units, width),
            fixed(1, width),
            fixed(1, width),
        ],
        out_specs=[
            fixed(rows, width),
            chunk(width),
            chunk(units),
            chunk(units),
            first(width),
            second(width),
            first(width),
            second(width),
        ],
        out_shape=[
            jax.ShapeDtypeStruct((rows, width), F32),
            out(chunks, width),
            out(chunks, units),
            out(chunks, units),
            out(half, width),
            out(half, width),
            out(half, width),
            out(half, width),
        ],
        compiler_params=params(),
        cost_estimate=cost(18),
        name="feed_forward",
    )(latents, near, far, cot, w_output, w_exp, w_red, gain, shift)


def ff_weights_kernel(ln_ref, gpre_ref, act_ref, cot_ref, *rest):
    out_ref = rest[-1]
    count, rows, width = out_ref.shape
    half = rows // 2
    for part, (left, right) in enumerate(((ln_ref, gpre_ref), (act_ref, cot_ref))):
        product = dot(left[...], right[...], TN).astype(BF)
        out_ref[:, part * half : (part + 1) * half, :] = product.reshape(count, half, width)


def ff_weights_call(ln_ff, grad_pre, hidden_act, cot, imgs, deps):
    tokens, width = ln_ff.shape
    units = grad_pre.shape[1]
    half = units // imgs
    steps = 2
    left = pl.BlockSpec((tokens, width // steps), lambda i: (0, i))
    right = pl.BlockSpec((tokens, width), lambda i: (0, 0))
    return pl.pallas_call(
        ff_weights_kernel,
        grid=(steps,),
        in_specs=[left, right, left, right] + [ANY] * len(deps),
        out_specs=pl.BlockSpec((imgs // steps, 2 * half, width), lambda i: (i, 0, 0)),
        out_shape=jax.ShapeDtypeStruct((imgs, 2 * half, width), BF),
        compiler_params=params(),
        cost_estimate=cost(9),
        name="ff_weights",
    )(ln_ff, grad_pre, hidden_act, cot, *deps)


def mixed_back_kernel(near_ref, far_ref, mixed_ref, cot_ref, wo_ref, gain_ref, *rest):
    gm_ref, gb_ref, ga_ref, dg_ref, ds_ref = rest[-5:]
    up = near_ref[...].astype(F32) + far_ref[...].astype(F32)
    hat, inv = standardize(mixed_ref[...])
    back, gains = norm_back(hat, inv, gain_ref[...], up)
    grad = cot_ref[...].astype(F32) + back
    gm_ref[...] = grad
    branch = grad.astype(BF)
    gb_ref[...] = branch
    ga_ref[...] = dot(branch, wo_ref[...], NT).astype(BF)
    dg_ref[...] = jnp.sum(gains, axis=0, keepdims=True)
    ds_ref[...] = jnp.sum(up, axis=0, keepdims=True)


def mixed_back_call(near, far, mixed, cot, w_output, gain, deps):
    rows, width = mixed.shape
    inner = w_output.shape[0]
    return pl.pallas_call(
        mixed_back_kernel,
        in_specs=[pl.BlockSpec(memory_space=pltpu.VMEM)] * 6 + [ANY] * len(deps),
        out_shape=[
            jax.ShapeDtypeStruct((rows, width), F32),
            jax.ShapeDtypeStruct((rows, width), BF),
            jax.ShapeDtypeStruct((rows, inner), BF),
            jax.ShapeDtypeStruct((1, width), F32),
            jax.ShapeDtypeStruct((1, width), F32),
        ],
        compiler_params=pltpu.CompilerParams(vmem_limit_bytes=VMEM),
        cost_estimate=cost(4),
        name="mixed_back",
    )(near, far, mixed, cot, w_output, gain, *deps)


def part_kernel(index_ref, e_ref, r_ref, eo_ref, ro_ref):
    eo_ref[...] = e_ref[...]
    ro_ref[...] = r_ref[...]


def part_call(index, w_expand, w_reduce, imgs, parts):
    width, ff = w_expand.shape
    unit = ff // (imgs * parts)
    return pl.pallas_call(
        part_kernel,
        grid_spec=pltpu.PrefetchScalarGridSpec(
            num_scalar_prefetch=1,
            grid=(imgs,),
            in_specs=[
                pl.BlockSpec((width, unit), lambda i, p: (0, i * parts + p[0])),
                pl.BlockSpec((unit, width), lambda i, p: (i * parts + p[0], 0)),
            ],
            out_specs=[
                pl.BlockSpec((width, unit), lambda i, p: (0, i)),
                pl.BlockSpec((unit, width), lambda i, p: (i, 0)),
            ],
        ),
        out_shape=[
            jax.ShapeDtypeStruct((width, imgs * unit), BF),
            jax.ShapeDtypeStruct((imgs * unit, width), BF),
        ],
        compiler_params=params(),
        name="weight_part",
    )(index, w_expand, w_reduce)


def attend_back_kernel(
    group,
    deps,
    doc_ref,
    index_ref,
    q_ref,
    go_ref,
    att_ref,
    lse_ref,
    k_ref,
    v_ref,
    kl_ref,
    vl_ref,
    hat_ref,
    lat_hat_ref,
    wk_ref,
    wv_ref,
    wq_ref,
    norm_ref,
    extra_ref,
    vec_in,
    *rest,
):
    gkv_ref, gkvl_ref, gq_ref, keep_ref, send_ref, vec_ref = rest[deps : deps + 6]
    bdq, bdo, acc, stat, h_med, h_lat, sums, wide_rows = rest[deps + 6 :]
    chunks, _, span = q_ref.shape
    docs, lat_rows = kl_ref.shape[1:3]
    lats = chunks * lat_rows
    slots, keys = k_ref.shape[1:3]
    micro = pl.program_id(0)
    mask = block_mask(span // GROUP, lats)
    every = slice(None)
    scale = (span // GROUP) ** (-0.5)

    spans = doc_spans(doc_ref, micro, docs, slots)
    tall = CHUNK * keys

    def pair(key, value, bias, d):
        score = dot(key, bdq[d], NT) + bias
        prob = jnp.exp(score - stat[d, 0:1])
        dprob = dot(value, bdo[d], NT)
        dscore = (prob * (dprob - stat[d, 1:2])).astype(BF)
        grad_key = dot(dscore, bdq[d], NN).astype(BF)
        grad_value = dot(prob.astype(BF), bdo[d], NN).astype(BF)
        grad_query = dot(dscore, key, TN)
        return grad_key, grad_value, grad_query

    def load(ref, at):
        return ref[0, pl.ds(at, CHUNK)].reshape(tall, span)

    def store(at, own, grad_key, grad_value):
        part = pl.ds(pl.multiple_of(at * keys, keys), tall)
        gkv_ref[part, :span] = jnp.where(own, grad_key, gkv_ref[part, :span])
        gkv_ref[part, span:] = jnp.where(own, grad_value, gkv_ref[part, span:])

    sel = pick((HEADS, LANES), lambda r, c: holds(c, r, 0))
    size = span // GROUP
    head_sel = pick((HEADS, span), lambda r, c: c // size == r)

    def row(by_head, at):
        return jnp.concatenate([by_head[at + h : at + h + 1] for h in range(GROUP)], axis=1)

    for d in range(docs):
        out_grad = doc_rows(go_ref, d, lat_rows, every)
        bdq[d] = spread_heads(doc_rows(q_ref, d, lat_rows, every), mask)
        bdo[d] = spread_heads(out_grad, mask)
        lse = dot(sel, doc_rows(lse_ref, d, lat_rows, every), NT)
        stat[d, 0:1] = row(lse, group * GROUP)
        attended = doc_rows(att_ref, d, lat_rows, every)
        high, low, _ = terms(out_grad.astype(F32) * attended.astype(F32))
        stat[d, 1:2] = row(dot(head_sel, high, NT) + dot(head_sel, low, NT), 0)
    for d in range(docs):
        rows_d = slice(d * lat_rows, (d + 1) * lat_rows)
        at, low, high = slot_chunk(spans[d], 0, slots)
        own = own_rows_of(at, low, high, keys)
        bias = jnp.concatenate([jnp.where(own, 0.0, FAR), jnp.zeros((lat_rows, 1), F32)], axis=0)
        key = jnp.concatenate([load(k_ref, at), kl_ref[0, d]], axis=0)
        value = jnp.concatenate([load(v_ref, at), vl_ref[0, d]], axis=0)
        grad_key, grad_value, grad_query = pair(key, value, bias, d)
        store(at, own, grad_key[:tall], grad_value[:tall])
        gkvl_ref[rows_d, :span] = grad_key[tall:]
        gkvl_ref[rows_d, span:] = grad_value[tall:]
        acc[d] = grad_query
    for d in range(docs):

        def more(step, carry, d=d):
            at, low, high = slot_chunk(spans[d], step, slots)
            own = own_rows_of(at, low, high, keys)
            grad_key, grad_value, grad_query = pair(
                load(k_ref, at), load(v_ref, at), jnp.where(own, 0.0, FAR), d
            )
            store(at, own, grad_key, grad_value)
            acc[d] = acc[d] + grad_query
            return carry

        lax.fori_loop(1, steps_of(spans[d]), more, 0)
    for d in range(docs):
        full = gather_heads(acc[d], mask, lats).astype(BF)
        for c in range(chunks):
            gq_ref[c, pl.ds(micro * docs * lat_rows + d * lat_rows, lat_rows)] = full[
                c * lat_rows : (c + 1) * lat_rows
            ]
    part = dot(hat_ref[...], gkv_ref[...], TN)
    part_sum = dot(jnp.ones((8, gkv_ref.shape[0]), BF), gkv_ref[...], NN)[0:1]
    lat_part = dot(lat_hat_ref[0, pl.ds(micro * docs * lat_rows, docs * lat_rows)], gkvl_ref[...], TN)
    lat_sum_part = jnp.sum(gkvl_ref[...].astype(F32), axis=0, keepdims=True)

    @pl.when(micro == 0)
    def _():
        h_med[...] = part
        h_lat[...] = lat_part
        sums[0:1, :] = part_sum
        sums[1:2, :] = lat_sum_part

    @pl.when(micro > 0)
    def _():
        h_med[...] = h_med[...] + part
        h_lat[...] = h_lat[...] + lat_part
        sums[0:1, :] = sums[0:1, :] + part_sum
        sums[1:2, :] = sums[1:2, :] + lat_sum_part

    @pl.when(micro == pl.num_programs(0) - 1)
    def _():
        width = h_med.shape[0]
        step = 128
        tokens = lat_hat_ref.shape[0] * lat_hat_ref.shape[1]
        quer_all = gq_ref[...].reshape(tokens, span)
        h_q = dot(lat_hat_ref[...].reshape(tokens, width), quer_all, TN)
        quer_sum = dot(jnp.ones((8, tokens), BF), quer_all, NN)[0:1] * scale
        for at in range(0, width, step):
            part = slice(at, at + step)
            norm = norm_ref[part, :]
            med, lat, quer = h_med[part, :], h_lat[part, :], h_q[part] * scale
            med_sum, lat_sum = sums[0:1, :], sums[1:2, :]
            wide_rows[part, : 2 * span] = (
                norm[:, 0:1] * med
                + norm[:, 1:2] * med_sum
                + norm[:, 2:3] * lat
                + norm[:, 3:4] * lat_sum
            ).astype(BF)
            wide_rows[part, 2 * span :] = (
                norm[:, 2:3] * quer + norm[:, 3:4] * quer_sum
            ).astype(BF)
            wkv = jnp.concatenate([wk_ref[part, :], wv_ref[part, :]], axis=1).astype(F32)
            wq = wq_ref[part, :].astype(F32)

            def total(value):
                return jnp.sum(value, axis=1, keepdims=True)

            vec = jnp.concatenate(
                [
                    total(wkv * med),
                    total(wkv * med_sum),
                    total(wkv * lat) + total(wq * quer),
                    total(wkv * lat_sum) + total(wq * quer_sum),
                    jnp.zeros((step, step - 4), F32),
                ],
                axis=1,
            )
            vec_ref[:, part] = vec_in[:, part] + vec.T[: vec_ref.shape[0]]
        if len(keep_ref.shape) == 2:
            keep_ref[...] = wide_rows[...]
            return
        imgs, two, height, _ = keep_ref.shape
        share = width // imgs
        tall = share // (2 * two)
        bit = lax.rem(index_ref[0], 2)
        for ref, mine in ((keep_ref, bit), (send_ref, 1 - bit)):
            for i in range(imgs):
                for y in range(two):
                    at = pl.multiple_of(i * share + 2 * y * tall + mine * tall, tall)
                    rows = wide_rows[pl.ds(at, tall), :]
                    ref[i, y, :tall] = rows[:, : 2 * span]
                    ref[i, y, tall : tall + tall // 2, :span] = rows[: tall // 2, 2 * span :]
                    ref[i, y, tall : tall + tall // 2, span:] = rows[tall // 2 :, 2 * span :]
                    start = tall + tall // 2
                    if group == 0:
                        size = extra_ref.shape[0] // (2 * two * imgs)
                        at = pl.multiple_of((i * two + y) * 2 * size + mine * size, size)
                        rows = extra_ref[pl.ds(at, size), :]
                        ref[i, y, start : start + size] = rows[:, : 2 * span]
                        ref[i, y, start + size : start + 2 * size] = rows[:, 2 * span :]
                    else:
                        rows = jnp.zeros((height - start, 2 * span), F32)
                        if y == 0:
                            at = slice(i * share, (i + 1) * share)
                            six = jnp.concatenate([vec_ref[:4, at], extra_ref[:2, at]], axis=0)
                            six = jnp.where(mine == 0, six, 0.0)
                            six = jnp.pad(six, ((0, height - start - 6), (0, 2 * span - share)))
                            rows = six
                        ref[i, y, start:] = rows.astype(BF)


def laid_out(width, imgs, inner):
    share = width // imgs
    return share % 128 == 0 and share <= inner and inner % (64 * imgs) == 0


def attend_back_call(
    group,
    doc_ids,
    queries,
    grad_att,
    att,
    kv_med,
    kv_lat,
    hat_med,
    hat_lat,
    w_keyval,
    w_query,
    norms,
    extra,
    vectors,
    index,
    imgs,
    deps,
):
    chunks, _, inner = queries.shape
    micro, slots, keys, both = kv_med.shape
    docs, lat_rows = kv_lat.shape[1:3]
    lats = chunks * lat_rows
    width = hat_med.shape[1]
    groups = HEADS // GROUP
    span = inner // groups
    wide = GROUP * lats
    rows = slots * keys
    lat_block = docs * lat_rows

    if laid_out(width, imgs, inner):
        tall = width // (imgs * chunks)
        height = tall + tall // 2 + (2 * inner // (imgs * chunks) if group == 0 else 16)
        result = jax.ShapeDtypeStruct((imgs, chunks // 2, height, inner), BF)
    else:
        result = jax.ShapeDtypeStruct((width, 3 * span), BF)
    result_spec = pl.BlockSpec(result.shape, lambda i, ids, p: (0,) * len(result.shape))

    def cols(at, *tail):
        return pl.BlockSpec(
            (1,) + tail, lambda i, ids, p: (i,) + (0,) * (len(tail) - 1) + (at,)
        )

    def tokens(at, size):
        return pl.BlockSpec((chunks, lat_block, size), lambda i, ids, p: (0, i, at))

    def fixed(at, size):
        return pl.BlockSpec((width, size), lambda i, ids, p: (0, at))

    return pl.pallas_call(
        functools.partial(attend_back_kernel, group, len(deps)),
        grid_spec=pltpu.PrefetchScalarGridSpec(
            num_scalar_prefetch=2,
            grid=(micro,),
            in_specs=[
                tokens(group, span),
                tokens(group, span),
                tokens(group, span),
                tokens(inner // LANES, LANES),
                cols(group, slots, keys, span),
                cols(groups + group, slots, keys, span),
                cols(group, docs, lat_rows, span),
                cols(groups + group, docs, lat_rows, span),
                pl.BlockSpec((rows, width), lambda i, ids, p: (i, 0)),
                pl.BlockSpec(hat_lat.shape, lambda i, ids, p: (0, 0, 0)),
                fixed(group, span),
                fixed(groups + group, span),
                fixed(group, span),
                fixed(0, norms.shape[1]),
                pl.BlockSpec(extra.shape, lambda i, ids, p: (0, 0)),
                pl.BlockSpec(vectors.shape, lambda i, ids, p: (0, 0)),
            ]
            + [ANY] * len(deps),
            out_specs=[
                pl.BlockSpec((rows, 2 * span), lambda i, ids, p: (i, 0)),
                pl.BlockSpec((lat_block, 2 * span), lambda i, ids, p: (i, 0)),
                pl.BlockSpec((chunks, micro * lat_block, span), lambda i, ids, p: (0, 0, 0)),
                result_spec,
                result_spec,
                pl.BlockSpec(vectors.shape, lambda i, ids, p: (0, 0)),
            ],
            scratch_shapes=[
                pltpu.VMEM((docs, wide, span), BF),
                pltpu.VMEM((docs, wide, span), BF),
                pltpu.VMEM((docs, wide, span), F32),
                pltpu.VMEM((docs, 2, wide), F32),
                pltpu.VMEM((width, 2 * span), F32),
                pltpu.VMEM((width, 2 * span), F32),
                pltpu.VMEM((2, 2 * span), F32),
                pltpu.VMEM((width, 3 * span), BF),
            ],
        ),
        out_shape=[
            jax.ShapeDtypeStruct((micro * rows, 2 * span), BF),
            jax.ShapeDtypeStruct((micro * lat_block, 2 * span), BF),
            jax.ShapeDtypeStruct((chunks, micro * lat_block, span), BF),
            result,
            result,
            jax.ShapeDtypeStruct(vectors.shape, F32),
        ],
        compiler_params=params(),
        cost_estimate=cost(27),
        name="attend_back",
    )(
        doc_ids,
        index,
        queries,
        grad_att,
        att,
        att,
        kv_med,
        kv_med,
        kv_lat,
        kv_lat,
        hat_med,
        hat_lat,
        w_keyval,
        w_keyval,
        w_query,
        norms,
        extra,
        vectors,
        *deps,
    )


def media_back_kernel(media_ref, ga_ref, gb_ref, wa_ref, wb_ref, gain_ref, *rest):
    out_ref = rest[-1]
    rows = media_ref.shape[0]
    step = min(rows, 256)

    for at in range(0, rows, step):
        part = pl.ds(at, step)
        up = dot(ga_ref[part, :], wa_ref[...], NN) + dot(gb_ref[part, :], wb_ref[...], NN)
        hat, inv = standardize(media_ref[part, :].astype(F32))
        back, _ = norm_back(hat, inv, gain_ref[...], up)
        out_ref[part, :] = back.astype(BF)


def media_back_call(media, grad_a, grad_b, w_a, w_b, gain, first, steps, whole, deps):
    rows, width = media.shape
    half = grad_a.shape[1]
    block = 512
    fixed = lambda i: (0, 0)
    moving = lambda i: (first + i, 0)
    extra = tuple(deps) if whole is None else tuple(deps) + (whole,)
    return pl.pallas_call(
        media_back_kernel,
        grid=(steps,),
        in_specs=[
            pl.BlockSpec((block, width), moving),
            pl.BlockSpec((block, half), moving),
            pl.BlockSpec((block, half), moving),
            pl.BlockSpec((half, width), fixed),
            pl.BlockSpec((half, width), fixed),
            pl.BlockSpec((1, width), fixed),
        ]
        + [ANY] * len(extra),
        out_specs=pl.BlockSpec((block, width), moving),
        out_shape=jax.ShapeDtypeStruct((rows, width), BF),
        input_output_aliases={} if whole is None else {5 + len(extra): 0},
        compiler_params=params(),
        cost_estimate=cost(2.5 * steps),
        name="media_back",
    )(media, grad_a, grad_b, w_a, w_b, gain, *extra)


def swap(value, axis, bit):
    size = lax.axis_size(axis)
    return lax.ppermute(value, axis, [(i, i ^ bit) for i in range(size)])


def gather_chunks(own):
    far = swap(own, "patch", 2)
    return own, far, swap(own, "patch", 1), swap(far, "patch", 1)


def gather_patch(own):
    return jnp.stack(gather_chunks(own))


def add(first, second):
    return (first.astype(F32) + second.astype(F32)).astype(BF)


def scatter_patch(keep, send):
    near = add(keep, swap(send, "patch", 1))
    return near[0], swap(near[1], "patch", 2)


def sum_kernel(two, *refs):
    values = [ref[...] for ref in refs[1 : 1 + (4 if two else 2)]]
    if two:
        values = [
            (values[i].astype(F32) + values[i + 2].astype(F32)).astype(BF) for i in range(2)
        ]
    refs[-2][...], refs[-1][...] = values


def split_sum(first, second, place, mine, deps):
    shape = first.shape
    lead, tail = shape[:place], shape[place + 1 :]
    count = 1
    for size in lead:
        count *= size
    flat = (count, 2) + ((1,) * max(0, 2 - len(tail)) + tail)
    steps = 2 if count % 2 == 0 and first.size * 2 > (1 << 20) else 1
    block = (count // steps, 1) + flat[2:]
    zeros = (0,) * (len(flat) - 2)
    keep = pl.BlockSpec(block, lambda i, m: (i, m[0]) + zeros)
    send = pl.BlockSpec(block, lambda i, m: (i, 1 - m[0]) + zeros)
    out = pl.BlockSpec(block, lambda i, m: (i, 0) + zeros)
    shape_out = jax.ShapeDtypeStruct((count, 1) + flat[2:], BF)
    values = [v.reshape(flat) for v in (first, second) if v is not None]
    halves = pl.pallas_call(
        functools.partial(sum_kernel, second is not None),
        grid_spec=pltpu.PrefetchScalarGridSpec(
            num_scalar_prefetch=1,
            grid=(steps,),
            in_specs=[keep, send] * len(values) + [ANY] * len(deps),
            out_specs=[out, out],
        ),
        out_shape=[shape_out, shape_out],
        compiler_params=params(),
        cost_estimate=cost(2),
        name="split_sum",
    )(mine[None], *[v for v in values for _ in range(2)], *deps)
    return [h.reshape(lead + tail) for h in halves]


def last_sum_kernel(a_ref, b_ref, *refs):
    refs[-1][...] = (a_ref[...].astype(F32) + b_ref[...].astype(F32)).astype(BF)


def plain_sum(first, second, deps=()):
    return pl.pallas_call(
        last_sum_kernel,
        in_specs=[pl.BlockSpec(memory_space=pltpu.VMEM)] * 2 + [ANY] * len(deps),
        out_shape=jax.ShapeDtypeStruct(first.shape, BF),
        compiler_params=pltpu.CompilerParams(vmem_limit_bytes=VMEM),
        cost_estimate=cost(1),
        name="plain_sum",
    )(first, second, *deps)


class Scatter:
    def __init__(self, value, transit, axes, order, scope):
        self.places = [
            (axis, bit)
            for axis in axes
            for bit in reversed(range(lax.axis_size(axis).bit_length() - 1))
            if (axis, bit) in order
        ]
        self.order = list(order)
        self.scope = scope
        self.transit = transit
        self.value, self.transit = (
            v.reshape((2,) * len(self.places) + v.shape[len(axes) :]) for v in (value, transit)
        )

    def step(self, deps=()):
        with jax.named_scope(self.scope):
            if not self.order:
                if self.transit is not None:
                    self.value = plain_sum(self.value, self.transit, deps)
                    self.transit = None
                return (self.value,)
            axis, bit = self.order.pop(0)
            place = self.places.index((axis, bit))
            self.places.pop(place)
            mine = lax.rem(lax.div(lax.axis_index(axis), 1 << bit), 2)
            self.value, send = split_sum(self.value, self.transit, place, mine, deps)
            self.transit = swap(send, axis, 1 << bit)
            return self.value, send

    def finish(self, deps=()):
        while self.order or self.transit is not None:
            self.step(deps)
        return self.value


def img_bits():
    return [("img", bit) for bit in range(lax.axis_size("img").bit_length() - 1)]


def reduce_rest(keep, send, scope):
    with jax.named_scope(scope):
        transit = swap(send, "patch", 1)
    return Scatter(keep, transit, ("img", "patch"), [("patch", 1)] + img_bits(), scope)


def in_order(chunks):
    me = lax.axis_index("patch")
    order = (0, 2, 1, 3)
    return jnp.stack(
        [
            lax.dynamic_index_in_dim(
                chunks, jnp.take(jnp.array(order), jnp.bitwise_xor(me, j)), 0, keepdims=False
            )
            for j in range(4)
        ]
    )


def gather_rows(own):
    return in_order(gather_patch(own))


def place_kernel(index_ref, chunks_ref, out_ref):
    parts, _, unit = chunks_ref.shape
    for j in range(parts):
        apart = jnp.bitwise_xor(index_ref[0], j)
        at = jnp.where(apart == 1, 2, jnp.where(apart == 2, 1, apart))
        out_ref[:, j * unit : (j + 1) * unit] = chunks_ref[at].astype(F32)


def place_call(index, chunks, rows, imgs):
    parts, _, units = chunks.shape
    unit = units // imgs
    return pl.pallas_call(
        place_kernel,
        grid_spec=pltpu.PrefetchScalarGridSpec(
            num_scalar_prefetch=1,
            grid=(imgs,),
            in_specs=[pl.BlockSpec((parts, rows, unit), lambda i, p: (0, 0, i))],
            out_specs=pl.BlockSpec((rows, parts * unit), lambda i, p: (0, i)),
        ),
        out_shape=jax.ShapeDtypeStruct((rows, parts * units), F32),
        compiler_params=params(),
        name="place_units",
    )(index, chunks)


def local(
    latents,
    media,
    doc_ids,
    w_query,
    w_keyval,
    w_output,
    w_expand,
    w_reduce,
    media_gain,
    media_shift,
    latent_gain,
    latent_shift,
    ff_gain,
    ff_shift,
    out_grad,
):
    micro, docs, lat_rows, width = latents.shape
    slots, keys = media.shape[1:3]
    inner = w_query.shape[1]
    ff = w_expand.shape[1]
    head_size = inner // HEADS
    scale = head_size ** (-0.5)
    parts = lax.axis_size("patch")
    imgs = lax.axis_size("img")
    patch_index = lax.axis_index("patch")
    own_rows = micro * docs * lat_rows
    all_rows = own_rows * parts
    groups = HEADS // GROUP
    span = inner // groups
    unit = ff // (imgs * parts)

    latents_own = latents.reshape(own_rows, width)
    cot_own = out_grad.reshape(own_rows, width)
    media_flat = media.reshape(-1, width)
    with jax.named_scope("gather_latents"):
        latents_all = gather_patch(latents_own)
    with jax.named_scope("gather_cotangent"):
        cot_chunks = gather_chunks(cot_own)
        cot_all = jnp.stack(cot_chunks)

    hat_med, kv_med = kv_call(media_flat, media_gain[None], media_shift[None], w_keyval)
    kv_med = kv_med.reshape(micro, slots, keys, 2 * inner)
    if unit % 128 == 0:
        w_exp, w_red = part_call(patch_index[None], w_expand, w_reduce, imgs, parts)
    else:
        w_exp = lax.dynamic_index_in_dim(
            w_expand.reshape(width, imgs, parts, unit), patch_index, 2, keepdims=False
        ).reshape(width, imgs * unit)
        w_red = lax.dynamic_index_in_dim(
            w_reduce.reshape(imgs, parts, unit, width), patch_index, 1, keepdims=False
        ).reshape(imgs * unit, width)

    lat_hat, lat_inv = standardize(latents_own.astype(F32))
    ln_lat = (lat_hat * latent_gain + latent_shift).astype(BF)
    kv_lat = dot(ln_lat, w_keyval, NN).astype(BF).reshape(micro, docs, lat_rows, 2 * inner)
    all_hat, _ = standardize(latents_all.astype(F32))
    hat_all = all_hat.astype(BF)
    ln_all = (all_hat * latent_gain + latent_shift).astype(BF).reshape(all_rows, width)
    queries = (dot(ln_all, w_query, NN).astype(BF).astype(F32) * scale).astype(BF)
    queries = queries.reshape(parts, own_rows, inner)
    w_keyval_t = w_keyval.T
    w_parts = [
        jnp.concatenate(
            [
                w_keyval_t[g * span : (g + 1) * span],
                w_keyval_t[inner + g * span : inner + (g + 1) * span],
            ]
        )
        for g in range(groups)
    ]

    keep, send = attend_call(doc_ids, queries, kv_med, kv_lat, cot_chunks[1:])
    with jax.named_scope("join_near"):
        near = join_call(keep, swap(send, "patch", 1), False, False)
    with jax.named_scope("join_far"):
        att_near = join_call(
            near, swap(near, "patch", 2), True, True, (latents_all, cot_all, w_exp, w_red, *w_parts)
        )
        att_far = swap(att_near, "patch", 1)

    mixed, ln_ff, hidden_act, grad_pre, up_keep, up_send, out_keep, out_send = ff_call(
        latents_all,
        att_near,
        att_far,
        cot_all,
        w_output,
        w_exp,
        w_red,
        ff_gain[None],
        ff_shift[None],
    )
    with jax.named_scope("sum_up"):
        up_near, up_far = scatter_patch(up_keep, up_send)

    def flat(value):
        return value.reshape(all_rows, -1)

    ff_grads = ff_weights_call(
        flat(ln_ff), flat(grad_pre), flat(hidden_act), flat(cot_all), imgs, (up_near,)
    )
    grad_mixed, grad_branch, grad_att_own, ff_gain_part, ff_shift_part = mixed_back_call(
        up_near, up_far, mixed, cot_own, w_output, ff_gain[None], (ff_grads,)
    )
    with jax.named_scope("gather_att"):
        grad_att = gather_patch(grad_att_own)
    att = jnp.concatenate([att_near, att_far])
    grad_output = dot(att_near[0, :, :inner], grad_branch, TN).astype(BF)

    with jax.named_scope("sum_ff"):
        ff_own = lax.psum_scatter(ff_grads, "img", scatter_dimension=0, tiled=True)[0]

    norms = jnp.stack([media_gain, media_shift, latent_gain, latent_shift], axis=1)
    ff_vectors = jnp.pad(jnp.concatenate([ff_gain_part, ff_shift_part]), ((0, 6), (0, 0)))
    share = width // imgs
    tall = share // parts
    direct = laid_out(width, imgs, inner)

    def back_call(group, extra, vectors, deps):
        gkv, gkv_lat, gq, keep, send, vectors = attend_back_call(
            group,
            doc_ids,
            queries,
            grad_att,
            att,
            kv_med,
            kv_lat,
            hat_med,
            hat_all,
            w_keyval,
            w_query,
            norms,
            extra,
            vectors,
            patch_index[None],
            imgs,
            deps,
        )
        if not direct:

            def split(value):
                size = value.shape[0] // (imgs * parts)
                return value.reshape(imgs, parts // 2, 2, size, value.shape[1])

            rows = split(keep)
            fold = [rows[..., : tall // 2, 2 * span :], rows[..., tall // 2 :, 2 * span :]]
            blocks = [rows[..., : 2 * span], jnp.concatenate(fold, axis=-1)]
            if group == 0:
                blocks += [split(extra)[..., :inner], split(extra)[..., inner:]]
            else:
                six = jnp.concatenate([vectors[:4], extra[:2]]).astype(BF)
                six = jnp.swapaxes(six.reshape(6, imgs, share), 0, 1)
                six = jnp.pad(six, ((0, 0), (0, 10), (0, width - share)))[:, None, None, :, :inner]
                blocks.append(
                    jnp.pad(six, ((0, 0), (0, parts // 2 - 1), (0, 1), (0, 0), (0, 0)))
                )
            blocks = jnp.concatenate(blocks, axis=3)
            bit = lax.rem(patch_index, 2)
            keep = lax.dynamic_index_in_dim(blocks, bit, 2, keepdims=False)
            send = lax.dynamic_index_in_dim(blocks, 1 - bit, 2, keepdims=False)
        return gkv, gkv_lat, gq, keep, send, vectors

    out_keep, out_send = gate((out_keep, out_send), (grad_att,))
    with jax.named_scope("sum_out"):
        out_near, out_far = scatter_patch(out_keep, out_send)
    gkv_0, gkv_lat_0, gq_0, keep, send, vectors = back_call(
        0, grad_output, jnp.zeros((8, width), F32), (ff_grads,)
    )
    first = reduce_rest(keep, send, "sum_weights_0")
    gkv_1, gkv_lat_1, gq_1, keep, send, vectors = back_call(
        1, ff_vectors, vectors, first.step()
    )
    done = first.step((gq_1,))
    keep, send, gq_0, gq_1 = gate((keep, send, gq_0, gq_1), done)
    second = reduce_rest(keep, send, "sum_weights_1")
    with jax.named_scope("sum_query"):
        gq_keep = jnp.concatenate([gq_0[:2], gq_1[:2]], axis=-1)
        gq_far = swap(jnp.concatenate([gq_0[2:], gq_1[2:]], axis=-1), "patch", 1)
        gq_own = add(gq_keep[0], gq_far[0])
        gq_near = add(gq_keep[1], gq_far[1])
        gq_far = swap(gq_near, "patch", 2)

    media_grad = None
    deps = (*second.step(), gq_near)
    pieces = ((0, 4), (4, 2), (6, 2))
    for at, size in pieces:
        media_grad = media_back_call(
            media_flat,
            gkv_0,
            gkv_1,
            w_parts[0],
            w_parts[1],
            media_gain[None],
            at,
            size,
            media_grad,
            deps,
        )
        done = (media_grad,)
        deps = (*first.step(done), *second.step(done))

    gq_own, gq_far, out_near, out_far = gate((gq_own, gq_far, out_near, out_far), done)
    grad_q = ((gq_own.astype(F32) + gq_far.astype(F32)) * scale).astype(BF)
    grad_ln_lat = (
        dot(grad_q, w_query, NT)
        + dot(gkv_lat_0, w_parts[0], NN)
        + dot(gkv_lat_1, w_parts[1], NN)
    )
    latent_back, _ = norm_back(lat_hat, lat_inv, latent_gain, grad_ln_lat)
    latents_grad = (grad_mixed + latent_back).astype(BF)
    latents_out = (mixed + (out_near.astype(F32) + out_far.astype(F32))).astype(BF)

    first = first.finish(done)
    second = second.finish(done)

    def rows_of(value):
        return value.reshape(-1, value.shape[-1])

    with jax.named_scope("gather_weights"):
        whole = gather_rows(jnp.concatenate([first, second]))
    cut = first.shape[0]
    first, second = whole[:, :cut], whole[:, cut:]
    keyval_rows = [rows_of(first[:, :tall]), rows_of(second[:, :tall])]
    grad_keyval = jnp.concatenate(
        [rows[:, at * span : (at + 1) * span] for at in range(2) for rows in keyval_rows], axis=1
    ).astype(F32)
    end = tall + tall // 2

    def unfold(value):
        return rows_of(jnp.concatenate([value[..., :span], value[..., span:]], axis=1))

    query_rows = jnp.concatenate(
        [unfold(first[:, tall:end]), unfold(second[:, tall:end])], axis=1
    ).astype(F32)
    out_rows = first[:, end:]
    size = out_rows.shape[1] // 2
    out_rows = rows_of(
        jnp.concatenate([out_rows[:, :size], out_rows[:, size:]], axis=2)
    ).astype(F32)
    vectors = second[0, end : end + 6, :share].astype(F32)

    with jax.named_scope("gather_ff"):
        chunks = gather_patch(ff_own)
        expand, reduce = chunks[:, :share], chunks[:, share:]
        if unit % 128 == 0:
            expand_rows = place_call(patch_index[None], chunks, share, imgs)
        else:
            expand_rows = in_order(expand).reshape(parts, -1, imgs, unit)
            expand_rows = jnp.transpose(expand_rows, (1, 2, 0, 3)).reshape(-1, ff).astype(F32)
        reduce_rows = rows_of(in_order(reduce)).astype(F32)

    return (
        latents_out.reshape(latents.shape),
        latents_grad.reshape(latents.shape),
        media_grad.reshape(media.shape),
        query_rows,
        grad_keyval,
        out_rows,
        expand_rows,
        reduce_rows,
    ) + tuple(vectors[i] for i in range(6))


def solution(mesh):
    tokens = P(None, "img", "patch", None)
    return jax.shard_map(
        local,
        mesh=mesh,
        in_specs=(tokens, tokens, P(None, "img")) + (P(),) * 11 + (tokens,),
        out_specs=(tokens,) * 3 + (P("img", None),) * 5 + (P("img"),) * 6,
        check_vma=False,
    )
```

```python
import functools

import jax
import jax.numpy as jnp
from jax import lax
from jax.experimental import pallas as pl
from jax.experimental.pallas import tpu as pltpu
from jax.sharding import PartitionSpec as P

HEADS = 8
GROUP = 4
EPS = 1e-05
CHUNK = 4
FAR = -1e30
BF = jnp.bfloat16
F32 = jnp.float32
ANY = pl.BlockSpec(memory_space=pl.ANY)
TOKEN = jax.ShapeDtypeStruct((8, 128), jnp.float32)


def params(mib=56):
    return pltpu.CompilerParams(vmem_limit_bytes=mib << 20)


def cost(us):
    return pl.CostEstimate(flops=int(us * 1.1e9), bytes_accessed=0, transcendentals=0)


def hbm_call(kernel, held, kept, **options):
    shapes = options.pop("out_shape")
    if isinstance(shapes, list):
        shapes = [pltpu.HBM(v.shape, v.dtype) if i in kept else v for i, v in enumerate(shapes)]
    options["out_shape"] = shapes
    scalars = options["grid_spec"].num_scalar_prefetch if "grid_spec" in options else 0
    inner = pl.pallas_call(kernel, **options)

    def run(*operands):
        return inner(
            *operands[:scalars],
            *[
                pltpu.with_memory_space_constraint(x, pltpu.HBM)
                if i in held or x.size >= 1 << 20 and held
                else x
                for i, x in enumerate(operands[scalars:])
            ],
        )

    return run


def nothing_kernel(*refs):
    pass


def gate(carry, deps):
    return pl.pallas_call(
        nothing_kernel,
        in_specs=[ANY] * (len(carry) + len(deps)),
        out_specs=[ANY] * len(carry),
        out_shape=[jax.ShapeDtypeStruct(c.shape, c.dtype) for c in carry],
        input_output_aliases={i: i for i in range(len(carry))},
        name="gate",
    )(*carry, *deps)


def dot(a, b, dims):
    return lax.dot_general(a, b, (dims, ((), ())), preferred_element_type=F32)


NN = ((1,), (0,))
NT = ((1,), (1,))
TN = ((0,), (0,))


def standardize(values):
    center = values - jnp.mean(values, axis=-1, keepdims=True)
    inv = lax.rsqrt(jnp.mean(center * center, axis=-1, keepdims=True) + EPS)
    return center * inv, inv


def norm_back(hat, inv, gain, upstream):
    scaled = upstream * gain
    back = inv * (
        scaled
        - jnp.mean(scaled, axis=-1, keepdims=True)
        - hat * jnp.mean(scaled * hat, axis=-1, keepdims=True)
    )
    return back, upstream * hat


def kv_kernel(media_ref, gain_ref, shift_ref, w_ref, hat_ref, kv_ref, token_ref):
    token_ref[...] = jnp.zeros_like(token_ref)
    rows = media_ref.shape[0]
    step = min(rows, 256)
    for at in range(0, rows, step):
        part = pl.ds(at, step)
        hat, _ = standardize(media_ref[part, :].astype(F32))
        ln = (hat * gain_ref[...] + shift_ref[...]).astype(BF)
        hat_ref[part, :] = hat.astype(BF)
        kv_ref[part, :] = dot(ln, w_ref[...], NN).astype(BF)


def kv_call(media, gain, shift, w_keyval):
    rows, width = media.shape
    outs = w_keyval.shape[1]
    block = 512
    return hbm_call(
        kv_kernel,
        range(4),
        (0, 1),
        grid=(rows // block,),
        in_specs=[
            pl.BlockSpec((block, width), lambda i: (i, 0)),
            pl.BlockSpec((1, width), lambda i: (0, 0)),
            pl.BlockSpec((1, width), lambda i: (0, 0)),
            pl.BlockSpec((width, outs), lambda i: (0, 0)),
        ],
        out_specs=[
            pl.BlockSpec((block, width), lambda i: (i, 0)),
            pl.BlockSpec((block, outs), lambda i: (i, 0)),
            pl.BlockSpec(TOKEN.shape, lambda i: (0, 0)),
        ],
        out_shape=[
            jax.ShapeDtypeStruct((rows, width), BF),
            jax.ShapeDtypeStruct((rows, outs), BF),
            TOKEN,
        ],
        compiler_params=params(20),
        cost_estimate=cost(16),
        name="media_keyval",
    )(media, gain, shift, w_keyval)


def latent_kernel(own, far, near, both, gain_ref, shift_ref, wq_ref, wkv_ref, *rest):
    raw_ref, hat_ref, q_ref, kv_ref = rest[-4:]
    scale = (wq_ref.shape[1] // HEADS) ** (-0.5)
    for c, ref in enumerate((own, far, near, both)):
        raw = ref[...]
        raw_ref[c] = raw
        hat, _ = standardize(raw.astype(F32))
        hat_ref[c] = hat.astype(BF)
        ln = (hat * gain_ref[...] + shift_ref[...]).astype(BF)
        q_ref[c] = (dot(ln, wq_ref[...], NN).astype(BF).astype(F32) * scale).astype(BF)
        if c == 0:
            kv_ref[...] = dot(ln, wkv_ref[...], NN).astype(BF)


def latent_call(chunks, gain, shift, w_query, w_keyval, deps):
    rows, width = chunks[0].shape
    inner = w_query.shape[1]
    count = len(chunks)
    return hbm_call(
        latent_kernel,
        (0, 6, 7),
        range(4),
        in_specs=[pl.BlockSpec(memory_space=pltpu.VMEM)] * (count + 4) + [ANY] * len(deps),
        out_shape=[
            jax.ShapeDtypeStruct((count, rows, width), BF),
            jax.ShapeDtypeStruct((count, rows, width), BF),
            jax.ShapeDtypeStruct((count, rows, inner), BF),
            jax.ShapeDtypeStruct((rows, 2 * inner), BF),
        ],
        compiler_params=params(28),
        cost_estimate=cost(6),
        name="latents",
    )(*chunks, gain, shift, w_query, w_keyval, *deps)


def kv_columns(first, second):
    span = first.shape[1] // 2
    return jnp.concatenate(
        [first[:, :span], second[:, :span], first[:, span:], second[:, span:]], axis=1
    )


def latent_back_kernel(
    scale, raw_ref, mixed_ref, own_ref, far_ref, kv_a, kv_b, wq_ref, w_ref, gain_ref, *rest
):
    grad_q = ((own_ref[...].astype(F32) + far_ref[...].astype(F32)) * scale).astype(BF)
    up = (
        dot(grad_q, wq_ref[...], NT)
        + dot(kv_columns(kv_a[...], kv_b[...]), w_ref[...], NT)
    )
    hat, inv = standardize(raw_ref[...].astype(F32))
    back, _ = norm_back(hat, inv, gain_ref[...], up)
    rest[-1][...] = (mixed_ref[...] + back).astype(BF)


def latent_back_call(scale, args, deps):
    return hbm_call(
        functools.partial(latent_back_kernel, scale),
        (0, 1, 6, 7),
        (),
        in_specs=[pl.BlockSpec(memory_space=pltpu.VMEM)] * len(args) + [ANY] * len(deps),
        out_shape=jax.ShapeDtypeStruct(args[0].shape, BF),
        compiler_params=params(24),
        cost_estimate=cost(4),
        name="latent_back",
    )(*args, *deps)


def out_kernel(mixed_ref, near_ref, far_ref, *rest):
    rest[-1][...] = (
        mixed_ref[...] + (near_ref[...].astype(F32) + far_ref[...].astype(F32))
    ).astype(BF)


def out_call(mixed, near, far, deps):
    return hbm_call(
        out_kernel,
        (0, 1, 2),
        (),
        in_specs=[pl.BlockSpec(memory_space=pltpu.VMEM)] * 3 + [ANY] * len(deps),
        out_shape=jax.ShapeDtypeStruct(mixed.shape, BF),
        compiler_params=params(8),
        cost_estimate=cost(1.5),
        name="latents_out",
    )(mixed, near, far, *deps)


def block_mask(head_size, lats):
    rows = GROUP * lats
    cols = GROUP * head_size
    row_head = lax.broadcasted_iota(jnp.int32, (rows, cols), 0) // lats
    col_head = lax.broadcasted_iota(jnp.int32, (rows, cols), 1) // head_size
    return row_head == col_head


def spread_heads(values, mask):
    tiled = jnp.concatenate([values] * GROUP, axis=0)
    return jnp.where(mask, tiled, jnp.zeros_like(tiled))


def gather_heads(full, mask, lats):
    kept = jnp.where(mask, full, 0.0)
    total = kept[:lats]
    for head in range(1, GROUP):
        total = total + kept[head * lats : (head + 1) * lats]
    return total


LANES = 128


def terms(value):
    first = value.astype(BF)
    rest = value - first.astype(F32)
    second = rest.astype(BF)
    return first, second, (rest - second.astype(F32)).astype(BF)


def pick(shape, fn):
    row = lax.broadcasted_iota(jnp.int32, shape, 0)
    col = lax.broadcasted_iota(jnp.int32, shape, 1)
    return jnp.where(fn(row, col), 1.0, 0.0).astype(BF)


def holds(lane, head, figure):
    return (lane < 24 * figure + 24) & (lane >= 24 * figure) & (lane % HEADS == head)


def pack_rows(figures):
    rows = jnp.concatenate([t for f in figures for t in terms(f)], axis=0)
    eye = pick((rows.shape[0], LANES), lambda r, c: r == c)
    return dot(rows, eye, TN).astype(BF)


def pack_cols(figures):
    total = None
    for i, figure in enumerate(figures):
        for k, term in enumerate(terms(figure)):
            at = HEADS * (3 * i + k)
            place = pick((LANES, LANES), lambda r, c: (r < HEADS) & (c == r + at))
            part = dot(term, place, NN)
            total = part if total is None else total + part
    return total.astype(BF)


def widen(packed, figure, inner):
    size = inner // HEADS
    return dot(packed, pick((LANES, inner), lambda r, c: holds(r, c // size, figure)), NN)


def narrow(packed, figure):
    return dot(
        packed, pick((LANES, LANES), lambda r, c: (c < HEADS) & holds(r, c, figure)), NN
    )


def doc_rows(ref, d, lat_rows, cols):
    rows = slice(d * lat_rows, (d + 1) * lat_rows)
    return jnp.concatenate([ref[c, rows, cols] for c in range(ref.shape[0])], axis=0)


def doc_spans(doc_ref, micro, docs, slots):
    counts = []
    for d in range(docs):
        total = 0
        for s in range(slots):
            total = total + jnp.where(doc_ref[micro, s] == d, 1, 0)
        counts.append(total)
    first = 0
    spans = []
    for count in counts:
        spans.append((first, count))
        first = first + count
    return spans


def slot_chunk(span, step, slots):
    first, count = span
    low = first + step * CHUNK
    return jnp.minimum(low, slots - CHUNK), low, first + count


def own_rows_of(at, low, high, keys):
    slot = at + lax.broadcasted_iota(jnp.int32, (CHUNK * keys, 1), 0) // keys
    return (slot >= low) & (slot < high)


def steps_of(span):
    return (span[1] + CHUNK - 1) // CHUNK


def attend_kernel(deps, doc_ref, q_ref, kv_ref, kvl_ref, *rest):
    keep_ref, send_ref, bd, score, acc, top, tot = rest[deps:]
    chunks, rows, inner = q_ref.shape
    docs, lat_rows = kvl_ref.shape[1:3]
    lats = chunks * lat_rows
    slots, keys = kv_ref.shape[1:3]
    groups = HEADS // GROUP
    span = inner // groups
    micro = pl.program_id(0)
    mask = block_mask(inner // HEADS, lats)
    cols = [slice(g * span, (g + 1) * span) for g in range(groups)]
    vals = [slice(inner + g * span, inner + (g + 1) * span) for g in range(groups)]
    spans = doc_spans(doc_ref, micro, docs, slots)
    tall = CHUNK * keys

    def load(at, part):
        return kv_ref[0, pl.ds(at, CHUNK), :, part].reshape(tall, span)

    for d in range(docs):
        at, low, high = slot_chunk(spans[d], 0, slots)
        bias = jnp.where(own_rows_of(at, low, high, keys), 0.0, FAR)
        bias = jnp.concatenate([bias, jnp.zeros((lat_rows, 1), F32)], axis=0)
        for g in range(groups):
            spread = spread_heads(doc_rows(q_ref, d, lat_rows, cols[g]), mask)
            bd[d, g] = spread
            key = jnp.concatenate([load(at, cols[g]), kvl_ref[0, d, :, cols[g]]], axis=0)
            val = dot(key, spread, NT) + bias
            score[d, g, 0] = val
            top[d, g] = jnp.max(val, axis=0, keepdims=True)
    for d in range(docs):

        def more(step, carry, d=d):
            at, low, high = slot_chunk(spans[d], step, slots)
            bias = jnp.where(own_rows_of(at, low, high, keys), 0.0, FAR)
            for g in range(groups):
                val = dot(load(at, cols[g]), bd[d, g], NT) + bias
                score[d, g, step, :tall] = val
                top[d, g] = jnp.maximum(top[d, g], jnp.max(val, axis=0, keepdims=True))
            return carry

        lax.fori_loop(1, steps_of(spans[d]), more, 0)
    for d in range(docs):
        at, low, high = slot_chunk(spans[d], 0, slots)
        for g in range(groups):
            expo = jnp.exp(score[d, g, 0] - top[d, g])
            tot[d, g] = jnp.sum(expo, axis=0, keepdims=True)
            val = jnp.concatenate([load(at, vals[g]), kvl_ref[0, d, :, vals[g]]], axis=0)
            acc[d, g] = dot(expo.astype(BF), val, TN)
    for d in range(docs):

        def more_values(step, carry, d=d):
            at, low, high = slot_chunk(spans[d], step, slots)
            for g in range(groups):
                expo = jnp.exp(score[d, g, step, :tall] - top[d, g])
                tot[d, g] = tot[d, g] + jnp.sum(expo, axis=0, keepdims=True)
                acc[d, g] = acc[d, g] + dot(expo.astype(BF), load(at, vals[g]), TN)
            return carry

        lax.fori_loop(1, steps_of(spans[d]), more_values, 0)
    half = chunks // 2
    for d in range(docs):
        rows_d = slice(d * lat_rows, (d + 1) * lat_rows)

        def by_head(ref):
            return jnp.concatenate(
                [
                    ref[d, g][:, h * lats : (h + 1) * lats]
                    for g in range(groups)
                    for h in range(GROUP)
                ],
                axis=0,
            )

        packed = pack_rows([by_head(top), by_head(tot)])
        outs = [gather_heads(acc[d, g], mask, lats).astype(BF) for g in range(groups)]
        for c in range(chunks):
            ref = keep_ref if c < half else send_ref
            part = slice(c * lat_rows, (c + 1) * lat_rows)
            for g in range(groups):
                ref[c % half, rows_d, cols[g]] = outs[g][part]
            ref[c % half, rows_d, inner:] = packed[part]


def attend_call(doc_ids, queries, kv_med, kv_lat, deps):
    chunks, _, inner = queries.shape
    micro, slots, keys, both = kv_med.shape
    docs, lat_rows = kv_lat.shape[1:3]
    lats = chunks * lat_rows
    rows = docs * lat_rows
    groups = HEADS // GROUP
    span = inner // groups
    wide = GROUP * lats
    half = chunks // 2
    longest = (slots - docs + CHUNK) // CHUNK
    out_spec = pl.BlockSpec((half, rows, inner + LANES), lambda i, ids: (0, i, 0))
    out_shape = jax.ShapeDtypeStruct((half, micro * rows, inner + LANES), BF)
    return hbm_call(
        functools.partial(attend_kernel, len(deps)),
        range(3),
        (),
        grid_spec=pltpu.PrefetchScalarGridSpec(
            num_scalar_prefetch=1,
            grid=(micro,),
            in_specs=[
                pl.BlockSpec((chunks, rows, inner), lambda i, ids: (0, i, 0)),
                pl.BlockSpec((1, slots, keys, both), lambda i, ids: (i, 0, 0, 0)),
                pl.BlockSpec((1, docs, lat_rows, both), lambda i, ids: (i, 0, 0, 0)),
            ]
            + [ANY] * len(deps),
            out_specs=[out_spec, out_spec],
            scratch_shapes=[
                pltpu.VMEM((docs, groups, wide, span), BF),
                pltpu.VMEM((docs, groups, longest, CHUNK * keys + lat_rows, wide), F32),
                pltpu.VMEM((docs, groups, wide, span), F32),
                pltpu.VMEM((docs, groups, 1, wide), F32),
                pltpu.VMEM((docs, groups, 1, wide), F32),
            ],
        ),
        out_shape=[out_shape, out_shape],
        compiler_params=params(40),
        cost_estimate=cost(13),
        name="attend",
    )(doc_ids, queries, kv_med, kv_lat, *deps)


def join_kernel(last, flip, a_ref, b_ref, *rest):
    out_ref = rest[-1]
    inner = a_ref.shape[2] - LANES
    count = a_ref.shape[0]
    for c in range(count):
        first, second = a_ref[c], b_ref[count - 1 - c if flip else c]
        pack_a, pack_b = first[:, inner:], second[:, inner:]
        top_a, top_b = widen(pack_a, 0, inner), widen(pack_b, 0, inner)
        best = jnp.maximum(top_a, top_b)
        fac_a, fac_b = jnp.exp(top_a - best), jnp.exp(top_b - best)
        out = fac_a * first[:, :inner].astype(F32) + fac_b * second[:, :inner].astype(F32)
        if last:
            total = fac_a * widen(pack_a, 1, inner) + fac_b * widen(pack_b, 1, inner)
            out = out / total
        out_ref[c, :, :inner] = out.astype(BF)
        small_a, small_b = narrow(pack_a, 0), narrow(pack_b, 0)
        small = jnp.maximum(small_a, small_b)
        sum_ab = jnp.exp(small_a - small) * narrow(pack_a, 1) + jnp.exp(
            small_b - small
        ) * narrow(pack_b, 1)
        if last:
            lane = lax.broadcasted_iota(jnp.int32, sum_ab.shape, 1)
            lse = jnp.where(lane < HEADS, small + jnp.log(jnp.maximum(sum_ab, 1e-30)), 0.0)
            out_ref[c, :, inner:] = pack_cols([lse])
        else:
            out_ref[c, :, inner:] = pack_cols([small, sum_ab])


def join_call(first, second, last, flip, deps=()):
    count, rows, cols = first.shape
    block = min(rows, 128)
    spec = pl.BlockSpec((count, block, cols), lambda i: (0, i, 0))
    return pl.pallas_call(
        functools.partial(join_kernel, last, flip),
        grid=(rows // block,),
        in_specs=[spec, spec] + [ANY] * len(deps),
        out_specs=spec,
        out_shape=jax.ShapeDtypeStruct(first.shape, BF),
        compiler_params=params(10),
        cost_estimate=cost(3.5),
        name="join_last" if last else "join_first",
    )(first, second, *deps)


def ff_kernel(
    lat_ref,
    near_ref,
    far_ref,
    cot_ref,
    wo_ref,
    we_ref,
    wr_ref,
    gain_ref,
    shift_ref,
    mixed_ref,
    ln_ref,
    act_ref,
    gpre_ref,
    up_own,
    up_keep,
    up_send,
    out_keep,
    out_send,
):
    i = pl.program_id(0)
    half = pl.num_programs(0) // 2
    att = jnp.where(i < half, near_ref[0], far_ref[0])
    mixed = lat_ref[0].astype(F32) + dot(att, wo_ref[...], NN)
    hat, _ = standardize(mixed)
    ln = (hat * gain_ref[...] + shift_ref[...]).astype(BF)
    ln_ref[0] = ln
    pre = dot(ln, we_ref[...], NN)
    cdf = 0.5 + 0.5 * lax.erf(pre * (0.5**0.5))
    slope = cdf + pre * (0.3989422804014327 * jnp.exp(-0.5 * pre * pre))
    act = (pre * cdf).astype(BF)
    act_ref[0] = act
    gpre = (dot(cot_ref[0], wr_ref[...], NT) * slope).astype(BF)
    gpre_ref[0] = gpre
    up = dot(gpre, we_ref[...], NT).astype(BF)
    out = dot(act, wr_ref[...], NN).astype(BF)

    @pl.when(i == 0)
    def _():
        mixed_ref[...] = mixed
        up_own[...] = up

    @pl.when(i == 1)
    def _():
        up_keep[...] = up

    @pl.when(i < half)
    def _():
        out_keep[0] = out

    @pl.when(i >= half)
    def _():
        up_send[0] = up
        out_send[0] = out


def ff_call(latents, near, far, cot, w_output, w_exp, w_red, gain, shift):
    chunks, rows, width = latents.shape
    inner = w_output.shape[0]
    units = w_exp.shape[1]
    half = chunks // 2

    def chunk(cols):
        return pl.BlockSpec((1, rows, cols), lambda i: (i, 0, 0))

    def first(cols):
        return pl.BlockSpec((1, rows, cols), lambda i: (jnp.minimum(i, half - 1), 0, 0))

    def second(cols):
        return pl.BlockSpec((1, rows, cols), lambda i: (jnp.maximum(i - half, 0), 0, 0))

    def fixed(*shape):
        return pl.BlockSpec(shape, lambda i: (0,) * len(shape))

    def out(count, cols):
        return jax.ShapeDtypeStruct((count, rows, cols), BF)

    return hbm_call(
        ff_kernel,
        (0, 4, 5, 6),
        (0, 7, 8),
        grid=(chunks,),
        in_specs=[
            chunk(width),
            first(inner),
            second(inner),
            chunk(width),
            fixed(inner, width),
            fixed(width, units),
            fixed(units, width),
            fixed(1, width),
            fixed(1, width),
        ],
        out_specs=[
            fixed(rows, width),
            chunk(width),
            chunk(units),
            chunk(units),
            fixed(rows, width),
            fixed(rows, width),
            second(width),
            first(width),
            second(width),
        ],
        out_shape=[
            jax.ShapeDtypeStruct((rows, width), F32),
            out(chunks, width),
            out(chunks, units),
            out(chunks, units),
            jax.ShapeDtypeStruct((rows, width), BF),
            jax.ShapeDtypeStruct((rows, width), BF),
            out(half, width),
            out(half, width),
            out(half, width),
        ],
        compiler_params=params(40),
        cost_estimate=cost(18),
        name="feed_forward",
    )(latents, near, far, cot, w_output, w_exp, w_red, gain, shift)


def ff_weights_kernel(ln_ref, gpre_ref, act_ref, cot_ref, *rest):
    out_ref = rest[-1]
    count, rows, width = out_ref.shape
    half = rows // 2
    for part, (left, right) in enumerate(((ln_ref, gpre_ref), (act_ref, cot_ref))):
        product = dot(left[...], right[...], TN).astype(BF)
        out_ref[:, part * half : (part + 1) * half, :] = product.reshape(count, half, width)


def ff_weights_call(ln_ff, grad_pre, hidden_act, cot, imgs, deps):
    tokens, width = ln_ff.shape
    units = grad_pre.shape[1]
    half = units // imgs
    steps = 2
    left = pl.BlockSpec((tokens, width // steps), lambda i: (0, i))
    right = pl.BlockSpec((tokens, width), lambda i: (0, 0))
    return hbm_call(
        ff_weights_kernel,
        (3,),
        (),
        grid=(steps,),
        in_specs=[left, right, left, right] + [ANY] * len(deps),
        out_specs=pl.BlockSpec((imgs // steps, 2 * half, width), lambda i: (i, 0, 0)),
        out_shape=pltpu.HBM((imgs, 2 * half, width), BF),
        compiler_params=params(28),
        cost_estimate=cost(9),
        name="ff_weights",
    )(ln_ff, grad_pre, hidden_act, cot, *deps)


def mixed_back_kernel(own_ref, near_ref, far_ref, mixed_ref, cot_ref, wo_ref, gain_ref, *rest):
    gm_ref, gb_ref, ga_ref, dg_ref, ds_ref = rest[-5:]
    up = own_ref[...].astype(F32) + near_ref[0].astype(F32) + far_ref[...].astype(F32)
    hat, inv = standardize(mixed_ref[...])
    back, gains = norm_back(hat, inv, gain_ref[...], up)
    grad = cot_ref[...].astype(F32) + back
    gm_ref[...] = grad
    branch = grad.astype(BF)
    gb_ref[...] = branch
    ga_ref[...] = dot(branch, wo_ref[...], NT).astype(BF)
    dg_ref[...] = jnp.sum(gains, axis=0, keepdims=True)
    ds_ref[...] = jnp.sum(up, axis=0, keepdims=True)


def mixed_back_call(own, near, far, mixed, cot, w_output, gain, deps):
    rows, width = mixed.shape
    inner = w_output.shape[0]
    return hbm_call(
        mixed_back_kernel,
        (3, 4, 5),
        (0,),
        in_specs=[pl.BlockSpec(memory_space=pltpu.VMEM)] * 7 + [ANY] * len(deps),
        out_shape=[
            jax.ShapeDtypeStruct((rows, width), F32),
            jax.ShapeDtypeStruct((rows, width), BF),
            jax.ShapeDtypeStruct((rows, inner), BF),
            jax.ShapeDtypeStruct((1, width), F32),
            jax.ShapeDtypeStruct((1, width), F32),
        ],
        compiler_params=params(20),
        cost_estimate=cost(4),
        name="mixed_back",
    )(own, near, far, mixed, cot, w_output, gain, *deps)


def part_kernel(index_ref, e_ref, r_ref, eo_ref, ro_ref):
    eo_ref[...] = e_ref[...]
    ro_ref[...] = r_ref[...]


def part_call(index, w_expand, w_reduce, imgs, parts):
    width, ff = w_expand.shape
    unit = ff // (imgs * parts)
    return hbm_call(
        part_kernel,
        range(2),
        range(2),
        grid_spec=pltpu.PrefetchScalarGridSpec(
            num_scalar_prefetch=1,
            grid=(imgs,),
            in_specs=[
                pl.BlockSpec((width, unit), lambda i, p: (0, i * parts + p[0])),
                pl.BlockSpec((unit, width), lambda i, p: (i * parts + p[0], 0)),
            ],
            out_specs=[
                pl.BlockSpec((width, unit), lambda i, p: (0, i)),
                pl.BlockSpec((unit, width), lambda i, p: (i, 0)),
            ],
        ),
        out_shape=[
            jax.ShapeDtypeStruct((width, imgs * unit), BF),
            jax.ShapeDtypeStruct((imgs * unit, width), BF),
        ],
        compiler_params=params(6),
        name="weight_part",
    )(index, w_expand, w_reduce)


def attend_back_kernel(
    group,
    deps,
    doc_ref,
    index_ref,
    q_ref,
    go_ref,
    att_ref,
    lse_ref,
    k_ref,
    v_ref,
    kl_ref,
    vl_ref,
    hat_ref,
    lat_hat_ref,
    wk_ref,
    wv_ref,
    wq_ref,
    norm_ref,
    extra_ref,
    vec_in,
    *rest,
):
    gkv_ref, gkvl_ref, gq_ref, keep_ref, send_ref, vec_ref = rest[deps : deps + 6]
    bdq, bdo, acc, stat, h_med, h_lat, sums, wide_rows = rest[deps + 6 :]
    chunks, _, span = q_ref.shape
    docs, lat_rows = kl_ref.shape[1:3]
    lats = chunks * lat_rows
    slots, keys = k_ref.shape[1:3]
    micro = pl.program_id(0)
    mask = block_mask(span // GROUP, lats)
    every = slice(None)
    scale = (span // GROUP) ** (-0.5)

    spans = doc_spans(doc_ref, micro, docs, slots)
    tall = CHUNK * keys

    def pair(key, value, bias, d):
        score = dot(key, bdq[d], NT) + bias
        prob = jnp.exp(score - stat[d, 0:1])
        dprob = dot(value, bdo[d], NT)
        dscore = (prob * (dprob - stat[d, 1:2])).astype(BF)
        grad_key = dot(dscore, bdq[d], NN).astype(BF)
        grad_value = dot(prob.astype(BF), bdo[d], NN).astype(BF)
        grad_query = dot(dscore, key, TN)
        return grad_key, grad_value, grad_query

    def load(ref, at):
        return ref[0, pl.ds(at, CHUNK)].reshape(tall, span)

    def store(at, own, grad_key, grad_value):
        part = pl.ds(pl.multiple_of(at * keys, keys), tall)
        gkv_ref[part, :span] = jnp.where(own, grad_key, gkv_ref[part, :span])
        gkv_ref[part, span:] = jnp.where(own, grad_value, gkv_ref[part, span:])

    sel = pick((HEADS, LANES), lambda r, c: holds(c, r, 0))
    size = span // GROUP
    head_sel = pick((HEADS, span), lambda r, c: c // size == r)

    def row(by_head, at):
        return jnp.concatenate([by_head[at + h : at + h + 1] for h in range(GROUP)], axis=1)

    for d in range(docs):
        out_grad = doc_rows(go_ref, d, lat_rows, every)
        bdq[d] = spread_heads(doc_rows(q_ref, d, lat_rows, every), mask)
        bdo[d] = spread_heads(out_grad, mask)
        lse = dot(sel, doc_rows(lse_ref, d, lat_rows, every), NT)
        stat[d, 0:1] = row(lse, group * GROUP)
        attended = doc_rows(att_ref, d, lat_rows, every)
        high, low, _ = terms(out_grad.astype(F32) * attended.astype(F32))
        stat[d, 1:2] = row(dot(head_sel, high, NT) + dot(head_sel, low, NT), 0)
    for d in range(docs):
        rows_d = slice(d * lat_rows, (d + 1) * lat_rows)
        at, low, high = slot_chunk(spans[d], 0, slots)
        own = own_rows_of(at, low, high, keys)
        bias = jnp.concatenate([jnp.where(own, 0.0, FAR), jnp.zeros((lat_rows, 1), F32)], axis=0)
        key = jnp.concatenate([load(k_ref, at), kl_ref[0, d]], axis=0)
        value = jnp.concatenate([load(v_ref, at), vl_ref[0, d]], axis=0)
        grad_key, grad_value, grad_query = pair(key, value, bias, d)
        store(at, own, grad_key[:tall], grad_value[:tall])
        gkvl_ref[rows_d, :span] = grad_key[tall:]
        gkvl_ref[rows_d, span:] = grad_value[tall:]
        acc[d] = grad_query
    for d in range(docs):

        def more(step, carry, d=d):
            at, low, high = slot_chunk(spans[d], step, slots)
            own = own_rows_of(at, low, high, keys)
            grad_key, grad_value, grad_query = pair(
                load(k_ref, at), load(v_ref, at), jnp.where(own, 0.0, FAR), d
            )
            store(at, own, grad_key, grad_value)
            acc[d] = acc[d] + grad_query
            return carry

        lax.fori_loop(1, steps_of(spans[d]), more, 0)
    for d in range(docs):
        full = gather_heads(acc[d], mask, lats).astype(BF)
        for c in range(chunks):
            gq_ref[c, pl.ds(micro * docs * lat_rows + d * lat_rows, lat_rows)] = full[
                c * lat_rows : (c + 1) * lat_rows
            ]
    part = dot(hat_ref[...], gkv_ref[...], TN)
    part_sum = dot(jnp.ones((8, gkv_ref.shape[0]), BF), gkv_ref[...], NN)[0:1]
    lat_part = dot(lat_hat_ref[0, pl.ds(micro * docs * lat_rows, docs * lat_rows)], gkvl_ref[...], TN)
    lat_sum_part = jnp.sum(gkvl_ref[...].astype(F32), axis=0, keepdims=True)

    @pl.when(micro == 0)
    def _():
        h_med[...] = part
        h_lat[...] = lat_part
        sums[0:1, :] = part_sum
        sums[1:2, :] = lat_sum_part

    @pl.when(micro > 0)
    def _():
        h_med[...] = h_med[...] + part
        h_lat[...] = h_lat[...] + lat_part
        sums[0:1, :] = sums[0:1, :] + part_sum
        sums[1:2, :] = sums[1:2, :] + lat_sum_part

    @pl.when(micro == pl.num_programs(0) - 1)
    def _():
        width = h_med.shape[0]
        step = 128
        tokens = lat_hat_ref.shape[0] * lat_hat_ref.shape[1]
        quer_all = gq_ref[...].reshape(tokens, span)
        h_q = dot(lat_hat_ref[...].reshape(tokens, width), quer_all, TN)
        quer_sum = dot(jnp.ones((8, tokens), BF), quer_all, NN)[0:1] * scale
        for at in range(0, width, step):
            part = slice(at, at + step)
            norm = norm_ref[part, :]
            med, lat, quer = h_med[part, :], h_lat[part, :], h_q[part] * scale
            med_sum, lat_sum = sums[0:1, :], sums[1:2, :]
            wide_rows[part, : 2 * span] = (
                norm[:, 0:1] * med
                + norm[:, 1:2] * med_sum
                + norm[:, 2:3] * lat
                + norm[:, 3:4] * lat_sum
            ).astype(BF)
            wide_rows[part, 2 * span :] = (
                norm[:, 2:3] * quer + norm[:, 3:4] * quer_sum
            ).astype(BF)
            wkv = jnp.concatenate([wk_ref[part, :], wv_ref[part, :]], axis=1).astype(F32)
            wq = wq_ref[part, :].astype(F32)

            def total(value):
                return jnp.sum(value, axis=1, keepdims=True)

            vec = jnp.concatenate(
                [
                    total(wkv * med),
                    total(wkv * med_sum),
                    total(wkv * lat) + total(wq * quer),
                    total(wkv * lat_sum) + total(wq * quer_sum),
                    jnp.zeros((step, step - 4), F32),
                ],
                axis=1,
            )
            vec_ref[:, part] = vec_in[:, part] + vec.T[: vec_ref.shape[0]]
        if len(keep_ref.shape) == 2:
            keep_ref[...] = wide_rows[...]
            return
        imgs, two, height, _ = keep_ref.shape
        share = width // imgs
        tall = share // (2 * two)
        bit = lax.rem(index_ref[0], 2)
        for ref, mine in ((keep_ref, bit), (send_ref, 1 - bit)):
            for i in range(imgs):
                for y in range(two):
                    at = pl.multiple_of(i * share + 2 * y * tall + mine * tall, tall)
                    rows = wide_rows[pl.ds(at, tall), :]
                    ref[i, y, :tall] = rows[:, : 2 * span]
                    ref[i, y, tall : tall + tall // 2, :span] = rows[: tall // 2, 2 * span :]
                    ref[i, y, tall : tall + tall // 2, span:] = rows[tall // 2 :, 2 * span :]
                    start = tall + tall // 2
                    if group == 0:
                        size = extra_ref.shape[0] // (2 * two * imgs)
                        at = pl.multiple_of((i * two + y) * 2 * size + mine * size, size)
                        rows = extra_ref[pl.ds(at, size), :]
                        ref[i, y, start : start + size] = rows[:, : 2 * span]
                        ref[i, y, start + size : start + 2 * size] = rows[:, 2 * span :]
                    else:
                        rows = jnp.zeros((height - start, 2 * span), F32)
                        if y == 0:
                            at = slice(i * share, (i + 1) * share)
                            six = jnp.concatenate([vec_ref[:4, at], extra_ref[:2, at]], axis=0)
                            six = jnp.where(mine == 0, six, 0.0)
                            six = jnp.pad(six, ((0, height - start - 6), (0, 2 * span - share)))
                            rows = six
                        ref[i, y, start:] = rows.astype(BF)


def laid_out(width, imgs, inner):
    share = width // imgs
    return share % 128 == 0 and share <= inner and inner % (64 * imgs) == 0


def attend_back_call(
    group,
    doc_ids,
    queries,
    grad_att,
    att,
    kv_med,
    kv_lat,
    hat_med,
    hat_lat,
    w_keyval,
    w_query,
    norms,
    extra,
    vectors,
    index,
    imgs,
    deps,
):
    chunks, _, inner = queries.shape
    micro, slots, keys, both = kv_med.shape
    docs, lat_rows = kv_lat.shape[1:3]
    lats = chunks * lat_rows
    width = hat_med.shape[1]
    groups = HEADS // GROUP
    span = inner // groups
    wide = GROUP * lats
    rows = slots * keys
    lat_block = docs * lat_rows

    if laid_out(width, imgs, inner):
        tall = width // (imgs * chunks)
        height = tall + tall // 2 + (2 * inner // (imgs * chunks) if group == 0 else 16)
        result = jax.ShapeDtypeStruct((imgs, chunks // 2, height, inner), BF)
    else:
        result = jax.ShapeDtypeStruct((width, 3 * span), BF)
    result_spec = pl.BlockSpec(result.shape, lambda i, ids, p: (0,) * len(result.shape))

    def cols(at, *tail):
        return pl.BlockSpec(
            (1,) + tail, lambda i, ids, p: (i,) + (0,) * (len(tail) - 1) + (at,)
        )

    def tokens(at, size):
        return pl.BlockSpec((chunks, lat_block, size), lambda i, ids, p: (0, i, at))

    def fixed(at, size):
        return pl.BlockSpec((width, size), lambda i, ids, p: (0, at))

    return hbm_call(
        functools.partial(attend_back_kernel, group, len(deps)),
        range(16),
        (0, 1),
        grid_spec=pltpu.PrefetchScalarGridSpec(
            num_scalar_prefetch=2,
            grid=(micro,),
            in_specs=[
                tokens(group, span),
                tokens(group, span),
                tokens(group, span),
                tokens(inner // LANES, LANES),
                cols(group, slots, keys, span),
                cols(groups + group, slots, keys, span),
                cols(group, docs, lat_rows, span),
                cols(groups + group, docs, lat_rows, span),
                pl.BlockSpec((rows, width), lambda i, ids, p: (i, 0)),
                pl.BlockSpec(hat_lat.shape, lambda i, ids, p: (0, 0, 0)),
                fixed(group, span),
                fixed(groups + group, span),
                fixed(group, span),
                fixed(0, norms.shape[1]),
                pl.BlockSpec(extra.shape, lambda i, ids, p: (0, 0)),
                pl.BlockSpec(vectors.shape, lambda i, ids, p: (0, 0)),
            ]
            + [ANY] * len(deps),
            out_specs=[
                pl.BlockSpec((rows, 2 * span), lambda i, ids, p: (i, 0)),
                pl.BlockSpec((lat_block, 2 * span), lambda i, ids, p: (i, 0)),
                pl.BlockSpec((chunks, micro * lat_block, span), lambda i, ids, p: (0, 0, 0)),
                result_spec,
                result_spec,
                pl.BlockSpec(vectors.shape, lambda i, ids, p: (0, 0)),
            ],
            scratch_shapes=[
                pltpu.VMEM((docs, wide, span), BF),
                pltpu.VMEM((docs, wide, span), BF),
                pltpu.VMEM((docs, wide, span), F32),
                pltpu.VMEM((docs, 2, wide), F32),
                pltpu.VMEM((width, 2 * span), F32),
                pltpu.VMEM((width, 2 * span), F32),
                pltpu.VMEM((2, 2 * span), F32),
                pltpu.VMEM((width, 3 * span), BF),
            ],
        ),
        out_shape=[
            jax.ShapeDtypeStruct((micro * rows, 2 * span), BF),
            jax.ShapeDtypeStruct((micro * lat_block, 2 * span), BF),
            jax.ShapeDtypeStruct((chunks, micro * lat_block, span), BF),
            result,
            result,
            jax.ShapeDtypeStruct(vectors.shape, F32),
        ],
        compiler_params=params(48),
        cost_estimate=cost(3),
        name="attend_back",
    )(
        doc_ids,
        index,
        queries,
        grad_att,
        att,
        att,
        kv_med,
        kv_med,
        kv_lat,
        kv_lat,
        hat_med,
        hat_lat,
        w_keyval,
        w_keyval,
        w_query,
        norms,
        extra,
        vectors,
        *deps,
    )


def media_back_kernel(media_ref, ga_ref, gb_ref, wka_ref, wva_ref, wkb_ref, wvb_ref, gain_ref, *rest):
    out_ref, token_ref = rest[-2:]
    token_ref[...] = jnp.zeros_like(token_ref)
    wa = jnp.concatenate([wka_ref[...], wva_ref[...]], axis=1)
    wb = jnp.concatenate([wkb_ref[...], wvb_ref[...]], axis=1)
    rows = media_ref.shape[0]
    step = min(rows, 256)

    for at in range(0, rows, step):
        part = pl.ds(at, step)
        up = dot(ga_ref[part, :], wa, NT) + dot(gb_ref[part, :], wb, NT)
        hat, inv = standardize(media_ref[part, :].astype(F32))
        back, _ = norm_back(hat, inv, gain_ref[...], up)
        out_ref[part, :] = back.astype(BF)


def key_value_blocks(width, span):
    groups = HEADS // GROUP
    return [
        pl.BlockSpec((width, span), lambda i, at=at: (0, at))
        for g in range(groups)
        for at in (g, groups + g)
    ]


def media_back_call(media, grad_a, grad_b, w_keyval, gain, first, steps, whole, deps):
    rows, width = media.shape
    half = grad_a.shape[1]
    block = 512
    fixed = lambda i: (0, 0)
    moving = lambda i: (first + i, 0)
    extra = tuple(deps) if whole is None else tuple(deps) + (whole,)
    return hbm_call(
        media_back_kernel,
        range(8),
        (0,),
        grid=(steps,),
        in_specs=[
            pl.BlockSpec((block, width), moving),
            pl.BlockSpec((block, half), moving),
            pl.BlockSpec((block, half), moving),
            *key_value_blocks(width, half // 2),
            pl.BlockSpec((1, width), fixed),
        ]
        + [ANY] * len(extra),
        out_specs=[pl.BlockSpec((block, width), moving), pl.BlockSpec(TOKEN.shape, fixed)],
        out_shape=[jax.ShapeDtypeStruct((rows, width), BF), TOKEN],
        input_output_aliases={} if whole is None else {7 + len(extra): 0},
        compiler_params=params(28),
        cost_estimate=cost(2.5 * steps),
        name="media_back",
    )(media, grad_a, grad_b, w_keyval, w_keyval, w_keyval, w_keyval, gain, *extra)


def swap(value, axis, bit):
    size = lax.axis_size(axis)
    return lax.ppermute(value, axis, [(i, i ^ bit) for i in range(size)])


def gather_chunks(own):
    far = swap(own, "patch", 2)
    return own, far, swap(own, "patch", 1), swap(far, "patch", 1)


def gather_patch(own):
    return jnp.stack(gather_chunks(own))


def add(first, second):
    return (first.astype(F32) + second.astype(F32)).astype(BF)


def scatter_patch(keep, send):
    near = add(keep, swap(send, "patch", 1))
    return near[0], swap(near[1], "patch", 2)


def sum_kernel(two, *refs):
    values = [ref[...] for ref in refs[1 : 1 + (4 if two else 2)]]
    if two:
        values = [
            (values[i].astype(F32) + values[i + 2].astype(F32)).astype(BF) for i in range(2)
        ]
    refs[-2][...], refs[-1][...] = values


def split_sum(first, second, place, mine, deps):
    shape = first.shape
    lead, tail = shape[:place], shape[place + 1 :]
    count = 1
    for size in lead:
        count *= size
    flat = (count, 2) + ((1,) * max(0, 2 - len(tail)) + tail)
    steps = 2 if count % 2 == 0 and first.size * 2 > (1 << 20) else 1
    block = (count // steps, 1) + flat[2:]
    zeros = (0,) * (len(flat) - 2)
    keep = pl.BlockSpec(block, lambda i, m: (i, m[0]) + zeros)
    send = pl.BlockSpec(block, lambda i, m: (i, 1 - m[0]) + zeros)
    out = pl.BlockSpec(block, lambda i, m: (i, 0) + zeros)
    shape_out = jax.ShapeDtypeStruct((count, 1) + flat[2:], BF)
    values = [v.reshape(flat) for v in (first, second) if v is not None]
    halves = pl.pallas_call(
        functools.partial(sum_kernel, second is not None),
        grid_spec=pltpu.PrefetchScalarGridSpec(
            num_scalar_prefetch=1,
            grid=(steps,),
            in_specs=[keep, send] * len(values) + [ANY] * len(deps),
            out_specs=[out, out],
        ),
        out_shape=[shape_out, shape_out],
        compiler_params=params(12),
        cost_estimate=cost(2),
        name="split_sum",
    )(mine[None], *[v for v in values for _ in range(2)], *deps)
    return [h.reshape(lead + tail) for h in halves]


def last_sum_kernel(a_ref, b_ref, *refs):
    refs[-1][...] = (a_ref[...].astype(F32) + b_ref[...].astype(F32)).astype(BF)


def plain_sum(first, second, deps=()):
    return pl.pallas_call(
        last_sum_kernel,
        in_specs=[pl.BlockSpec(memory_space=pltpu.VMEM)] * 2 + [ANY] * len(deps),
        out_shape=jax.ShapeDtypeStruct(first.shape, BF),
        compiler_params=params(4),
        cost_estimate=cost(1),
        name="plain_sum",
    )(first, second, *deps)


class Scatter:
    def __init__(self, value, transit, axes, order, scope):
        self.places = [
            (axis, bit)
            for axis in axes
            for bit in reversed(range(lax.axis_size(axis).bit_length() - 1))
            if (axis, bit) in order
        ]
        self.order = list(order)
        self.scope = scope
        self.transit = transit
        self.value, self.transit = (
            v.reshape((2,) * len(self.places) + v.shape[len(axes) :]) for v in (value, transit)
        )

    def step(self, deps=()):
        with jax.named_scope(self.scope):
            if not self.order:
                if self.transit is not None:
                    self.value = plain_sum(self.value, self.transit, deps)
                    self.transit = None
                return (self.value,)
            axis, bit = self.order.pop(0)
            place = self.places.index((axis, bit))
            self.places.pop(place)
            mine = lax.rem(lax.div(lax.axis_index(axis), 1 << bit), 2)
            self.value, send = split_sum(self.value, self.transit, place, mine, deps)
            self.transit = swap(send, axis, 1 << bit)
            return self.value, send

    def finish(self, deps=()):
        while self.order or self.transit is not None:
            self.step(deps)
        return self.value


def img_bits():
    return [("img", bit) for bit in range(lax.axis_size("img").bit_length() - 1)]


def reduce_rest(keep, send, scope):
    with jax.named_scope(scope):
        transit = swap(send, "patch", 1)
    return Scatter(keep, transit, ("img", "patch"), [("patch", 1)] + img_bits(), scope)


def in_order(chunks):
    me = lax.axis_index("patch")
    order = (0, 2, 1, 3)
    return jnp.stack(
        [
            lax.dynamic_index_in_dim(
                chunks, jnp.take(jnp.array(order), jnp.bitwise_xor(me, j)), 0, keepdims=False
            )
            for j in range(4)
        ]
    )


def gather_rows(own):
    return in_order(gather_patch(own))


def place_kernel(index_ref, chunks_ref, out_ref):
    parts, _, unit = chunks_ref.shape
    for j in range(parts):
        apart = jnp.bitwise_xor(index_ref[0], j)
        at = jnp.where(apart == 1, 2, jnp.where(apart == 2, 1, apart))
        out_ref[:, j * unit : (j + 1) * unit] = chunks_ref[at].astype(F32)


def place_call(index, chunks, rows, imgs):
    parts, _, units = chunks.shape
    unit = units // imgs
    return pl.pallas_call(
        place_kernel,
        grid_spec=pltpu.PrefetchScalarGridSpec(
            num_scalar_prefetch=1,
            grid=(imgs,),
            in_specs=[pl.BlockSpec((parts, rows, unit), lambda i, p: (0, 0, i))],
            out_specs=pl.BlockSpec((rows, parts * unit), lambda i, p: (0, i)),
        ),
        out_shape=jax.ShapeDtypeStruct((rows, parts * units), F32),
        compiler_params=params(6),
        name="place_units",
    )(index, chunks)


def local(
    latents,
    media,
    doc_ids,
    w_query,
    w_keyval,
    w_output,
    w_expand,
    w_reduce,
    media_gain,
    media_shift,
    latent_gain,
    latent_shift,
    ff_gain,
    ff_shift,
    out_grad,
):
    micro, docs, lat_rows, width = latents.shape
    slots, keys = media.shape[1:3]
    inner = w_query.shape[1]
    ff = w_expand.shape[1]
    head_size = inner // HEADS
    scale = head_size ** (-0.5)
    parts = lax.axis_size("patch")
    imgs = lax.axis_size("img")
    patch_index = lax.axis_index("patch")
    own_rows = micro * docs * lat_rows
    all_rows = own_rows * parts
    groups = HEADS // GROUP
    span = inner // groups
    unit = ff // (imgs * parts)

    latents_own = latents.reshape(own_rows, width)
    cot_own = out_grad.reshape(own_rows, width)
    media_flat = media.reshape(-1, width)
    with jax.named_scope("gather_latents"):
        latents_far = swap(latents_own, "patch", 2)
        latents_near = swap(latents_own, "patch", 1)

    hat_med, kv_med, token = kv_call(media_flat, media_gain[None], media_shift[None], w_keyval)
    kv_med = kv_med.reshape(micro, slots, keys, 2 * inner)
    if unit % 128 == 0:
        w_exp, w_red = part_call(patch_index[None], w_expand, w_reduce, imgs, parts)
    else:
        w_exp = lax.dynamic_index_in_dim(
            w_expand.reshape(width, imgs, parts, unit), patch_index, 2, keepdims=False
        ).reshape(width, imgs * unit)
        w_red = lax.dynamic_index_in_dim(
            w_reduce.reshape(imgs, parts, unit, width), patch_index, 1, keepdims=False
        ).reshape(imgs * unit, width)

    (latents_far,) = gate((latents_far,), (token,))
    with jax.named_scope("gather_latents"):
        latents_both = swap(latents_far, "patch", 1)
    latents_all, hat_all, queries, kv_lat = latent_call(
        (latents_own, latents_far, latents_near, latents_both), latent_gain[None], latent_shift[None], w_query, w_keyval, (token,)
    )
    kv_lat = kv_lat.reshape(micro, docs, lat_rows, 2 * inner)
    (cot_sent,) = gate((cot_own,), (queries,))
    with jax.named_scope("gather_cotangent"):
        cot_chunks = gather_chunks(cot_sent)
        cot_all = jnp.stack(cot_chunks)
    keep, send = attend_call(doc_ids, queries, kv_med, kv_lat, ())
    with jax.named_scope("join_near"):
        near = join_call(keep, swap(send, "patch", 1), False, False, cot_chunks[1:])
    with jax.named_scope("join_far"):
        att_near = join_call(
            near, swap(near, "patch", 2), True, True, (latents_all, cot_all, w_exp, w_red)
        )
        att_far = swap(att_near, "patch", 1)

    mixed, ln_ff, hidden_act, grad_pre, up_own, up_keep, up_send, out_keep, out_send = ff_call(
        latents_all,
        att_near,
        att_far,
        cot_all,
        w_output,
        w_exp,
        w_red,
        ff_gain[None],
        ff_shift[None],
    )
    with jax.named_scope("sum_up"):
        up_sent = swap(up_send, "patch", 1)
        up_near = add(up_keep, up_sent[1])
        up_far = swap(up_near, "patch", 2)

    def flat(value):
        return value.reshape(all_rows, -1)

    ff_grads = ff_weights_call(
        flat(ln_ff), flat(grad_pre), flat(hidden_act), flat(cot_all), imgs, (up_near,)
    )
    grad_mixed, grad_branch, grad_att_own, ff_gain_part, ff_shift_part = mixed_back_call(
        up_own, up_sent, up_far, mixed, cot_own, w_output, ff_gain[None], (ff_grads,)
    )
    with jax.named_scope("gather_att"):
        grad_att = gather_patch(grad_att_own)
    att = jnp.concatenate([att_near, att_far])
    grad_output = dot(att_near[0, :, :inner], grad_branch, TN).astype(BF)

    with jax.named_scope("sum_ff"):
        ff_own = lax.psum_scatter(ff_grads, "img", scatter_dimension=0, tiled=True)[0]

    norms = jnp.stack([media_gain, media_shift, latent_gain, latent_shift], axis=1)
    ff_vectors = jnp.pad(jnp.concatenate([ff_gain_part, ff_shift_part]), ((0, 6), (0, 0)))
    share = width // imgs
    tall = share // parts
    direct = laid_out(width, imgs, inner)

    def back_call(group, extra, vectors, deps):
        gkv, gkv_lat, gq, keep, send, vectors = attend_back_call(
            group,
            doc_ids,
            queries,
            grad_att,
            att,
            kv_med,
            kv_lat,
            hat_med,
            hat_all,
            w_keyval,
            w_query,
            norms,
            extra,
            vectors,
            patch_index[None],
            imgs,
            deps,
        )
        if not direct:

            def split(value):
                size = value.shape[0] // (imgs * parts)
                return value.reshape(imgs, parts // 2, 2, size, value.shape[1])

            rows = split(keep)
            fold = [rows[..., : tall // 2, 2 * span :], rows[..., tall // 2 :, 2 * span :]]
            blocks = [rows[..., : 2 * span], jnp.concatenate(fold, axis=-1)]
            if group == 0:
                blocks += [split(extra)[..., :inner], split(extra)[..., inner:]]
            else:
                six = jnp.concatenate([vectors[:4], extra[:2]]).astype(BF)
                six = jnp.swapaxes(six.reshape(6, imgs, share), 0, 1)
                six = jnp.pad(six, ((0, 0), (0, 10), (0, width - share)))[:, None, None, :, :inner]
                blocks.append(
                    jnp.pad(six, ((0, 0), (0, parts // 2 - 1), (0, 1), (0, 0), (0, 0)))
                )
            blocks = jnp.concatenate(blocks, axis=3)
            bit = lax.rem(patch_index, 2)
            keep = lax.dynamic_index_in_dim(blocks, bit, 2, keepdims=False)
            send = lax.dynamic_index_in_dim(blocks, 1 - bit, 2, keepdims=False)
        return gkv, gkv_lat, gq, keep, send, vectors

    out_keep, out_send = gate((out_keep, out_send), (grad_att,))
    with jax.named_scope("sum_out"):
        out_near, out_far = scatter_patch(out_keep, out_send)
    gkv_0, gkv_lat_0, gq_0, keep, send, vectors = back_call(
        0, grad_output, jnp.zeros((8, width), F32), (ff_grads,)
    )
    first = reduce_rest(keep, send, "sum_weights_0")
    gkv_1, gkv_lat_1, gq_1, keep, send, vectors = back_call(
        1, ff_vectors, vectors, first.step()
    )
    done = first.step((vectors,))
    (out_far,) = gate((out_far,), (vectors,))
    keep, send, gq_0, gq_1 = gate((keep, send, gq_0, gq_1), (*done, out_far))
    second = reduce_rest(keep, send, "sum_weights_1")
    with jax.named_scope("sum_query"):
        gq_keep = jnp.concatenate([gq_0[:2], gq_1[:2]], axis=-1)
        gq_sent = swap(jnp.concatenate([gq_0[2:], gq_1[2:]], axis=-1), "patch", 1)

    def media_piece(at, size, whole, deps):
        return media_back_call(
            media_flat,
            gkv_0,
            gkv_1,
            w_keyval,
            media_gain[None],
            at,
            size,
            whole,
            deps,
        )

    media_grad, *done = media_piece(0, 4, None, (*second.step(), gq_keep))
    deps = (*first.step(done), *second.step(done))
    (gq_keep,) = gate((gq_keep,), done)
    with jax.named_scope("sum_query"):
        gq_near = add(gq_keep, gq_sent)
        gq_far = swap(gq_near[1], "patch", 2)
    media_grad, *done = media_piece(4, 2, media_grad, (*deps, gq_near))
    deps = (*first.step(done), *second.step(done))
    (ff_own,) = gate((ff_own,), deps)
    with jax.named_scope("gather_ff"):
        chunks = gather_patch(ff_own)
    media_grad, *done = media_piece(6, 2, media_grad, (*deps, ff_own))
    first.step(done)
    second.step(done)
    latents_out = out_call(mixed, out_near, out_far, done)
    latents_grad = latent_back_call(
        scale,
        (
            latents_own,
            grad_mixed,
            gq_near[0],
            gq_far,
            gkv_lat_0,
            gkv_lat_1,
            w_query,
            w_keyval,
            latent_gain[None],
        ),
        done,
    )

    first = first.finish(done)
    second = second.finish(done)

    def rows_of(value):
        return value.reshape(-1, value.shape[-1])

    with jax.named_scope("gather_weights"):
        whole = gather_rows(jnp.concatenate([first, second]))
    cut = first.shape[0]
    first, second = whole[:, :cut], whole[:, cut:]
    keyval_rows = [rows_of(first[:, :tall]), rows_of(second[:, :tall])]
    grad_keyval = jnp.concatenate(
        [rows[:, at * span : (at + 1) * span] for at in range(2) for rows in keyval_rows], axis=1
    ).astype(F32)
    end = tall + tall // 2

    def unfold(value):
        return rows_of(jnp.concatenate([value[..., :span], value[..., span:]], axis=1))

    query_rows = jnp.concatenate(
        [unfold(first[:, tall:end]), unfold(second[:, tall:end])], axis=1
    ).astype(F32)
    out_rows = first[:, end:]
    size = out_rows.shape[1] // 2
    out_rows = rows_of(
        jnp.concatenate([out_rows[:, :size], out_rows[:, size:]], axis=2)
    ).astype(F32)
    vectors = second[0, end : end + 6, :share].astype(F32)

    with jax.named_scope("place_ff"):
        expand, reduce = chunks[:, :share], chunks[:, share:]
        if unit % 128 == 0:
            expand_rows = place_call(patch_index[None], chunks, share, imgs)
        else:
            expand_rows = in_order(expand).reshape(parts, -1, imgs, unit)
            expand_rows = jnp.transpose(expand_rows, (1, 2, 0, 3)).reshape(-1, ff).astype(F32)
        reduce_rows = rows_of(in_order(reduce)).astype(F32)

    return (
        latents_out.reshape(latents.shape),
        latents_grad.reshape(latents.shape),
        media_grad.reshape(media.shape),
        query_rows,
        grad_keyval,
        out_rows,
        expand_rows,
        reduce_rows,
    ) + tuple(vectors[i] for i in range(6))


def solution(mesh):
    tokens = P(None, "img", "patch", None)
    return jax.shard_map(
        local,
        mesh=mesh,
        in_specs=(tokens, tokens, P(None, "img")) + (P(),) * 11 + (tokens,),
        out_specs=(tokens,) * 3 + (P("img", None),) * 5 + (P("img"),) * 6,
        check_vma=False,
    )
```

```python
import functools

import jax
import jax.numpy as jnp
from jax import lax
from jax.experimental import pallas as pl
from jax.experimental.pallas import tpu as pltpu
from jax.sharding import PartitionSpec as P

HEADS = 8
GROUP = 4
EPS = 1e-05
CHUNK = 4
FAR = -1e30
BF = jnp.bfloat16
F32 = jnp.float32
ANY = pl.BlockSpec(memory_space=pl.ANY)
TOKEN = jax.ShapeDtypeStruct((8, 128), jnp.float32)


def params(mib=56):
    return pltpu.CompilerParams(vmem_limit_bytes=mib << 20)


def cost(us):
    return pl.CostEstimate(flops=int(us * 1.1e9), bytes_accessed=0, transcendentals=0)


def hbm_call(kernel, held, kept, inside=(), **options):
    shapes = options.pop("out_shape")
    if isinstance(shapes, list):
        shapes = [pltpu.HBM(v.shape, v.dtype) if i in kept else v for i, v in enumerate(shapes)]
    options["out_shape"] = shapes
    scalars = options["grid_spec"].num_scalar_prefetch if "grid_spec" in options else 0
    inner = pl.pallas_call(kernel, **options)

    def run(*operands):
        def place(i, x):
            if i in inside:
                return pltpu.with_memory_space_constraint(x, pltpu.VMEM)
            if i in held or x.size >= 1 << 20:
                return pltpu.with_memory_space_constraint(x, pltpu.HBM)
            return x

        arrays = [place(i, x) for i, x in enumerate(operands[scalars:])]
        return inner(*operands[:scalars], *arrays)

    return run


def nothing_kernel(*refs):
    pass


def gate(carry, deps, space):
    return pl.pallas_call(
        nothing_kernel,
        in_specs=[ANY] * (len(carry) + len(deps)),
        out_specs=[ANY] * len(carry),
        out_shape=[space(c.shape, c.dtype) for c in carry],
        input_output_aliases={i: i for i in range(len(carry))},
        compiler_params=params(1),
        name="gate",
    )(
        *[pltpu.with_memory_space_constraint(c, space) for c in carry],
        *[
            pltpu.with_memory_space_constraint(d, pltpu.HBM) if d.size >= 1 << 20 else d
            for d in deps
        ],
    )


def dot(a, b, dims):
    return lax.dot_general(a, b, (dims, ((), ())), preferred_element_type=F32)


NN = ((1,), (0,))
NT = ((1,), (1,))
TN = ((0,), (0,))


def standardize(values):
    center = values - jnp.mean(values, axis=-1, keepdims=True)
    inv = lax.rsqrt(jnp.mean(center * center, axis=-1, keepdims=True) + EPS)
    return center * inv, inv


def norm_back(hat, inv, gain, upstream):
    scaled = upstream * gain
    back = inv * (
        scaled
        - jnp.mean(scaled, axis=-1, keepdims=True)
        - hat * jnp.mean(scaled * hat, axis=-1, keepdims=True)
    )
    return back, upstream * hat


def kv_kernel(media_ref, gain_ref, shift_ref, w_ref, hat_ref, kv_ref, token_ref):
    token_ref[...] = jnp.zeros_like(token_ref)
    rows = media_ref.shape[0]
    step = min(rows, 256)
    for at in range(0, rows, step):
        part = pl.ds(at, step)
        hat, _ = standardize(media_ref[part, :].astype(F32))
        ln = (hat * gain_ref[...] + shift_ref[...]).astype(BF)
        hat_ref[part, :] = hat.astype(BF)
        kv_ref[part, :] = dot(ln, w_ref[...], NN).astype(BF)


def kv_call(media, gain, shift, w_keyval):
    rows, width = media.shape
    outs = w_keyval.shape[1]
    block = 512
    return hbm_call(
        kv_kernel,
        range(4),
        (0, 1),
        grid=(rows // block,),
        in_specs=[
            pl.BlockSpec((block, width), lambda i: (i, 0)),
            pl.BlockSpec((1, width), lambda i: (0, 0)),
            pl.BlockSpec((1, width), lambda i: (0, 0)),
            pl.BlockSpec((width, outs), lambda i: (0, 0)),
        ],
        out_specs=[
            pl.BlockSpec((block, width), lambda i: (i, 0)),
            pl.BlockSpec((block, outs), lambda i: (i, 0)),
            pl.BlockSpec(TOKEN.shape, lambda i: (0, 0)),
        ],
        out_shape=[
            jax.ShapeDtypeStruct((rows, width), BF),
            jax.ShapeDtypeStruct((rows, outs), BF),
            TOKEN,
        ],
        compiler_params=params(20),
        cost_estimate=cost(16),
        name="media_keyval",
    )(media, gain, shift, w_keyval)


def latent_kernel(own, far, near, both, gain_ref, shift_ref, wq_ref, wkv_ref, cot_ref, *rest):
    raw_ref, hat_ref, q_ref, kv_ref, cot_out = rest[-5:]
    scale = (wq_ref.shape[1] // HEADS) ** (-0.5)
    cot_out[...] = cot_ref[...]
    for c, ref in enumerate((own, far, near, both)):
        raw = ref[...]
        raw_ref[c] = raw
        hat, _ = standardize(raw.astype(F32))
        hat_ref[c] = hat.astype(BF)
        ln = (hat * gain_ref[...] + shift_ref[...]).astype(BF)
        q_ref[c] = (dot(ln, wq_ref[...], NN).astype(BF).astype(F32) * scale).astype(BF)
        if c == 0:
            kv_ref[...] = dot(ln, wkv_ref[...], NN).astype(BF)


def latent_call(chunks, gain, shift, w_query, w_keyval, cot, deps):
    rows, width = chunks[0].shape
    inner = w_query.shape[1]
    count = len(chunks)
    return hbm_call(
        latent_kernel,
        (6, 7),
        range(4),
        (1, 2, 3),
        in_specs=[pl.BlockSpec(memory_space=pltpu.VMEM)] * (count + 5) + [ANY] * len(deps),
        out_shape=[
            jax.ShapeDtypeStruct((count, rows, width), BF),
            jax.ShapeDtypeStruct((count, rows, width), BF),
            jax.ShapeDtypeStruct((count, rows, inner), BF),
            jax.ShapeDtypeStruct((rows, 2 * inner), BF),
            jax.ShapeDtypeStruct(cot.shape, BF),
        ],
        compiler_params=params(28),
        cost_estimate=cost(6),
        name="latents",
    )(*chunks, gain, shift, w_query, w_keyval, cot, *deps)


def kv_columns(first, second):
    span = first.shape[1] // 2
    return jnp.concatenate(
        [first[:, :span], second[:, :span], first[:, span:], second[:, span:]], axis=1
    )


def latent_back_kernel(
    scale, raw_ref, mixed_ref, own_ref, far_ref, kv_a, kv_b, wq_ref, w_ref, gain_ref, *rest
):
    grad_q = ((own_ref[...].astype(F32) + far_ref[...].astype(F32)) * scale).astype(BF)
    up = (
        dot(grad_q, wq_ref[...], NT)
        + dot(kv_columns(kv_a[...], kv_b[...]), w_ref[...], NT)
    )
    hat, inv = standardize(raw_ref[...].astype(F32))
    back, _ = norm_back(hat, inv, gain_ref[...], up)
    rest[-1][...] = (mixed_ref[...] + back).astype(BF)


def latent_back_call(scale, args, deps):
    return hbm_call(
        functools.partial(latent_back_kernel, scale),
        (1, 4, 5, 6, 7),
        (),
        (2, 3),
        in_specs=[pl.BlockSpec(memory_space=pltpu.VMEM)] * len(args) + [ANY] * len(deps),
        out_shape=jax.ShapeDtypeStruct(args[0].shape, BF),
        compiler_params=params(24),
        cost_estimate=cost(4),
        name="latent_back",
    )(*args, *deps)


def out_kernel(mixed_ref, near_ref, far_ref, *rest):
    rest[-1][...] = (
        mixed_ref[...] + (near_ref[...].astype(F32) + far_ref[...].astype(F32))
    ).astype(BF)


def out_call(mixed, near, far, deps):
    return hbm_call(
        out_kernel,
        (0,),
        (),
        (1, 2),
        in_specs=[pl.BlockSpec(memory_space=pltpu.VMEM)] * 3 + [ANY] * len(deps),
        out_shape=jax.ShapeDtypeStruct(mixed.shape, BF),
        compiler_params=params(8),
        cost_estimate=cost(1.5),
        name="latents_out",
    )(mixed, near, far, *deps)


def block_mask(head_size, lats):
    rows = GROUP * lats
    cols = GROUP * head_size
    row_head = lax.broadcasted_iota(jnp.int32, (rows, cols), 0) // lats
    col_head = lax.broadcasted_iota(jnp.int32, (rows, cols), 1) // head_size
    return row_head == col_head


def spread_heads(values, mask):
    tiled = jnp.concatenate([values] * GROUP, axis=0)
    return jnp.where(mask, tiled, jnp.zeros_like(tiled))


def gather_heads(full, mask, lats):
    kept = jnp.where(mask, full, 0.0)
    total = kept[:lats]
    for head in range(1, GROUP):
        total = total + kept[head * lats : (head + 1) * lats]
    return total


LANES = 128


def terms(value):
    first = value.astype(BF)
    rest = value - first.astype(F32)
    second = rest.astype(BF)
    return first, second, (rest - second.astype(F32)).astype(BF)


def pick(shape, fn):
    row = lax.broadcasted_iota(jnp.int32, shape, 0)
    col = lax.broadcasted_iota(jnp.int32, shape, 1)
    return jnp.where(fn(row, col), 1.0, 0.0).astype(BF)


def holds(lane, head, figure):
    return (lane < 24 * figure + 24) & (lane >= 24 * figure) & (lane % HEADS == head)


def pack_rows(figures):
    rows = jnp.concatenate([t for f in figures for t in terms(f)], axis=0)
    eye = pick((rows.shape[0], LANES), lambda r, c: r == c)
    return dot(rows, eye, TN).astype(BF)


def pack_cols(figures):
    total = None
    for i, figure in enumerate(figures):
        for k, term in enumerate(terms(figure)):
            at = HEADS * (3 * i + k)
            place = pick((LANES, LANES), lambda r, c: (r < HEADS) & (c == r + at))
            part = dot(term, place, NN)
            total = part if total is None else total + part
    return total.astype(BF)


def widen(packed, figure, inner):
    size = inner // HEADS
    return dot(packed, pick((LANES, inner), lambda r, c: holds(r, c // size, figure)), NN)


def narrow(packed, figure):
    return dot(
        packed, pick((LANES, LANES), lambda r, c: (c < HEADS) & holds(r, c, figure)), NN
    )


def doc_rows(ref, d, lat_rows, cols):
    rows = slice(d * lat_rows, (d + 1) * lat_rows)
    return jnp.concatenate([ref[c, rows, cols] for c in range(ref.shape[0])], axis=0)


def doc_spans(doc_ref, micro, docs, slots):
    counts = []
    for d in range(docs):
        total = 0
        for s in range(slots):
            total = total + jnp.where(doc_ref[micro, s] == d, 1, 0)
        counts.append(total)
    first = 0
    spans = []
    for count in counts:
        spans.append((first, count))
        first = first + count
    return spans


def slot_chunk(span, step, slots):
    first, count = span
    low = first + step * CHUNK
    return jnp.minimum(low, slots - CHUNK), low, first + count


def own_rows_of(at, low, high, keys):
    slot = at + lax.broadcasted_iota(jnp.int32, (CHUNK * keys, 1), 0) // keys
    return (slot >= low) & (slot < high)


def steps_of(span):
    return (span[1] + CHUNK - 1) // CHUNK


def attend_kernel(deps, doc_ref, q_ref, kv_ref, kvl_ref, *rest):
    keep_ref, send_ref, bd, score, acc, top, tot = rest[deps:]
    chunks, rows, inner = q_ref.shape
    docs, lat_rows = kvl_ref.shape[1:3]
    lats = chunks * lat_rows
    slots, keys = kv_ref.shape[1:3]
    groups = HEADS // GROUP
    span = inner // groups
    micro = pl.program_id(0)
    mask = block_mask(inner // HEADS, lats)
    cols = [slice(g * span, (g + 1) * span) for g in range(groups)]
    vals = [slice(inner + g * span, inner + (g + 1) * span) for g in range(groups)]
    spans = doc_spans(doc_ref, micro, docs, slots)
    tall = CHUNK * keys

    def load(at, part):
        return kv_ref[0, pl.ds(at, CHUNK), :, part].reshape(tall, span)

    for d in range(docs):
        at, low, high = slot_chunk(spans[d], 0, slots)
        bias = jnp.where(own_rows_of(at, low, high, keys), 0.0, FAR)
        bias = jnp.concatenate([bias, jnp.zeros((lat_rows, 1), F32)], axis=0)
        for g in range(groups):
            spread = spread_heads(doc_rows(q_ref, d, lat_rows, cols[g]), mask)
            bd[d, g] = spread
            key = jnp.concatenate([load(at, cols[g]), kvl_ref[0, d, :, cols[g]]], axis=0)
            val = dot(key, spread, NT) + bias
            score[d, g, 0] = val
            top[d, g] = jnp.max(val, axis=0, keepdims=True)
    for d in range(docs):

        def more(step, carry, d=d):
            at, low, high = slot_chunk(spans[d], step, slots)
            bias = jnp.where(own_rows_of(at, low, high, keys), 0.0, FAR)
            for g in range(groups):
                val = dot(load(at, cols[g]), bd[d, g], NT) + bias
                score[d, g, step, :tall] = val
                top[d, g] = jnp.maximum(top[d, g], jnp.max(val, axis=0, keepdims=True))
            return carry

        lax.fori_loop(1, steps_of(spans[d]), more, 0)
    for d in range(docs):
        at, low, high = slot_chunk(spans[d], 0, slots)
        for g in range(groups):
            expo = jnp.exp(score[d, g, 0] - top[d, g])
            tot[d, g] = jnp.sum(expo, axis=0, keepdims=True)
            val = jnp.concatenate([load(at, vals[g]), kvl_ref[0, d, :, vals[g]]], axis=0)
            acc[d, g] = dot(expo.astype(BF), val, TN)
    for d in range(docs):

        def more_values(step, carry, d=d):
            at, low, high = slot_chunk(spans[d], step, slots)
            for g in range(groups):
                expo = jnp.exp(score[d, g, step, :tall] - top[d, g])
                tot[d, g] = tot[d, g] + jnp.sum(expo, axis=0, keepdims=True)
                acc[d, g] = acc[d, g] + dot(expo.astype(BF), load(at, vals[g]), TN)
            return carry

        lax.fori_loop(1, steps_of(spans[d]), more_values, 0)
    half = chunks // 2
    for d in range(docs):
        rows_d = slice(d * lat_rows, (d + 1) * lat_rows)

        def by_head(ref):
            return jnp.concatenate(
                [
                    ref[d, g][:, h * lats : (h + 1) * lats]
                    for g in range(groups)
                    for h in range(GROUP)
                ],
                axis=0,
            )

        packed = pack_rows([by_head(top), by_head(tot)])
        outs = [gather_heads(acc[d, g], mask, lats).astype(BF) for g in range(groups)]
        for c in range(chunks):
            ref = keep_ref if c < half else send_ref
            part = slice(c * lat_rows, (c + 1) * lat_rows)
            for g in range(groups):
                ref[c % half, rows_d, cols[g]] = outs[g][part]
            ref[c % half, rows_d, inner:] = packed[part]


def attend_call(doc_ids, queries, kv_med, kv_lat, deps):
    chunks, _, inner = queries.shape
    micro, slots, keys, both = kv_med.shape
    docs, lat_rows = kv_lat.shape[1:3]
    lats = chunks * lat_rows
    rows = docs * lat_rows
    groups = HEADS // GROUP
    span = inner // groups
    wide = GROUP * lats
    half = chunks // 2
    longest = (slots - docs + CHUNK) // CHUNK
    out_spec = pl.BlockSpec((half, rows, inner + LANES), lambda i, ids: (0, i, 0))
    out_shape = jax.ShapeDtypeStruct((half, micro * rows, inner + LANES), BF)
    return hbm_call(
        functools.partial(attend_kernel, len(deps)),
        range(3),
        (),
        grid_spec=pltpu.PrefetchScalarGridSpec(
            num_scalar_prefetch=1,
            grid=(micro,),
            in_specs=[
                pl.BlockSpec((chunks, rows, inner), lambda i, ids: (0, i, 0)),
                pl.BlockSpec((1, slots, keys, both), lambda i, ids: (i, 0, 0, 0)),
                pl.BlockSpec((1, docs, lat_rows, both), lambda i, ids: (i, 0, 0, 0)),
            ]
            + [ANY] * len(deps),
            out_specs=[out_spec, out_spec],
            scratch_shapes=[
                pltpu.VMEM((docs, groups, wide, span), BF),
                pltpu.VMEM((docs, groups, longest, CHUNK * keys + lat_rows, wide), F32),
                pltpu.VMEM((docs, groups, wide, span), F32),
                pltpu.VMEM((docs, groups, 1, wide), F32),
                pltpu.VMEM((docs, groups, 1, wide), F32),
            ],
        ),
        out_shape=[out_shape, out_shape],
        compiler_params=params(40),
        cost_estimate=cost(13),
        name="attend",
    )(doc_ids, queries, kv_med, kv_lat, *deps)


def join_kernel(last, flip, a_ref, b_ref, *rest):
    out_ref = rest[-1]
    inner = a_ref.shape[2] - LANES
    count = a_ref.shape[0]
    for c in range(count):
        first, second = a_ref[c], b_ref[count - 1 - c if flip else c]
        pack_a, pack_b = first[:, inner:], second[:, inner:]
        top_a, top_b = widen(pack_a, 0, inner), widen(pack_b, 0, inner)
        best = jnp.maximum(top_a, top_b)
        fac_a, fac_b = jnp.exp(top_a - best), jnp.exp(top_b - best)
        out = fac_a * first[:, :inner].astype(F32) + fac_b * second[:, :inner].astype(F32)
        if last:
            total = fac_a * widen(pack_a, 1, inner) + fac_b * widen(pack_b, 1, inner)
            out = out / total
        out_ref[c, :, :inner] = out.astype(BF)
        small_a, small_b = narrow(pack_a, 0), narrow(pack_b, 0)
        small = jnp.maximum(small_a, small_b)
        sum_ab = jnp.exp(small_a - small) * narrow(pack_a, 1) + jnp.exp(
            small_b - small
        ) * narrow(pack_b, 1)
        if last:
            lane = lax.broadcasted_iota(jnp.int32, sum_ab.shape, 1)
            lse = jnp.where(lane < HEADS, small + jnp.log(jnp.maximum(sum_ab, 1e-30)), 0.0)
            out_ref[c, :, inner:] = pack_cols([lse])
        else:
            out_ref[c, :, inner:] = pack_cols([small, sum_ab])


def join_call(first, second, last, flip, deps=()):
    count, rows, cols = first.shape
    block = min(rows, 128)
    spec = pl.BlockSpec((count, block, cols), lambda i: (0, i, 0))
    return pl.pallas_call(
        functools.partial(join_kernel, last, flip),
        grid=(rows // block,),
        in_specs=[spec, spec] + [ANY] * len(deps),
        out_specs=spec,
        out_shape=jax.ShapeDtypeStruct(first.shape, BF),
        compiler_params=params(10),
        cost_estimate=cost(3.5),
        name="join_last" if last else "join_first",
    )(first, second, *deps)


def ff_kernel(
    lat_ref,
    near_ref,
    far_ref,
    cot_ref,
    wo_ref,
    we_ref,
    wr_ref,
    gain_ref,
    shift_ref,
    mixed_ref,
    ln_ref,
    act_ref,
    gpre_ref,
    up_own,
    up_keep,
    up_send,
    out_keep,
    out_send,
):
    i = pl.program_id(0)
    half = pl.num_programs(0) // 2
    att = jnp.where(i < half, near_ref[0], far_ref[0])
    mixed = lat_ref[0].astype(F32) + dot(att, wo_ref[...], NN)
    hat, _ = standardize(mixed)
    ln = (hat * gain_ref[...] + shift_ref[...]).astype(BF)
    ln_ref[0] = ln
    pre = dot(ln, we_ref[...], NN)
    cdf = 0.5 + 0.5 * lax.erf(pre * (0.5**0.5))
    slope = cdf + pre * (0.3989422804014327 * jnp.exp(-0.5 * pre * pre))
    act = (pre * cdf).astype(BF)
    act_ref[0] = act
    gpre = (dot(cot_ref[0], wr_ref[...], NT) * slope).astype(BF)
    gpre_ref[0] = gpre
    up = dot(gpre, we_ref[...], NT).astype(BF)
    out = dot(act, wr_ref[...], NN).astype(BF)

    @pl.when(i == 0)
    def _():
        mixed_ref[...] = mixed
        up_own[...] = up

    @pl.when(i == 1)
    def _():
        up_keep[...] = up

    @pl.when(i < half)
    def _():
        out_keep[0] = out

    @pl.when(i >= half)
    def _():
        up_send[0] = up
        out_send[0] = out


def ff_call(latents, near, far, cot, w_output, w_exp, w_red, gain, shift):
    chunks, rows, width = latents.shape
    inner = w_output.shape[0]
    units = w_exp.shape[1]
    half = chunks // 2

    def chunk(cols):
        return pl.BlockSpec((1, rows, cols), lambda i: (i, 0, 0))

    def first(cols):
        return pl.BlockSpec((1, rows, cols), lambda i: (jnp.minimum(i, half - 1), 0, 0))

    def second(cols):
        return pl.BlockSpec((1, rows, cols), lambda i: (jnp.maximum(i - half, 0), 0, 0))

    def fixed(*shape):
        return pl.BlockSpec(shape, lambda i: (0,) * len(shape))

    def out(count, cols):
        return jax.ShapeDtypeStruct((count, rows, cols), BF)

    return hbm_call(
        ff_kernel,
        (0, 4, 5, 6),
        (0, 1, 2, 3, 7, 8),
        (1, 2),
        grid=(chunks,),
        in_specs=[
            chunk(width),
            first(inner),
            second(inner),
            chunk(width),
            fixed(inner, width),
            fixed(width, units),
            fixed(units, width),
            fixed(1, width),
            fixed(1, width),
        ],
        out_specs=[
            fixed(rows, width),
            chunk(width),
            chunk(units),
            chunk(units),
            fixed(rows, width),
            fixed(rows, width),
            second(width),
            first(width),
            second(width),
        ],
        out_shape=[
            jax.ShapeDtypeStruct((rows, width), F32),
            out(chunks, width),
            out(chunks, units),
            out(chunks, units),
            jax.ShapeDtypeStruct((rows, width), BF),
            jax.ShapeDtypeStruct((rows, width), BF),
            out(half, width),
            out(half, width),
            out(half, width),
        ],
        compiler_params=params(40),
        cost_estimate=cost(18),
        name="feed_forward",
    )(latents, near, far, cot, w_output, w_exp, w_red, gain, shift)


def ff_weights_kernel(ln_ref, gpre_ref, act_ref, cot_ref, *rest):
    out_ref = rest[-1]
    count, rows, width = out_ref.shape
    half = rows // 2
    for part, (left, right) in enumerate(((ln_ref, gpre_ref), (act_ref, cot_ref))):
        product = dot(left[...], right[...], TN).astype(BF)
        out_ref[:, part * half : (part + 1) * half, :] = product.reshape(count, half, width)


def ff_weights_call(ln_ff, grad_pre, hidden_act, cot, imgs, deps):
    tokens, width = ln_ff.shape
    units = grad_pre.shape[1]
    half = units // imgs
    steps = 2
    left = pl.BlockSpec((tokens, width // steps), lambda i: (0, i))
    right = pl.BlockSpec((tokens, width), lambda i: (0, 0))
    return hbm_call(
        ff_weights_kernel,
        range(4),
        (),
        grid=(steps,),
        in_specs=[left, right, left, right] + [ANY] * len(deps),
        out_specs=pl.BlockSpec((imgs // steps, 2 * half, width), lambda i: (i, 0, 0)),
        out_shape=pltpu.HBM((imgs, 2 * half, width), BF),
        compiler_params=params(28),
        cost_estimate=cost(9),
        name="ff_weights",
    )(ln_ff, grad_pre, hidden_act, cot, *deps)


def mixed_back_kernel(own_ref, near_ref, far_ref, mixed_ref, cot_ref, wo_ref, gain_ref, *rest):
    gm_ref, gb_ref, ga_ref, dg_ref, ds_ref = rest[-5:]
    up = own_ref[...].astype(F32) + near_ref[0].astype(F32) + far_ref[...].astype(F32)
    hat, inv = standardize(mixed_ref[...])
    back, gains = norm_back(hat, inv, gain_ref[...], up)
    grad = cot_ref[...].astype(F32) + back
    gm_ref[...] = grad
    branch = grad.astype(BF)
    gb_ref[...] = branch
    ga_ref[...] = dot(branch, wo_ref[...], NT).astype(BF)
    dg_ref[...] = jnp.sum(gains, axis=0, keepdims=True)
    ds_ref[...] = jnp.sum(up, axis=0, keepdims=True)


def mixed_back_call(own, near, far, mixed, cot, w_output, gain, deps):
    rows, width = mixed.shape
    inner = w_output.shape[0]
    return hbm_call(
        mixed_back_kernel,
        (3, 4, 5),
        (0,),
        (0, 1, 2),
        in_specs=[pl.BlockSpec(memory_space=pltpu.VMEM)] * 7 + [ANY] * len(deps),
        out_shape=[
            jax.ShapeDtypeStruct((rows, width), F32),
            jax.ShapeDtypeStruct((rows, width), BF),
            jax.ShapeDtypeStruct((rows, inner), BF),
            jax.ShapeDtypeStruct((1, width), F32),
            jax.ShapeDtypeStruct((1, width), F32),
        ],
        compiler_params=params(20),
        cost_estimate=cost(4),
        name="mixed_back",
    )(own, near, far, mixed, cot, w_output, gain, *deps)


def part_kernel(index_ref, e_ref, r_ref, eo_ref, ro_ref):
    eo_ref[...] = e_ref[...]
    ro_ref[...] = r_ref[...]


def part_call(index, w_expand, w_reduce, imgs, parts):
    width, ff = w_expand.shape
    unit = ff // (imgs * parts)
    return hbm_call(
        part_kernel,
        range(2),
        range(2),
        grid_spec=pltpu.PrefetchScalarGridSpec(
            num_scalar_prefetch=1,
            grid=(imgs,),
            in_specs=[
                pl.BlockSpec((width, unit), lambda i, p: (0, i * parts + p[0])),
                pl.BlockSpec((unit, width), lambda i, p: (i * parts + p[0], 0)),
            ],
            out_specs=[
                pl.BlockSpec((width, unit), lambda i, p: (0, i)),
                pl.BlockSpec((unit, width), lambda i, p: (i, 0)),
            ],
        ),
        out_shape=[
            jax.ShapeDtypeStruct((width, imgs * unit), BF),
            jax.ShapeDtypeStruct((imgs * unit, width), BF),
        ],
        compiler_params=params(6),
        name="weight_part",
    )(index, w_expand, w_reduce)


def attend_back_kernel(
    group,
    deps,
    doc_ref,
    index_ref,
    q_ref,
    go_ref,
    att_ref,
    lse_ref,
    k_ref,
    v_ref,
    kl_ref,
    vl_ref,
    hat_ref,
    lat_hat_ref,
    wk_ref,
    wv_ref,
    wq_ref,
    norm_ref,
    extra_ref,
    vec_in,
    *rest,
):
    gkv_ref, gkvl_ref, gq_ref, keep_ref, send_ref, vec_ref = rest[deps : deps + 6]
    bdq, bdo, acc, stat, h_med, h_lat, sums, wide_rows = rest[deps + 6 :]
    chunks, _, span = q_ref.shape
    docs, lat_rows = kl_ref.shape[1:3]
    lats = chunks * lat_rows
    slots, keys = k_ref.shape[1:3]
    micro = pl.program_id(0)
    mask = block_mask(span // GROUP, lats)
    every = slice(None)
    scale = (span // GROUP) ** (-0.5)

    spans = doc_spans(doc_ref, micro, docs, slots)
    tall = CHUNK * keys

    def pair(key, value, bias, d):
        score = dot(key, bdq[d], NT) + bias
        prob = jnp.exp(score - stat[d, 0:1])
        dprob = dot(value, bdo[d], NT)
        dscore = (prob * (dprob - stat[d, 1:2])).astype(BF)
        grad_key = dot(dscore, bdq[d], NN).astype(BF)
        grad_value = dot(prob.astype(BF), bdo[d], NN).astype(BF)
        grad_query = dot(dscore, key, TN)
        return grad_key, grad_value, grad_query

    def load(ref, at):
        return ref[0, pl.ds(at, CHUNK)].reshape(tall, span)

    def store(at, own, grad_key, grad_value):
        part = pl.ds(pl.multiple_of(at * keys, keys), tall)
        gkv_ref[part, :span] = jnp.where(own, grad_key, gkv_ref[part, :span])
        gkv_ref[part, span:] = jnp.where(own, grad_value, gkv_ref[part, span:])

    sel = pick((HEADS, LANES), lambda r, c: holds(c, r, 0))
    size = span // GROUP
    head_sel = pick((HEADS, span), lambda r, c: c // size == r)

    def row(by_head, at):
        return jnp.concatenate([by_head[at + h : at + h + 1] for h in range(GROUP)], axis=1)

    for d in range(docs):
        out_grad = doc_rows(go_ref, d, lat_rows, every)
        bdq[d] = spread_heads(doc_rows(q_ref, d, lat_rows, every), mask)
        bdo[d] = spread_heads(out_grad, mask)
        lse = dot(sel, doc_rows(lse_ref, d, lat_rows, every), NT)
        stat[d, 0:1] = row(lse, group * GROUP)
        attended = doc_rows(att_ref, d, lat_rows, every)
        high, low, _ = terms(out_grad.astype(F32) * attended.astype(F32))
        stat[d, 1:2] = row(dot(head_sel, high, NT) + dot(head_sel, low, NT), 0)
    for d in range(docs):
        rows_d = slice(d * lat_rows, (d + 1) * lat_rows)
        at, low, high = slot_chunk(spans[d], 0, slots)
        own = own_rows_of(at, low, high, keys)
        bias = jnp.concatenate([jnp.where(own, 0.0, FAR), jnp.zeros((lat_rows, 1), F32)], axis=0)
        key = jnp.concatenate([load(k_ref, at), kl_ref[0, d]], axis=0)
        value = jnp.concatenate([load(v_ref, at), vl_ref[0, d]], axis=0)
        grad_key, grad_value, grad_query = pair(key, value, bias, d)
        store(at, own, grad_key[:tall], grad_value[:tall])
        gkvl_ref[rows_d, :span] = grad_key[tall:]
        gkvl_ref[rows_d, span:] = grad_value[tall:]
        acc[d] = grad_query
    for d in range(docs):

        def more(step, carry, d=d):
            at, low, high = slot_chunk(spans[d], step, slots)
            own = own_rows_of(at, low, high, keys)
            grad_key, grad_value, grad_query = pair(
                load(k_ref, at), load(v_ref, at), jnp.where(own, 0.0, FAR), d
            )
            store(at, own, grad_key, grad_value)
            acc[d] = acc[d] + grad_query
            return carry

        lax.fori_loop(1, steps_of(spans[d]), more, 0)
    for d in range(docs):
        full = gather_heads(acc[d], mask, lats).astype(BF)
        for c in range(chunks):
            gq_ref[c, pl.ds(micro * docs * lat_rows + d * lat_rows, lat_rows)] = full[
                c * lat_rows : (c + 1) * lat_rows
            ]
    part = dot(hat_ref[...], gkv_ref[...], TN)
    part_sum = dot(jnp.ones((8, gkv_ref.shape[0]), BF), gkv_ref[...], NN)[0:1]
    lat_part = dot(lat_hat_ref[0, pl.ds(micro * docs * lat_rows, docs * lat_rows)], gkvl_ref[...], TN)
    lat_sum_part = jnp.sum(gkvl_ref[...].astype(F32), axis=0, keepdims=True)

    @pl.when(micro == 0)
    def _():
        h_med[...] = part
        h_lat[...] = lat_part
        sums[0:1, :] = part_sum
        sums[1:2, :] = lat_sum_part

    @pl.when(micro > 0)
    def _():
        h_med[...] = h_med[...] + part
        h_lat[...] = h_lat[...] + lat_part
        sums[0:1, :] = sums[0:1, :] + part_sum
        sums[1:2, :] = sums[1:2, :] + lat_sum_part

    @pl.when(micro == pl.num_programs(0) - 1)
    def _():
        width = h_med.shape[0]
        step = 128
        tokens = lat_hat_ref.shape[0] * lat_hat_ref.shape[1]
        quer_all = gq_ref[...].reshape(tokens, span)
        h_q = dot(lat_hat_ref[...].reshape(tokens, width), quer_all, TN)
        quer_sum = dot(jnp.ones((8, tokens), BF), quer_all, NN)[0:1] * scale
        for at in range(0, width, step):
            part = slice(at, at + step)
            norm = norm_ref[part, :]
            med, lat, quer = h_med[part, :], h_lat[part, :], h_q[part] * scale
            med_sum, lat_sum = sums[0:1, :], sums[1:2, :]
            wide_rows[part, : 2 * span] = (
                norm[:, 0:1] * med
                + norm[:, 1:2] * med_sum
                + norm[:, 2:3] * lat
                + norm[:, 3:4] * lat_sum
            ).astype(BF)
            wide_rows[part, 2 * span :] = (
                norm[:, 2:3] * quer + norm[:, 3:4] * quer_sum
            ).astype(BF)
            wkv = jnp.concatenate([wk_ref[part, :], wv_ref[part, :]], axis=1).astype(F32)
            wq = wq_ref[part, :].astype(F32)

            def total(value):
                return jnp.sum(value, axis=1, keepdims=True)

            vec = jnp.concatenate(
                [
                    total(wkv * med),
                    total(wkv * med_sum),
                    total(wkv * lat) + total(wq * quer),
                    total(wkv * lat_sum) + total(wq * quer_sum),
                    jnp.zeros((step, step - 4), F32),
                ],
                axis=1,
            )
            vec_ref[:, part] = vec_in[:, part] + vec.T[: vec_ref.shape[0]]
        if len(keep_ref.shape) == 2:
            keep_ref[...] = wide_rows[...]
            return
        imgs, two, height, _ = keep_ref.shape
        share = width // imgs
        tall = share // (2 * two)
        bit = lax.rem(index_ref[0], 2)
        for ref, mine in ((keep_ref, bit), (send_ref, 1 - bit)):
            for i in range(imgs):
                for y in range(two):
                    at = pl.multiple_of(i * share + 2 * y * tall + mine * tall, tall)
                    rows = wide_rows[pl.ds(at, tall), :]
                    ref[i, y, :tall] = rows[:, : 2 * span]
                    ref[i, y, tall : tall + tall // 2, :span] = rows[: tall // 2, 2 * span :]
                    ref[i, y, tall : tall + tall // 2, span:] = rows[tall // 2 :, 2 * span :]
                    start = tall + tall // 2
                    if group == 0:
                        size = extra_ref.shape[0] // (2 * two * imgs)
                        at = pl.multiple_of((i * two + y) * 2 * size + mine * size, size)
                        rows = extra_ref[pl.ds(at, size), :]
                        ref[i, y, start : start + size] = rows[:, : 2 * span]
                        ref[i, y, start + size : start + 2 * size] = rows[:, 2 * span :]
                    else:
                        rows = jnp.zeros((height - start, 2 * span), F32)
                        if y == 0:
                            at = slice(i * share, (i + 1) * share)
                            six = jnp.concatenate([vec_ref[:4, at], extra_ref[:2, at]], axis=0)
                            six = jnp.where(mine == 0, six, 0.0)
                            six = jnp.pad(six, ((0, height - start - 6), (0, 2 * span - share)))
                            rows = six
                        ref[i, y, start:] = rows.astype(BF)


def laid_out(width, imgs, inner):
    share = width // imgs
    return share % 128 == 0 and share <= inner and inner % (64 * imgs) == 0


def attend_back_call(
    group,
    doc_ids,
    queries,
    grad_att,
    att,
    kv_med,
    kv_lat,
    hat_med,
    hat_lat,
    w_keyval,
    w_query,
    norms,
    extra,
    vectors,
    index,
    imgs,
    deps,
):
    chunks, _, inner = queries.shape
    micro, slots, keys, both = kv_med.shape
    docs, lat_rows = kv_lat.shape[1:3]
    lats = chunks * lat_rows
    width = hat_med.shape[1]
    groups = HEADS // GROUP
    span = inner // groups
    wide = GROUP * lats
    rows = slots * keys
    lat_block = docs * lat_rows

    if laid_out(width, imgs, inner):
        tall = width // (imgs * chunks)
        height = tall + tall // 2 + (2 * inner // (imgs * chunks) if group == 0 else 16)
        result = jax.ShapeDtypeStruct((imgs, chunks // 2, height, inner), BF)
    else:
        result = jax.ShapeDtypeStruct((width, 3 * span), BF)
    result_spec = pl.BlockSpec(result.shape, lambda i, ids, p: (0,) * len(result.shape))

    def cols(at, *tail):
        return pl.BlockSpec(
            (1,) + tail, lambda i, ids, p: (i,) + (0,) * (len(tail) - 1) + (at,)
        )

    def tokens(at, size):
        return pl.BlockSpec((chunks, lat_block, size), lambda i, ids, p: (0, i, at))

    def fixed(at, size):
        return pl.BlockSpec((width, size), lambda i, ids, p: (0, at))

    return hbm_call(
        functools.partial(attend_back_kernel, group, len(deps)),
        range(16),
        (0, 1),
        grid_spec=pltpu.PrefetchScalarGridSpec(
            num_scalar_prefetch=2,
            grid=(micro,),
            in_specs=[
                tokens(group, span),
                tokens(group, span),
                tokens(group, span),
                tokens(inner // LANES, LANES),
                cols(group, slots, keys, span),
                cols(groups + group, slots, keys, span),
                cols(group, docs, lat_rows, span),
                cols(groups + group, docs, lat_rows, span),
                pl.BlockSpec((rows, width), lambda i, ids, p: (i, 0)),
                pl.BlockSpec(hat_lat.shape, lambda i, ids, p: (0, 0, 0)),
                fixed(group, span),
                fixed(groups + group, span),
                fixed(group, span),
                fixed(0, norms.shape[1]),
                pl.BlockSpec(extra.shape, lambda i, ids, p: (0, 0)),
                pl.BlockSpec(vectors.shape, lambda i, ids, p: (0, 0)),
            ]
            + [ANY] * len(deps),
            out_specs=[
                pl.BlockSpec((rows, 2 * span), lambda i, ids, p: (i, 0)),
                pl.BlockSpec((lat_block, 2 * span), lambda i, ids, p: (i, 0)),
                pl.BlockSpec((chunks, micro * lat_block, span), lambda i, ids, p: (0, 0, 0)),
                result_spec,
                result_spec,
                pl.BlockSpec(vectors.shape, lambda i, ids, p: (0, 0)),
            ],
            scratch_shapes=[
                pltpu.VMEM((docs, wide, span), BF),
                pltpu.VMEM((docs, wide, span), BF),
                pltpu.VMEM((docs, wide, span), F32),
                pltpu.VMEM((docs, 2, wide), F32),
                pltpu.VMEM((width, 2 * span), F32),
                pltpu.VMEM((width, 2 * span), F32),
                pltpu.VMEM((2, 2 * span), F32),
                pltpu.VMEM((width, 3 * span), BF),
            ],
        ),
        out_shape=[
            jax.ShapeDtypeStruct((micro * rows, 2 * span), BF),
            jax.ShapeDtypeStruct((micro * lat_block, 2 * span), BF),
            jax.ShapeDtypeStruct((chunks, micro * lat_block, span), BF),
            result,
            result,
            jax.ShapeDtypeStruct(vectors.shape, F32),
        ],
        compiler_params=params(48),
        cost_estimate=cost(3),
        name="attend_back",
    )(
        doc_ids,
        index,
        queries,
        grad_att,
        att,
        att,
        kv_med,
        kv_med,
        kv_lat,
        kv_lat,
        hat_med,
        hat_lat,
        w_keyval,
        w_keyval,
        w_query,
        norms,
        extra,
        vectors,
        *deps,
    )


def media_back_kernel(media_ref, ga_ref, gb_ref, wka_ref, wva_ref, wkb_ref, wvb_ref, gain_ref, *rest):
    out_ref, token_ref = rest[-2:]
    token_ref[...] = jnp.zeros_like(token_ref)
    wa = jnp.concatenate([wka_ref[...], wva_ref[...]], axis=1)
    wb = jnp.concatenate([wkb_ref[...], wvb_ref[...]], axis=1)
    rows = media_ref.shape[0]
    step = min(rows, 256)

    for at in range(0, rows, step):
        part = pl.ds(at, step)
        up = dot(ga_ref[part, :], wa, NT) + dot(gb_ref[part, :], wb, NT)
        hat, inv = standardize(media_ref[part, :].astype(F32))
        back, _ = norm_back(hat, inv, gain_ref[...], up)
        out_ref[part, :] = back.astype(BF)


def key_value_blocks(width, span):
    groups = HEADS // GROUP
    return [
        pl.BlockSpec((width, span), lambda i, at=at: (0, at))
        for g in range(groups)
        for at in (g, groups + g)
    ]


def media_back_call(media, grad_a, grad_b, w_keyval, gain, first, steps, whole, deps):
    rows, width = media.shape
    half = grad_a.shape[1]
    block = 512
    fixed = lambda i: (0, 0)
    moving = lambda i: (first + i, 0)
    extra = tuple(deps) if whole is None else tuple(deps) + (whole,)
    return hbm_call(
        media_back_kernel,
        range(8),
        (0,),
        grid=(steps,),
        in_specs=[
            pl.BlockSpec((block, width), moving),
            pl.BlockSpec((block, half), moving),
            pl.BlockSpec((block, half), moving),
            *key_value_blocks(width, half // 2),
            pl.BlockSpec((1, width), fixed),
        ]
        + [ANY] * len(extra),
        out_specs=[pl.BlockSpec((block, width), moving), pl.BlockSpec(TOKEN.shape, fixed)],
        out_shape=[jax.ShapeDtypeStruct((rows, width), BF), TOKEN],
        input_output_aliases={} if whole is None else {7 + len(extra): 0},
        compiler_params=params(28),
        cost_estimate=cost(2.5 * steps),
        name="media_back",
    )(media, grad_a, grad_b, w_keyval, w_keyval, w_keyval, w_keyval, gain, *extra)


def swap(value, axis, bit):
    size = lax.axis_size(axis)
    return lax.ppermute(value, axis, [(i, i ^ bit) for i in range(size)])


def gather_chunks(own):
    far = swap(own, "patch", 2)
    return own, far, swap(own, "patch", 1), swap(far, "patch", 1)


def gather_patch(own):
    return jnp.stack(gather_chunks(own))


def add(first, second):
    return (first.astype(F32) + second.astype(F32)).astype(BF)


def scatter_patch(keep, send):
    near = add(keep, swap(send, "patch", 1))
    return near[0], swap(near[1], "patch", 2)


def sum_kernel(two, *refs):
    refs[-1][...] = jnp.zeros_like(refs[-1])
    values = [ref[...] for ref in refs[1 : 1 + (4 if two else 2)]]
    if two:
        values = [
            (values[i].astype(F32) + values[i + 2].astype(F32)).astype(BF) for i in range(2)
        ]
    refs[-3][...], refs[-2][...] = values


def split_sum(first, second, place, mine, deps):
    shape = first.shape
    lead, tail = shape[:place], shape[place + 1 :]
    count = 1
    for size in lead:
        count *= size
    flat = (count, 2) + ((1,) * max(0, 2 - len(tail)) + tail)
    steps = 2 if count % 2 == 0 and first.size * 2 > (1 << 20) else 1
    block = (count // steps, 1) + flat[2:]
    zeros = (0,) * (len(flat) - 2)
    keep = pl.BlockSpec(block, lambda i, m: (i, m[0]) + zeros)
    send = pl.BlockSpec(block, lambda i, m: (i, 1 - m[0]) + zeros)
    out = pl.BlockSpec(block, lambda i, m: (i, 0) + zeros)
    shape_out = jax.ShapeDtypeStruct((count, 1) + flat[2:], BF)
    values = [v.reshape(flat) for v in (first, second) if v is not None]
    *halves, token = pl.pallas_call(
        functools.partial(sum_kernel, second is not None),
        grid_spec=pltpu.PrefetchScalarGridSpec(
            num_scalar_prefetch=1,
            grid=(steps,),
            in_specs=[keep, send] * len(values) + [ANY] * len(deps),
            out_specs=[out, out, pl.BlockSpec(TOKEN.shape, lambda i, m: (0, 0))],
        ),
        out_shape=[shape_out, shape_out, TOKEN],
        compiler_params=params(12),
        cost_estimate=cost(0.3),
        name="split_sum",
    )(mine[None], *[v for v in values for _ in range(2)], *deps)
    return *[h.reshape(lead + tail) for h in halves], token


class Scatter:
    def __init__(self, value, transit, axes, order, scope):
        self.places = [
            (axis, bit)
            for axis in axes
            for bit in reversed(range(lax.axis_size(axis).bit_length() - 1))
            if (axis, bit) in order
        ]
        self.order = list(order)
        self.scope = scope
        self.transit = transit
        self.value, self.transit = (
            v.reshape((2,) * len(self.places) + v.shape[len(axes) :]) for v in (value, transit)
        )

    def step(self, deps=()):
        with jax.named_scope(self.scope):
            if not self.order:
                if self.transit is not None:
                    self.value = add(self.value, self.transit)
                    self.transit = None
                return ()
            axis, bit = self.order.pop(0)
            place = self.places.index((axis, bit))
            self.places.pop(place)
            mine = lax.rem(lax.div(lax.axis_index(axis), 1 << bit), 2)
            self.value, send, token = split_sum(self.value, self.transit, place, mine, deps)
            self.transit = swap(send, axis, 1 << bit)
            return (token,)

    def finish(self, deps=()):
        while self.order or self.transit is not None:
            self.step(deps)
        return self.value


def img_bits():
    return [("img", bit) for bit in range(lax.axis_size("img").bit_length() - 1)]


def reduce_rest(keep, send, scope):
    with jax.named_scope(scope):
        transit = swap(send, "patch", 1)
    return Scatter(keep, transit, ("img", "patch"), [("patch", 1)] + img_bits(), scope)


def in_order(chunks):
    me = lax.axis_index("patch")
    out = []
    for j in range(4):
        apart = jnp.bitwise_xor(me, j)
        at = 2 * jnp.bitwise_and(apart, 1) + lax.shift_right_logical(apart, 1)
        out.append(lax.dynamic_index_in_dim(chunks, at, 0, keepdims=False))
    return jnp.stack(out)


def gather_rows(own):
    return in_order(gather_patch(own))


def place_kernel(index_ref, chunks_ref, out_ref):
    parts, _, unit = chunks_ref.shape
    for j in range(parts):
        apart = jnp.bitwise_xor(index_ref[0], j)
        at = jnp.where(apart == 1, 2, jnp.where(apart == 2, 1, apart))
        out_ref[:, j * unit : (j + 1) * unit] = chunks_ref[at].astype(F32)


def place_call(index, chunks, rows, imgs):
    parts, _, units = chunks.shape
    unit = units // imgs
    return pl.pallas_call(
        place_kernel,
        grid_spec=pltpu.PrefetchScalarGridSpec(
            num_scalar_prefetch=1,
            grid=(imgs,),
            in_specs=[pl.BlockSpec((parts, rows, unit), lambda i, p: (0, 0, i))],
            out_specs=pl.BlockSpec((rows, parts * unit), lambda i, p: (0, i)),
        ),
        out_shape=jax.ShapeDtypeStruct((rows, parts * units), F32),
        compiler_params=params(6),
        name="place_units",
    )(index, chunks)


def local(
    latents,
    media,
    doc_ids,
    w_query,
    w_keyval,
    w_output,
    w_expand,
    w_reduce,
    media_gain,
    media_shift,
    latent_gain,
    latent_shift,
    ff_gain,
    ff_shift,
    out_grad,
):
    micro, docs, lat_rows, width = latents.shape
    slots, keys = media.shape[1:3]
    inner = w_query.shape[1]
    ff = w_expand.shape[1]
    head_size = inner // HEADS
    scale = head_size ** (-0.5)
    parts = lax.axis_size("patch")
    imgs = lax.axis_size("img")
    patch_index = lax.axis_index("patch")
    own_rows = micro * docs * lat_rows
    all_rows = own_rows * parts
    groups = HEADS // GROUP
    span = inner // groups
    unit = ff // (imgs * parts)

    latents_own = latents.reshape(own_rows, width)
    cot_own = out_grad.reshape(own_rows, width)
    media_flat = media.reshape(-1, width)
    with jax.named_scope("gather_latents"):
        latents_far = swap(latents_own, "patch", 2)
        latents_near = swap(latents_own, "patch", 1)

    hat_med, kv_med, token = kv_call(media_flat, media_gain[None], media_shift[None], w_keyval)
    kv_med = kv_med.reshape(micro, slots, keys, 2 * inner)
    if unit % 128 == 0:
        w_exp, w_red = part_call(patch_index[None], w_expand, w_reduce, imgs, parts)
    else:
        w_exp = lax.dynamic_index_in_dim(
            w_expand.reshape(width, imgs, parts, unit), patch_index, 2, keepdims=False
        ).reshape(width, imgs * unit)
        w_red = lax.dynamic_index_in_dim(
            w_reduce.reshape(imgs, parts, unit, width), patch_index, 1, keepdims=False
        ).reshape(imgs * unit, width)

    (latents_far,) = gate((latents_far,), (token,), pltpu.VMEM)
    with jax.named_scope("gather_latents"):
        latents_both = swap(latents_far, "patch", 1)
    latents_all, hat_all, queries, kv_lat, cot_sent = latent_call(
        (latents_own, latents_far, latents_near, latents_both),
        latent_gain[None],
        latent_shift[None],
        w_query,
        w_keyval,
        cot_own,
        (token,),
    )
    kv_lat = kv_lat.reshape(micro, docs, lat_rows, 2 * inner)
    with jax.named_scope("gather_cotangent"):
        cot_far = swap(cot_sent, "patch", 2)
    keep, send = attend_call(doc_ids, queries, kv_med, kv_lat, ())
    send, cot_far = gate((send, cot_far), (), pltpu.VMEM)
    with jax.named_scope("join_near"):
        near = join_call(keep, swap(send, "patch", 1), False, False)
    with jax.named_scope("gather_cotangent"):
        cot_all = jnp.stack(
            [cot_sent, cot_far, swap(cot_sent, "patch", 1), swap(cot_far, "patch", 1)]
        )
    with jax.named_scope("join_far"):
        att_near = join_call(
            near, swap(near, "patch", 2), True, True, (latents_all, cot_all, w_exp, w_red)
        )
        att_far = swap(att_near, "patch", 1)

    mixed, ln_ff, hidden_act, grad_pre, up_own, up_keep, up_send, out_keep, out_send = ff_call(
        latents_all,
        att_near,
        att_far,
        cot_all,
        w_output,
        w_exp,
        w_red,
        ff_gain[None],
        ff_shift[None],
    )
    with jax.named_scope("sum_up"):
        up_sent = swap(up_send, "patch", 1)
        up_near = add(up_keep, up_sent[1])
        up_far = swap(up_near, "patch", 2)

    def flat(value):
        return value.reshape(all_rows, -1)

    ff_grads = ff_weights_call(
        flat(ln_ff), flat(grad_pre), flat(hidden_act), flat(cot_all), imgs, (up_near,)
    )
    (up_far,) = gate((up_far,), (ff_grads,), pltpu.VMEM)
    (ff_grads,) = gate((ff_grads,), (up_far,), pltpu.HBM)
    grad_mixed, grad_branch, grad_att_own, ff_gain_part, ff_shift_part = mixed_back_call(
        up_own, up_sent, up_far, mixed, cot_sent, w_output, ff_gain[None], ()
    )
    with jax.named_scope("gather_att"):
        grad_att = gather_patch(grad_att_own)
    att = jnp.concatenate([att_near, att_far])
    grad_output = dot(att_near[0, :, :inner], grad_branch, TN).astype(BF)

    with jax.named_scope("sum_ff"):
        ff_own = lax.psum_scatter(ff_grads, "img", scatter_dimension=0, tiled=True)[0]

    norms = jnp.stack([media_gain, media_shift, latent_gain, latent_shift], axis=1)
    ff_vectors = jnp.pad(jnp.concatenate([ff_gain_part, ff_shift_part]), ((0, 6), (0, 0)))
    share = width // imgs
    tall = share // parts
    direct = laid_out(width, imgs, inner)

    def back_call(group, extra, vectors, deps):
        gkv, gkv_lat, gq, keep, send, vectors = attend_back_call(
            group,
            doc_ids,
            queries,
            grad_att,
            att,
            kv_med,
            kv_lat,
            hat_med,
            hat_all,
            w_keyval,
            w_query,
            norms,
            extra,
            vectors,
            patch_index[None],
            imgs,
            deps,
        )
        if not direct:

            def split(value):
                size = value.shape[0] // (imgs * parts)
                return value.reshape(imgs, parts // 2, 2, size, value.shape[1])

            rows = split(keep)
            fold = [rows[..., : tall // 2, 2 * span :], rows[..., tall // 2 :, 2 * span :]]
            blocks = [rows[..., : 2 * span], jnp.concatenate(fold, axis=-1)]
            if group == 0:
                blocks += [split(extra)[..., :inner], split(extra)[..., inner:]]
            else:
                six = jnp.concatenate([vectors[:4], extra[:2]]).astype(BF)
                six = jnp.swapaxes(six.reshape(6, imgs, share), 0, 1)
                six = jnp.pad(six, ((0, 0), (0, 10), (0, width - share)))[:, None, None, :, :inner]
                blocks.append(
                    jnp.pad(six, ((0, 0), (0, parts // 2 - 1), (0, 1), (0, 0), (0, 0)))
                )
            blocks = jnp.concatenate(blocks, axis=3)
            bit = lax.rem(patch_index, 2)
            keep = lax.dynamic_index_in_dim(blocks, bit, 2, keepdims=False)
            send = lax.dynamic_index_in_dim(blocks, 1 - bit, 2, keepdims=False)
        return gkv, gkv_lat, gq, keep, send, vectors

    out_keep, out_send = gate((out_keep, out_send), (grad_att,), pltpu.HBM)
    with jax.named_scope("sum_out"):
        out_near, out_far = scatter_patch(out_keep, out_send)
    gkv_0, gkv_lat_0, gq_0, keep, send, vectors = back_call(
        0, grad_output, jnp.zeros((8, width), F32), (ff_grads,)
    )
    first = reduce_rest(keep, send, "sum_weights_0")
    gkv_1, gkv_lat_1, gq_1, keep, send, vectors = back_call(
        1, ff_vectors, vectors, first.step()
    )
    done = first.step((vectors,))
    latents_out = out_call(mixed, out_near, out_far, (vectors,))
    keep, send, gq_0, gq_1 = gate((keep, send, gq_0, gq_1), (*done, latents_out), pltpu.VMEM)
    second = reduce_rest(keep, send, "sum_weights_1")
    with jax.named_scope("sum_query"):
        gq_keep = jnp.concatenate([gq_0[:2], gq_1[:2]], axis=-1)
        gq_sent = swap(jnp.concatenate([gq_0[2:], gq_1[2:]], axis=-1), "patch", 1)

    def media_piece(at, size, whole, deps):
        return media_back_call(
            media_flat,
            gkv_0,
            gkv_1,
            w_keyval,
            media_gain[None],
            at,
            size,
            whole,
            deps,
        )

    media_grad, *done = media_piece(0, 4, None, second.step())
    deps = (*first.step(done), *second.step(done))
    (gq_keep,) = gate((gq_keep,), done, pltpu.VMEM)
    with jax.named_scope("sum_query"):
        gq_near = add(gq_keep, gq_sent)
        gq_far = swap(gq_near[1], "patch", 2)
    media_grad, *done = media_piece(4, 2, media_grad, deps)
    deps = (*first.step(done), *second.step(done))
    (ff_own,) = gate((ff_own,), deps, pltpu.HBM)
    with jax.named_scope("gather_ff"):
        expand_far = swap(ff_own[:share], "patch", 2)
    media_grad, *done = media_piece(6, 2, media_grad, (*deps, ff_own))
    (expand_far,) = gate((expand_far,), done, pltpu.VMEM)
    done = (*done, expand_far)
    first.step(done)
    second.step(done)
    latents_grad = latent_back_call(
        scale,
        (
            latents_own,
            grad_mixed,
            gq_near[0],
            gq_far,
            gkv_lat_0,
            gkv_lat_1,
            w_query,
            w_keyval,
            latent_gain[None],
        ),
        done,
    )

    first = first.finish(done)
    second = second.finish(done)

    def rows_of(value):
        return value.reshape(-1, value.shape[-1])

    with jax.named_scope("gather_weights"):
        whole = gather_rows(jnp.concatenate([first, second]))
    cut = first.shape[0]
    first, second = whole[:, :cut], whole[:, cut:]
    keyval_rows = [rows_of(first[:, :tall]), rows_of(second[:, :tall])]
    grad_keyval = jnp.concatenate(
        [rows[:, at * span : (at + 1) * span] for at in range(2) for rows in keyval_rows], axis=1
    ).astype(F32)
    end = tall + tall // 2

    def unfold(value):
        return rows_of(jnp.concatenate([value[..., :span], value[..., span:]], axis=1))

    query_rows = jnp.concatenate(
        [unfold(first[:, tall:end]), unfold(second[:, tall:end])], axis=1
    ).astype(F32)
    out_rows = first[:, end:]
    size = out_rows.shape[1] // 2
    out_rows = rows_of(
        jnp.concatenate([out_rows[:, :size], out_rows[:, size:]], axis=2)
    ).astype(F32)
    vectors = second[0, end : end + 6, :share].astype(F32)

    def gather_half(own, far):
        return jnp.stack([own, far, swap(own, "patch", 1), swap(far, "patch", 1)])

    with jax.named_scope("gather_ff"):
        expand = gather_half(ff_own[:share], expand_far)
        reduce = gather_patch(ff_own[share:])
    with jax.named_scope("place_ff"):
        if unit % 128 == 0:
            expand_rows = place_call(patch_index[None], expand, share, imgs)
        else:
            expand_rows = in_order(expand).reshape(parts, -1, imgs, unit)
            expand_rows = jnp.transpose(expand_rows, (1, 2, 0, 3)).reshape(-1, ff).astype(F32)
        reduce_rows = rows_of(in_order(reduce)).astype(F32)

    return (
        latents_out.reshape(latents.shape),
        latents_grad.reshape(latents.shape),
        media_grad.reshape(media.shape),
        query_rows,
        grad_keyval,
        out_rows,
        expand_rows,
        reduce_rows,
    ) + tuple(vectors[i] for i in range(6))


def solution(mesh):
    tokens = P(None, "img", "patch", None)
    return jax.shard_map(
        local,
        mesh=mesh,
        in_specs=(tokens, tokens, P(None, "img")) + (P(),) * 11 + (tokens,),
        out_specs=(tokens,) * 3 + (P("img", None),) * 5 + (P("img"),) * 6,
        check_vma=False,
    )
```

```python
import functools

import jax
import jax.numpy as jnp
from jax import lax
from jax.experimental import pallas as pl
from jax.experimental.pallas import tpu as pltpu
from jax.sharding import PartitionSpec as P

HEADS = 8
GROUP = 4
EPS = 1e-05
CHUNK = 4
FAR = -1e30
BF = jnp.bfloat16
F32 = jnp.float32
ANY = pl.BlockSpec(memory_space=pl.ANY)
TOKEN = jax.ShapeDtypeStruct((8, 128), jnp.float32)


def params(mib=56):
    return pltpu.CompilerParams(vmem_limit_bytes=mib << 20)


def cost(us):
    return pl.CostEstimate(flops=int(us * 1.1e9), bytes_accessed=0, transcendentals=0)


def hbm_call(kernel, held, kept, inside=(), **options):
    shapes = options.pop("out_shape")
    if isinstance(shapes, list):
        shapes = [pltpu.HBM(v.shape, v.dtype) if i in kept else v for i, v in enumerate(shapes)]
    options["out_shape"] = shapes
    scalars = options["grid_spec"].num_scalar_prefetch if "grid_spec" in options else 0
    inner = pl.pallas_call(kernel, **options)

    def run(*operands):
        def place(i, x):
            if i in inside:
                return pltpu.with_memory_space_constraint(x, pltpu.VMEM)
            if i in held or x.size >= 1 << 20:
                return pltpu.with_memory_space_constraint(x, pltpu.HBM)
            return x

        arrays = [place(i, x) for i, x in enumerate(operands[scalars:])]
        return inner(*operands[:scalars], *arrays)

    return run


def nothing_kernel(*refs):
    pass


def gate(carry, deps, space):
    return pl.pallas_call(
        nothing_kernel,
        in_specs=[ANY] * (len(carry) + len(deps)),
        out_specs=[ANY] * len(carry),
        out_shape=[space(c.shape, c.dtype) for c in carry],
        input_output_aliases={i: i for i in range(len(carry))},
        compiler_params=params(1),
        name="gate",
    )(
        *[pltpu.with_memory_space_constraint(c, space) for c in carry],
        *[
            pltpu.with_memory_space_constraint(d, pltpu.HBM) if d.size >= 1 << 20 else d
            for d in deps
        ],
    )


def dot(a, b, dims):
    return lax.dot_general(a, b, (dims, ((), ())), preferred_element_type=F32)


NN = ((1,), (0,))
NT = ((1,), (1,))
TN = ((0,), (0,))


def standardize(values):
    center = values - jnp.mean(values, axis=-1, keepdims=True)
    inv = lax.rsqrt(jnp.mean(center * center, axis=-1, keepdims=True) + EPS)
    return center * inv, inv


def norm_back(hat, inv, gain, upstream):
    scaled = upstream * gain
    back = inv * (
        scaled
        - jnp.mean(scaled, axis=-1, keepdims=True)
        - hat * jnp.mean(scaled * hat, axis=-1, keepdims=True)
    )
    return back, upstream * hat


def kv_kernel(media_ref, gain_ref, shift_ref, w_ref, hat_ref, kv_ref, token_ref):
    token_ref[...] = jnp.zeros_like(token_ref)
    rows = media_ref.shape[0]
    step = min(rows, 256)
    for at in range(0, rows, step):
        part = pl.ds(at, step)
        hat, _ = standardize(media_ref[part, :].astype(F32))
        ln = (hat * gain_ref[...] + shift_ref[...]).astype(BF)
        hat_ref[part, :] = hat.astype(BF)
        kv_ref[part, :] = dot(ln, w_ref[...], NN).astype(BF)


def kv_call(media, gain, shift, w_keyval):
    rows, width = media.shape
    outs = w_keyval.shape[1]
    block = 512
    return hbm_call(
        kv_kernel,
        range(4),
        (0, 1),
        grid=(rows // block,),
        in_specs=[
            pl.BlockSpec((block, width), lambda i: (i, 0)),
            pl.BlockSpec((1, width), lambda i: (0, 0)),
            pl.BlockSpec((1, width), lambda i: (0, 0)),
            pl.BlockSpec((width, outs), lambda i: (0, 0)),
        ],
        out_specs=[
            pl.BlockSpec((block, width), lambda i: (i, 0)),
            pl.BlockSpec((block, outs), lambda i: (i, 0)),
            pl.BlockSpec(TOKEN.shape, lambda i: (0, 0)),
        ],
        out_shape=[
            jax.ShapeDtypeStruct((rows, width), BF),
            jax.ShapeDtypeStruct((rows, outs), BF),
            TOKEN,
        ],
        compiler_params=params(20),
        cost_estimate=cost(16),
        name="media_keyval",
    )(media, gain, shift, w_keyval)


def latent_kernel(own, far, near, both, gain_ref, shift_ref, wq_ref, wkv_ref, cot_ref, *rest):
    raw_ref, hat_ref, q_ref, kv_ref, cot_out = rest[-5:]
    scale = (wq_ref.shape[1] // HEADS) ** (-0.5)
    cot_out[...] = cot_ref[...]
    for c, ref in enumerate((own, far, near, both)):
        raw = ref[...]
        raw_ref[c] = raw
        hat, _ = standardize(raw.astype(F32))
        hat_ref[c] = hat.astype(BF)
        ln = (hat * gain_ref[...] + shift_ref[...]).astype(BF)
        q_ref[c] = (dot(ln, wq_ref[...], NN).astype(BF).astype(F32) * scale).astype(BF)
        if c == 0:
            kv_ref[...] = dot(ln, wkv_ref[...], NN).astype(BF)


def latent_call(chunks, gain, shift, w_query, w_keyval, cot, deps):
    rows, width = chunks[0].shape
    inner = w_query.shape[1]
    count = len(chunks)
    return hbm_call(
        latent_kernel,
        (6, 7),
        range(4),
        (1, 2, 3),
        in_specs=[pl.BlockSpec(memory_space=pltpu.VMEM)] * (count + 5) + [ANY] * len(deps),
        out_shape=[
            jax.ShapeDtypeStruct((count, rows, width), BF),
            jax.ShapeDtypeStruct((count, rows, width), BF),
            jax.ShapeDtypeStruct((count, rows, inner), BF),
            jax.ShapeDtypeStruct((rows, 2 * inner), BF),
            jax.ShapeDtypeStruct(cot.shape, BF),
        ],
        compiler_params=params(28),
        cost_estimate=cost(6),
        name="latents",
    )(*chunks, gain, shift, w_query, w_keyval, cot, *deps)


def kv_columns(first, second):
    span = first.shape[1] // 2
    return jnp.concatenate(
        [first[:, :span], second[:, :span], first[:, span:], second[:, span:]], axis=1
    )


def latent_back_kernel(
    scale, raw_ref, mixed_ref, own_ref, far_ref, kv_a, kv_b, wq_ref, w_ref, gain_ref, *rest
):
    grad_q = ((own_ref[...].astype(F32) + far_ref[...].astype(F32)) * scale).astype(BF)
    up = (
        dot(grad_q, wq_ref[...], NT)
        + dot(kv_columns(kv_a[...], kv_b[...]), w_ref[...], NT)
    )
    hat, inv = standardize(raw_ref[...].astype(F32))
    back, _ = norm_back(hat, inv, gain_ref[...], up)
    rest[-1][...] = (mixed_ref[...] + back).astype(BF)


def latent_back_call(scale, args, deps):
    return hbm_call(
        functools.partial(latent_back_kernel, scale),
        (1, 4, 5, 6, 7),
        (),
        (2, 3),
        in_specs=[pl.BlockSpec(memory_space=pltpu.VMEM)] * len(args) + [ANY] * len(deps),
        out_shape=jax.ShapeDtypeStruct(args[0].shape, BF),
        compiler_params=params(24),
        cost_estimate=cost(4),
        name="latent_back",
    )(*args, *deps)


def out_kernel(mixed_ref, own_ref, near_ref, far_ref, *rest):
    total = own_ref[...].astype(F32) + near_ref[0].astype(F32) + far_ref[...].astype(F32)
    rest[-2][...] = (mixed_ref[...] + total).astype(BF)
    rest[-1][...] = jnp.zeros_like(rest[-1])


def out_call(mixed, own, near, far, deps):
    return hbm_call(
        out_kernel,
        (0, 1),
        (0,),
        (2, 3),
        in_specs=[pl.BlockSpec(memory_space=pltpu.VMEM)] * 4 + [ANY] * len(deps),
        out_shape=[jax.ShapeDtypeStruct(mixed.shape, BF), TOKEN],
        compiler_params=params(8),
        cost_estimate=cost(1.5),
        name="latents_out",
    )(mixed, own, near, far, *deps)


def block_mask(head_size, lats):
    rows = GROUP * lats
    cols = GROUP * head_size
    row_head = lax.broadcasted_iota(jnp.int32, (rows, cols), 0) // lats
    col_head = lax.broadcasted_iota(jnp.int32, (rows, cols), 1) // head_size
    return row_head == col_head


def spread_heads(values, mask):
    tiled = jnp.concatenate([values] * GROUP, axis=0)
    return jnp.where(mask, tiled, jnp.zeros_like(tiled))


def gather_heads(full, mask, lats):
    kept = jnp.where(mask, full, 0.0)
    total = kept[:lats]
    for head in range(1, GROUP):
        total = total + kept[head * lats : (head + 1) * lats]
    return total


LANES = 128


def terms(value):
    first = value.astype(BF)
    rest = value - first.astype(F32)
    second = rest.astype(BF)
    return first, second, (rest - second.astype(F32)).astype(BF)


def pick(shape, fn):
    row = lax.broadcasted_iota(jnp.int32, shape, 0)
    col = lax.broadcasted_iota(jnp.int32, shape, 1)
    return jnp.where(fn(row, col), 1.0, 0.0).astype(BF)


def holds(lane, head, figure):
    return (lane < 24 * figure + 24) & (lane >= 24 * figure) & (lane % HEADS == head)


def pack_rows(figures):
    rows = jnp.concatenate([t for f in figures for t in terms(f)], axis=0)
    eye = pick((rows.shape[0], LANES), lambda r, c: r == c)
    return dot(rows, eye, TN).astype(BF)


def pack_cols(figures):
    total = None
    for i, figure in enumerate(figures):
        for k, term in enumerate(terms(figure)):
            at = HEADS * (3 * i + k)
            place = pick((LANES, LANES), lambda r, c: (r < HEADS) & (c == r + at))
            part = dot(term, place, NN)
            total = part if total is None else total + part
    return total.astype(BF)


def widen(packed, figure, inner):
    size = inner // HEADS
    return dot(packed, pick((LANES, inner), lambda r, c: holds(r, c // size, figure)), NN)


def narrow(packed, figure):
    return dot(
        packed, pick((LANES, LANES), lambda r, c: (c < HEADS) & holds(r, c, figure)), NN
    )


def doc_rows(refs, d, lat_rows, cols):
    rows = slice(d * lat_rows, (d + 1) * lat_rows)
    return jnp.concatenate(
        [ref[c, rows, cols] for ref in refs for c in range(ref.shape[0])], axis=0
    )


def doc_spans(doc_ref, micro, docs, slots):
    counts = []
    for d in range(docs):
        total = 0
        for s in range(slots):
            total = total + jnp.where(doc_ref[micro, s] == d, 1, 0)
        counts.append(total)
    first = 0
    spans = []
    for count in counts:
        spans.append((first, count))
        first = first + count
    return spans


def slot_chunk(span, step, slots):
    first, count = span
    low = first + step * CHUNK
    return jnp.minimum(low, slots - CHUNK), low, first + count


def own_rows_of(at, low, high, keys):
    slot = at + lax.broadcasted_iota(jnp.int32, (CHUNK * keys, 1), 0) // keys
    return (slot >= low) & (slot < high)


def steps_of(span):
    return (span[1] + CHUNK - 1) // CHUNK


PAIR = 1


def more_chunks(spans, slots, body):
    counts = [steps_of(span) - 1 for span in spans]
    total = sum(counts)

    def locate(e):
        d, before, end = 0, 0, 0
        for count in counts[:-1]:
            end = end + count
            d = d + jnp.where(e >= end, 1, 0)
            before = jnp.where(e >= end, end, before)
        step = e - before + 1
        first, count = 0, 0
        for i, span in enumerate(spans):
            first = first + jnp.where(d == i, span[0], 0)
            count = count + jnp.where(d == i, span[1], 0)
        at, low, high = slot_chunk((first, count), step, slots)
        return d, step, at, low, jnp.where(e < total, high, low)

    def pair(i, carry):
        body([locate(PAIR * i + k) for k in range(PAIR)])
        return carry

    lax.fori_loop(0, (total + PAIR - 1) // PAIR, pair, 0)


def attend_kernel(deps, doc_ref, q_ref, kv_ref, kvl_ref, *rest):
    keep_ref, send_ref, bd, score, acc, top, tot = rest[deps:]
    chunks, rows, inner = q_ref.shape
    docs, lat_rows = kvl_ref.shape[1:3]
    lats = chunks * lat_rows
    slots, keys = kv_ref.shape[1:3]
    groups = HEADS // GROUP
    span = inner // groups
    micro = pl.program_id(0)
    mask = block_mask(inner // HEADS, lats)
    cols = [slice(g * span, (g + 1) * span) for g in range(groups)]
    vals = [slice(inner + g * span, inner + (g + 1) * span) for g in range(groups)]
    spans = doc_spans(doc_ref, micro, docs, slots)
    tall = CHUNK * keys

    def load(at, part):
        return kv_ref[0, pl.ds(at, CHUNK), :, part].reshape(tall, span)

    for d in range(docs):
        at, low, high = slot_chunk(spans[d], 0, slots)
        bias = jnp.where(own_rows_of(at, low, high, keys), 0.0, FAR)
        bias = jnp.concatenate([bias, jnp.zeros((lat_rows, 1), F32)], axis=0)
        for g in range(groups):
            spread = spread_heads(doc_rows((q_ref,), d, lat_rows, cols[g]), mask)
            bd[d, g] = spread
            key = jnp.concatenate([load(at, cols[g]), kvl_ref[0, d, :, cols[g]]], axis=0)
            val = dot(key, spread, NT) + bias
            score[d, g, 0] = val
            top[d, g] = jnp.max(val, axis=0, keepdims=True)

    def more(parts):
        for k, (d, step, at, low, high) in enumerate(parts):
            bias = jnp.where(own_rows_of(at, low, high, keys), 0.0, FAR)
            for g in range(groups):
                val = dot(load(at, cols[g]), bd[d, g], NT) + bias
                score[d, g, jnp.minimum(step, score.shape[2] - 1), :tall] = val
                top[d, g] = jnp.maximum(top[d, g], jnp.max(val, axis=0, keepdims=True))

    more_chunks(spans, slots, more)
    for d in range(docs):
        at, low, high = slot_chunk(spans[d], 0, slots)
        for g in range(groups):
            expo = jnp.exp(score[d, g, 0] - top[d, g])
            tot[d, g] = jnp.sum(expo, axis=0, keepdims=True)
            val = jnp.concatenate([load(at, vals[g]), kvl_ref[0, d, :, vals[g]]], axis=0)
            acc[d, g] = dot(expo.astype(BF), val, TN)

    def more_values(parts):
        for d, step, at, low, high in parts:
            step = jnp.minimum(step, score.shape[2] - 1)
            own = own_rows_of(at, low, high, keys)
            for g in range(groups):
                expo = jnp.where(own, jnp.exp(score[d, g, step, :tall] - top[d, g]), 0.0)
                tot[d, g] = tot[d, g] + jnp.sum(expo, axis=0, keepdims=True)
                acc[d, g] = acc[d, g] + dot(expo.astype(BF), load(at, vals[g]), TN)

    more_chunks(spans, slots, more_values)
    half = chunks // 2
    for d in range(docs):
        rows_d = slice(d * lat_rows, (d + 1) * lat_rows)

        def by_head(ref):
            return jnp.concatenate(
                [
                    ref[d, g][:, h * lats : (h + 1) * lats]
                    for g in range(groups)
                    for h in range(GROUP)
                ],
                axis=0,
            )

        packed = pack_rows([by_head(top), by_head(tot)])
        outs = [gather_heads(acc[d, g], mask, lats).astype(BF) for g in range(groups)]
        for c in range(chunks):
            ref = keep_ref if c < half else send_ref
            part = slice(c * lat_rows, (c + 1) * lat_rows)
            for g in range(groups):
                ref[c % half, rows_d, cols[g]] = outs[g][part]
            ref[c % half, rows_d, inner:] = packed[part]


def attend_call(doc_ids, queries, kv_med, kv_lat, deps):
    chunks, _, inner = queries.shape
    micro, slots, keys, both = kv_med.shape
    docs, lat_rows = kv_lat.shape[1:3]
    lats = chunks * lat_rows
    rows = docs * lat_rows
    groups = HEADS // GROUP
    span = inner // groups
    wide = GROUP * lats
    half = chunks // 2
    longest = (slots - docs + CHUNK) // CHUNK
    out_spec = pl.BlockSpec((half, rows, inner + LANES), lambda i, ids: (0, i, 0))
    out_shape = jax.ShapeDtypeStruct((half, micro * rows, inner + LANES), BF)
    return hbm_call(
        functools.partial(attend_kernel, len(deps)),
        range(3),
        (),
        grid_spec=pltpu.PrefetchScalarGridSpec(
            num_scalar_prefetch=1,
            grid=(micro,),
            in_specs=[
                pl.BlockSpec((chunks, rows, inner), lambda i, ids: (0, i, 0)),
                pl.BlockSpec((1, slots, keys, both), lambda i, ids: (i, 0, 0, 0)),
                pl.BlockSpec((1, docs, lat_rows, both), lambda i, ids: (i, 0, 0, 0)),
            ]
            + [ANY] * len(deps),
            out_specs=[out_spec, out_spec],
            scratch_shapes=[
                pltpu.VMEM((docs, groups, wide, span), BF),
                pltpu.VMEM((docs, groups, longest, CHUNK * keys + lat_rows, wide), F32),
                pltpu.VMEM((docs, groups, wide, span), F32),
                pltpu.VMEM((docs, groups, 1, wide), F32),
                pltpu.VMEM((docs, groups, 1, wide), F32),
            ],
        ),
        out_shape=[out_shape, out_shape],
        compiler_params=params(40),
        cost_estimate=cost(13),
        name="attend",
    )(doc_ids, queries, kv_med, kv_lat, *deps)


def join_kernel(last, flip, a_ref, b_ref, *rest):
    out_ref = rest[-1]
    inner = a_ref.shape[2] - LANES
    count = a_ref.shape[0]
    for c in range(count):
        first, second = a_ref[c], b_ref[count - 1 - c if flip else c]
        pack_a, pack_b = first[:, inner:], second[:, inner:]
        top_a, top_b = widen(pack_a, 0, inner), widen(pack_b, 0, inner)
        best = jnp.maximum(top_a, top_b)
        fac_a, fac_b = jnp.exp(top_a - best), jnp.exp(top_b - best)
        out = fac_a * first[:, :inner].astype(F32) + fac_b * second[:, :inner].astype(F32)
        if last:
            total = fac_a * widen(pack_a, 1, inner) + fac_b * widen(pack_b, 1, inner)
            out = out / total
        out_ref[c, :, :inner] = out.astype(BF)
        small_a, small_b = narrow(pack_a, 0), narrow(pack_b, 0)
        small = jnp.maximum(small_a, small_b)
        sum_ab = jnp.exp(small_a - small) * narrow(pack_a, 1) + jnp.exp(
            small_b - small
        ) * narrow(pack_b, 1)
        if last:
            lane = lax.broadcasted_iota(jnp.int32, sum_ab.shape, 1)
            lse = jnp.where(lane < HEADS, small + jnp.log(jnp.maximum(sum_ab, 1e-30)), 0.0)
            out_ref[c, :, inner:] = pack_cols([lse])
        else:
            out_ref[c, :, inner:] = pack_cols([small, sum_ab])


def join_call(first, second, last, flip, deps=()):
    count, rows, cols = first.shape
    block = min(rows, 128)
    spec = pl.BlockSpec((count, block, cols), lambda i: (0, i, 0))
    return pl.pallas_call(
        functools.partial(join_kernel, last, flip),
        grid=(rows // block,),
        in_specs=[spec, spec] + [ANY] * len(deps),
        out_specs=spec,
        out_shape=jax.ShapeDtypeStruct(first.shape, BF),
        compiler_params=params(10),
        cost_estimate=cost(3.5),
        name="join_last" if last else "join_first",
    )(first, second, *deps)


def ff_kernel(
    lat_ref,
    near_ref,
    far_ref,
    cot_ref,
    wo_ref,
    we_ref,
    wr_ref,
    gain_ref,
    shift_ref,
    mixed_ref,
    ln_ref,
    act_ref,
    gpre_ref,
    up_own,
    up_keep,
    up_send,
    out_own,
    out_keep,
    out_send,
):
    i = pl.program_id(0)
    half = pl.num_programs(0) // 2
    att = jnp.where(i < half, near_ref[0], far_ref[0])
    mixed = lat_ref[0].astype(F32) + dot(att, wo_ref[...], NN)
    hat, _ = standardize(mixed)
    ln = (hat * gain_ref[...] + shift_ref[...]).astype(BF)
    ln_ref[0] = ln
    pre = dot(ln, we_ref[...], NN)
    cdf = 0.5 + 0.5 * lax.erf(pre * (0.5**0.5))
    slope = cdf + pre * (0.3989422804014327 * jnp.exp(-0.5 * pre * pre))
    act = (pre * cdf).astype(BF)
    act_ref[0] = act
    gpre = (dot(cot_ref[0], wr_ref[...], NT) * slope).astype(BF)
    gpre_ref[0] = gpre
    up = dot(gpre, we_ref[...], NT).astype(BF)
    out = dot(act, wr_ref[...], NN).astype(BF)

    @pl.when(i == 0)
    def _():
        mixed_ref[...] = mixed
        up_own[...] = up
        out_own[...] = out

    @pl.when(i == 1)
    def _():
        up_keep[...] = up
        out_keep[...] = out

    @pl.when(i >= half)
    def _():
        up_send[0] = up
        out_send[0] = out


def ff_call(latents, near, far, cot, w_output, w_exp, w_red, gain, shift):
    chunks, rows, width = latents.shape
    inner = w_output.shape[0]
    units = w_exp.shape[1]
    half = chunks // 2

    def chunk(cols):
        return pl.BlockSpec((1, rows, cols), lambda i: (i, 0, 0))

    def first(cols):
        return pl.BlockSpec((1, rows, cols), lambda i: (jnp.minimum(i, half - 1), 0, 0))

    def second(cols):
        return pl.BlockSpec((1, rows, cols), lambda i: (jnp.maximum(i - half, 0), 0, 0))

    def fixed(*shape):
        return pl.BlockSpec(shape, lambda i: (0,) * len(shape))

    def out(count, cols):
        return jax.ShapeDtypeStruct((count, rows, cols), BF)

    return hbm_call(
        ff_kernel,
        (0, 4, 5, 6),
        (0, 1, 2, 3, 4, 7, 8, 9),
        (1, 2),
        grid=(chunks,),
        in_specs=[
            chunk(width),
            first(inner),
            second(inner),
            chunk(width),
            fixed(inner, width),
            fixed(width, units),
            fixed(units, width),
            fixed(1, width),
            fixed(1, width),
        ],
        out_specs=[
            fixed(rows, width),
            chunk(width),
            chunk(units),
            chunk(units),
            fixed(rows, width),
            fixed(rows, width),
            second(width),
            fixed(rows, width),
            fixed(rows, width),
            second(width),
        ],
        out_shape=[
            jax.ShapeDtypeStruct((rows, width), F32),
            out(chunks, width),
            out(chunks, units),
            out(chunks, units),
            jax.ShapeDtypeStruct((rows, width), BF),
            jax.ShapeDtypeStruct((rows, width), BF),
            out(half, width),
            jax.ShapeDtypeStruct((rows, width), BF),
            jax.ShapeDtypeStruct((rows, width), BF),
            out(half, width),
        ],
        compiler_params=params(40),
        cost_estimate=cost(18),
        name="feed_forward",
    )(latents, near, far, cot, w_output, w_exp, w_red, gain, shift)


def ff_weights_kernel(ln_ref, gpre_ref, act_ref, cot_ref, *rest):
    out_ref = rest[-1]
    count, rows, width = out_ref.shape
    half = rows // 2
    for part, (left, right) in enumerate(((ln_ref, gpre_ref), (act_ref, cot_ref))):
        product = dot(left[...], right[...], TN).astype(BF)
        out_ref[:, part * half : (part + 1) * half, :] = product.reshape(count, half, width)


def ff_weights_call(ln_ff, grad_pre, hidden_act, cot, imgs, deps):
    tokens, width = ln_ff.shape
    units = grad_pre.shape[1]
    half = units // imgs
    steps = 2
    left = pl.BlockSpec((tokens, width // steps), lambda i: (0, i))
    right = pl.BlockSpec((tokens, width), lambda i: (0, 0))
    return hbm_call(
        ff_weights_kernel,
        range(4),
        (),
        grid=(steps,),
        in_specs=[left, right, left, right] + [ANY] * len(deps),
        out_specs=pl.BlockSpec((imgs // steps, 2 * half, width), lambda i: (i, 0, 0)),
        out_shape=pltpu.HBM((imgs, 2 * half, width), BF),
        compiler_params=params(28),
        cost_estimate=cost(9),
        name="ff_weights",
    )(ln_ff, grad_pre, hidden_act, cot, *deps)


def mixed_back_kernel(own_ref, near_ref, far_ref, mixed_ref, cot_ref, wo_ref, gain_ref, *rest):
    gm_ref, gb_ref, ga_ref, dg_ref, ds_ref = rest[-5:]
    up = own_ref[...].astype(F32) + near_ref[0].astype(F32) + far_ref[...].astype(F32)
    hat, inv = standardize(mixed_ref[...])
    back, gains = norm_back(hat, inv, gain_ref[...], up)
    grad = cot_ref[...].astype(F32) + back
    gm_ref[...] = grad
    branch = grad.astype(BF)
    gb_ref[...] = branch
    ga_ref[...] = dot(branch, wo_ref[...], NT).astype(BF)
    dg_ref[...] = jnp.sum(gains, axis=0, keepdims=True)
    ds_ref[...] = jnp.sum(up, axis=0, keepdims=True)


def mixed_back_call(own, near, far, mixed, cot, w_output, gain, deps):
    rows, width = mixed.shape
    inner = w_output.shape[0]
    return hbm_call(
        mixed_back_kernel,
        (0, 3, 4, 5),
        (0,),
        (1, 2),
        in_specs=[pl.BlockSpec(memory_space=pltpu.VMEM)] * 7 + [ANY] * len(deps),
        out_shape=[
            jax.ShapeDtypeStruct((rows, width), F32),
            jax.ShapeDtypeStruct((rows, width), BF),
            jax.ShapeDtypeStruct((rows, inner), BF),
            jax.ShapeDtypeStruct((1, width), F32),
            jax.ShapeDtypeStruct((1, width), F32),
        ],
        compiler_params=params(20),
        cost_estimate=cost(4),
        name="mixed_back",
    )(own, near, far, mixed, cot, w_output, gain, *deps)


def part_kernel(index_ref, e_ref, r_ref, eo_ref, ro_ref, token_ref):
    token_ref[...] = jnp.zeros_like(token_ref)
    eo_ref[...] = e_ref[...]
    ro_ref[...] = r_ref[...]


def part_call(index, w_expand, w_reduce, imgs, parts):
    width, ff = w_expand.shape
    unit = ff // (imgs * parts)
    return hbm_call(
        part_kernel,
        range(2),
        range(2),
        grid_spec=pltpu.PrefetchScalarGridSpec(
            num_scalar_prefetch=1,
            grid=(imgs,),
            in_specs=[
                pl.BlockSpec((width, unit), lambda i, p: (0, i * parts + p[0])),
                pl.BlockSpec((unit, width), lambda i, p: (i * parts + p[0], 0)),
            ],
            out_specs=[
                pl.BlockSpec((width, unit), lambda i, p: (0, i)),
                pl.BlockSpec((unit, width), lambda i, p: (i, 0)),
                pl.BlockSpec(TOKEN.shape, lambda i, p: (0, 0)),
            ],
        ),
        out_shape=[
            jax.ShapeDtypeStruct((width, imgs * unit), BF),
            jax.ShapeDtypeStruct((imgs * unit, width), BF),
            TOKEN,
        ],
        compiler_params=params(6),
        name="weight_part",
    )(index, w_expand, w_reduce)


def attend_back_kernel(
    group,
    deps,
    doc_ref,
    index_ref,
    q_ref,
    go_own,
    go_far,
    go_near,
    go_both,
    att_near,
    att_far,
    lse_near,
    lse_far,
    k_ref,
    v_ref,
    kl_ref,
    vl_ref,
    hat_ref,
    norm_ref,
    vec_in,
    lat_hat_hbm,
    wkv_hbm,
    wq_hbm,
    extra_hbm,
    *rest,
):
    gkv_ref, gkvl_ref, gq_ref, keep_ref, send_ref, vec_ref = rest[deps : deps + 6]
    bdq, bdo, acc, stat, h_med, h_lat, sums, wide_rows = rest[deps + 6 : -6]
    lat_hat_ref, wk_ref, wv_ref, wq_ref, extra_ref, sems = rest[-6:]
    chunks, _, span = q_ref.shape
    docs, lat_rows = kl_ref.shape[1:3]
    lats = chunks * lat_rows
    slots, keys = k_ref.shape[1:3]
    micro = pl.program_id(0)
    mask = block_mask(span // GROUP, lats)
    every = slice(None)
    scale = (span // GROUP) ** (-0.5)
    go_refs = (go_own, go_far, go_near, go_both)
    att_refs, lse_refs = (att_near, att_far), (lse_near, lse_far)

    groups = HEADS // GROUP

    def columns(ref, at):
        return ref.at[:, at * span : (at + 1) * span]

    copies = [
        pltpu.make_async_copy(source, target, sems.at[i])
        for i, (source, target) in enumerate(
            (
                (lat_hat_hbm, lat_hat_ref),
                (columns(wkv_hbm, group), wk_ref),
                (columns(wkv_hbm, groups + group), wv_ref),
                (columns(wq_hbm, group), wq_ref),
                (extra_hbm, extra_ref),
            )
        )
    ]

    @pl.when(micro == 0)
    def _():
        for copy in copies:
            copy.start()

    spans = doc_spans(doc_ref, micro, docs, slots)
    tall = CHUNK * keys

    def pair(key, value, bias, d):
        score = dot(key, bdq[d], NT) + bias
        prob = jnp.exp(score - stat[d, 0:1])
        dprob = dot(value, bdo[d], NT)
        dscore = (prob * (dprob - stat[d, 1:2])).astype(BF)
        grad_key = dot(dscore, bdq[d], NN).astype(BF)
        grad_value = dot(prob.astype(BF), bdo[d], NN).astype(BF)
        grad_query = dot(dscore, key, TN)
        return grad_key, grad_value, grad_query

    def load(ref, at):
        return ref[0, pl.ds(at, CHUNK)].reshape(tall, span)

    def store(at, own, grad_key, grad_value):
        part = pl.ds(pl.multiple_of(at * keys, keys), tall)
        gkv_ref[part, :span] = jnp.where(own, grad_key, gkv_ref[part, :span])
        gkv_ref[part, span:] = jnp.where(own, grad_value, gkv_ref[part, span:])

    sel = pick((HEADS, LANES), lambda r, c: holds(c, r, 0))
    size = span // GROUP
    head_sel = pick((HEADS, span), lambda r, c: c // size == r)

    def row(by_head, at):
        return jnp.concatenate([by_head[at + h : at + h + 1] for h in range(GROUP)], axis=1)

    for d in range(docs):
        out_grad = doc_rows(go_refs, d, lat_rows, every)
        bdq[d] = spread_heads(doc_rows((q_ref,), d, lat_rows, every), mask)
        bdo[d] = spread_heads(out_grad, mask)
        lse = dot(sel, doc_rows(lse_refs, d, lat_rows, every), NT)
        stat[d, 0:1] = row(lse, group * GROUP)
        attended = doc_rows(att_refs, d, lat_rows, every)
        high, low, _ = terms(out_grad.astype(F32) * attended.astype(F32))
        stat[d, 1:2] = row(dot(head_sel, high, NT) + dot(head_sel, low, NT), 0)
    for d in range(docs):
        rows_d = pl.ds((micro * docs + d) * lat_rows, lat_rows)
        at, low, high = slot_chunk(spans[d], 0, slots)
        own = own_rows_of(at, low, high, keys)
        bias = jnp.concatenate([jnp.where(own, 0.0, FAR), jnp.zeros((lat_rows, 1), F32)], axis=0)
        key = jnp.concatenate([load(k_ref, at), kl_ref[0, d]], axis=0)
        value = jnp.concatenate([load(v_ref, at), vl_ref[0, d]], axis=0)
        grad_key, grad_value, grad_query = pair(key, value, bias, d)
        store(at, own, grad_key[:tall], grad_value[:tall])
        gkvl_ref[rows_d, :span] = grad_key[tall:]
        gkvl_ref[rows_d, span:] = grad_value[tall:]
        acc[d] = grad_query

    def more(parts):
        done = []
        for d, step, at, low, high in parts:
            own = own_rows_of(at, low, high, keys)
            bias = jnp.where(own, 0.0, FAR)
            done.append((d, at, own, *pair(load(k_ref, at), load(v_ref, at), bias, d)))
        for d, at, own, grad_key, grad_value, grad_query in done:
            store(at, own, grad_key, grad_value)
            acc[d] = acc[d] + grad_query

    more_chunks(spans, slots, more)
    for d in range(docs):
        full = gather_heads(acc[d], mask, lats).astype(BF)
        for c in range(chunks):
            gq_ref[c, pl.ds(micro * docs * lat_rows + d * lat_rows, lat_rows)] = full[
                c * lat_rows : (c + 1) * lat_rows
            ]
    part = dot(hat_ref[...], gkv_ref[...], TN)
    part_sum = jnp.sum(gkv_ref[...].astype(F32), axis=0, keepdims=True)

    @pl.when(micro == 0)
    def _():
        h_med[...] = part
        sums[0:1, :] = part_sum

    @pl.when(micro > 0)
    def _():
        h_med[...] = h_med[...] + part
        sums[0:1, :] = sums[0:1, :] + part_sum

    @pl.when(micro == pl.num_programs(0) - 1)
    def _():
        width = h_med.shape[0]
        step = 128
        tokens = lat_hat_ref.shape[0] * lat_hat_ref.shape[1]
        for copy in copies:
            copy.wait()
        h_lat[...] = dot(lat_hat_ref[0], gkvl_ref[...], TN)
        sums[1:2, :] = jnp.sum(gkvl_ref[...].astype(F32), axis=0, keepdims=True)
        quer_all = gq_ref[...].reshape(tokens, span)
        h_q = dot(lat_hat_ref[...].reshape(tokens, width), quer_all, TN)
        quer_sum = jnp.sum(quer_all.astype(F32), axis=0, keepdims=True) * scale
        for at in range(0, width, step):
            part = slice(at, at + step)
            norm = norm_ref[:, part].T
            med, lat, quer = h_med[part, :], h_lat[part, :], h_q[part] * scale
            med_sum, lat_sum = sums[0:1, :], sums[1:2, :]
            wide_rows[part, : 2 * span] = (
                norm[:, 0:1] * med
                + norm[:, 1:2] * med_sum
                + norm[:, 2:3] * lat
                + norm[:, 3:4] * lat_sum
            ).astype(BF)
            wide_rows[part, 2 * span :] = (
                norm[:, 2:3] * quer + norm[:, 3:4] * quer_sum
            ).astype(BF)
            wkv = jnp.concatenate([wk_ref[part, :], wv_ref[part, :]], axis=1).astype(F32)
            wq = wq_ref[part, :].astype(F32)

            def total(value):
                return jnp.sum(value, axis=1, keepdims=True)

            vec = jnp.concatenate(
                [
                    total(wkv * med),
                    total(wkv * med_sum),
                    total(wkv * lat) + total(wq * quer),
                    total(wkv * lat_sum) + total(wq * quer_sum),
                    jnp.zeros((step, step - 4), F32),
                ],
                axis=1,
            )
            rows = vec.T[: vec_ref.shape[0]]
            vec_ref[:, part] = rows if group == 0 else vec_in[:, part] + rows
        if len(keep_ref.shape) == 2:
            keep_ref[...] = wide_rows[...]
            return
        imgs, two, height, _ = keep_ref.shape
        share = width // imgs
        tall = share // (2 * two)
        bit = lax.rem(index_ref[0], 2)
        for ref, mine in ((keep_ref, bit), (send_ref, 1 - bit)):
            for i in range(imgs):
                for y in range(two):
                    at = pl.multiple_of(i * share + 2 * y * tall + mine * tall, tall)
                    rows = wide_rows[pl.ds(at, tall), :]
                    ref[i, y, :tall] = rows[:, : 2 * span]
                    ref[i, y, tall : tall + tall // 2, :span] = rows[: tall // 2, 2 * span :]
                    ref[i, y, tall : tall + tall // 2, span:] = rows[tall // 2 :, 2 * span :]
                    start = tall + tall // 2
                    if group == 0:
                        size = extra_ref.shape[0] // (2 * two * imgs)
                        at = pl.multiple_of((i * two + y) * 2 * size + mine * size, size)
                        rows = extra_ref[pl.ds(at, size), :]
                        ref[i, y, start : start + size] = rows[:, : 2 * span]
                        ref[i, y, start + size : start + 2 * size] = rows[:, 2 * span :]
                    else:
                        rows = jnp.zeros((height - start, 2 * span), F32)
                        if y == 0:
                            at = slice(i * share, (i + 1) * share)
                            six = jnp.concatenate([vec_ref[:4, at], extra_ref[:2, at]], axis=0)
                            six = jnp.where(mine == 0, six, 0.0)
                            six = jnp.pad(six, ((0, height - start - 6), (0, 2 * span - share)))
                            rows = six
                        ref[i, y, start:] = rows.astype(BF)


def laid_out(width, imgs, inner):
    share = width // imgs
    return share % 128 == 0 and share <= inner and inner % (64 * imgs) == 0


def attend_back_call(
    group,
    doc_ids,
    queries,
    grad_att,
    att,
    kv_med,
    kv_lat,
    hat_med,
    hat_lat,
    w_keyval,
    w_query,
    norms,
    extra,
    vectors,
    index,
    imgs,
    deps,
):
    chunks, _, inner = queries.shape
    micro, slots, keys, both = kv_med.shape
    docs, lat_rows = kv_lat.shape[1:3]
    lats = chunks * lat_rows
    width = hat_med.shape[1]
    groups = HEADS // GROUP
    span = inner // groups
    wide = GROUP * lats
    rows = slots * keys
    lat_block = docs * lat_rows

    if laid_out(width, imgs, inner):
        tall = width // (imgs * chunks)
        height = tall + tall // 2 + (2 * inner // (imgs * chunks) if group == 0 else 16)
        result = jax.ShapeDtypeStruct((imgs, chunks // 2, height, inner), BF)
    else:
        result = jax.ShapeDtypeStruct((width, 3 * span), BF)
    result_spec = pl.BlockSpec(result.shape, lambda i, ids, p: (0,) * len(result.shape))

    def cols(at, *tail):
        return pl.BlockSpec(
            (1,) + tail, lambda i, ids, p: (i,) + (0,) * (len(tail) - 1) + (at,)
        )

    def tokens(at, size, count=chunks):
        return pl.BlockSpec((count, lat_block, size), lambda i, ids, p: (0, i, at))

    def fixed(at, size):
        return pl.BlockSpec((width, size), lambda i, ids, p: (0, at))

    return hbm_call(
        functools.partial(attend_back_kernel, group, len(deps)),
        range(20),
        (0, 1),
        grid_spec=pltpu.PrefetchScalarGridSpec(
            num_scalar_prefetch=2,
            grid=(micro,),
            in_specs=[
                tokens(group, span),
                *[tokens(group, span, 1)] * 4,
                *[tokens(group, span, 2)] * 2,
                *[tokens(inner // LANES, LANES, 2)] * 2,
                cols(group, slots, keys, span),
                cols(groups + group, slots, keys, span),
                cols(group, docs, lat_rows, span),
                cols(groups + group, docs, lat_rows, span),
                pl.BlockSpec((rows, width), lambda i, ids, p: (i, 0)),
                pl.BlockSpec(norms.shape, lambda i, ids, p: (0, 0)),
                pl.BlockSpec(vectors.shape, lambda i, ids, p: (0, 0)),
                ANY,
                ANY,
                ANY,
                ANY,
            ]
            + [ANY] * len(deps),
            out_specs=[
                pl.BlockSpec((rows, 2 * span), lambda i, ids, p: (i, 0)),
                pl.BlockSpec((micro * lat_block, 2 * span), lambda i, ids, p: (0, 0)),
                pl.BlockSpec((chunks, micro * lat_block, span), lambda i, ids, p: (0, 0, 0)),
                result_spec,
                result_spec,
                pl.BlockSpec(vectors.shape, lambda i, ids, p: (0, 0)),
            ],
            scratch_shapes=[
                pltpu.VMEM((docs, wide, span), BF),
                pltpu.VMEM((docs, wide, span), BF),
                pltpu.VMEM((docs, wide, span), F32),
                pltpu.VMEM((docs, 2, wide), F32),
                pltpu.VMEM((width, 2 * span), F32),
                pltpu.VMEM((width, 2 * span), F32),
                pltpu.VMEM((2, 2 * span), F32),
                pltpu.VMEM((width, 3 * span), BF),
                pltpu.VMEM(hat_lat.shape, BF),
                pltpu.VMEM((width, span), BF),
                pltpu.VMEM((width, span), BF),
                pltpu.VMEM((width, span), BF),
                pltpu.VMEM(extra.shape, extra.dtype),
                pltpu.SemaphoreType.DMA((5,)),
            ],
        ),
        out_shape=[
            jax.ShapeDtypeStruct((micro * rows, 2 * span), BF),
            jax.ShapeDtypeStruct((micro * lat_block, 2 * span), BF),
            jax.ShapeDtypeStruct((chunks, micro * lat_block, span), BF),
            result,
            result,
            jax.ShapeDtypeStruct(vectors.shape, F32),
        ],
        compiler_params=params(48),
        cost_estimate=cost(3),
        name="attend_back",
    )(
        doc_ids,
        index,
        queries,
        *grad_att,
        *att,
        *att,
        kv_med,
        kv_med,
        kv_lat,
        kv_lat,
        hat_med,
        norms,
        vectors,
        hat_lat,
        w_keyval,
        w_query,
        extra,
        *deps,
    )


def media_back_kernel(media_ref, ga_ref, gb_ref, wka_ref, wva_ref, wkb_ref, wvb_ref, gain_ref, *rest):
    out_ref, token_ref = rest[-2:]
    token_ref[...] = jnp.zeros_like(token_ref)
    wa = jnp.concatenate([wka_ref[...], wva_ref[...]], axis=1)
    wb = jnp.concatenate([wkb_ref[...], wvb_ref[...]], axis=1)
    rows = media_ref.shape[0]
    step = min(rows, 256)

    for at in range(0, rows, step):
        part = pl.ds(at, step)
        up = dot(ga_ref[part, :], wa, NT) + dot(gb_ref[part, :], wb, NT)
        hat, inv = standardize(media_ref[part, :].astype(F32))
        back, _ = norm_back(hat, inv, gain_ref[...], up)
        out_ref[part, :] = back.astype(BF)


def key_value_blocks(width, span):
    groups = HEADS // GROUP
    return [
        pl.BlockSpec((width, span), lambda i, at=at: (0, at))
        for g in range(groups)
        for at in (g, groups + g)
    ]


def media_back_call(media, grad_a, grad_b, w_keyval, gain, first, steps, whole, deps):
    rows, width = media.shape
    half = grad_a.shape[1]
    block = 512
    fixed = lambda i: (0, 0)
    moving = lambda i: (first + i, 0)
    extra = tuple(deps) if whole is None else tuple(deps) + (whole,)
    return hbm_call(
        media_back_kernel,
        range(8),
        (0,),
        grid=(steps,),
        in_specs=[
            pl.BlockSpec((block, width), moving),
            pl.BlockSpec((block, half), moving),
            pl.BlockSpec((block, half), moving),
            *key_value_blocks(width, half // 2),
            pl.BlockSpec((1, width), fixed),
        ]
        + [ANY] * len(extra),
        out_specs=[pl.BlockSpec((block, width), moving), pl.BlockSpec(TOKEN.shape, fixed)],
        out_shape=[jax.ShapeDtypeStruct((rows, width), BF), TOKEN],
        input_output_aliases={} if whole is None else {7 + len(extra): 0},
        compiler_params=params(28),
        cost_estimate=cost(2.5 * steps),
        name="media_back",
    )(media, grad_a, grad_b, w_keyval, w_keyval, w_keyval, w_keyval, gain, *extra)


def swap(value, axis, bit):
    size = lax.axis_size(axis)
    return lax.ppermute(value, axis, [(i, i ^ bit) for i in range(size)])


def gather_chunks(own):
    far = swap(own, "patch", 2)
    return own, far, swap(own, "patch", 1), swap(far, "patch", 1)


def gather_patch(own):
    return jnp.stack(gather_chunks(own))


def add(first, second):
    return (first.astype(F32) + second.astype(F32)).astype(BF)


def sum_kernel(two, *refs):
    refs[-1][...] = jnp.zeros_like(refs[-1])
    values = [ref[...] for ref in refs[1 : 1 + (4 if two else 2)]]
    if two:
        values = [
            (values[i].astype(F32) + values[i + 2].astype(F32)).astype(BF) for i in range(2)
        ]
    refs[-3][...], refs[-2][...] = values


def split_sum(first, second, place, mine, deps):
    shape = first.shape
    lead, tail = shape[:place], shape[place + 1 :]
    count = 1
    for size in lead:
        count *= size
    flat = (count, 2) + ((1,) * max(0, 2 - len(tail)) + tail)
    steps = 2 if count % 2 == 0 and first.size * 2 > (1 << 20) else 1
    block = (count // steps, 1) + flat[2:]
    zeros = (0,) * (len(flat) - 2)
    keep = pl.BlockSpec(block, lambda i, m: (i, m[0]) + zeros)
    send = pl.BlockSpec(block, lambda i, m: (i, 1 - m[0]) + zeros)
    out = pl.BlockSpec(block, lambda i, m: (i, 0) + zeros)
    shape_out = jax.ShapeDtypeStruct((count, 1) + flat[2:], BF)
    values = [v.reshape(flat) for v in (first, second) if v is not None]
    *halves, token = pl.pallas_call(
        functools.partial(sum_kernel, second is not None),
        grid_spec=pltpu.PrefetchScalarGridSpec(
            num_scalar_prefetch=1,
            grid=(steps,),
            in_specs=[keep, send] * len(values) + [ANY] * len(deps),
            out_specs=[out, out, pl.BlockSpec(TOKEN.shape, lambda i, m: (0, 0))],
        ),
        out_shape=[shape_out, shape_out, TOKEN],
        compiler_params=params(12),
        cost_estimate=cost(0.3),
        name="split_sum",
    )(mine[None], *[v for v in values for _ in range(2)], *deps)
    return *[h.reshape(lead + tail) for h in halves], token


class Scatter:
    def __init__(self, value, transit, axes, order, scope):
        self.places = [
            (axis, bit)
            for axis in axes
            for bit in reversed(range(lax.axis_size(axis).bit_length() - 1))
            if (axis, bit) in order
        ]
        self.order = list(order)
        self.scope = scope
        self.transit = transit
        self.value, self.transit = (
            v.reshape((2,) * len(self.places) + v.shape[len(axes) :]) for v in (value, transit)
        )

    def step(self, deps=()):
        with jax.named_scope(self.scope):
            if not self.order:
                if self.transit is not None:
                    self.value = add(self.value, self.transit)
                    self.transit = None
                return ()
            axis, bit = self.order.pop(0)
            place = self.places.index((axis, bit))
            self.places.pop(place)
            mine = lax.rem(lax.div(lax.axis_index(axis), 1 << bit), 2)
            self.value, send, token = split_sum(self.value, self.transit, place, mine, deps)
            self.transit = swap(send, axis, 1 << bit)
            return (token,)

    def finish(self, deps=()):
        while self.order or self.transit is not None:
            self.step(deps)
        return self.value


def img_bits():
    return [("img", bit) for bit in range(lax.axis_size("img").bit_length() - 1)]


def reduce_rest(keep, send, scope):
    with jax.named_scope(scope):
        transit = swap(send, "patch", 1)
    return Scatter(keep, transit, ("img", "patch"), [("patch", 1)] + img_bits(), scope)


def in_order(chunks):
    me = lax.axis_index("patch")
    out = []
    for j in range(4):
        apart = jnp.bitwise_xor(me, j)
        at = 2 * jnp.bitwise_and(apart, 1) + lax.shift_right_logical(apart, 1)
        out.append(lax.dynamic_index_in_dim(chunks, at, 0, keepdims=False))
    return jnp.stack(out)


def gather_rows(own):
    return in_order(gather_patch(own))


def place_kernel(index_ref, chunks_ref, out_ref):
    parts, _, unit = chunks_ref.shape
    for j in range(parts):
        apart = jnp.bitwise_xor(index_ref[0], j)
        at = jnp.where(apart == 1, 2, jnp.where(apart == 2, 1, apart))
        out_ref[:, j * unit : (j + 1) * unit] = chunks_ref[at].astype(F32)


def place_call(index, chunks, rows, imgs):
    parts, _, units = chunks.shape
    unit = units // imgs
    return pl.pallas_call(
        place_kernel,
        grid_spec=pltpu.PrefetchScalarGridSpec(
            num_scalar_prefetch=1,
            grid=(imgs,),
            in_specs=[pl.BlockSpec((parts, rows, unit), lambda i, p: (0, 0, i))],
            out_specs=pl.BlockSpec((rows, parts * unit), lambda i, p: (0, i)),
        ),
        out_shape=jax.ShapeDtypeStruct((rows, parts * units), F32),
        compiler_params=params(6),
        name="place_units",
    )(index, chunks)


def local(
    latents,
    media,
    doc_ids,
    w_query,
    w_keyval,
    w_output,
    w_expand,
    w_reduce,
    media_gain,
    media_shift,
    latent_gain,
    latent_shift,
    ff_gain,
    ff_shift,
    out_grad,
):
    micro, docs, lat_rows, width = latents.shape
    slots, keys = media.shape[1:3]
    inner = w_query.shape[1]
    ff = w_expand.shape[1]
    head_size = inner // HEADS
    scale = head_size ** (-0.5)
    parts = lax.axis_size("patch")
    imgs = lax.axis_size("img")
    patch_index = lax.axis_index("patch")
    own_rows = micro * docs * lat_rows
    all_rows = own_rows * parts
    groups = HEADS // GROUP
    span = inner // groups
    unit = ff // (imgs * parts)

    latents_own = latents.reshape(own_rows, width)
    cot_own = out_grad.reshape(own_rows, width)
    media_flat = media.reshape(-1, width)
    with jax.named_scope("gather_latents"):
        latents_far = swap(latents_own, "patch", 2)
        latents_near = swap(latents_own, "patch", 1)

    hat_med, kv_med, token = kv_call(media_flat, media_gain[None], media_shift[None], w_keyval)
    kv_med = kv_med.reshape(micro, slots, keys, 2 * inner)
    if unit % 128 == 0:
        w_exp, w_red, *part_done = part_call(
            patch_index[None], w_expand, w_reduce, imgs, parts
        )
    else:
        w_exp = lax.dynamic_index_in_dim(
            w_expand.reshape(width, imgs, parts, unit), patch_index, 2, keepdims=False
        ).reshape(width, imgs * unit)
        w_red = lax.dynamic_index_in_dim(
            w_reduce.reshape(imgs, parts, unit, width), patch_index, 1, keepdims=False
        ).reshape(imgs * unit, width)
        part_done = []

    (latents_far,) = gate((latents_far,), (token,), pltpu.VMEM)
    with jax.named_scope("gather_latents"):
        latents_both = swap(latents_far, "patch", 1)
    latents_all, hat_all, queries, kv_lat, cot_sent = latent_call(
        (latents_own, latents_far, latents_near, latents_both),
        latent_gain[None],
        latent_shift[None],
        w_query,
        w_keyval,
        cot_own,
        (token,),
    )
    kv_lat = kv_lat.reshape(micro, docs, lat_rows, 2 * inner)
    with jax.named_scope("gather_cotangent"):
        cot_far = swap(cot_sent, "patch", 2)
    keep, send = attend_call(doc_ids, queries, kv_med, kv_lat, ())
    send, cot_far = gate((send, cot_far), (), pltpu.VMEM)
    with jax.named_scope("join_near"):
        near = join_call(keep, swap(send, "patch", 1), False, False)
    with jax.named_scope("gather_cotangent"):
        cot_all = jnp.stack(
            [cot_sent, cot_far, swap(cot_sent, "patch", 1), swap(cot_far, "patch", 1)]
        )
    with jax.named_scope("join_far"):
        att_near = join_call(
            near, swap(near, "patch", 2), True, True, part_done
        )
        att_far = swap(att_near, "patch", 1)

    mixed, ln_ff, hidden_act, grad_pre, *ff_parts = ff_call(
        latents_all,
        att_near,
        att_far,
        cot_all,
        w_output,
        w_exp,
        w_red,
        ff_gain[None],
        ff_shift[None],
    )
    up_own, up_keep, up_send, out_own, out_keep, out_send = ff_parts
    with jax.named_scope("sum_up"):
        up_sent = swap(up_send, "patch", 1)
        up_near = add(up_keep, up_sent[1])
        up_far = swap(up_near, "patch", 2)

    def flat(value):
        return value.reshape(all_rows, -1)

    ff_grads = ff_weights_call(
        flat(ln_ff), flat(grad_pre), flat(hidden_act), flat(cot_all), imgs, (up_near,)
    )
    (up_far,) = gate((up_far,), (ff_grads,), pltpu.VMEM)
    (ff_grads,) = gate((ff_grads,), (up_far,), pltpu.HBM)
    grad_mixed, grad_branch, grad_att_own, ff_gain_part, ff_shift_part = mixed_back_call(
        up_own, up_sent, up_far, mixed, cot_sent, w_output, ff_gain[None], ()
    )
    with jax.named_scope("gather_att"):
        grad_att = [chunk[None] for chunk in gather_chunks(grad_att_own)]
    att = (att_near, att_far)
    grad_output = dot(att_near[0, :, :inner], grad_branch, TN).astype(BF)

    with jax.named_scope("sum_ff"):
        ff_own = lax.psum_scatter(ff_grads, "img", scatter_dimension=0, tiled=True)[0]

    zero = jnp.zeros_like(media_gain)
    norms = jnp.stack(
        [media_gain, media_shift, latent_gain, latent_shift, zero, zero, zero, zero]
    )
    ff_vectors = jnp.pad(jnp.concatenate([ff_gain_part, ff_shift_part]), ((0, 6), (0, 0)))
    share = width // imgs
    tall = share // parts
    direct = laid_out(width, imgs, inner)

    def back_call(group, extra, vectors, deps):
        gkv, gkv_lat, gq, keep, send, vectors = attend_back_call(
            group,
            doc_ids,
            queries,
            grad_att,
            att,
            kv_med,
            kv_lat,
            hat_med,
            hat_all,
            w_keyval,
            w_query,
            norms,
            extra,
            vectors,
            patch_index[None],
            imgs,
            deps,
        )
        if not direct:

            def split(value):
                size = value.shape[0] // (imgs * parts)
                return value.reshape(imgs, parts // 2, 2, size, value.shape[1])

            rows = split(keep)
            fold = [rows[..., : tall // 2, 2 * span :], rows[..., tall // 2 :, 2 * span :]]
            blocks = [rows[..., : 2 * span], jnp.concatenate(fold, axis=-1)]
            if group == 0:
                blocks += [split(extra)[..., :inner], split(extra)[..., inner:]]
            else:
                six = jnp.concatenate([vectors[:4], extra[:2]]).astype(BF)
                six = jnp.swapaxes(six.reshape(6, imgs, share), 0, 1)
                six = jnp.pad(six, ((0, 0), (0, 10), (0, width - share)))[:, None, None, :, :inner]
                blocks.append(
                    jnp.pad(six, ((0, 0), (0, parts // 2 - 1), (0, 1), (0, 0), (0, 0)))
                )
            blocks = jnp.concatenate(blocks, axis=3)
            bit = lax.rem(patch_index, 2)
            keep = lax.dynamic_index_in_dim(blocks, bit, 2, keepdims=False)
            send = lax.dynamic_index_in_dim(blocks, 1 - bit, 2, keepdims=False)
        return gkv, gkv_lat, gq, keep, send, vectors

    out_keep, out_send = gate((out_keep, out_send), grad_att[3:], pltpu.HBM)
    with jax.named_scope("sum_out"):
        out_sent = swap(out_send, "patch", 1)
        out_far = swap(add(out_keep, out_sent[1]), "patch", 2)
    gkv_0, gkv_lat_0, gq_0, keep, send, vectors = back_call(
        0, grad_output, norms, ()
    )
    first = reduce_rest(keep, send, "sum_weights_0")
    gkv_1, gkv_lat_1, gq_1, keep, send, vectors = back_call(
        1, ff_vectors, vectors, first.step()
    )
    done = first.step((vectors,))
    latents_out, token = out_call(mixed, out_own, out_sent, out_far, (vectors,))
    keep, send, gq_0, gq_1 = gate((keep, send, gq_0, gq_1), (*done, token), pltpu.VMEM)
    second = reduce_rest(keep, send, "sum_weights_1")
    with jax.named_scope("sum_query"):
        gq_keep = jnp.concatenate([gq_0[:2], gq_1[:2]], axis=-1)
        gq_sent = swap(jnp.concatenate([gq_0[2:], gq_1[2:]], axis=-1), "patch", 1)

    def media_piece(at, size, whole, deps):
        return media_back_call(
            media_flat,
            gkv_0,
            gkv_1,
            w_keyval,
            media_gain[None],
            at,
            size,
            whole,
            deps,
        )

    media_grad, *done = media_piece(0, 4, None, second.step())
    deps = (*first.step(done), *second.step(done))
    (gq_keep,) = gate((gq_keep,), done, pltpu.VMEM)
    with jax.named_scope("sum_query"):
        gq_near = add(gq_keep, gq_sent)
        gq_far = swap(gq_near[1], "patch", 2)
    media_grad, *done = media_piece(4, 2, media_grad, deps)
    deps = (*first.step(done), *second.step(done))
    (ff_own,) = gate((ff_own,), deps, pltpu.HBM)
    with jax.named_scope("gather_ff"):
        expand_far = swap(ff_own[:share], "patch", 2)
    media_grad, *done = media_piece(6, 2, media_grad, deps)
    (expand_far,) = gate((expand_far,), done, pltpu.VMEM)
    done = (*done, expand_far)
    first.step(done)
    second.step(done)
    latents_grad = latent_back_call(
        scale,
        (
            latents_own,
            grad_mixed,
            gq_near[0],
            gq_far,
            gkv_lat_0,
            gkv_lat_1,
            w_query,
            w_keyval,
            latent_gain[None],
        ),
        done,
    )

    first = first.finish(done)
    second = second.finish(done)

    def rows_of(value):
        return value.reshape(-1, value.shape[-1])

    with jax.named_scope("gather_weights"):
        whole = gather_rows(jnp.concatenate([first, second]))
    cut = first.shape[0]
    first, second = whole[:, :cut], whole[:, cut:]
    keyval_rows = [rows_of(first[:, :tall]), rows_of(second[:, :tall])]
    grad_keyval = jnp.concatenate(
        [rows[:, at * span : (at + 1) * span] for at in range(2) for rows in keyval_rows], axis=1
    ).astype(F32)
    end = tall + tall // 2

    def unfold(value):
        return rows_of(jnp.concatenate([value[..., :span], value[..., span:]], axis=1))

    query_rows = jnp.concatenate(
        [unfold(first[:, tall:end]), unfold(second[:, tall:end])], axis=1
    ).astype(F32)
    out_rows = first[:, end:]
    size = out_rows.shape[1] // 2
    out_rows = rows_of(
        jnp.concatenate([out_rows[:, :size], out_rows[:, size:]], axis=2)
    ).astype(F32)
    vectors = second[0, end : end + 6, :share].astype(F32)

    def gather_half(own, far):
        return jnp.stack([own, far, swap(own, "patch", 1), swap(far, "patch", 1)])

    with jax.named_scope("gather_ff"):
        expand = gather_half(ff_own[:share], expand_far)
        reduce = gather_patch(ff_own[share:])
    with jax.named_scope("place_ff"):
        if unit % 128 == 0:
            expand_rows = place_call(patch_index[None], expand, share, imgs)
        else:
            expand_rows = in_order(expand).reshape(parts, -1, imgs, unit)
            expand_rows = jnp.transpose(expand_rows, (1, 2, 0, 3)).reshape(-1, ff).astype(F32)
        reduce_rows = rows_of(in_order(reduce)).astype(F32)

    return (
        latents_out.reshape(latents.shape),
        latents_grad.reshape(latents.shape),
        media_grad.reshape(media.shape),
        query_rows,
        grad_keyval,
        out_rows,
        expand_rows,
        reduce_rows,
    ) + tuple(vectors[i] for i in range(6))


def solution(mesh):
    tokens = P(None, "img", "patch", None)
    return jax.shard_map(
        local,
        mesh=mesh,
        in_specs=(tokens, tokens, P(None, "img")) + (P(),) * 11 + (tokens,),
        out_specs=(tokens,) * 3 + (P("img", None),) * 5 + (P("img"),) * 6,
        check_vma=False,
    )
```

```python
import functools

import jax
import jax.numpy as jnp
from jax import lax
from jax.experimental import pallas as pl
from jax.experimental.pallas import tpu as pltpu
from jax.sharding import PartitionSpec as P

HEADS = 8
GROUP = 4
EPS = 1e-05
CHUNK = 6
FAR = -1e30
BF = jnp.bfloat16
F32 = jnp.float32
ANY = pl.BlockSpec(memory_space=pl.ANY)
TOKEN = jax.ShapeDtypeStruct((8, 128), jnp.float32)


def params(mib=56):
    return pltpu.CompilerParams(vmem_limit_bytes=mib << 20)


def cost(us):
    return pl.CostEstimate(flops=int(us * 1.1e9), bytes_accessed=0, transcendentals=0)


def hbm_call(kernel, held, kept, inside=(), **options):
    shapes = options.pop("out_shape")
    if isinstance(shapes, list):
        shapes = [pltpu.HBM(v.shape, v.dtype) if i in kept else v for i, v in enumerate(shapes)]
    options["out_shape"] = shapes
    scalars = options["grid_spec"].num_scalar_prefetch if "grid_spec" in options else 0
    inner = pl.pallas_call(kernel, **options)

    def run(*operands):
        def place(i, x):
            if i in inside:
                return pltpu.with_memory_space_constraint(x, pltpu.VMEM)
            if i in held or x.size >= 1 << 20:
                return pltpu.with_memory_space_constraint(x, pltpu.HBM)
            return x

        arrays = [place(i, x) for i, x in enumerate(operands[scalars:])]
        return inner(*operands[:scalars], *arrays)

    return run


def nothing_kernel(*refs):
    pass


def gate(carry, deps, space):
    return pl.pallas_call(
        nothing_kernel,
        in_specs=[ANY] * (len(carry) + len(deps)),
        out_specs=[ANY] * len(carry),
        out_shape=[space(c.shape, c.dtype) for c in carry],
        input_output_aliases={i: i for i in range(len(carry))},
        compiler_params=params(1),
        name="gate",
    )(
        *[pltpu.with_memory_space_constraint(c, space) for c in carry],
        *[
            pltpu.with_memory_space_constraint(d, pltpu.HBM) if d.size >= 1 << 20 else d
            for d in deps
        ],
    )


def dot(a, b, dims):
    return lax.dot_general(a, b, (dims, ((), ())), preferred_element_type=F32)


NN = ((1,), (0,))
NT = ((1,), (1,))
TN = ((0,), (0,))


def standardize(values):
    center = values - jnp.mean(values, axis=-1, keepdims=True)
    inv = lax.rsqrt(jnp.mean(center * center, axis=-1, keepdims=True) + EPS)
    return center * inv, inv


def norm_back(hat, inv, gain, upstream):
    scaled = upstream * gain
    back = inv * (
        scaled
        - jnp.mean(scaled, axis=-1, keepdims=True)
        - hat * jnp.mean(scaled * hat, axis=-1, keepdims=True)
    )
    return back, upstream * hat


def kv_kernel(media_ref, gain_ref, shift_ref, w_ref, hat_ref, kv_ref, token_ref):
    token_ref[...] = jnp.zeros_like(token_ref)
    rows = media_ref.shape[0]
    step = min(rows, 256)
    for at in range(0, rows, step):
        part = pl.ds(at, step)
        hat, _ = standardize(media_ref[part, :].astype(F32))
        ln = (hat * gain_ref[...] + shift_ref[...]).astype(BF)
        hat_ref[part, :] = hat.astype(BF)
        kv_ref[part, :] = dot(ln, w_ref[...], NN).astype(BF)


def kv_call(media, gain, shift, w_keyval):
    rows, width = media.shape
    outs = w_keyval.shape[1]
    block = 1024
    return hbm_call(
        kv_kernel,
        range(4),
        (0, 1),
        grid=(rows // block,),
        in_specs=[
            pl.BlockSpec((block, width), lambda i: (i, 0)),
            pl.BlockSpec((1, width), lambda i: (0, 0)),
            pl.BlockSpec((1, width), lambda i: (0, 0)),
            pl.BlockSpec((width, outs), lambda i: (0, 0)),
        ],
        out_specs=[
            pl.BlockSpec((block, width), lambda i: (i, 0)),
            pl.BlockSpec((block, outs), lambda i: (i, 0)),
            pl.BlockSpec(TOKEN.shape, lambda i: (0, 0)),
        ],
        out_shape=[
            jax.ShapeDtypeStruct((rows, width), BF),
            jax.ShapeDtypeStruct((rows, outs), BF),
            TOKEN,
        ],
        compiler_params=params(20),
        cost_estimate=cost(16),
        name="media_keyval",
    )(media, gain, shift, w_keyval)


def latent_kernel(own, far, near, both, gain_ref, shift_ref, wq_ref, wkv_ref, cot_ref, *rest):
    raw_ref, hat_ref, q_ref, kv_ref, cot_out = rest[-5:]
    scale = (wq_ref.shape[1] // HEADS) ** (-0.5)
    cot_out[...] = cot_ref[...]
    for c, ref in enumerate((own, far, near, both)):
        raw = ref[...]
        raw_ref[c] = raw
        hat, _ = standardize(raw.astype(F32))
        hat_ref[c] = hat.astype(BF)
        ln = (hat * gain_ref[...] + shift_ref[...]).astype(BF)
        q_ref[c] = (dot(ln, wq_ref[...], NN).astype(BF).astype(F32) * scale).astype(BF)
        if c == 0:
            kv_ref[...] = dot(ln, wkv_ref[...], NN).astype(BF)


def latent_call(chunks, gain, shift, w_query, w_keyval, cot, deps):
    rows, width = chunks[0].shape
    inner = w_query.shape[1]
    count = len(chunks)
    return hbm_call(
        latent_kernel,
        (6, 7),
        range(4),
        (1, 2, 3),
        in_specs=[pl.BlockSpec(memory_space=pltpu.VMEM)] * (count + 5) + [ANY] * len(deps),
        out_shape=[
            jax.ShapeDtypeStruct((count, rows, width), BF),
            jax.ShapeDtypeStruct((count, rows, width), BF),
            jax.ShapeDtypeStruct((count, rows, inner), BF),
            jax.ShapeDtypeStruct((rows, 2 * inner), BF),
            jax.ShapeDtypeStruct(cot.shape, BF),
        ],
        compiler_params=params(28),
        cost_estimate=cost(6),
        name="latents",
    )(*chunks, gain, shift, w_query, w_keyval, cot, *deps)


def kv_columns(first, second):
    span = first.shape[1] // 2
    return jnp.concatenate(
        [first[:, :span], second[:, :span], first[:, span:], second[:, span:]], axis=1
    )


def latent_back_kernel(
    scale, raw_ref, mixed_ref, own_ref, far_ref, kv_a, kv_b, wq_ref, w_ref, gain_ref, *rest
):
    grad_q = ((own_ref[...].astype(F32) + far_ref[...].astype(F32)) * scale).astype(BF)
    up = (
        dot(grad_q, wq_ref[...], NT)
        + dot(kv_columns(kv_a[...], kv_b[...]), w_ref[...], NT)
    )
    hat, inv = standardize(raw_ref[...].astype(F32))
    back, _ = norm_back(hat, inv, gain_ref[...], up)
    rest[-2][...] = (mixed_ref[...] + back).astype(BF)
    rest[-1][...] = jnp.zeros_like(rest[-1])


def latent_back_call(scale, args, deps):
    return hbm_call(
        functools.partial(latent_back_kernel, scale),
        (1, 4, 5, 6, 7),
        (0,),
        (2, 3),
        in_specs=[pl.BlockSpec(memory_space=pltpu.VMEM)] * len(args) + [ANY] * len(deps),
        out_shape=[jax.ShapeDtypeStruct(args[0].shape, BF), TOKEN],
        compiler_params=params(24),
        cost_estimate=cost(0.1),
        name="latent_back",
    )(*args, *deps)


def out_kernel(mixed_ref, own_ref, near_ref, far_ref, *rest):
    total = own_ref[...].astype(F32) + near_ref[0].astype(F32) + far_ref[...].astype(F32)
    rest[-2][...] = (mixed_ref[...] + total).astype(BF)
    rest[-1][...] = jnp.zeros_like(rest[-1])


def out_call(mixed, own, near, far, deps):
    return hbm_call(
        out_kernel,
        (0, 1),
        (0,),
        (2, 3),
        in_specs=[pl.BlockSpec(memory_space=pltpu.VMEM)] * 4 + [ANY] * len(deps),
        out_shape=[jax.ShapeDtypeStruct(mixed.shape, BF), TOKEN],
        compiler_params=params(8),
        cost_estimate=cost(1.5),
        name="latents_out",
    )(mixed, own, near, far, *deps)


def block_mask(head_size, lats):
    rows = GROUP * lats
    cols = GROUP * head_size
    row_head = lax.broadcasted_iota(jnp.int32, (rows, cols), 0) // lats
    col_head = lax.broadcasted_iota(jnp.int32, (rows, cols), 1) // head_size
    return row_head == col_head


def spread_heads(values, mask):
    tiled = jnp.concatenate([values] * GROUP, axis=0)
    return jnp.where(mask, tiled, jnp.zeros_like(tiled))


def gather_heads(full, mask, lats):
    kept = jnp.where(mask, full, 0.0)
    total = kept[:lats]
    for head in range(1, GROUP):
        total = total + kept[head * lats : (head + 1) * lats]
    return total


LANES = 128


def terms(value):
    first = value.astype(BF)
    rest = value - first.astype(F32)
    second = rest.astype(BF)
    return first, second, (rest - second.astype(F32)).astype(BF)


def pick(shape, fn):
    row = lax.broadcasted_iota(jnp.int32, shape, 0)
    col = lax.broadcasted_iota(jnp.int32, shape, 1)
    return jnp.where(fn(row, col), 1.0, 0.0).astype(BF)


def holds(lane, head, figure):
    return (lane < 24 * figure + 24) & (lane >= 24 * figure) & (lane % HEADS == head)


def pack_rows(figures):
    rows = jnp.concatenate([t for f in figures for t in terms(f)], axis=0)
    eye = pick((rows.shape[0], LANES), lambda r, c: r == c)
    return dot(rows, eye, TN).astype(BF)


def pack_cols(figures):
    total = None
    for i, figure in enumerate(figures):
        for k, term in enumerate(terms(figure)):
            at = HEADS * (3 * i + k)
            place = pick((LANES, LANES), lambda r, c: (r < HEADS) & (c == r + at))
            part = dot(term, place, NN)
            total = part if total is None else total + part
    return total.astype(BF)


def widen(packed, figure, inner):
    size = inner // HEADS
    return dot(packed, pick((LANES, inner), lambda r, c: holds(r, c // size, figure)), NN)


def narrow(packed, figure):
    return dot(
        packed, pick((LANES, LANES), lambda r, c: (c < HEADS) & holds(r, c, figure)), NN
    )


def doc_rows(refs, d, lat_rows, cols):
    rows = slice(d * lat_rows, (d + 1) * lat_rows)
    return jnp.concatenate(
        [ref[c, rows, cols] for ref in refs for c in range(ref.shape[0])], axis=0
    )


def doc_spans(doc_ref, micro, docs, slots):
    counts = []
    for d in range(docs):
        total = 0
        for s in range(slots):
            total = total + jnp.where(doc_ref[micro, s] == d, 1, 0)
        counts.append(total)
    first = 0
    spans = []
    for count in counts:
        spans.append((first, count))
        first = first + count
    return spans


def slot_chunk(span, step, slots):
    first, count = span
    low = first + step * CHUNK
    return jnp.minimum(low, slots - CHUNK), low, first + count


def own_rows_of(at, low, high, keys):
    slot = at + lax.broadcasted_iota(jnp.int32, (CHUNK * keys, 1), 0) // keys
    return (slot >= low) & (slot < high)


def steps_of(span):
    return (span[1] + CHUNK - 1) // CHUNK


PAIR = 1


def more_chunks(spans, slots, body):
    counts = [steps_of(span) - 1 for span in spans]
    total = sum(counts)

    def locate(e):
        d, before, end = 0, 0, 0
        for count in counts[:-1]:
            end = end + count
            d = d + jnp.where(e >= end, 1, 0)
            before = jnp.where(e >= end, end, before)
        step = e - before + 1
        first, count = 0, 0
        for i, span in enumerate(spans):
            first = first + jnp.where(d == i, span[0], 0)
            count = count + jnp.where(d == i, span[1], 0)
        at, low, high = slot_chunk((first, count), step, slots)
        return d, step, at, low, jnp.where(e < total, high, low)

    def pair(i, carry):
        body([locate(PAIR * i + k) for k in range(PAIR)])
        return carry

    lax.fori_loop(0, (total + PAIR - 1) // PAIR, pair, 0)


def attend_kernel(deps, doc_ref, q_ref, kv_ref, kvl_ref, *rest):
    keep_ref, send_ref, bd, score, acc, top, tot = rest[deps:]
    chunks, rows, inner = q_ref.shape
    docs, lat_rows = kvl_ref.shape[1:3]
    lats = chunks * lat_rows
    slots, keys = kv_ref.shape[1:3]
    groups = HEADS // GROUP
    span = inner // groups
    micro = pl.program_id(0)
    mask = block_mask(inner // HEADS, lats)
    cols = [slice(g * span, (g + 1) * span) for g in range(groups)]
    vals = [slice(inner + g * span, inner + (g + 1) * span) for g in range(groups)]
    spans = doc_spans(doc_ref, micro, docs, slots)
    tall = CHUNK * keys

    def load(at, part):
        return kv_ref[0, pl.ds(at, CHUNK), :, part].reshape(tall, span)

    for d in range(docs):
        at, low, high = slot_chunk(spans[d], 0, slots)
        bias = jnp.where(own_rows_of(at, low, high, keys), 0.0, FAR)
        bias = jnp.concatenate([bias, jnp.zeros((lat_rows, 1), F32)], axis=0)
        for g in range(groups):
            spread = spread_heads(doc_rows((q_ref,), d, lat_rows, cols[g]), mask)
            bd[d, g] = spread
            key = jnp.concatenate([load(at, cols[g]), kvl_ref[0, d, :, cols[g]]], axis=0)
            val = dot(key, spread, NT) + bias
            score[d, g, 0] = val
            top[d, g] = jnp.max(val, axis=0, keepdims=True)

    def more(parts):
        for k, (d, step, at, low, high) in enumerate(parts):
            bias = jnp.where(own_rows_of(at, low, high, keys), 0.0, FAR)
            for g in range(groups):
                val = dot(load(at, cols[g]), bd[d, g], NT) + bias
                score[d, g, jnp.minimum(step, score.shape[2] - 1), :tall] = val
                top[d, g] = jnp.maximum(top[d, g], jnp.max(val, axis=0, keepdims=True))

    more_chunks(spans, slots, more)
    for d in range(docs):
        at, low, high = slot_chunk(spans[d], 0, slots)
        for g in range(groups):
            expo = jnp.exp(score[d, g, 0] - top[d, g])
            tot[d, g] = jnp.sum(expo, axis=0, keepdims=True)
            val = jnp.concatenate([load(at, vals[g]), kvl_ref[0, d, :, vals[g]]], axis=0)
            acc[d, g] = dot(expo.astype(BF), val, TN)

    def more_values(parts):
        for d, step, at, low, high in parts:
            step = jnp.minimum(step, score.shape[2] - 1)
            own = own_rows_of(at, low, high, keys)
            for g in range(groups):
                expo = jnp.where(own, jnp.exp(score[d, g, step, :tall] - top[d, g]), 0.0)
                tot[d, g] = tot[d, g] + jnp.sum(expo, axis=0, keepdims=True)
                acc[d, g] = acc[d, g] + dot(expo.astype(BF), load(at, vals[g]), TN)

    more_chunks(spans, slots, more_values)
    half = chunks // 2
    for d in range(docs):
        rows_d = slice(d * lat_rows, (d + 1) * lat_rows)

        def by_head(ref):
            return jnp.concatenate(
                [
                    ref[d, g][:, h * lats : (h + 1) * lats]
                    for g in range(groups)
                    for h in range(GROUP)
                ],
                axis=0,
            )

        packed = pack_rows([by_head(top), by_head(tot)])
        outs = [gather_heads(acc[d, g], mask, lats).astype(BF) for g in range(groups)]
        for c in range(chunks):
            ref = keep_ref if c < half else send_ref
            part = slice(c * lat_rows, (c + 1) * lat_rows)
            for g in range(groups):
                ref[c % half, rows_d, cols[g]] = outs[g][part]
            ref[c % half, rows_d, inner:] = packed[part]


def attend_call(doc_ids, queries, kv_med, kv_lat, deps):
    chunks, _, inner = queries.shape
    micro, slots, keys, both = kv_med.shape
    docs, lat_rows = kv_lat.shape[1:3]
    lats = chunks * lat_rows
    rows = docs * lat_rows
    groups = HEADS // GROUP
    span = inner // groups
    wide = GROUP * lats
    half = chunks // 2
    longest = (slots - docs + CHUNK) // CHUNK
    out_spec = pl.BlockSpec((half, rows, inner + LANES), lambda i, ids: (0, i, 0))
    out_shape = jax.ShapeDtypeStruct((half, micro * rows, inner + LANES), BF)
    return hbm_call(
        functools.partial(attend_kernel, len(deps)),
        range(3),
        (),
        grid_spec=pltpu.PrefetchScalarGridSpec(
            num_scalar_prefetch=1,
            grid=(micro,),
            in_specs=[
                pl.BlockSpec((chunks, rows, inner), lambda i, ids: (0, i, 0)),
                pl.BlockSpec((1, slots, keys, both), lambda i, ids: (i, 0, 0, 0)),
                pl.BlockSpec((1, docs, lat_rows, both), lambda i, ids: (i, 0, 0, 0)),
            ]
            + [ANY] * len(deps),
            out_specs=[out_spec, out_spec],
            scratch_shapes=[
                pltpu.VMEM((docs, groups, wide, span), BF),
                pltpu.VMEM((docs, groups, longest, CHUNK * keys + lat_rows, wide), F32),
                pltpu.VMEM((docs, groups, wide, span), F32),
                pltpu.VMEM((docs, groups, 1, wide), F32),
                pltpu.VMEM((docs, groups, 1, wide), F32),
            ],
        ),
        out_shape=[out_shape, out_shape],
        compiler_params=params(40),
        cost_estimate=cost(13),
        name="attend",
    )(doc_ids, queries, kv_med, kv_lat, *deps)


def join_kernel(last, flip, a_ref, b_ref, *rest):
    out_ref = rest[-1]
    inner = a_ref.shape[2] - LANES
    count = a_ref.shape[0]
    for c in range(count):
        first, second = a_ref[c], b_ref[count - 1 - c if flip else c]
        pack_a, pack_b = first[:, inner:], second[:, inner:]
        top_a, top_b = widen(pack_a, 0, inner), widen(pack_b, 0, inner)
        best = jnp.maximum(top_a, top_b)
        fac_a, fac_b = jnp.exp(top_a - best), jnp.exp(top_b - best)
        out = fac_a * first[:, :inner].astype(F32) + fac_b * second[:, :inner].astype(F32)
        if last:
            total = fac_a * widen(pack_a, 1, inner) + fac_b * widen(pack_b, 1, inner)
            out = out / total
        out_ref[c, :, :inner] = out.astype(BF)
        small_a, small_b = narrow(pack_a, 0), narrow(pack_b, 0)
        small = jnp.maximum(small_a, small_b)
        sum_ab = jnp.exp(small_a - small) * narrow(pack_a, 1) + jnp.exp(
            small_b - small
        ) * narrow(pack_b, 1)
        if last:
            lane = lax.broadcasted_iota(jnp.int32, sum_ab.shape, 1)
            lse = jnp.where(lane < HEADS, small + jnp.log(jnp.maximum(sum_ab, 1e-30)), 0.0)
            out_ref[c, :, inner:] = pack_cols([lse])
        else:
            out_ref[c, :, inner:] = pack_cols([small, sum_ab])


def join_call(first, second, last, flip, deps=()):
    count, rows, cols = first.shape
    block = min(rows, 128)
    spec = pl.BlockSpec((count, block, cols), lambda i: (0, i, 0))
    return pl.pallas_call(
        functools.partial(join_kernel, last, flip),
        grid=(rows // block,),
        in_specs=[spec, spec] + [ANY] * len(deps),
        out_specs=spec,
        out_shape=jax.ShapeDtypeStruct(first.shape, BF),
        compiler_params=params(10),
        cost_estimate=cost(3.5),
        name="join_last" if last else "join_first",
    )(first, second, *deps)


def cot_units_kernel(own, far, near, both, wr_ref, units_ref, cot_ref, token_ref):
    token_ref[...] = jnp.zeros_like(token_ref)
    for c, ref in enumerate((own, far, near, both)):
        cot_ref[c] = ref[...]
    for c in range(0, 4, 2):
        rows = own.shape[0]
        pair = cot_ref[c : c + 2].reshape(2 * rows, own.shape[1])
        units_ref[c : c + 2] = dot(pair, wr_ref[...], NT).reshape(2, rows, wr_ref.shape[0])


def cot_units_call(chunks, w_red):
    rows, width = chunks[0].shape
    count = len(chunks)
    return hbm_call(
        cot_units_kernel,
        (0, 4),
        (0, 1),
        (1, 2, 3),
        in_specs=[pl.BlockSpec(memory_space=pltpu.VMEM)] * 5,
        out_shape=[
            jax.ShapeDtypeStruct((count, rows, w_red.shape[0]), F32),
            jax.ShapeDtypeStruct((count, rows, width), BF),
            TOKEN,
        ],
        compiler_params=params(24),
        cost_estimate=cost(6),
        name="cot_units",
    )(*chunks, w_red)


def ff_kernel(
    lat_ref,
    near_ref,
    far_ref,
    units_ref,
    wo_ref,
    we_ref,
    wr_ref,
    gain_ref,
    shift_ref,
    mixed_ref,
    ln_ref,
    act_ref,
    gpre_ref,
    up_own,
    up_keep,
    up_send,
    out_own,
    out_keep,
    out_send,
):
    i = pl.program_id(0)
    half = pl.num_programs(0) // 2
    att = jnp.where(i < half, near_ref[0], far_ref[0])
    mixed = lat_ref[0].astype(F32) + dot(att, wo_ref[...], NN)
    hat, _ = standardize(mixed)
    ln = (hat * gain_ref[...] + shift_ref[...]).astype(BF)
    ln_ref[0] = ln
    pre = dot(ln, we_ref[...], NN)
    cdf = 0.5 + 0.5 * lax.erf(pre * (0.5**0.5))
    slope = cdf + pre * (0.3989422804014327 * jnp.exp(-0.5 * pre * pre))
    act = (pre * cdf).astype(BF)
    act_ref[0] = act
    gpre = (units_ref[0] * slope).astype(BF)
    gpre_ref[0] = gpre
    up = dot(gpre, we_ref[...], NT).astype(BF)
    out = dot(act, wr_ref[...], NN).astype(BF)

    @pl.when(i == 0)
    def _():
        mixed_ref[...] = mixed
        up_own[...] = up
        out_own[...] = out

    @pl.when(i == 1)
    def _():
        up_keep[...] = up
        out_keep[...] = out

    @pl.when(i >= half)
    def _():
        up_send[0] = up
        out_send[0] = out


def ff_call(latents, near, far, cot_units, w_output, w_exp, w_red, gain, shift):
    chunks, rows, width = latents.shape
    inner = w_output.shape[0]
    units = w_exp.shape[1]
    half = chunks // 2

    def chunk(cols):
        return pl.BlockSpec((1, rows, cols), lambda i: (i, 0, 0))

    def first(cols):
        return pl.BlockSpec((1, rows, cols), lambda i: (jnp.minimum(i, half - 1), 0, 0))

    def second(cols):
        return pl.BlockSpec((1, rows, cols), lambda i: (jnp.maximum(i - half, 0), 0, 0))

    def fixed(*shape):
        return pl.BlockSpec(shape, lambda i: (0,) * len(shape))

    def out(count, cols):
        return jax.ShapeDtypeStruct((count, rows, cols), BF)

    return hbm_call(
        ff_kernel,
        (0, 3, 4, 5, 6),
        (0, 1, 2, 3, 4, 7, 8, 9),
        (1, 2),
        grid=(chunks,),
        in_specs=[
            chunk(width),
            first(inner),
            second(inner),
            chunk(units),
            fixed(inner, width),
            fixed(width, units),
            fixed(units, width),
            fixed(1, width),
            fixed(1, width),
        ],
        out_specs=[
            fixed(rows, width),
            chunk(width),
            chunk(units),
            chunk(units),
            fixed(rows, width),
            fixed(rows, width),
            second(width),
            fixed(rows, width),
            fixed(rows, width),
            second(width),
        ],
        out_shape=[
            jax.ShapeDtypeStruct((rows, width), F32),
            out(chunks, width),
            out(chunks, units),
            out(chunks, units),
            jax.ShapeDtypeStruct((rows, width), BF),
            jax.ShapeDtypeStruct((rows, width), BF),
            out(half, width),
            jax.ShapeDtypeStruct((rows, width), BF),
            jax.ShapeDtypeStruct((rows, width), BF),
            out(half, width),
        ],
        compiler_params=params(40),
        cost_estimate=cost(18),
        name="feed_forward",
    )(latents, near, far, cot_units, w_output, w_exp, w_red, gain, shift)


def ff_weights_kernel(ln_ref, gpre_ref, act_ref, cot_ref, *rest):
    out_ref = rest[-1]
    count, rows, width = out_ref.shape
    half = rows // 2
    for part, (left, right) in enumerate(((ln_ref, gpre_ref), (act_ref, cot_ref))):
        product = dot(left[...], right[...], TN).astype(BF)
        out_ref[:, part * half : (part + 1) * half, :] = product.reshape(count, half, width)


def ff_weights_call(ln_ff, grad_pre, hidden_act, cot, imgs, deps):
    tokens, width = ln_ff.shape
    units = grad_pre.shape[1]
    half = units // imgs
    steps = 2
    left = pl.BlockSpec((tokens, width // steps), lambda i: (0, i))
    right = pl.BlockSpec((tokens, width), lambda i: (0, 0))
    return hbm_call(
        ff_weights_kernel,
        range(4),
        (),
        grid=(steps,),
        in_specs=[left, right, left, right] + [ANY] * len(deps),
        out_specs=pl.BlockSpec((imgs // steps, 2 * half, width), lambda i: (i, 0, 0)),
        out_shape=pltpu.HBM((imgs, 2 * half, width), BF),
        compiler_params=params(28),
        cost_estimate=cost(9),
        name="ff_weights",
    )(ln_ff, grad_pre, hidden_act, cot, *deps)


def mixed_back_kernel(own_ref, near_ref, far_ref, mixed_ref, cot_ref, wo_ref, gain_ref, *rest):
    gm_ref, gb_ref, ga_ref, dg_ref, ds_ref = rest[-5:]
    up = own_ref[...].astype(F32) + near_ref[0].astype(F32) + far_ref[...].astype(F32)
    hat, inv = standardize(mixed_ref[...])
    back, gains = norm_back(hat, inv, gain_ref[...], up)
    grad = cot_ref[...].astype(F32) + back
    gm_ref[...] = grad
    branch = grad.astype(BF)
    gb_ref[...] = branch
    ga_ref[...] = dot(branch, wo_ref[...], NT).astype(BF)
    dg_ref[...] = jnp.sum(gains, axis=0, keepdims=True)
    ds_ref[...] = jnp.sum(up, axis=0, keepdims=True)


def mixed_back_call(own, near, far, mixed, cot, w_output, gain, deps):
    rows, width = mixed.shape
    inner = w_output.shape[0]
    return hbm_call(
        mixed_back_kernel,
        (0, 3, 4, 5),
        (0,),
        (1, 2),
        in_specs=[pl.BlockSpec(memory_space=pltpu.VMEM)] * 7 + [ANY] * len(deps),
        out_shape=[
            jax.ShapeDtypeStruct((rows, width), F32),
            jax.ShapeDtypeStruct((rows, width), BF),
            jax.ShapeDtypeStruct((rows, inner), BF),
            jax.ShapeDtypeStruct((1, width), F32),
            jax.ShapeDtypeStruct((1, width), F32),
        ],
        compiler_params=params(20),
        cost_estimate=cost(4),
        name="mixed_back",
    )(own, near, far, mixed, cot, w_output, gain, *deps)


def part_kernel(index_ref, e_ref, r_ref, eo_ref, ro_ref):
    eo_ref[...] = e_ref[...]
    ro_ref[...] = r_ref[...]


def part_call(index, w_expand, w_reduce, imgs, parts):
    width, ff = w_expand.shape
    unit = ff // (imgs * parts)
    return hbm_call(
        part_kernel,
        range(2),
        range(2),
        grid_spec=pltpu.PrefetchScalarGridSpec(
            num_scalar_prefetch=1,
            grid=(imgs,),
            in_specs=[
                pl.BlockSpec((width, unit), lambda i, p: (0, i * parts + p[0])),
                pl.BlockSpec((unit, width), lambda i, p: (i * parts + p[0], 0)),
            ],
            out_specs=[
                pl.BlockSpec((width, unit), lambda i, p: (0, i)),
                pl.BlockSpec((unit, width), lambda i, p: (i, 0)),
            ],
        ),
        out_shape=[
            jax.ShapeDtypeStruct((width, imgs * unit), BF),
            jax.ShapeDtypeStruct((imgs * unit, width), BF),
        ],
        compiler_params=params(6),
        name="weight_part",
    )(index, w_expand, w_reduce)


def attend_back_kernel(
    group,
    deps,
    doc_ref,
    index_ref,
    q_ref,
    go_own,
    go_far,
    go_near,
    go_both,
    att_near,
    att_far,
    lse_near,
    lse_far,
    k_ref,
    v_ref,
    kl_ref,
    vl_ref,
    hat_ref,
    norm_ref,
    vec_in,
    lat_hat_hbm,
    wkv_hbm,
    wq_hbm,
    extra_hbm,
    *rest,
):
    gkv_ref, gkvl_ref, gq_ref, keep_ref, send_ref, vec_ref = rest[deps : deps + 6]
    bdq, bdo, acc, stat, h_med, h_lat, sums, wide_rows = rest[deps + 6 : -6]
    lat_hat_ref, wk_ref, wv_ref, wq_ref, extra_ref, sems = rest[-6:]
    chunks, _, span = q_ref.shape
    docs, lat_rows = kl_ref.shape[1:3]
    lats = chunks * lat_rows
    slots, keys = k_ref.shape[1:3]
    micro = pl.program_id(0)
    mask = block_mask(span // GROUP, lats)
    every = slice(None)
    scale = (span // GROUP) ** (-0.5)
    go_refs = (go_own, go_far, go_near, go_both)
    att_refs, lse_refs = (att_near, att_far), (lse_near, lse_far)

    groups = HEADS // GROUP

    def columns(ref, at):
        return ref.at[:, at * span : (at + 1) * span]

    copies = [
        pltpu.make_async_copy(source, target, sems.at[i])
        for i, (source, target) in enumerate(
            (
                (lat_hat_hbm, lat_hat_ref),
                (columns(wkv_hbm, group), wk_ref),
                (columns(wkv_hbm, groups + group), wv_ref),
                (columns(wq_hbm, group), wq_ref),
                (extra_hbm, extra_ref),
            )
        )
    ]

    @pl.when(micro == 0)
    def _():
        for copy in copies:
            copy.start()

    spans = doc_spans(doc_ref, micro, docs, slots)
    tall = CHUNK * keys

    def pair(key, value, bias, d):
        score = dot(key, bdq[d], NT) + bias
        prob = jnp.exp(score - stat[d, 0:1])
        dprob = dot(value, bdo[d], NT)
        dscore = (prob * (dprob - stat[d, 1:2])).astype(BF)
        grad_key = dot(dscore, bdq[d], NN).astype(BF)
        grad_value = dot(prob.astype(BF), bdo[d], NN).astype(BF)
        grad_query = dot(dscore, key, TN)
        return grad_key, grad_value, grad_query

    def load(ref, at):
        return ref[0, pl.ds(at, CHUNK)].reshape(tall, span)

    def store(at, own, grad_key, grad_value):
        part = pl.ds(pl.multiple_of(at * keys, keys), tall)
        gkv_ref[part, :span] = jnp.where(own, grad_key, gkv_ref[part, :span])
        gkv_ref[part, span:] = jnp.where(own, grad_value, gkv_ref[part, span:])

    sel = pick((HEADS, LANES), lambda r, c: holds(c, r, 0))
    size = span // GROUP
    head_sel = pick((HEADS, span), lambda r, c: c // size == r)

    def row(by_head, at):
        return jnp.concatenate([by_head[at + h : at + h + 1] for h in range(GROUP)], axis=1)

    for d in range(docs):
        out_grad = doc_rows(go_refs, d, lat_rows, every)
        bdq[d] = spread_heads(doc_rows((q_ref,), d, lat_rows, every), mask)
        bdo[d] = spread_heads(out_grad, mask)
        lse = dot(sel, doc_rows(lse_refs, d, lat_rows, every), NT)
        stat[d, 0:1] = row(lse, group * GROUP)
        attended = doc_rows(att_refs, d, lat_rows, every)
        high, low, _ = terms(out_grad.astype(F32) * attended.astype(F32))
        stat[d, 1:2] = row(dot(head_sel, high, NT) + dot(head_sel, low, NT), 0)
    for d in range(docs):
        rows_d = pl.ds((micro * docs + d) * lat_rows, lat_rows)
        at, low, high = slot_chunk(spans[d], 0, slots)
        own = own_rows_of(at, low, high, keys)
        bias = jnp.concatenate([jnp.where(own, 0.0, FAR), jnp.zeros((lat_rows, 1), F32)], axis=0)
        key = jnp.concatenate([load(k_ref, at), kl_ref[0, d]], axis=0)
        value = jnp.concatenate([load(v_ref, at), vl_ref[0, d]], axis=0)
        grad_key, grad_value, grad_query = pair(key, value, bias, d)
        store(at, own, grad_key[:tall], grad_value[:tall])
        gkvl_ref[rows_d, :span] = grad_key[tall:]
        gkvl_ref[rows_d, span:] = grad_value[tall:]
        acc[d] = grad_query

    def more(parts):
        done = []
        for d, step, at, low, high in parts:
            own = own_rows_of(at, low, high, keys)
            bias = jnp.where(own, 0.0, FAR)
            done.append((d, at, own, *pair(load(k_ref, at), load(v_ref, at), bias, d)))
        for d, at, own, grad_key, grad_value, grad_query in done:
            store(at, own, grad_key, grad_value)
            acc[d] = acc[d] + grad_query

    more_chunks(spans, slots, more)
    for d in range(docs):
        full = gather_heads(acc[d], mask, lats).astype(BF)
        for c in range(chunks):
            gq_ref[c, pl.ds(micro * docs * lat_rows + d * lat_rows, lat_rows)] = full[
                c * lat_rows : (c + 1) * lat_rows
            ]
    part = dot(hat_ref[...], gkv_ref[...], TN)
    part_sum = jnp.sum(gkv_ref[...].astype(F32), axis=0, keepdims=True)

    @pl.when(micro == 0)
    def _():
        h_med[...] = part
        sums[0:1, :] = part_sum

    @pl.when(micro > 0)
    def _():
        h_med[...] = h_med[...] + part
        sums[0:1, :] = sums[0:1, :] + part_sum

    @pl.when(micro == pl.num_programs(0) - 1)
    def _():
        width = h_med.shape[0]
        step = 128
        tokens = lat_hat_ref.shape[0] * lat_hat_ref.shape[1]
        for copy in copies:
            copy.wait()
        h_lat[...] = dot(lat_hat_ref[0], gkvl_ref[...], TN)
        sums[1:2, :] = jnp.sum(gkvl_ref[...].astype(F32), axis=0, keepdims=True)
        quer_all = gq_ref[...].reshape(tokens, span)
        h_q = dot(lat_hat_ref[...].reshape(tokens, width), quer_all, TN)
        quer_sum = jnp.sum(quer_all.astype(F32), axis=0, keepdims=True) * scale
        for at in range(0, width, step):
            part = slice(at, at + step)
            norm = norm_ref[:, part].T
            med, lat, quer = h_med[part, :], h_lat[part, :], h_q[part] * scale
            med_sum, lat_sum = sums[0:1, :], sums[1:2, :]
            wide_rows[part, : 2 * span] = (
                norm[:, 0:1] * med
                + norm[:, 1:2] * med_sum
                + norm[:, 2:3] * lat
                + norm[:, 3:4] * lat_sum
            ).astype(BF)
            wide_rows[part, 2 * span :] = (
                norm[:, 2:3] * quer + norm[:, 3:4] * quer_sum
            ).astype(BF)
            wkv = jnp.concatenate([wk_ref[part, :], wv_ref[part, :]], axis=1).astype(F32)
            wq = wq_ref[part, :].astype(F32)

            def total(value):
                return jnp.sum(value, axis=1, keepdims=True)

            vec = jnp.concatenate(
                [
                    total(wkv * med),
                    total(wkv * med_sum),
                    total(wkv * lat) + total(wq * quer),
                    total(wkv * lat_sum) + total(wq * quer_sum),
                    jnp.zeros((step, step - 4), F32),
                ],
                axis=1,
            )
            rows = vec.T[: vec_ref.shape[0]]
            vec_ref[:, part] = rows if group == 0 else vec_in[:, part] + rows
        if len(keep_ref.shape) == 2:
            keep_ref[...] = wide_rows[...]
            return
        imgs, two, height, _ = keep_ref.shape
        share = width // imgs
        tall = share // (2 * two)
        bit = lax.rem(index_ref[0], 2)
        for ref, mine in ((keep_ref, bit), (send_ref, 1 - bit)):
            for i in range(imgs):
                for y in range(two):
                    at = pl.multiple_of(i * share + 2 * y * tall + mine * tall, tall)
                    rows = wide_rows[pl.ds(at, tall), :]
                    ref[i, y, :tall] = rows[:, : 2 * span]
                    ref[i, y, tall : tall + tall // 2, :span] = rows[: tall // 2, 2 * span :]
                    ref[i, y, tall : tall + tall // 2, span:] = rows[tall // 2 :, 2 * span :]
                    start = tall + tall // 2
                    if group == 0:
                        size = extra_ref.shape[0] // (2 * two * imgs)
                        at = pl.multiple_of((i * two + y) * 2 * size + mine * size, size)
                        rows = extra_ref[pl.ds(at, size), :]
                        ref[i, y, start : start + size] = rows[:, : 2 * span]
                        ref[i, y, start + size : start + 2 * size] = rows[:, 2 * span :]
                    else:
                        rows = jnp.zeros((height - start, 2 * span), F32)
                        if y == 0:
                            at = slice(i * share, (i + 1) * share)
                            six = jnp.concatenate([vec_ref[:4, at], extra_ref[:2, at]], axis=0)
                            six = jnp.where(mine == 0, six, 0.0)
                            six = jnp.pad(six, ((0, height - start - 6), (0, 2 * span - share)))
                            rows = six
                        ref[i, y, start:] = rows.astype(BF)


def laid_out(width, imgs, inner):
    share = width // imgs
    return share % 128 == 0 and share <= inner and inner % (64 * imgs) == 0


def attend_back_call(
    group,
    doc_ids,
    queries,
    grad_att,
    att,
    kv_med,
    kv_lat,
    hat_med,
    hat_lat,
    w_keyval,
    w_query,
    norms,
    extra,
    vectors,
    index,
    imgs,
    deps,
):
    chunks, _, inner = queries.shape
    micro, slots, keys, both = kv_med.shape
    docs, lat_rows = kv_lat.shape[1:3]
    lats = chunks * lat_rows
    width = hat_med.shape[1]
    groups = HEADS // GROUP
    span = inner // groups
    wide = GROUP * lats
    rows = slots * keys
    lat_block = docs * lat_rows

    if laid_out(width, imgs, inner):
        tall = width // (imgs * chunks)
        height = tall + tall // 2 + (2 * inner // (imgs * chunks) if group == 0 else 16)
        result = jax.ShapeDtypeStruct((imgs, chunks // 2, height, inner), BF)
    else:
        result = jax.ShapeDtypeStruct((width, 3 * span), BF)
    result_spec = pl.BlockSpec(result.shape, lambda i, ids, p: (0,) * len(result.shape))

    def cols(at, *tail):
        return pl.BlockSpec(
            (1,) + tail, lambda i, ids, p: (i,) + (0,) * (len(tail) - 1) + (at,)
        )

    def tokens(at, size, count=chunks):
        return pl.BlockSpec((count, lat_block, size), lambda i, ids, p: (0, i, at))

    def fixed(at, size):
        return pl.BlockSpec((width, size), lambda i, ids, p: (0, at))

    return hbm_call(
        functools.partial(attend_back_kernel, group, len(deps)),
        range(20),
        (0, 1),
        grid_spec=pltpu.PrefetchScalarGridSpec(
            num_scalar_prefetch=2,
            grid=(micro,),
            in_specs=[
                tokens(group, span),
                *[tokens(group, span, 1)] * 4,
                *[tokens(group, span, 2)] * 2,
                *[tokens(inner // LANES, LANES, 2)] * 2,
                cols(group, slots, keys, span),
                cols(groups + group, slots, keys, span),
                cols(group, docs, lat_rows, span),
                cols(groups + group, docs, lat_rows, span),
                pl.BlockSpec((rows, width), lambda i, ids, p: (i, 0)),
                pl.BlockSpec(norms.shape, lambda i, ids, p: (0, 0)),
                pl.BlockSpec(vectors.shape, lambda i, ids, p: (0, 0)),
                ANY,
                ANY,
                ANY,
                ANY,
            ]
            + [ANY] * len(deps),
            out_specs=[
                pl.BlockSpec((rows, 2 * span), lambda i, ids, p: (i, 0)),
                pl.BlockSpec((micro * lat_block, 2 * span), lambda i, ids, p: (0, 0)),
                pl.BlockSpec((chunks, micro * lat_block, span), lambda i, ids, p: (0, 0, 0)),
                result_spec,
                result_spec,
                pl.BlockSpec(vectors.shape, lambda i, ids, p: (0, 0)),
            ],
            scratch_shapes=[
                pltpu.VMEM((docs, wide, span), BF),
                pltpu.VMEM((docs, wide, span), BF),
                pltpu.VMEM((docs, wide, span), F32),
                pltpu.VMEM((docs, 2, wide), F32),
                pltpu.VMEM((width, 2 * span), F32),
                pltpu.VMEM((width, 2 * span), F32),
                pltpu.VMEM((2, 2 * span), F32),
                pltpu.VMEM((width, 3 * span), BF),
                pltpu.VMEM(hat_lat.shape, BF),
                pltpu.VMEM((width, span), BF),
                pltpu.VMEM((width, span), BF),
                pltpu.VMEM((width, span), BF),
                pltpu.VMEM(extra.shape, extra.dtype),
                pltpu.SemaphoreType.DMA((5,)),
            ],
        ),
        out_shape=[
            jax.ShapeDtypeStruct((micro * rows, 2 * span), BF),
            jax.ShapeDtypeStruct((micro * lat_block, 2 * span), BF),
            jax.ShapeDtypeStruct((chunks, micro * lat_block, span), BF),
            result,
            result,
            jax.ShapeDtypeStruct(vectors.shape, F32),
        ],
        compiler_params=params(48),
        cost_estimate=cost(3),
        name="attend_back",
    )(
        doc_ids,
        index,
        queries,
        *grad_att,
        *att,
        *att,
        kv_med,
        kv_med,
        kv_lat,
        kv_lat,
        hat_med,
        norms,
        vectors,
        hat_lat,
        w_keyval,
        w_query,
        extra,
        *deps,
    )


def media_back_kernel(media_ref, ga_ref, gb_ref, wka_ref, wva_ref, wkb_ref, wvb_ref, gain_ref, *rest):
    out_ref, token_ref = rest[-2:]
    token_ref[...] = jnp.zeros_like(token_ref)
    wa = jnp.concatenate([wka_ref[...], wva_ref[...]], axis=1)
    wb = jnp.concatenate([wkb_ref[...], wvb_ref[...]], axis=1)
    rows = media_ref.shape[0]
    step = min(rows, 256)

    for at in range(0, rows, step):
        part = pl.ds(at, step)
        up = dot(ga_ref[part, :], wa, NT) + dot(gb_ref[part, :], wb, NT)
        hat, inv = standardize(media_ref[part, :].astype(F32))
        back, _ = norm_back(hat, inv, gain_ref[...], up)
        out_ref[part, :] = back.astype(BF)


def key_value_blocks(width, span):
    groups = HEADS // GROUP
    return [
        pl.BlockSpec((width, span), lambda i, at=at: (0, at))
        for g in range(groups)
        for at in (g, groups + g)
    ]


def media_back_call(media, grad_a, grad_b, w_keyval, gain, first, steps, whole, deps):
    rows, width = media.shape
    half = grad_a.shape[1]
    block = 512
    fixed = lambda i: (0, 0)
    moving = lambda i: (first + i, 0)
    extra = tuple(deps) if whole is None else tuple(deps) + (whole,)
    return hbm_call(
        media_back_kernel,
        range(8),
        (0,),
        grid=(steps,),
        in_specs=[
            pl.BlockSpec((block, width), moving),
            pl.BlockSpec((block, half), moving),
            pl.BlockSpec((block, half), moving),
            *key_value_blocks(width, half // 2),
            pl.BlockSpec((1, width), fixed),
        ]
        + [ANY] * len(extra),
        out_specs=[pl.BlockSpec((block, width), moving), pl.BlockSpec(TOKEN.shape, fixed)],
        out_shape=[jax.ShapeDtypeStruct((rows, width), BF), TOKEN],
        input_output_aliases={} if whole is None else {7 + len(extra): 0},
        compiler_params=params(28),
        cost_estimate=cost(2.5 * steps),
        name="media_back",
    )(media, grad_a, grad_b, w_keyval, w_keyval, w_keyval, w_keyval, gain, *extra)


def swap(value, axis, bit):
    size = lax.axis_size(axis)
    return lax.ppermute(value, axis, [(i, i ^ bit) for i in range(size)])


def gather_chunks(own):
    far = swap(own, "patch", 2)
    return own, far, swap(own, "patch", 1), swap(far, "patch", 1)


def gather_patch(own):
    return jnp.stack(gather_chunks(own))


def add(first, second):
    return (first.astype(F32) + second.astype(F32)).astype(BF)


def sum_kernel(ways, terms_in, *refs):
    refs[-1][...] = jnp.zeros_like(refs[-1])
    for k in range(ways):
        value = refs[1 + k][...]
        if terms_in == 2:
            value = (value.astype(F32) + refs[1 + ways + k][...].astype(F32)).astype(BF)
        refs[k - ways - 1][...] = value


def split_sum(first, second, lead, rest, ways, mine, deps):
    count = 1
    for size in lead:
        count *= size
    tail = first.shape[-2:]
    inner = 1
    for size in rest:
        inner *= size
    flat = (count, ways, inner) + tail
    steps = 2 if count % 2 == 0 and first.size * 2 > (1 << 20) else 1
    block = (count // steps, 1, inner) + tail
    outs = [pl.BlockSpec(block, lambda i, m: (i, 0, 0, 0, 0))] * ways
    parts = [
        pl.BlockSpec(block, lambda i, m, k=k: (i, jnp.bitwise_xor(m[0], k), 0, 0, 0))
        for k in range(ways)
    ]
    values = [v.reshape(flat) for v in (first, second) if v is not None]
    *halves, token = pl.pallas_call(
        functools.partial(sum_kernel, ways, len(values)),
        grid_spec=pltpu.PrefetchScalarGridSpec(
            num_scalar_prefetch=1,
            grid=(steps,),
            in_specs=parts * len(values) + [ANY] * len(deps),
            out_specs=outs + [pl.BlockSpec(TOKEN.shape, lambda i, m: (0, 0))],
        ),
        out_shape=[jax.ShapeDtypeStruct((count, 1, inner) + tail, BF)] * ways + [TOKEN],
        compiler_params=params(12),
        cost_estimate=cost(0.3),
        name="split_sum",
    )(mine[None], *[v for v in values for _ in range(ways)], *deps)
    return [h.reshape(lead + rest + tail) for h in halves], token


class Scatter:
    def __init__(self, value, transit, axes, order, scope):
        self.places = [
            (axis, bit)
            for axis in axes
            for bit in reversed(range(lax.axis_size(axis).bit_length() - 1))
            if axis == "img" or any(axis == a and bit in bits for a, bits in order)
        ]
        self.order = list(order)
        self.scope = scope
        self.value, transit = (
            v.reshape((2,) * len(self.places) + v.shape[len(axes) :]) for v in (value, transit)
        )
        self.transit = [transit]

    def step(self, deps=()):
        with jax.named_scope(self.scope):
            if not self.order:
                return ()
            axis, bits = self.order.pop(0)
            place = self.places.index((axis, bits[-1]))
            lead = (2,) * place
            for bit in bits:
                self.places.remove((axis, bit))
            ways = 2 ** len(bits)
            mine = lax.rem(lax.shift_right_logical(lax.axis_index(axis), bits[0]), ways)
            rest = (2,) * (len(self.places) - place)
            (self.value, *send), token = split_sum(
                self.value, self.transit[0], lead, rest, ways, mine, deps
            )
            self.transit = [
                swap(part, axis, (k + 1) << bits[0]) for k, part in enumerate(send)
            ]
            return (token,)


def first_bits():
    return [("img", (bit,)) for bit in range(lax.axis_size("img").bit_length() - 3)]


def last_kernel(index_ref, *refs):
    refs[-1][...] = jnp.zeros_like(refs[-1])
    cut = refs[0].shape[1]
    outs = refs[-1 - refs[0].shape[0] : -1]
    for k, out in enumerate(outs):
        at = jnp.bitwise_xor(index_ref[0], k)
        for part, value, other in ((slice(0, cut), *refs[:2]), (slice(cut, None), *refs[2:4])):
            out[part] = (value[at].astype(F32) + other[at].astype(F32)).astype(BF)


def last_step(first, second, deps):
    count = lax.axis_size("img").bit_length() - 1
    low = max(count - 2, 0)
    ways = 2 ** (count - low)
    values = [
        v.reshape((ways,) + v.shape[-2:])
        for v in (first.value, first.transit[0], second.value, second.transit[0])
    ]
    rows = values[0].shape[1] + values[2].shape[1]
    shape = jax.ShapeDtypeStruct((rows, values[0].shape[2]), BF)
    mine = lax.shift_right_logical(lax.axis_index("img"), low)
    whole = lambda v: pl.BlockSpec(v.shape, lambda i, m: (0,) * len(v.shape))
    own, *send, token = pl.pallas_call(
        last_kernel,
        grid_spec=pltpu.PrefetchScalarGridSpec(
            num_scalar_prefetch=1,
            grid=(1,),
            in_specs=[whole(v) for v in values] + [ANY] * len(deps),
            out_specs=[whole(shape)] * ways + [whole(TOKEN)],
        ),
        out_shape=[shape] * ways + [TOKEN],
        compiler_params=params(6),
        cost_estimate=cost(0.3),
        name="last_sum",
    )(mine[None], *values, *deps)
    sent = [swap(part, "img", (k + 1) << low) for k, part in enumerate(send)]
    return own, sent, token


def reduce_rest(keep, send, scope):
    with jax.named_scope(scope):
        transit = swap(send, "patch", 1)
    return Scatter(keep, transit, ("img", "patch"), [("patch", (1,))] + first_bits(), scope)


def in_order(chunks):
    me = lax.axis_index("patch")
    out = []
    for j in range(4):
        apart = jnp.bitwise_xor(me, j)
        at = 2 * jnp.bitwise_and(apart, 1) + lax.shift_right_logical(apart, 1)
        out.append(lax.dynamic_index_in_dim(chunks, at, 0, keepdims=False))
    return jnp.stack(out)


def place_kernel(index_ref, chunks_ref, *rest):
    out_ref, token_ref = rest[-2:]
    token_ref[...] = jnp.zeros_like(token_ref)
    parts, _, unit = chunks_ref.shape
    for j in range(parts):
        apart = jnp.bitwise_xor(index_ref[0], j)
        at = jnp.where(apart == 1, 2, jnp.where(apart == 2, 1, apart))
        out_ref[:, j * unit : (j + 1) * unit] = chunks_ref[at].astype(F32)


def place_call(index, chunks, rows, imgs, deps):
    parts, _, units = chunks.shape
    unit = units // imgs
    return pl.pallas_call(
        place_kernel,
        grid_spec=pltpu.PrefetchScalarGridSpec(
            num_scalar_prefetch=1,
            grid=(imgs,),
            in_specs=[pl.BlockSpec((parts, rows, unit), lambda i, p: (0, 0, i))]
            + [ANY] * len(deps),
            out_specs=[
                pl.BlockSpec((rows, parts * unit), lambda i, p: (0, i)),
                pl.BlockSpec(TOKEN.shape, lambda i, p: (0, 0)),
            ],
        ),
        out_shape=[jax.ShapeDtypeStruct((rows, parts * units), F32), TOKEN],
        compiler_params=params(6),
        cost_estimate=cost(0.1),
        name="place_units",
    )(index, chunks, *deps)


def local(
    latents,
    media,
    doc_ids,
    w_query,
    w_keyval,
    w_output,
    w_expand,
    w_reduce,
    media_gain,
    media_shift,
    latent_gain,
    latent_shift,
    ff_gain,
    ff_shift,
    out_grad,
):
    micro, docs, lat_rows, width = latents.shape
    slots, keys = media.shape[1:3]
    inner = w_query.shape[1]
    ff = w_expand.shape[1]
    head_size = inner // HEADS
    scale = head_size ** (-0.5)
    parts = lax.axis_size("patch")
    imgs = lax.axis_size("img")
    patch_index = lax.axis_index("patch")
    own_rows = micro * docs * lat_rows
    all_rows = own_rows * parts
    groups = HEADS // GROUP
    span = inner // groups
    unit = ff // (imgs * parts)

    latents_own = latents.reshape(own_rows, width)
    cot_own = out_grad.reshape(own_rows, width)
    media_flat = media.reshape(-1, width)
    with jax.named_scope("gather_latents"):
        latents_far = swap(latents_own, "patch", 2)
        latents_near = swap(latents_own, "patch", 1)

    hat_med, kv_med, token = kv_call(media_flat, media_gain[None], media_shift[None], w_keyval)
    kv_med = kv_med.reshape(micro, slots, keys, 2 * inner)
    if unit % 128 == 0:
        w_exp, w_red = part_call(
            patch_index[None], w_expand, w_reduce, imgs, parts
        )
    else:
        w_exp = lax.dynamic_index_in_dim(
            w_expand.reshape(width, imgs, parts, unit), patch_index, 2, keepdims=False
        ).reshape(width, imgs * unit)
        w_red = lax.dynamic_index_in_dim(
            w_reduce.reshape(imgs, parts, unit, width), patch_index, 1, keepdims=False
        ).reshape(imgs * unit, width)

    (latents_far,) = gate((latents_far,), (token,), pltpu.VMEM)
    with jax.named_scope("gather_latents"):
        latents_both = swap(latents_far, "patch", 1)
    latents_all, hat_all, queries, kv_lat, cot_sent = latent_call(
        (latents_own, latents_far, latents_near, latents_both),
        latent_gain[None],
        latent_shift[None],
        w_query,
        w_keyval,
        cot_own,
        (token,),
    )
    kv_lat = kv_lat.reshape(micro, docs, lat_rows, 2 * inner)
    with jax.named_scope("gather_cotangent"):
        cot_far = swap(cot_sent, "patch", 2)
    keep, send = attend_call(doc_ids, queries, kv_med, kv_lat, ())
    send, cot_far = gate((send, cot_far), (), pltpu.VMEM)
    with jax.named_scope("join_near"):
        near = join_call(keep, swap(send, "patch", 1), False, False)
    with jax.named_scope("gather_cotangent"):
        cot_chunks = (cot_sent, cot_far, swap(cot_sent, "patch", 1), swap(cot_far, "patch", 1))
    cot_units, cot_all, token = cot_units_call(cot_chunks, w_red)
    with jax.named_scope("join_far"):
        att_near = join_call(
            near, swap(near, "patch", 2), True, True, (token,)
        )
        att_far = swap(att_near, "patch", 1)

    mixed, ln_ff, hidden_act, grad_pre, *ff_parts = ff_call(
        latents_all,
        att_near,
        att_far,
        cot_units,
        w_output,
        w_exp,
        w_red,
        ff_gain[None],
        ff_shift[None],
    )
    up_own, up_keep, up_send, out_own, out_keep, out_send = ff_parts
    with jax.named_scope("sum_up"):
        up_sent = swap(up_send, "patch", 1)
        up_near = add(up_keep, up_sent[1])
        up_far = swap(up_near, "patch", 2)

    def flat(value):
        return value.reshape(all_rows, -1)

    ff_grads = ff_weights_call(
        flat(ln_ff), flat(grad_pre), flat(hidden_act), flat(cot_all), imgs, (up_near,)
    )
    (up_far,) = gate((up_far,), (ff_grads,), pltpu.VMEM)
    (ff_grads,) = gate((ff_grads,), (up_far,), pltpu.HBM)
    grad_mixed, grad_branch, grad_att_own, ff_gain_part, ff_shift_part = mixed_back_call(
        up_own, up_sent, up_far, mixed, cot_sent, w_output, ff_gain[None], ()
    )
    with jax.named_scope("gather_att"):
        grad_att = [chunk[None] for chunk in gather_chunks(grad_att_own)]
    att = (att_near, att_far)
    grad_output = dot(att_near[0, :, :inner], grad_branch, TN).astype(BF)

    with jax.named_scope("sum_ff"):
        ff_own = lax.psum_scatter(ff_grads, "img", scatter_dimension=0, tiled=True)[0]

    zero = jnp.zeros_like(media_gain)
    norms = jnp.stack(
        [media_gain, media_shift, latent_gain, latent_shift, zero, zero, zero, zero]
    )
    ff_vectors = jnp.pad(jnp.concatenate([ff_gain_part, ff_shift_part]), ((0, 6), (0, 0)))
    share = width // imgs
    tall = share // parts
    direct = laid_out(width, imgs, inner)

    def back_call(group, extra, vectors, deps):
        gkv, gkv_lat, gq, keep, send, vectors = attend_back_call(
            group,
            doc_ids,
            queries,
            grad_att,
            att,
            kv_med,
            kv_lat,
            hat_med,
            hat_all,
            w_keyval,
            w_query,
            norms,
            extra,
            vectors,
            patch_index[None],
            imgs,
            deps,
        )
        if not direct:

            def split(value):
                size = value.shape[0] // (imgs * parts)
                return value.reshape(imgs, parts // 2, 2, size, value.shape[1])

            rows = split(keep)
            fold = [rows[..., : tall // 2, 2 * span :], rows[..., tall // 2 :, 2 * span :]]
            blocks = [rows[..., : 2 * span], jnp.concatenate(fold, axis=-1)]
            if group == 0:
                blocks += [split(extra)[..., :inner], split(extra)[..., inner:]]
            else:
                six = jnp.concatenate([vectors[:4], extra[:2]]).astype(BF)
                six = jnp.swapaxes(six.reshape(6, imgs, share), 0, 1)
                six = jnp.pad(six, ((0, 0), (0, 10), (0, width - share)))[:, None, None, :, :inner]
                blocks.append(
                    jnp.pad(six, ((0, 0), (0, parts // 2 - 1), (0, 1), (0, 0), (0, 0)))
                )
            blocks = jnp.concatenate(blocks, axis=3)
            bit = lax.rem(patch_index, 2)
            keep = lax.dynamic_index_in_dim(blocks, bit, 2, keepdims=False)
            send = lax.dynamic_index_in_dim(blocks, 1 - bit, 2, keepdims=False)
        return gkv, gkv_lat, gq, keep, send, vectors

    out_keep, out_send = gate((out_keep, out_send), grad_att[3:], pltpu.HBM)
    with jax.named_scope("sum_out"):
        out_sent = swap(out_send, "patch", 1)
        out_far = swap(add(out_keep, out_sent[1]), "patch", 2)
    gkv_0, gkv_lat_0, gq_0, keep, send, vectors = back_call(
        0, grad_output, norms, (ff_vectors,)
    )
    first = reduce_rest(keep, send, "sum_weights_0")
    gkv_1, gkv_lat_1, gq_1, keep, send, vectors = back_call(
        1, ff_vectors, vectors, first.step()
    )
    done = first.step((vectors,))
    latents_out, token = out_call(mixed, out_own, out_sent, out_far, (vectors,))
    keep, send, gq_0, gq_1 = gate((keep, send, gq_0, gq_1), (*done, token), pltpu.VMEM)
    second = reduce_rest(keep, send, "sum_weights_1")
    with jax.named_scope("sum_query"):
        gq_keep = jnp.concatenate([gq_0[:2], gq_1[:2]], axis=-1)
        gq_sent = swap(jnp.concatenate([gq_0[2:], gq_1[2:]], axis=-1), "patch", 1)

    def media_piece(at, size, whole, deps):
        return media_back_call(
            media_flat,
            gkv_0,
            gkv_1,
            w_keyval,
            media_gain[None],
            at,
            size,
            whole,
            deps,
        )

    media_grad, *done = media_piece(0, 4, None, second.step())
    deps = second.step(done)
    (gq_keep,) = gate((gq_keep,), deps or done, pltpu.VMEM)
    with jax.named_scope("sum_query"):
        gq_near = add(gq_keep, gq_sent)
        gq_far = swap(gq_near[1], "patch", 2)
    (ff_own,) = gate((ff_own,), deps or done, pltpu.HBM)
    with jax.named_scope("gather_ff"):
        expand_far = swap(ff_own[:share], "patch", 2)
    media_grad, *done = media_piece(4, 2, media_grad, deps)
    while first.order or second.order:
        first.step(done)
        second.step(done)
    with jax.named_scope("sum_weights"):
        own, sent, token = last_step(first, second, done)
    media_grad, *done = media_piece(6, 2, media_grad, (token,))
    (gq_far,) = gate((gq_far,), done, pltpu.VMEM)
    latents_grad, token = latent_back_call(
        scale,
        (
            latents_own,
            grad_mixed,
            gq_near[0],
            gq_far,
            gkv_lat_0,
            gkv_lat_1,
            w_query,
            w_keyval,
            latent_gain[None],
        ),
        done,
    )
    own, expand_far, *sent = gate((own, expand_far, *sent), (token,), pltpu.VMEM)
    with jax.named_scope("gather_ff"):
        expand = jnp.stack(
            [
                ff_own[:share],
                expand_far,
                swap(ff_own[:share], "patch", 1),
                swap(expand_far, "patch", 1),
            ]
        )
        reduce_far = swap(ff_own[share:], "patch", 2)
    with jax.named_scope("place_ff"):
        if unit % 128 == 0:
            expand_rows, placed = place_call(patch_index[None], expand, share, imgs, (token,))
        else:
            placed = token
            expand_rows = in_order(expand).reshape(parts, -1, imgs, unit)
            expand_rows = jnp.transpose(expand_rows, (1, 2, 0, 3)).reshape(-1, ff).astype(F32)
    with jax.named_scope("gather_ff"):
        reduce = jnp.stack(
            [
                ff_own[share:],
                reduce_far,
                swap(ff_own[share:], "patch", 1),
                swap(reduce_far, "patch", 1),
            ]
        )
    reduce_rows = in_order(reduce).reshape(-1, width).astype(F32)

    def rows_of(value):
        return value.reshape(-1, value.shape[-1])

    with jax.named_scope("gather_weights"):
        own = own.astype(F32)
        for part in sent:
            own = own + part.astype(F32)
        own = own.astype(BF)
        far = swap(own, "patch", 2)
        near = swap(own, "patch", 1)
        (far,) = gate((far,), (placed,), pltpu.VMEM)
        whole = in_order(jnp.stack([own, far, near, swap(far, "patch", 1)]))
    cut = first.value.shape[-2]
    first, second = whole[:, :cut], whole[:, cut:]
    keyval_rows = [rows_of(first[:, :tall]), rows_of(second[:, :tall])]
    grad_keyval = jnp.concatenate(
        [rows[:, at * span : (at + 1) * span] for at in range(2) for rows in keyval_rows], axis=1
    ).astype(F32)
    end = tall + tall // 2

    def unfold(value):
        return rows_of(jnp.concatenate([value[..., :span], value[..., span:]], axis=1))

    query_rows = jnp.concatenate(
        [unfold(first[:, tall:end]), unfold(second[:, tall:end])], axis=1
    ).astype(F32)
    out_rows = first[:, end:]
    size = out_rows.shape[1] // 2
    out_rows = rows_of(
        jnp.concatenate([out_rows[:, :size], out_rows[:, size:]], axis=2)
    ).astype(F32)
    vectors = second[0, end : end + 6, :share].astype(F32)

    return (
        latents_out.reshape(latents.shape),
        latents_grad.reshape(latents.shape),
        media_grad.reshape(media.shape),
        query_rows,
        grad_keyval,
        out_rows,
        expand_rows,
        reduce_rows,
    ) + tuple(vectors[i] for i in range(6))


def solution(mesh):
    tokens = P(None, "img", "patch", None)
    return jax.shard_map(
        local,
        mesh=mesh,
        in_specs=(tokens, tokens, P(None, "img")) + (P(),) * 11 + (tokens,),
        out_specs=(tokens,) * 3 + (P("img", None),) * 5 + (P("img"),) * 6,
        check_vma=False,
    )
```

```python
import functools

import jax
import jax.numpy as jnp
from jax import lax
from jax.experimental import pallas as pl
from jax.experimental.pallas import tpu as pltpu
from jax.sharding import PartitionSpec as P

HEADS = 8
GROUP = 4
EPS = 1e-05
CHUNK = 6
FAR = -1e30
BF = jnp.bfloat16
F32 = jnp.float32
ANY = pl.BlockSpec(memory_space=pl.ANY)
TOKEN = jax.ShapeDtypeStruct((8, 128), jnp.float32)


def params(mib=56):
    return pltpu.CompilerParams(vmem_limit_bytes=mib << 20)


def cost(us):
    return pl.CostEstimate(flops=int(us * 1.1e9), bytes_accessed=0, transcendentals=0)


def hbm_call(kernel, held, kept, inside=(), **options):
    shapes = options.pop("out_shape")
    if isinstance(shapes, list):
        shapes = [pltpu.HBM(v.shape, v.dtype) if i in kept else v for i, v in enumerate(shapes)]
    options["out_shape"] = shapes
    scalars = options["grid_spec"].num_scalar_prefetch if "grid_spec" in options else 0
    inner = pl.pallas_call(kernel, **options)

    def run(*operands):
        def place(i, x):
            if i in inside:
                return pltpu.with_memory_space_constraint(x, pltpu.VMEM)
            if i in held or x.size >= 1 << 20:
                return pltpu.with_memory_space_constraint(x, pltpu.HBM)
            return x

        arrays = [place(i, x) for i, x in enumerate(operands[scalars:])]
        return inner(*operands[:scalars], *arrays)

    return run


def nothing_kernel(*refs):
    pass


def gate(carry, deps, space):
    return pl.pallas_call(
        nothing_kernel,
        in_specs=[ANY] * (len(carry) + len(deps)),
        out_specs=[ANY] * len(carry),
        out_shape=[space(c.shape, c.dtype) for c in carry],
        input_output_aliases={i: i for i in range(len(carry))},
        compiler_params=params(1),
        name="gate",
    )(
        *[pltpu.with_memory_space_constraint(c, space) for c in carry],
        *[
            pltpu.with_memory_space_constraint(d, pltpu.HBM) if d.size >= 1 << 19 else d
            for d in deps
        ],
    )


def dot(a, b, dims):
    return lax.dot_general(a, b, (dims, ((), ())), preferred_element_type=F32)


NN = ((1,), (0,))
NT = ((1,), (1,))
TN = ((0,), (0,))


def standardize(values):
    center = values - jnp.mean(values, axis=-1, keepdims=True)
    inv = lax.rsqrt(jnp.mean(center * center, axis=-1, keepdims=True) + EPS)
    return center * inv, inv


def norm_back(hat, inv, gain, upstream):
    scaled = upstream * gain
    back = inv * (
        scaled
        - jnp.mean(scaled, axis=-1, keepdims=True)
        - hat * jnp.mean(scaled * hat, axis=-1, keepdims=True)
    )
    return back, upstream * hat


def kv_kernel(media_ref, gain_ref, shift_ref, w_ref, hat_ref, kv_ref, token_ref):
    token_ref[...] = jnp.zeros_like(token_ref)
    rows = media_ref.shape[0]
    step = min(rows, 256)
    for at in range(0, rows, step):
        part = pl.ds(at, step)
        hat, _ = standardize(media_ref[part, :].astype(F32))
        ln = (hat * gain_ref[...] + shift_ref[...]).astype(BF)
        hat_ref[part, :] = hat.astype(BF)
        kv_ref[part, :] = dot(ln, w_ref[...], NN).astype(BF)


def kv_call(media, gain, shift, w_keyval):
    rows, width = media.shape
    outs = w_keyval.shape[1]
    block = 1024
    return hbm_call(
        kv_kernel,
        range(4),
        (0, 1),
        grid=(rows // block,),
        in_specs=[
            pl.BlockSpec((block, width), lambda i: (i, 0)),
            pl.BlockSpec((1, width), lambda i: (0, 0)),
            pl.BlockSpec((1, width), lambda i: (0, 0)),
            pl.BlockSpec((width, outs), lambda i: (0, 0)),
        ],
        out_specs=[
            pl.BlockSpec((block, width), lambda i: (i, 0)),
            pl.BlockSpec((block, outs), lambda i: (i, 0)),
            pl.BlockSpec(TOKEN.shape, lambda i: (0, 0)),
        ],
        out_shape=[
            jax.ShapeDtypeStruct((rows, width), BF),
            jax.ShapeDtypeStruct((rows, outs), BF),
            TOKEN,
        ],
        compiler_params=params(20),
        cost_estimate=cost(16),
        name="media_keyval",
    )(media, gain, shift, w_keyval)


def latent_kernel(own, far, near, both, gain_ref, shift_ref, wq_ref, wkv_ref, cot_ref, *rest):
    raw_ref, hat_ref, q_ref, kv_ref, cot_out = rest[-5:]
    scale = (wq_ref.shape[1] // HEADS) ** (-0.5)
    cot_out[...] = cot_ref[...]
    for c, ref in enumerate((own, far, near, both)):
        raw = ref[...]
        raw_ref[c] = raw
        hat, _ = standardize(raw.astype(F32))
        hat_ref[c] = hat.astype(BF)
        ln = (hat * gain_ref[...] + shift_ref[...]).astype(BF)
        q_ref[c] = (dot(ln, wq_ref[...], NN).astype(BF).astype(F32) * scale).astype(BF)
        if c == 0:
            kv_ref[...] = dot(ln, wkv_ref[...], NN).astype(BF)


def latent_call(chunks, gain, shift, w_query, w_keyval, cot, deps):
    rows, width = chunks[0].shape
    inner = w_query.shape[1]
    count = len(chunks)
    return hbm_call(
        latent_kernel,
        (6, 7),
        range(4),
        (1, 2, 3),
        in_specs=[pl.BlockSpec(memory_space=pltpu.VMEM)] * (count + 5) + [ANY] * len(deps),
        out_shape=[
            jax.ShapeDtypeStruct((count, rows, width), BF),
            jax.ShapeDtypeStruct((count, rows, width), BF),
            jax.ShapeDtypeStruct((count, rows, inner), BF),
            jax.ShapeDtypeStruct((rows, 2 * inner), BF),
            jax.ShapeDtypeStruct(cot.shape, BF),
        ],
        compiler_params=params(28),
        cost_estimate=cost(6),
        name="latents",
    )(*chunks, gain, shift, w_query, w_keyval, cot, *deps)


def kv_columns(first, second):
    span = first.shape[1] // 2
    return jnp.concatenate(
        [first[:, :span], second[:, :span], first[:, span:], second[:, span:]], axis=1
    )


def latent_back_kernel(
    scale, raw_ref, mixed_ref, own_ref, far_ref, kv_a, kv_b, wq_ref, w_ref, gain_ref, *rest
):
    grad_q = ((own_ref[...].astype(F32) + far_ref[...].astype(F32)) * scale).astype(BF)
    up = (
        dot(grad_q, wq_ref[...], NT)
        + dot(kv_columns(kv_a[...], kv_b[...]), w_ref[...], NT)
    )
    hat, inv = standardize(raw_ref[...].astype(F32))
    back, _ = norm_back(hat, inv, gain_ref[...], up)
    rest[-2][...] = (mixed_ref[...] + back).astype(BF)
    rest[-1][...] = jnp.zeros_like(rest[-1])


def latent_back_call(scale, args, deps):
    return hbm_call(
        functools.partial(latent_back_kernel, scale),
        (1, 4, 5, 6, 7),
        (0,),
        (2, 3),
        in_specs=[pl.BlockSpec(memory_space=pltpu.VMEM)] * len(args) + [ANY] * len(deps),
        out_shape=[jax.ShapeDtypeStruct(args[0].shape, BF), TOKEN],
        compiler_params=params(24),
        cost_estimate=cost(0.1),
        name="latent_back",
    )(*args, *deps)


def out_kernel(mixed_ref, own_ref, near_ref, far_ref, *rest):
    total = own_ref[...].astype(F32) + near_ref[0].astype(F32) + far_ref[...].astype(F32)
    rest[-2][...] = (mixed_ref[...] + total).astype(BF)
    rest[-1][...] = jnp.zeros_like(rest[-1])


def out_call(mixed, own, near, far, deps):
    return hbm_call(
        out_kernel,
        (0, 1),
        (0,),
        (2, 3),
        in_specs=[pl.BlockSpec(memory_space=pltpu.VMEM)] * 4 + [ANY] * len(deps),
        out_shape=[jax.ShapeDtypeStruct(mixed.shape, BF), TOKEN],
        compiler_params=params(8),
        cost_estimate=cost(1.5),
        name="latents_out",
    )(mixed, own, near, far, *deps)


def block_mask(head_size, lats):
    rows = GROUP * lats
    cols = GROUP * head_size
    row_head = lax.broadcasted_iota(jnp.int32, (rows, cols), 0) // lats
    col_head = lax.broadcasted_iota(jnp.int32, (rows, cols), 1) // head_size
    return row_head == col_head


def spread_heads(values, mask):
    tiled = jnp.concatenate([values] * GROUP, axis=0)
    return jnp.where(mask, tiled, jnp.zeros_like(tiled))


def gather_heads(full, mask, lats):
    kept = jnp.where(mask, full, 0.0)
    total = kept[:lats]
    for head in range(1, GROUP):
        total = total + kept[head * lats : (head + 1) * lats]
    return total


LANES = 128


def terms(value):
    first = value.astype(BF)
    rest = value - first.astype(F32)
    second = rest.astype(BF)
    return first, second, (rest - second.astype(F32)).astype(BF)


def pick(shape, fn):
    row = lax.broadcasted_iota(jnp.int32, shape, 0)
    col = lax.broadcasted_iota(jnp.int32, shape, 1)
    return jnp.where(fn(row, col), 1.0, 0.0).astype(BF)


def holds(lane, head, figure):
    return (lane < 24 * figure + 24) & (lane >= 24 * figure) & (lane % HEADS == head)


def pack_rows(figures):
    rows = jnp.concatenate([t for f in figures for t in terms(f)], axis=0)
    eye = pick((rows.shape[0], LANES), lambda r, c: r == c)
    return dot(rows, eye, TN).astype(BF)


def pack_cols(figures):
    total = None
    for i, figure in enumerate(figures):
        for k, term in enumerate(terms(figure)):
            at = HEADS * (3 * i + k)
            place = pick((LANES, LANES), lambda r, c: (r < HEADS) & (c == r + at))
            part = dot(term, place, NN)
            total = part if total is None else total + part
    return total.astype(BF)


def widen(packed, figure, inner):
    size = inner // HEADS
    return dot(packed, pick((LANES, inner), lambda r, c: holds(r, c // size, figure)), NN)


def narrow(packed, figure):
    return dot(
        packed, pick((LANES, LANES), lambda r, c: (c < HEADS) & holds(r, c, figure)), NN
    )


def doc_rows(refs, d, lat_rows, cols):
    rows = slice(d * lat_rows, (d + 1) * lat_rows)
    return jnp.concatenate(
        [ref[c, rows, cols] for ref in refs for c in range(ref.shape[0])], axis=0
    )


def doc_spans(doc_ref, micro, docs, slots):
    counts = []
    for d in range(docs):
        total = 0
        for s in range(slots):
            total = total + jnp.where(doc_ref[micro, s] == d, 1, 0)
        counts.append(total)
    first = 0
    spans = []
    for count in counts:
        spans.append((first, count))
        first = first + count
    return spans


def slot_chunk(span, step, slots):
    first, count = span
    low = first + step * CHUNK
    return jnp.minimum(low, slots - CHUNK), low, first + count


def own_rows_of(at, low, high, keys):
    slot = at + lax.broadcasted_iota(jnp.int32, (CHUNK * keys, 1), 0) // keys
    return (slot >= low) & (slot < high)


def steps_of(span):
    return (span[1] + CHUNK - 1) // CHUNK


PAIR = 1


def more_chunks(spans, slots, body):
    counts = [steps_of(span) - 1 for span in spans]
    total = sum(counts)

    def locate(e):
        d, before, end = 0, 0, 0
        for count in counts[:-1]:
            end = end + count
            d = d + jnp.where(e >= end, 1, 0)
            before = jnp.where(e >= end, end, before)
        step = e - before + 1
        first, count = 0, 0
        for i, span in enumerate(spans):
            first = first + jnp.where(d == i, span[0], 0)
            count = count + jnp.where(d == i, span[1], 0)
        at, low, high = slot_chunk((first, count), step, slots)
        return d, step, at, low, jnp.where(e < total, high, low)

    def pair(i, carry):
        body([locate(PAIR * i + k) for k in range(PAIR)])
        return carry

    lax.fori_loop(0, (total + PAIR - 1) // PAIR, pair, 0)


def attend_kernel(deps, doc_ref, q_ref, kv_ref, kvl_ref, *rest):
    keep_ref, send_ref, bd, score, acc, top, tot = rest[deps:]
    chunks, rows, inner = q_ref.shape
    docs, lat_rows = kvl_ref.shape[1:3]
    lats = chunks * lat_rows
    slots, keys = kv_ref.shape[1:3]
    groups = HEADS // GROUP
    span = inner // groups
    micro = pl.program_id(0)
    mask = block_mask(inner // HEADS, lats)
    cols = [slice(g * span, (g + 1) * span) for g in range(groups)]
    vals = [slice(inner + g * span, inner + (g + 1) * span) for g in range(groups)]
    spans = doc_spans(doc_ref, micro, docs, slots)
    tall = CHUNK * keys

    def load(at, part):
        return kv_ref[0, pl.ds(at, CHUNK), :, part].reshape(tall, span)

    for d in range(docs):
        at, low, high = slot_chunk(spans[d], 0, slots)
        bias = jnp.where(own_rows_of(at, low, high, keys), 0.0, FAR)
        bias = jnp.concatenate([bias, jnp.zeros((lat_rows, 1), F32)], axis=0)
        for g in range(groups):
            spread = spread_heads(doc_rows((q_ref,), d, lat_rows, cols[g]), mask)
            bd[d, g] = spread
            key = jnp.concatenate([load(at, cols[g]), kvl_ref[0, d, :, cols[g]]], axis=0)
            val = dot(key, spread, NT) + bias
            score[d, g, 0] = val
            top[d, g] = jnp.max(val, axis=0, keepdims=True)

    def more(parts):
        for k, (d, step, at, low, high) in enumerate(parts):
            bias = jnp.where(own_rows_of(at, low, high, keys), 0.0, FAR)
            for g in range(groups):
                val = dot(load(at, cols[g]), bd[d, g], NT) + bias
                score[d, g, jnp.minimum(step, score.shape[2] - 1), :tall] = val
                top[d, g] = jnp.maximum(top[d, g], jnp.max(val, axis=0, keepdims=True))

    more_chunks(spans, slots, more)
    for d in range(docs):
        at, low, high = slot_chunk(spans[d], 0, slots)
        for g in range(groups):
            expo = jnp.exp(score[d, g, 0] - top[d, g])
            tot[d, g] = jnp.sum(expo, axis=0, keepdims=True)
            val = jnp.concatenate([load(at, vals[g]), kvl_ref[0, d, :, vals[g]]], axis=0)
            acc[d, g] = dot(expo.astype(BF), val, TN)

    def more_values(parts):
        for d, step, at, low, high in parts:
            step = jnp.minimum(step, score.shape[2] - 1)
            own = own_rows_of(at, low, high, keys)
            for g in range(groups):
                expo = jnp.where(own, jnp.exp(score[d, g, step, :tall] - top[d, g]), 0.0)
                tot[d, g] = tot[d, g] + jnp.sum(expo, axis=0, keepdims=True)
                acc[d, g] = acc[d, g] + dot(expo.astype(BF), load(at, vals[g]), TN)

    more_chunks(spans, slots, more_values)
    half = chunks // 2
    for d in range(docs):
        rows_d = slice(d * lat_rows, (d + 1) * lat_rows)

        def by_head(ref):
            return jnp.concatenate(
                [
                    ref[d, g][:, h * lats : (h + 1) * lats]
                    for g in range(groups)
                    for h in range(GROUP)
                ],
                axis=0,
            )

        packed = pack_rows([by_head(top), by_head(tot)])
        outs = [gather_heads(acc[d, g], mask, lats).astype(BF) for g in range(groups)]
        for c in range(chunks):
            ref = keep_ref if c < half else send_ref
            part = slice(c * lat_rows, (c + 1) * lat_rows)
            for g in range(groups):
                ref[c % half, rows_d, cols[g]] = outs[g][part]
            ref[c % half, rows_d, inner:] = packed[part]


def attend_call(doc_ids, queries, kv_med, kv_lat, deps):
    chunks, _, inner = queries.shape
    micro, slots, keys, both = kv_med.shape
    docs, lat_rows = kv_lat.shape[1:3]
    lats = chunks * lat_rows
    rows = docs * lat_rows
    groups = HEADS // GROUP
    span = inner // groups
    wide = GROUP * lats
    half = chunks // 2
    longest = (slots - docs + CHUNK) // CHUNK
    out_spec = pl.BlockSpec((half, rows, inner + LANES), lambda i, ids: (0, i, 0))
    out_shape = jax.ShapeDtypeStruct((half, micro * rows, inner + LANES), BF)
    return hbm_call(
        functools.partial(attend_kernel, len(deps)),
        range(3),
        (),
        grid_spec=pltpu.PrefetchScalarGridSpec(
            num_scalar_prefetch=1,
            grid=(micro,),
            in_specs=[
                pl.BlockSpec((chunks, rows, inner), lambda i, ids: (0, i, 0)),
                pl.BlockSpec((1, slots, keys, both), lambda i, ids: (i, 0, 0, 0)),
                pl.BlockSpec((1, docs, lat_rows, both), lambda i, ids: (i, 0, 0, 0)),
            ]
            + [ANY] * len(deps),
            out_specs=[out_spec, out_spec],
            scratch_shapes=[
                pltpu.VMEM((docs, groups, wide, span), BF),
                pltpu.VMEM((docs, groups, longest, CHUNK * keys + lat_rows, wide), F32),
                pltpu.VMEM((docs, groups, wide, span), F32),
                pltpu.VMEM((docs, groups, 1, wide), F32),
                pltpu.VMEM((docs, groups, 1, wide), F32),
            ],
        ),
        out_shape=[out_shape, out_shape],
        compiler_params=params(40),
        cost_estimate=cost(13),
        name="attend",
    )(doc_ids, queries, kv_med, kv_lat, *deps)


def join_kernel(last, flip, a_ref, b_ref, *rest):
    out_ref = rest[-1]
    inner = a_ref.shape[2] - LANES
    count = a_ref.shape[0]
    for c in range(count):
        first, second = a_ref[c], b_ref[count - 1 - c if flip else c]
        pack_a, pack_b = first[:, inner:], second[:, inner:]
        top_a, top_b = widen(pack_a, 0, inner), widen(pack_b, 0, inner)
        best = jnp.maximum(top_a, top_b)
        fac_a, fac_b = jnp.exp(top_a - best), jnp.exp(top_b - best)
        out = fac_a * first[:, :inner].astype(F32) + fac_b * second[:, :inner].astype(F32)
        if last:
            total = fac_a * widen(pack_a, 1, inner) + fac_b * widen(pack_b, 1, inner)
            out = out / total
        out_ref[c, :, :inner] = out.astype(BF)
        small_a, small_b = narrow(pack_a, 0), narrow(pack_b, 0)
        small = jnp.maximum(small_a, small_b)
        sum_ab = jnp.exp(small_a - small) * narrow(pack_a, 1) + jnp.exp(
            small_b - small
        ) * narrow(pack_b, 1)
        if last:
            lane = lax.broadcasted_iota(jnp.int32, sum_ab.shape, 1)
            lse = jnp.where(lane < HEADS, small + jnp.log(jnp.maximum(sum_ab, 1e-30)), 0.0)
            out_ref[c, :, inner:] = pack_cols([lse])
        else:
            out_ref[c, :, inner:] = pack_cols([small, sum_ab])


def join_call(first, second, last, flip, deps=()):
    count, rows, cols = first.shape
    block = min(rows, 128)
    spec = pl.BlockSpec((count, block, cols), lambda i: (0, i, 0))
    return pl.pallas_call(
        functools.partial(join_kernel, last, flip),
        grid=(rows // block,),
        in_specs=[spec, spec] + [ANY] * len(deps),
        out_specs=spec,
        out_shape=jax.ShapeDtypeStruct(first.shape, BF),
        compiler_params=params(10),
        cost_estimate=cost(3.5),
        name="join_last" if last else "join_first",
    )(first, second, *deps)


def cot_units_kernel(own, far, near, both, wr_ref, units_ref, cot_ref, token_ref):
    token_ref[...] = jnp.zeros_like(token_ref)
    for c, ref in enumerate((own, far, near, both)):
        cot_ref[c] = ref[...]
    for c in range(0, 4, 2):
        rows = own.shape[0]
        pair = cot_ref[c : c + 2].reshape(2 * rows, own.shape[1])
        units_ref[c : c + 2] = dot(pair, wr_ref[...], NT).reshape(2, rows, wr_ref.shape[0])


def cot_units_call(chunks, w_red):
    rows, width = chunks[0].shape
    count = len(chunks)
    return hbm_call(
        cot_units_kernel,
        (0, 4),
        (0, 1),
        (1, 2, 3),
        in_specs=[pl.BlockSpec(memory_space=pltpu.VMEM)] * 5,
        out_shape=[
            jax.ShapeDtypeStruct((count, rows, w_red.shape[0]), F32),
            jax.ShapeDtypeStruct((count, rows, width), BF),
            TOKEN,
        ],
        compiler_params=params(24),
        cost_estimate=cost(6),
        name="cot_units",
    )(*chunks, w_red)


def ff_kernel(
    lat_ref,
    near_ref,
    far_ref,
    units_ref,
    wo_ref,
    we_ref,
    wr_ref,
    gain_ref,
    shift_ref,
    mixed_ref,
    ln_ref,
    act_ref,
    gpre_ref,
    up_own,
    up_keep,
    up_send,
    out_own,
    out_keep,
    out_send,
):
    i = pl.program_id(0)
    half = pl.num_programs(0) // 2
    att = jnp.where(i < half, near_ref[0], far_ref[0])
    mixed = lat_ref[0].astype(F32) + dot(att, wo_ref[...], NN)
    hat, _ = standardize(mixed)
    ln = (hat * gain_ref[...] + shift_ref[...]).astype(BF)
    ln_ref[0] = ln
    pre = dot(ln, we_ref[...], NN)
    cdf = 0.5 + 0.5 * lax.erf(pre * (0.5**0.5))
    slope = cdf + pre * (0.3989422804014327 * jnp.exp(-0.5 * pre * pre))
    act = (pre * cdf).astype(BF)
    act_ref[0] = act
    gpre = (units_ref[0] * slope).astype(BF)
    gpre_ref[0] = gpre
    up = dot(gpre, we_ref[...], NT).astype(BF)
    out = dot(act, wr_ref[...], NN).astype(BF)

    @pl.when(i == 0)
    def _():
        mixed_ref[...] = mixed
        up_own[...] = up
        out_own[...] = out

    @pl.when(i == 1)
    def _():
        up_keep[...] = up
        out_keep[...] = out

    @pl.when(i >= half)
    def _():
        up_send[0] = up
        out_send[0] = out


def ff_call(latents, near, far, cot_units, w_output, w_exp, w_red, gain, shift):
    chunks, rows, width = latents.shape
    inner = w_output.shape[0]
    units = w_exp.shape[1]
    half = chunks // 2

    def chunk(cols):
        return pl.BlockSpec((1, rows, cols), lambda i: (i, 0, 0))

    def first(cols):
        return pl.BlockSpec((1, rows, cols), lambda i: (jnp.minimum(i, half - 1), 0, 0))

    def second(cols):
        return pl.BlockSpec((1, rows, cols), lambda i: (jnp.maximum(i - half, 0), 0, 0))

    def fixed(*shape):
        return pl.BlockSpec(shape, lambda i: (0,) * len(shape))

    def out(count, cols):
        return jax.ShapeDtypeStruct((count, rows, cols), BF)

    return hbm_call(
        ff_kernel,
        (0, 3, 4, 5, 6),
        (0, 1, 2, 3, 4, 7, 8, 9),
        (1, 2),
        grid=(chunks,),
        in_specs=[
            chunk(width),
            first(inner),
            second(inner),
            chunk(units),
            fixed(inner, width),
            fixed(width, units),
            fixed(units, width),
            fixed(1, width),
            fixed(1, width),
        ],
        out_specs=[
            fixed(rows, width),
            chunk(width),
            chunk(units),
            chunk(units),
            fixed(rows, width),
            fixed(rows, width),
            second(width),
            fixed(rows, width),
            fixed(rows, width),
            second(width),
        ],
        out_shape=[
            jax.ShapeDtypeStruct((rows, width), F32),
            out(chunks, width),
            out(chunks, units),
            out(chunks, units),
            jax.ShapeDtypeStruct((rows, width), BF),
            jax.ShapeDtypeStruct((rows, width), BF),
            out(half, width),
            jax.ShapeDtypeStruct((rows, width), BF),
            jax.ShapeDtypeStruct((rows, width), BF),
            out(half, width),
        ],
        compiler_params=params(40),
        cost_estimate=cost(18),
        name="feed_forward",
    )(latents, near, far, cot_units, w_output, w_exp, w_red, gain, shift)


def ff_weights_kernel(ln_ref, gpre_ref, act_ref, cot_ref, *rest):
    out_ref = rest[-1]
    count, rows, width = out_ref.shape
    half = rows // 2
    for part, (left, right) in enumerate(((ln_ref, gpre_ref), (act_ref, cot_ref))):
        product = dot(left[...], right[...], TN).astype(BF)
        out_ref[:, part * half : (part + 1) * half, :] = product.reshape(count, half, width)


def ff_weights_call(ln_ff, grad_pre, hidden_act, cot, imgs, deps):
    tokens, width = ln_ff.shape
    units = grad_pre.shape[1]
    half = units // imgs
    steps = 2
    left = pl.BlockSpec((tokens, width // steps), lambda i: (0, i))
    right = pl.BlockSpec((tokens, width), lambda i: (0, 0))
    return hbm_call(
        ff_weights_kernel,
        range(4),
        (),
        grid=(steps,),
        in_specs=[left, right, left, right] + [ANY] * len(deps),
        out_specs=pl.BlockSpec((imgs // steps, 2 * half, width), lambda i: (i, 0, 0)),
        out_shape=pltpu.HBM((imgs, 2 * half, width), BF),
        compiler_params=params(28),
        cost_estimate=cost(9),
        name="ff_weights",
    )(ln_ff, grad_pre, hidden_act, cot, *deps)


def half_sum_kernel(keep_ref, sent_ref, out_ref, token_ref):
    token_ref[...] = jnp.zeros_like(token_ref)
    out_ref[...] = (keep_ref[...].astype(F32) + sent_ref[1].astype(F32)).astype(BF)


def half_sum(keep, sent):
    return hbm_call(
        half_sum_kernel,
        (0,),
        (),
        (1,),
        in_specs=[pl.BlockSpec(memory_space=pltpu.VMEM)] * 2,
        out_shape=[jax.ShapeDtypeStruct(keep.shape, BF), TOKEN],
        compiler_params=params(6),
        cost_estimate=cost(0.1),
        name="half_sum",
    )(keep, sent)


def mixed_back_kernel(own_ref, near_ref, far_ref, mixed_ref, cot_ref, wo_ref, gain_ref, *rest):
    gm_ref, gb_ref, ga_ref, dg_ref, ds_ref = rest[-5:]
    up = own_ref[...].astype(F32) + near_ref[0].astype(F32) + far_ref[...].astype(F32)
    hat, inv = standardize(mixed_ref[...])
    back, gains = norm_back(hat, inv, gain_ref[...], up)
    grad = cot_ref[...].astype(F32) + back
    gm_ref[...] = grad
    branch = grad.astype(BF)
    gb_ref[...] = branch
    ga_ref[...] = dot(branch, wo_ref[...], NT).astype(BF)
    dg_ref[...] = jnp.sum(gains, axis=0, keepdims=True)
    ds_ref[...] = jnp.sum(up, axis=0, keepdims=True)


def mixed_back_call(own, near, far, mixed, cot, w_output, gain, deps):
    rows, width = mixed.shape
    inner = w_output.shape[0]
    return hbm_call(
        mixed_back_kernel,
        (0, 3, 4, 5),
        (0,),
        (1, 2),
        in_specs=[pl.BlockSpec(memory_space=pltpu.VMEM)] * 7 + [ANY] * len(deps),
        out_shape=[
            jax.ShapeDtypeStruct((rows, width), F32),
            jax.ShapeDtypeStruct((rows, width), BF),
            jax.ShapeDtypeStruct((rows, inner), BF),
            jax.ShapeDtypeStruct((1, width), F32),
            jax.ShapeDtypeStruct((1, width), F32),
        ],
        compiler_params=params(20),
        cost_estimate=cost(4),
        name="mixed_back",
    )(own, near, far, mixed, cot, w_output, gain, *deps)


def part_kernel(index_ref, e_ref, r_ref, eo_ref, ro_ref):
    eo_ref[...] = e_ref[...]
    ro_ref[...] = r_ref[...]


def part_call(index, w_expand, w_reduce, imgs, parts):
    width, ff = w_expand.shape
    unit = ff // (imgs * parts)
    return hbm_call(
        part_kernel,
        range(2),
        range(2),
        grid_spec=pltpu.PrefetchScalarGridSpec(
            num_scalar_prefetch=1,
            grid=(imgs,),
            in_specs=[
                pl.BlockSpec((width, unit), lambda i, p: (0, i * parts + p[0])),
                pl.BlockSpec((unit, width), lambda i, p: (i * parts + p[0], 0)),
            ],
            out_specs=[
                pl.BlockSpec((width, unit), lambda i, p: (0, i)),
                pl.BlockSpec((unit, width), lambda i, p: (i, 0)),
            ],
        ),
        out_shape=[
            jax.ShapeDtypeStruct((width, imgs * unit), BF),
            jax.ShapeDtypeStruct((imgs * unit, width), BF),
        ],
        compiler_params=params(6),
        name="weight_part",
    )(index, w_expand, w_reduce)


def attend_back_kernel(
    group,
    deps,
    doc_ref,
    index_ref,
    q_ref,
    go_own,
    go_far,
    go_near,
    go_both,
    att_near,
    att_far,
    lse_near,
    lse_far,
    k_ref,
    v_ref,
    kl_ref,
    vl_ref,
    hat_ref,
    norm_ref,
    vec_in,
    lat_hat_hbm,
    wkv_hbm,
    wq_hbm,
    extra_hbm,
    *rest,
):
    gkv_ref, gkvl_ref, gq_ref, keep_ref, send_ref, vec_ref = rest[deps : deps + 6]
    bdq, bdo, acc, stat, h_med, h_lat, sums, wide_rows = rest[deps + 6 : -6]
    lat_hat_ref, wk_ref, wv_ref, wq_ref, extra_ref, sems = rest[-6:]
    chunks, _, span = q_ref.shape
    docs, lat_rows = kl_ref.shape[1:3]
    lats = chunks * lat_rows
    slots, keys = k_ref.shape[1:3]
    micro = pl.program_id(0)
    mask = block_mask(span // GROUP, lats)
    every = slice(None)
    scale = (span // GROUP) ** (-0.5)
    go_refs = (go_own, go_far, go_near, go_both)
    att_refs, lse_refs = (att_near, att_far), (lse_near, lse_far)

    groups = HEADS // GROUP

    def columns(ref, at):
        return ref.at[:, at * span : (at + 1) * span]

    copies = [
        pltpu.make_async_copy(source, target, sems.at[i])
        for i, (source, target) in enumerate(
            (
                (lat_hat_hbm, lat_hat_ref),
                (columns(wkv_hbm, group), wk_ref),
                (columns(wkv_hbm, groups + group), wv_ref),
                (columns(wq_hbm, group), wq_ref),
                (extra_hbm, extra_ref),
            )
        )
    ]

    @pl.when(micro == 0)
    def _():
        for copy in copies:
            copy.start()

    spans = doc_spans(doc_ref, micro, docs, slots)
    tall = CHUNK * keys

    def pair(key, value, bias, d):
        score = dot(key, bdq[d], NT) + bias
        prob = jnp.exp(score - stat[d, 0:1])
        dprob = dot(value, bdo[d], NT)
        dscore = (prob * (dprob - stat[d, 1:2])).astype(BF)
        grad_key = dot(dscore, bdq[d], NN).astype(BF)
        grad_value = dot(prob.astype(BF), bdo[d], NN).astype(BF)
        grad_query = dot(dscore, key, TN)
        return grad_key, grad_value, grad_query

    def load(ref, at):
        return ref[0, pl.ds(at, CHUNK)].reshape(tall, span)

    def store(at, own, grad_key, grad_value):
        part = pl.ds(pl.multiple_of(at * keys, keys), tall)
        gkv_ref[part, :span] = jnp.where(own, grad_key, gkv_ref[part, :span])
        gkv_ref[part, span:] = jnp.where(own, grad_value, gkv_ref[part, span:])

    sel = pick((HEADS, LANES), lambda r, c: holds(c, r, 0))
    size = span // GROUP
    head_sel = pick((HEADS, span), lambda r, c: c // size == r)

    def row(by_head, at):
        return jnp.concatenate([by_head[at + h : at + h + 1] for h in range(GROUP)], axis=1)

    for d in range(docs):
        out_grad = doc_rows(go_refs, d, lat_rows, every)
        bdq[d] = spread_heads(doc_rows((q_ref,), d, lat_rows, every), mask)
        bdo[d] = spread_heads(out_grad, mask)
        lse = dot(sel, doc_rows(lse_refs, d, lat_rows, every), NT)
        stat[d, 0:1] = row(lse, group * GROUP)
        attended = doc_rows(att_refs, d, lat_rows, every)
        high, low, _ = terms(out_grad.astype(F32) * attended.astype(F32))
        stat[d, 1:2] = row(dot(head_sel, high, NT) + dot(head_sel, low, NT), 0)
    for d in range(docs):
        rows_d = pl.ds((micro * docs + d) * lat_rows, lat_rows)
        at, low, high = slot_chunk(spans[d], 0, slots)
        own = own_rows_of(at, low, high, keys)
        bias = jnp.concatenate([jnp.where(own, 0.0, FAR), jnp.zeros((lat_rows, 1), F32)], axis=0)
        key = jnp.concatenate([load(k_ref, at), kl_ref[0, d]], axis=0)
        value = jnp.concatenate([load(v_ref, at), vl_ref[0, d]], axis=0)
        grad_key, grad_value, grad_query = pair(key, value, bias, d)
        store(at, own, grad_key[:tall], grad_value[:tall])
        gkvl_ref[rows_d, :span] = grad_key[tall:]
        gkvl_ref[rows_d, span:] = grad_value[tall:]
        acc[d] = grad_query

    def more(parts):
        done = []
        for d, step, at, low, high in parts:
            own = own_rows_of(at, low, high, keys)
            bias = jnp.where(own, 0.0, FAR)
            done.append((d, at, own, *pair(load(k_ref, at), load(v_ref, at), bias, d)))
        for d, at, own, grad_key, grad_value, grad_query in done:
            store(at, own, grad_key, grad_value)
            acc[d] = acc[d] + grad_query

    more_chunks(spans, slots, more)
    for d in range(docs):
        full = gather_heads(acc[d], mask, lats).astype(BF)
        for c in range(chunks):
            gq_ref[c, pl.ds(micro * docs * lat_rows + d * lat_rows, lat_rows)] = full[
                c * lat_rows : (c + 1) * lat_rows
            ]
    part = dot(hat_ref[...], gkv_ref[...], TN)
    part_sum = jnp.sum(gkv_ref[...].astype(F32), axis=0, keepdims=True)

    @pl.when(micro == 0)
    def _():
        h_med[...] = part
        sums[0:1, :] = part_sum

    @pl.when(micro > 0)
    def _():
        h_med[...] = h_med[...] + part
        sums[0:1, :] = sums[0:1, :] + part_sum

    @pl.when(micro == pl.num_programs(0) - 1)
    def _():
        width = h_med.shape[0]
        step = 128
        tokens = lat_hat_ref.shape[0] * lat_hat_ref.shape[1]
        for copy in copies:
            copy.wait()
        h_lat[...] = dot(lat_hat_ref[0], gkvl_ref[...], TN)
        sums[1:2, :] = jnp.sum(gkvl_ref[...].astype(F32), axis=0, keepdims=True)
        quer_all = gq_ref[...].reshape(tokens, span)
        h_q = dot(lat_hat_ref[...].reshape(tokens, width), quer_all, TN)
        quer_sum = jnp.sum(quer_all.astype(F32), axis=0, keepdims=True) * scale
        for at in range(0, width, step):
            part = slice(at, at + step)
            norm = norm_ref[:, part].T
            med, lat, quer = h_med[part, :], h_lat[part, :], h_q[part] * scale
            med_sum, lat_sum = sums[0:1, :], sums[1:2, :]
            wide_rows[part, : 2 * span] = (
                norm[:, 0:1] * med
                + norm[:, 1:2] * med_sum
                + norm[:, 2:3] * lat
                + norm[:, 3:4] * lat_sum
            ).astype(BF)
            wide_rows[part, 2 * span :] = (
                norm[:, 2:3] * quer + norm[:, 3:4] * quer_sum
            ).astype(BF)
            wkv = jnp.concatenate([wk_ref[part, :], wv_ref[part, :]], axis=1).astype(F32)
            wq = wq_ref[part, :].astype(F32)

            def total(value):
                return jnp.sum(value, axis=1, keepdims=True)

            vec = jnp.concatenate(
                [
                    total(wkv * med),
                    total(wkv * med_sum),
                    total(wkv * lat) + total(wq * quer),
                    total(wkv * lat_sum) + total(wq * quer_sum),
                    jnp.zeros((step, step - 4), F32),
                ],
                axis=1,
            )
            rows = vec.T[: vec_ref.shape[0]]
            vec_ref[:, part] = rows if group == 0 else vec_in[:, part] + rows
        if len(keep_ref.shape) == 2:
            keep_ref[...] = wide_rows[...]
            return
        imgs, two, height, _ = keep_ref.shape
        share = width // imgs
        tall = share // (2 * two)
        bit = lax.rem(index_ref[0], 2)
        for ref, mine in ((keep_ref, bit), (send_ref, 1 - bit)):
            for i in range(imgs):
                for y in range(two):
                    at = pl.multiple_of(i * share + 2 * y * tall + mine * tall, tall)
                    rows = wide_rows[pl.ds(at, tall), :]
                    ref[i, y, :tall] = rows[:, : 2 * span]
                    ref[i, y, tall : tall + tall // 2, :span] = rows[: tall // 2, 2 * span :]
                    ref[i, y, tall : tall + tall // 2, span:] = rows[tall // 2 :, 2 * span :]
                    start = tall + tall // 2
                    if group == 0:
                        size = extra_ref.shape[0] // (2 * two * imgs)
                        at = pl.multiple_of((i * two + y) * 2 * size + mine * size, size)
                        rows = extra_ref[pl.ds(at, size), :]
                        ref[i, y, start : start + size] = rows[:, : 2 * span]
                        ref[i, y, start + size : start + 2 * size] = rows[:, 2 * span :]
                    else:
                        rows = jnp.zeros((height - start, 2 * span), F32)
                        if y == 0:
                            at = slice(i * share, (i + 1) * share)
                            six = jnp.concatenate([vec_ref[:4, at], extra_ref[:2, at]], axis=0)
                            six = jnp.where(mine == 0, six, 0.0)
                            six = jnp.pad(six, ((0, height - start - 6), (0, 2 * span - share)))
                            rows = six
                        ref[i, y, start:] = rows.astype(BF)


def laid_out(width, imgs, inner):
    share = width // imgs
    return share % 128 == 0 and share <= inner and inner % (64 * imgs) == 0


def attend_back_call(
    group,
    doc_ids,
    queries,
    grad_att,
    att,
    kv_med,
    kv_lat,
    hat_med,
    hat_lat,
    w_keyval,
    w_query,
    norms,
    extra,
    vectors,
    index,
    imgs,
    deps,
):
    chunks, _, inner = queries.shape
    micro, slots, keys, both = kv_med.shape
    docs, lat_rows = kv_lat.shape[1:3]
    lats = chunks * lat_rows
    width = hat_med.shape[1]
    groups = HEADS // GROUP
    span = inner // groups
    wide = GROUP * lats
    rows = slots * keys
    lat_block = docs * lat_rows

    if laid_out(width, imgs, inner):
        tall = width // (imgs * chunks)
        height = tall + tall // 2 + (2 * inner // (imgs * chunks) if group == 0 else 16)
        result = jax.ShapeDtypeStruct((imgs, chunks // 2, height, inner), BF)
    else:
        result = jax.ShapeDtypeStruct((width, 3 * span), BF)
    result_spec = pl.BlockSpec(result.shape, lambda i, ids, p: (0,) * len(result.shape))

    def cols(at, *tail):
        return pl.BlockSpec(
            (1,) + tail, lambda i, ids, p: (i,) + (0,) * (len(tail) - 1) + (at,)
        )

    def tokens(at, size, count=chunks):
        return pl.BlockSpec((count, lat_block, size), lambda i, ids, p: (0, i, at))

    def fixed(at, size):
        return pl.BlockSpec((width, size), lambda i, ids, p: (0, at))

    return hbm_call(
        functools.partial(attend_back_kernel, group, len(deps)),
        range(20),
        (0, 1, 2),
        grid_spec=pltpu.PrefetchScalarGridSpec(
            num_scalar_prefetch=2,
            grid=(micro,),
            in_specs=[
                tokens(group, span),
                *[tokens(group, span, 1)] * 4,
                *[tokens(group, span, 2)] * 2,
                *[tokens(inner // LANES, LANES, 2)] * 2,
                cols(group, slots, keys, span),
                cols(groups + group, slots, keys, span),
                cols(group, docs, lat_rows, span),
                cols(groups + group, docs, lat_rows, span),
                pl.BlockSpec((rows, width), lambda i, ids, p: (i, 0)),
                pl.BlockSpec(norms.shape, lambda i, ids, p: (0, 0)),
                pl.BlockSpec(vectors.shape, lambda i, ids, p: (0, 0)),
                ANY,
                ANY,
                ANY,
                ANY,
            ]
            + [ANY] * len(deps),
            out_specs=[
                pl.BlockSpec((rows, 2 * span), lambda i, ids, p: (i, 0)),
                pl.BlockSpec((micro * lat_block, 2 * span), lambda i, ids, p: (0, 0)),
                pl.BlockSpec((chunks, micro * lat_block, span), lambda i, ids, p: (0, 0, 0)),
                result_spec,
                result_spec,
                pl.BlockSpec(vectors.shape, lambda i, ids, p: (0, 0)),
            ],
            scratch_shapes=[
                pltpu.VMEM((docs, wide, span), BF),
                pltpu.VMEM((docs, wide, span), BF),
                pltpu.VMEM((docs, wide, span), F32),
                pltpu.VMEM((docs, 2, wide), F32),
                pltpu.VMEM((width, 2 * span), F32),
                pltpu.VMEM((width, 2 * span), F32),
                pltpu.VMEM((2, 2 * span), F32),
                pltpu.VMEM((width, 3 * span), BF),
                pltpu.VMEM(hat_lat.shape, BF),
                pltpu.VMEM((width, span), BF),
                pltpu.VMEM((width, span), BF),
                pltpu.VMEM((width, span), BF),
                pltpu.VMEM(extra.shape, extra.dtype),
                pltpu.SemaphoreType.DMA((5,)),
            ],
        ),
        out_shape=[
            jax.ShapeDtypeStruct((micro * rows, 2 * span), BF),
            jax.ShapeDtypeStruct((micro * lat_block, 2 * span), BF),
            jax.ShapeDtypeStruct((chunks, micro * lat_block, span), BF),
            result,
            result,
            jax.ShapeDtypeStruct(vectors.shape, F32),
        ],
        compiler_params=params(48),
        cost_estimate=cost(3),
        name="attend_back",
    )(
        doc_ids,
        index,
        queries,
        *grad_att,
        *att,
        *att,
        kv_med,
        kv_med,
        kv_lat,
        kv_lat,
        hat_med,
        norms,
        vectors,
        hat_lat,
        w_keyval,
        w_query,
        extra,
        *deps,
    )


def media_back_kernel(media_ref, ga_ref, gb_ref, wka_ref, wva_ref, wkb_ref, wvb_ref, gain_ref, *rest):
    out_ref, token_ref = rest[-2:]
    token_ref[...] = jnp.zeros_like(token_ref)
    wa = jnp.concatenate([wka_ref[...], wva_ref[...]], axis=1)
    wb = jnp.concatenate([wkb_ref[...], wvb_ref[...]], axis=1)
    rows = media_ref.shape[0]
    step = min(rows, 256)

    for at in range(0, rows, step):
        part = pl.ds(at, step)
        up = dot(ga_ref[part, :], wa, NT) + dot(gb_ref[part, :], wb, NT)
        hat, inv = standardize(media_ref[part, :].astype(F32))
        back, _ = norm_back(hat, inv, gain_ref[...], up)
        out_ref[part, :] = back.astype(BF)


def key_value_blocks(width, span):
    groups = HEADS // GROUP
    return [
        pl.BlockSpec((width, span), lambda i, at=at: (0, at))
        for g in range(groups)
        for at in (g, groups + g)
    ]


def media_back_call(media, grad_a, grad_b, w_keyval, gain, first, steps, whole, deps):
    rows, width = media.shape
    half = grad_a.shape[1]
    block = 512
    fixed = lambda i: (0, 0)
    moving = lambda i: (first + i, 0)
    extra = tuple(deps) if whole is None else tuple(deps) + (whole,)
    return hbm_call(
        media_back_kernel,
        range(8),
        (0,),
        grid=(steps,),
        in_specs=[
            pl.BlockSpec((block, width), moving),
            pl.BlockSpec((block, half), moving),
            pl.BlockSpec((block, half), moving),
            *key_value_blocks(width, half // 2),
            pl.BlockSpec((1, width), fixed),
        ]
        + [ANY] * len(extra),
        out_specs=[pl.BlockSpec((block, width), moving), pl.BlockSpec(TOKEN.shape, fixed)],
        out_shape=[jax.ShapeDtypeStruct((rows, width), BF), TOKEN],
        input_output_aliases={} if whole is None else {7 + len(extra): 0},
        compiler_params=params(28),
        cost_estimate=cost(2.5 * steps),
        name="media_back",
    )(media, grad_a, grad_b, w_keyval, w_keyval, w_keyval, w_keyval, gain, *extra)


def swap(value, axis, bit):
    size = lax.axis_size(axis)
    return lax.ppermute(value, axis, [(i, i ^ bit) for i in range(size)])


def gather_chunks(own):
    far = swap(own, "patch", 2)
    return own, far, swap(own, "patch", 1), swap(far, "patch", 1)


def gather_patch(own):
    return jnp.stack(gather_chunks(own))


def add(first, second):
    return (first.astype(F32) + second.astype(F32)).astype(BF)


def sum_kernel(ways, terms_in, *refs):
    refs[-1][...] = jnp.zeros_like(refs[-1])
    for k in range(ways):
        value = refs[1 + k][...]
        if terms_in == 2:
            value = (value.astype(F32) + refs[1 + ways + k][...].astype(F32)).astype(BF)
        refs[k - ways - 1][...] = value


def split_sum(first, second, lead, rest, ways, mine, deps):
    count = 1
    for size in lead:
        count *= size
    tail = first.shape[-2:]
    inner = 1
    for size in rest:
        inner *= size
    flat = (count, ways, inner) + tail
    steps = 2 if count % 2 == 0 and first.size * 2 > (1 << 20) else 1
    block = (count // steps, 1, inner) + tail
    outs = [pl.BlockSpec(block, lambda i, m: (i, 0, 0, 0, 0))] * ways
    parts = [
        pl.BlockSpec(block, lambda i, m, k=k: (i, jnp.bitwise_xor(m[0], k), 0, 0, 0))
        for k in range(ways)
    ]
    values = [v.reshape(flat) for v in (first, second) if v is not None]
    *halves, token = pl.pallas_call(
        functools.partial(sum_kernel, ways, len(values)),
        grid_spec=pltpu.PrefetchScalarGridSpec(
            num_scalar_prefetch=1,
            grid=(steps,),
            in_specs=parts * len(values) + [ANY] * len(deps),
            out_specs=outs + [pl.BlockSpec(TOKEN.shape, lambda i, m: (0, 0))],
        ),
        out_shape=[jax.ShapeDtypeStruct((count, 1, inner) + tail, BF)] * ways + [TOKEN],
        compiler_params=params(12),
        cost_estimate=cost(0.3),
        name="split_sum",
    )(mine[None], *[v for v in values for _ in range(ways)], *deps)
    return [h.reshape(lead + rest + tail) for h in halves], token


class Scatter:
    def __init__(self, value, transit, axes, order, scope):
        self.places = [
            (axis, bit)
            for axis in axes
            for bit in reversed(range(lax.axis_size(axis).bit_length() - 1))
            if axis == "img" or any(axis == a and bit in bits for a, bits in order)
        ]
        self.order = list(order)
        self.scope = scope
        self.value, transit = (
            v.reshape((2,) * len(self.places) + v.shape[len(axes) :]) for v in (value, transit)
        )
        self.transit = [transit]

    def step(self, deps=()):
        with jax.named_scope(self.scope):
            if not self.order:
                return ()
            axis, bits = self.order.pop(0)
            place = self.places.index((axis, bits[-1]))
            lead = (2,) * place
            for bit in bits:
                self.places.remove((axis, bit))
            ways = 2 ** len(bits)
            mine = lax.rem(lax.shift_right_logical(lax.axis_index(axis), bits[0]), ways)
            rest = (2,) * (len(self.places) - place)
            (self.value, *send), token = split_sum(
                self.value, self.transit[0], lead, rest, ways, mine, deps
            )
            self.transit = [
                swap(part, axis, (k + 1) << bits[0]) for k, part in enumerate(send)
            ]
            return (token,)


def first_bits():
    return [("img", (bit,)) for bit in range(lax.axis_size("img").bit_length() - 3)]


def last_kernel(index_ref, *refs):
    refs[-1][...] = jnp.zeros_like(refs[-1])
    cut = refs[0].shape[1]
    outs = refs[-1 - refs[0].shape[0] : -1]
    for k, out in enumerate(outs):
        at = jnp.bitwise_xor(index_ref[0], k)
        for part, value, other in ((slice(0, cut), *refs[:2]), (slice(cut, None), *refs[2:4])):
            out[part] = (value[at].astype(F32) + other[at].astype(F32)).astype(BF)


def last_step(first, second, deps):
    count = lax.axis_size("img").bit_length() - 1
    low = max(count - 2, 0)
    ways = 2 ** (count - low)
    values = [
        v.reshape((ways,) + v.shape[-2:])
        for v in (first.value, first.transit[0], second.value, second.transit[0])
    ]
    rows = values[0].shape[1] + values[2].shape[1]
    shape = jax.ShapeDtypeStruct((rows, values[0].shape[2]), BF)
    mine = lax.shift_right_logical(lax.axis_index("img"), low)
    whole = lambda v: pl.BlockSpec(v.shape, lambda i, m: (0,) * len(v.shape))
    own, *send, token = pl.pallas_call(
        last_kernel,
        grid_spec=pltpu.PrefetchScalarGridSpec(
            num_scalar_prefetch=1,
            grid=(1,),
            in_specs=[whole(v) for v in values] + [ANY] * len(deps),
            out_specs=[whole(shape)] * ways + [whole(TOKEN)],
        ),
        out_shape=[shape] * ways + [TOKEN],
        compiler_params=params(6),
        cost_estimate=cost(0.3),
        name="last_sum",
    )(mine[None], *values, *deps)
    sent = [swap(part, "img", (k + 1) << low) for k, part in enumerate(send)]
    return own, sent, token


def reduce_rest(keep, send, scope):
    with jax.named_scope(scope):
        transit = swap(send, "patch", 1)
    return Scatter(keep, transit, ("img", "patch"), [("patch", (1,))] + first_bits(), scope)


def in_order(chunks):
    me = lax.axis_index("patch")
    out = []
    for j in range(4):
        apart = jnp.bitwise_xor(me, j)
        at = 2 * jnp.bitwise_and(apart, 1) + lax.shift_right_logical(apart, 1)
        out.append(lax.dynamic_index_in_dim(chunks, at, 0, keepdims=False))
    return jnp.stack(out)


def place_kernel(index_ref, own, far, near, both, *rest):
    expand_ref, reduce_ref, token_ref = rest[-3:]
    token_ref[...] = jnp.zeros_like(token_ref)
    rows = expand_ref.shape[0]
    parts = 4
    unit = reduce_ref.shape[0] // parts
    blocks = expand_ref.shape[1] // (parts * unit)
    columns = reduce_ref.shape[1]
    step = pl.program_id(0)
    for bits, ref in enumerate((own, near, far, both)):
        part = jnp.bitwise_xor(index_ref[0], bits)
        for k in range(blocks):
            source = pl.ds(pl.multiple_of((step * blocks + k) * unit, unit), unit)
            target = pl.ds(pl.multiple_of((k * parts + part) * unit, unit), unit)
            expand_ref[:, target] = ref[:rows, source].astype(F32)
        source = pl.ds(pl.multiple_of(step * columns, columns), columns)
        target = pl.ds(pl.multiple_of(part * unit, unit), unit)
        reduce_ref[target, :] = ref[rows:, source].astype(F32)


def place_call(index, chunks, rows, imgs, deps):
    both, units = chunks[0].shape
    unit = units // imgs
    parts = len(chunks)
    steps = 2
    return pl.pallas_call(
        place_kernel,
        grid_spec=pltpu.PrefetchScalarGridSpec(
            num_scalar_prefetch=1,
            grid=(steps,),
            in_specs=[pl.BlockSpec((both, units), lambda i, p: (0, 0))] * parts
            + [ANY] * len(deps),
            out_specs=[
                pl.BlockSpec((rows, parts * units // steps), lambda i, p: (0, i)),
                pl.BlockSpec((parts * unit, units // steps), lambda i, p: (0, i)),
                pl.BlockSpec(TOKEN.shape, lambda i, p: (0, 0)),
            ],
        ),
        out_shape=[
            jax.ShapeDtypeStruct((rows, parts * units), F32),
            jax.ShapeDtypeStruct((parts * unit, units), F32),
            TOKEN,
        ],
        compiler_params=params(16),
        cost_estimate=cost(0.1),
        name="place_units",
    )(index, *chunks, *deps)


def local(
    latents,
    media,
    doc_ids,
    w_query,
    w_keyval,
    w_output,
    w_expand,
    w_reduce,
    media_gain,
    media_shift,
    latent_gain,
    latent_shift,
    ff_gain,
    ff_shift,
    out_grad,
):
    micro, docs, lat_rows, width = latents.shape
    slots, keys = media.shape[1:3]
    inner = w_query.shape[1]
    ff = w_expand.shape[1]
    head_size = inner // HEADS
    scale = head_size ** (-0.5)
    parts = lax.axis_size("patch")
    imgs = lax.axis_size("img")
    patch_index = lax.axis_index("patch")
    own_rows = micro * docs * lat_rows
    all_rows = own_rows * parts
    groups = HEADS // GROUP
    span = inner // groups
    unit = ff // (imgs * parts)

    latents_own = latents.reshape(own_rows, width)
    cot_own = out_grad.reshape(own_rows, width)
    media_flat = media.reshape(-1, width)
    with jax.named_scope("gather_latents"):
        latents_far = swap(latents_own, "patch", 2)
        latents_near = swap(latents_own, "patch", 1)

    hat_med, kv_med, token = kv_call(media_flat, media_gain[None], media_shift[None], w_keyval)
    kv_med = kv_med.reshape(micro, slots, keys, 2 * inner)
    if unit % 128 == 0:
        w_exp, w_red = part_call(
            patch_index[None], w_expand, w_reduce, imgs, parts
        )
    else:
        w_exp = lax.dynamic_index_in_dim(
            w_expand.reshape(width, imgs, parts, unit), patch_index, 2, keepdims=False
        ).reshape(width, imgs * unit)
        w_red = lax.dynamic_index_in_dim(
            w_reduce.reshape(imgs, parts, unit, width), patch_index, 1, keepdims=False
        ).reshape(imgs * unit, width)

    (latents_far,) = gate((latents_far,), (token,), pltpu.VMEM)
    with jax.named_scope("gather_latents"):
        latents_both = swap(latents_far, "patch", 1)
    latents_all, hat_all, queries, kv_lat, cot_sent = latent_call(
        (latents_own, latents_far, latents_near, latents_both),
        latent_gain[None],
        latent_shift[None],
        w_query,
        w_keyval,
        cot_own,
        (token,),
    )
    kv_lat = kv_lat.reshape(micro, docs, lat_rows, 2 * inner)
    with jax.named_scope("gather_cotangent"):
        cot_far = swap(cot_sent, "patch", 2)
    keep, send = attend_call(doc_ids, queries, kv_med, kv_lat, ())
    send, cot_far = gate((send, cot_far), (), pltpu.VMEM)
    with jax.named_scope("join_near"):
        near = join_call(keep, swap(send, "patch", 1), False, False)
    with jax.named_scope("gather_cotangent"):
        cot_chunks = (cot_sent, cot_far, swap(cot_sent, "patch", 1), swap(cot_far, "patch", 1))
    cot_units, cot_all, token = cot_units_call(cot_chunks, w_red)
    with jax.named_scope("join_far"):
        att_near = join_call(
            near, swap(near, "patch", 2), True, True, (token,)
        )
        att_far = swap(att_near, "patch", 1)

    mixed, ln_ff, hidden_act, grad_pre, *ff_parts = ff_call(
        latents_all,
        att_near,
        att_far,
        cot_units,
        w_output,
        w_exp,
        w_red,
        ff_gain[None],
        ff_shift[None],
    )
    up_own, up_keep, up_send, out_own, out_keep, out_send = ff_parts
    with jax.named_scope("sum_up"):
        up_sent = swap(up_send, "patch", 1)
        up_near = add(up_keep, up_sent[1])
        up_far = swap(up_near, "patch", 2)

    def flat(value):
        return value.reshape(all_rows, -1)

    ff_grads = ff_weights_call(
        flat(ln_ff), flat(grad_pre), flat(hidden_act), flat(cot_all), imgs, (up_near,)
    )
    (up_far,) = gate((up_far,), (ff_grads,), pltpu.VMEM)
    (ff_grads,) = gate((ff_grads,), (up_far,), pltpu.HBM)
    grad_mixed, grad_branch, grad_att_own, ff_gain_part, ff_shift_part = mixed_back_call(
        up_own, up_sent, up_far, mixed, cot_sent, w_output, ff_gain[None], ()
    )
    grad_output = dot(att_near[0, :, :inner], grad_branch, TN).astype(BF)
    with jax.named_scope("gather_att"):
        far = swap(grad_att_own, "patch", 2)
        near = swap(grad_att_own, "patch", 1)
        (far,) = gate((far,), (grad_output,), pltpu.VMEM)
        grad_att = [chunk[None] for chunk in (grad_att_own, far, near, swap(far, "patch", 1))]
    att = (att_near, att_far)

    with jax.named_scope("sum_ff"):
        ff_own = lax.psum_scatter(ff_grads, "img", scatter_dimension=0, tiled=True)[0]

    zero = jnp.zeros_like(media_gain)
    norms = jnp.stack(
        [media_gain, media_shift, latent_gain, latent_shift, zero, zero, zero, zero]
    )
    ff_vectors = jnp.pad(jnp.concatenate([ff_gain_part, ff_shift_part]), ((0, 6), (0, 0)))
    share = width // imgs
    tall = share // parts
    direct = laid_out(width, imgs, inner)

    def back_call(group, extra, vectors, deps):
        gkv, gkv_lat, gq, keep, send, vectors = attend_back_call(
            group,
            doc_ids,
            queries,
            grad_att,
            att,
            kv_med,
            kv_lat,
            hat_med,
            hat_all,
            w_keyval,
            w_query,
            norms,
            extra,
            vectors,
            patch_index[None],
            imgs,
            deps,
        )
        if not direct:

            def split(value):
                size = value.shape[0] // (imgs * parts)
                return value.reshape(imgs, parts // 2, 2, size, value.shape[1])

            rows = split(keep)
            fold = [rows[..., : tall // 2, 2 * span :], rows[..., tall // 2 :, 2 * span :]]
            blocks = [rows[..., : 2 * span], jnp.concatenate(fold, axis=-1)]
            if group == 0:
                blocks += [split(extra)[..., :inner], split(extra)[..., inner:]]
            else:
                six = jnp.concatenate([vectors[:4], extra[:2]]).astype(BF)
                six = jnp.swapaxes(six.reshape(6, imgs, share), 0, 1)
                six = jnp.pad(six, ((0, 0), (0, 10), (0, width - share)))[:, None, None, :, :inner]
                blocks.append(
                    jnp.pad(six, ((0, 0), (0, parts // 2 - 1), (0, 1), (0, 0), (0, 0)))
                )
            blocks = jnp.concatenate(blocks, axis=3)
            bit = lax.rem(patch_index, 2)
            keep = lax.dynamic_index_in_dim(blocks, bit, 2, keepdims=False)
            send = lax.dynamic_index_in_dim(blocks, 1 - bit, 2, keepdims=False)
        return gkv, gkv_lat, gq, keep, send, vectors

    out_keep, out_send = gate((out_keep, out_send), (ff_gain_part,), pltpu.HBM)
    with jax.named_scope("sum_out"):
        out_sent = swap(out_send, "patch", 1)
    gkv_0, gkv_lat_0, gq_0, keep, send, vectors = back_call(
        0, grad_output, norms, (ff_vectors,)
    )
    keep, send, out_sent = gate((keep, send, out_sent), (), pltpu.VMEM)
    with jax.named_scope("sum_out"):
        out_far, token = half_sum(out_keep, out_sent)
        out_far = swap(out_far, "patch", 2)
    first = reduce_rest(keep, send, "sum_weights_0")
    gkv_1, gkv_lat_1, gq_1, keep, send, vectors = back_call(
        1, ff_vectors, vectors, first.step((token,))
    )
    done = first.step((vectors,))
    keep, send, out_far = gate((keep, send, out_far), done, pltpu.VMEM)
    gq_0, gq_1 = gate((gq_0, gq_1), done, pltpu.HBM)
    second = reduce_rest(keep, send, "sum_weights_1")
    with jax.named_scope("sum_query"):
        gq_keep = jnp.concatenate([gq_0[:2], gq_1[:2]], axis=-1)
        gq_sent = swap(jnp.concatenate([gq_0[2:], gq_1[2:]], axis=-1), "patch", 1)

    def media_piece(at, size, whole, deps):
        return media_back_call(
            media_flat,
            gkv_0,
            gkv_1,
            w_keyval,
            media_gain[None],
            at,
            size,
            whole,
            deps,
        )

    media_grad, *done = media_piece(0, 4, None, second.step())
    latents_out, token = out_call(mixed, out_own, out_sent, out_far, done)
    deps = second.step(done)
    (gq_keep,) = gate((gq_keep,), deps or done, pltpu.VMEM)
    with jax.named_scope("sum_query"):
        gq_near = add(gq_keep, gq_sent)
        gq_far = swap(gq_near[1], "patch", 2)
    (ff_own,) = gate((ff_own,), deps or done, pltpu.HBM)
    with jax.named_scope("gather_ff"):
        ff_far = swap(ff_own, "patch", 2)
    media_grad, *done = media_piece(4, 2, media_grad, (*deps, token))
    while first.order or second.order:
        first.step(done)
        second.step(done)
    with jax.named_scope("sum_weights"):
        own, sent, token = last_step(first, second, done)
    media_grad, *done = media_piece(6, 2, media_grad, (token,))
    (gq_far,) = gate((gq_far,), done, pltpu.VMEM)
    latents_grad, token = latent_back_call(
        scale,
        (
            latents_own,
            grad_mixed,
            gq_near[0],
            gq_far,
            gkv_lat_0,
            gkv_lat_1,
            w_query,
            w_keyval,
            latent_gain[None],
        ),
        done,
    )
    own, ff_far, *sent = gate((own, ff_far, *sent), (token,), pltpu.VMEM)
    with jax.named_scope("gather_ff"):
        ff_chunks = (ff_own, ff_far, swap(ff_own, "patch", 1), swap(ff_far, "patch", 1))
    with jax.named_scope("place_ff"):
        if unit % 128 == 0 and share == unit:
            expand_rows, reduce_rows, placed = place_call(
                patch_index[None], ff_chunks, share, imgs, (token,)
            )
        else:
            placed = token
            ff_rows = in_order(jnp.stack(ff_chunks))
            expand_rows = ff_rows[:, :share].reshape(parts, -1, imgs, unit)
            expand_rows = jnp.transpose(expand_rows, (1, 2, 0, 3)).reshape(-1, ff).astype(F32)
            reduce_rows = ff_rows[:, share:].reshape(-1, width).astype(F32)

    def rows_of(value):
        return value.reshape(-1, value.shape[-1])

    with jax.named_scope("gather_weights"):
        own = own.astype(F32)
        for part in sent:
            own = own + part.astype(F32)
        own = own.astype(BF)
        far = swap(own, "patch", 2)
        near = swap(own, "patch", 1)
        (far,) = gate((far,), (placed,), pltpu.VMEM)
        whole = in_order(jnp.stack([own, far, near, swap(far, "patch", 1)]))
    cut = first.value.shape[-2]
    first, second = whole[:, :cut], whole[:, cut:]
    keyval_rows = [rows_of(first[:, :tall]), rows_of(second[:, :tall])]
    grad_keyval = jnp.concatenate(
        [rows[:, at * span : (at + 1) * span] for at in range(2) for rows in keyval_rows], axis=1
    ).astype(F32)
    end = tall + tall // 2

    def unfold(value):
        return rows_of(jnp.concatenate([value[..., :span], value[..., span:]], axis=1))

    query_rows = jnp.concatenate(
        [unfold(first[:, tall:end]), unfold(second[:, tall:end])], axis=1
    ).astype(F32)
    out_rows = first[:, end:]
    size = out_rows.shape[1] // 2
    out_rows = rows_of(
        jnp.concatenate([out_rows[:, :size], out_rows[:, size:]], axis=2)
    ).astype(F32)
    vectors = second[0, end : end + 6, :share].astype(F32)

    return (
        latents_out.reshape(latents.shape),
        latents_grad.reshape(latents.shape),
        media_grad.reshape(media.shape),
        query_rows,
        grad_keyval,
        out_rows,
        expand_rows,
        reduce_rows,
    ) + tuple(vectors[i] for i in range(6))


def solution(mesh):
    tokens = P(None, "img", "patch", None)
    return jax.shard_map(
        local,
        mesh=mesh,
        in_specs=(tokens, tokens, P(None, "img")) + (P(),) * 11 + (tokens,),
        out_specs=(tokens,) * 3 + (P("img", None),) * 5 + (P("img"),) * 6,
        check_vma=False,
    )
```

```python
import functools

import jax
import jax.numpy as jnp
from jax import lax
from jax.experimental import pallas as pl
from jax.experimental.pallas import tpu as pltpu
from jax.sharding import PartitionSpec as P

HEADS = 8
GROUP = 4
EPS = 1e-05
CHUNK = 6
FAR = -1e30
BF = jnp.bfloat16
F32 = jnp.float32
ANY = pl.BlockSpec(memory_space=pl.ANY)
TOKEN = jax.ShapeDtypeStruct((8, 128), jnp.float32)


def params(mib=56):
    return pltpu.CompilerParams(vmem_limit_bytes=mib << 20)


def cost(us):
    return pl.CostEstimate(flops=int(us * 1.1e9), bytes_accessed=0, transcendentals=0)


def hbm_call(kernel, held, kept, inside=(), **options):
    shapes = options.pop("out_shape")
    if isinstance(shapes, list):
        shapes = [pltpu.HBM(v.shape, v.dtype) if i in kept else v for i, v in enumerate(shapes)]
    options["out_shape"] = shapes
    scalars = options["grid_spec"].num_scalar_prefetch if "grid_spec" in options else 0
    inner = pl.pallas_call(kernel, **options)

    def run(*operands):
        def place(i, x):
            if i in inside:
                return pltpu.with_memory_space_constraint(x, pltpu.VMEM)
            if i in held or x.size >= 1 << 20:
                return pltpu.with_memory_space_constraint(x, pltpu.HBM)
            return x

        arrays = [place(i, x) for i, x in enumerate(operands[scalars:])]
        return inner(*operands[:scalars], *arrays)

    return run


def nothing_kernel(*refs):
    pass


def gate(carry, deps, space):
    return pl.pallas_call(
        nothing_kernel,
        in_specs=[ANY] * (len(carry) + len(deps)),
        out_specs=[ANY] * len(carry),
        out_shape=[space(c.shape, c.dtype) for c in carry],
        input_output_aliases={i: i for i in range(len(carry))},
        compiler_params=params(1),
        name="gate",
    )(
        *[pltpu.with_memory_space_constraint(c, space) for c in carry],
        *[
            pltpu.with_memory_space_constraint(d, pltpu.HBM) if d.size >= 1 << 19 else d
            for d in deps
        ],
    )


def dot(a, b, dims):
    return lax.dot_general(a, b, (dims, ((), ())), preferred_element_type=F32)


NN = ((1,), (0,))
NT = ((1,), (1,))
TN = ((0,), (0,))


def standardize(values):
    center = values - jnp.mean(values, axis=-1, keepdims=True)
    inv = lax.rsqrt(jnp.mean(center * center, axis=-1, keepdims=True) + EPS)
    return center * inv, inv


def norm_back(hat, inv, gain, upstream):
    scaled = upstream * gain
    back = inv * (
        scaled
        - jnp.mean(scaled, axis=-1, keepdims=True)
        - hat * jnp.mean(scaled * hat, axis=-1, keepdims=True)
    )
    return back, upstream * hat


def kv_kernel(media_ref, gain_ref, shift_ref, w_ref, hat_ref, kv_ref, token_ref):
    token_ref[...] = jnp.zeros_like(token_ref)
    rows = media_ref.shape[0]
    step = min(rows, 256)
    for at in range(0, rows, step):
        part = pl.ds(at, step)
        hat, _ = standardize(media_ref[part, :].astype(F32))
        ln = (hat * gain_ref[...] + shift_ref[...]).astype(BF)
        hat_ref[part, :] = hat.astype(BF)
        kv_ref[part, :] = dot(ln, w_ref[...], NN).astype(BF)


def kv_call(media, gain, shift, w_keyval):
    rows, width = media.shape
    outs = w_keyval.shape[1]
    block = 1024
    return hbm_call(
        kv_kernel,
        range(4),
        (0, 1),
        grid=(rows // block,),
        in_specs=[
            pl.BlockSpec((block, width), lambda i: (i, 0)),
            pl.BlockSpec((1, width), lambda i: (0, 0)),
            pl.BlockSpec((1, width), lambda i: (0, 0)),
            pl.BlockSpec((width, outs), lambda i: (0, 0)),
        ],
        out_specs=[
            pl.BlockSpec((block, width), lambda i: (i, 0)),
            pl.BlockSpec((block, outs), lambda i: (i, 0)),
            pl.BlockSpec(TOKEN.shape, lambda i: (0, 0)),
        ],
        out_shape=[
            jax.ShapeDtypeStruct((rows, width), BF),
            jax.ShapeDtypeStruct((rows, outs), BF),
            TOKEN,
        ],
        compiler_params=params(20),
        cost_estimate=cost(16),
        name="media_keyval",
    )(media, gain, shift, w_keyval)


def latent_kernel(own, far, near, both, gain_ref, shift_ref, wq_ref, wkv_ref, cot_ref, *rest):
    raw_ref, hat_ref, q_ref, kv_ref, cot_out = rest[-5:]
    scale = (wq_ref.shape[1] // HEADS) ** (-0.5)
    cot_out[...] = cot_ref[...]
    for c, ref in enumerate((own, far, near, both)):
        raw = ref[...]
        raw_ref[c] = raw
        hat, _ = standardize(raw.astype(F32))
        hat_ref[c] = hat.astype(BF)
        ln = (hat * gain_ref[...] + shift_ref[...]).astype(BF)
        q_ref[c] = (dot(ln, wq_ref[...], NN).astype(BF).astype(F32) * scale).astype(BF)
        if c == 0:
            kv_ref[...] = dot(ln, wkv_ref[...], NN).astype(BF)


def latent_call(chunks, gain, shift, w_query, w_keyval, cot, deps):
    rows, width = chunks[0].shape
    inner = w_query.shape[1]
    count = len(chunks)
    return hbm_call(
        latent_kernel,
        (6, 7),
        range(4),
        (1, 2, 3),
        in_specs=[pl.BlockSpec(memory_space=pltpu.VMEM)] * (count + 5) + [ANY] * len(deps),
        out_shape=[
            jax.ShapeDtypeStruct((count, rows, width), BF),
            jax.ShapeDtypeStruct((count, rows, width), BF),
            jax.ShapeDtypeStruct((count, rows, inner), BF),
            jax.ShapeDtypeStruct((rows, 2 * inner), BF),
            jax.ShapeDtypeStruct(cot.shape, BF),
        ],
        compiler_params=params(28),
        cost_estimate=cost(6),
        name="latents",
    )(*chunks, gain, shift, w_query, w_keyval, cot, *deps)


def kv_columns(first, second):
    span = first.shape[1] // 2
    return jnp.concatenate(
        [first[:, :span], second[:, :span], first[:, span:], second[:, span:]], axis=1
    )


def latent_back_kernel(
    scale, raw_ref, mixed_ref, own_ref, far_ref, kv_a, kv_b, wq_ref, w_ref, gain_ref, *rest
):
    grad_q = ((own_ref[...].astype(F32) + far_ref[...].astype(F32)) * scale).astype(BF)
    up = (
        dot(grad_q, wq_ref[...], NT)
        + dot(kv_columns(kv_a[...], kv_b[...]), w_ref[...], NT)
    )
    hat, inv = standardize(raw_ref[...].astype(F32))
    back, _ = norm_back(hat, inv, gain_ref[...], up)
    rest[-2][...] = (mixed_ref[...] + back).astype(BF)
    rest[-1][...] = jnp.zeros_like(rest[-1])


def latent_back_call(scale, args, deps):
    return hbm_call(
        functools.partial(latent_back_kernel, scale),
        (1, 4, 5, 6, 7),
        (0,),
        (2, 3),
        in_specs=[pl.BlockSpec(memory_space=pltpu.VMEM)] * len(args) + [ANY] * len(deps),
        out_shape=[jax.ShapeDtypeStruct(args[0].shape, BF), TOKEN],
        compiler_params=params(24),
        cost_estimate=cost(0.1),
        name="latent_back",
    )(*args, *deps)


def out_kernel(mixed_ref, own_ref, near_ref, far_ref, *rest):
    total = own_ref[...].astype(F32) + near_ref[0].astype(F32) + far_ref[...].astype(F32)
    rest[-2][...] = (mixed_ref[...] + total).astype(BF)
    rest[-1][...] = jnp.zeros_like(rest[-1])


def out_call(mixed, own, near, far, deps):
    return hbm_call(
        out_kernel,
        (0, 1),
        (0,),
        (2, 3),
        in_specs=[pl.BlockSpec(memory_space=pltpu.VMEM)] * 4 + [ANY] * len(deps),
        out_shape=[jax.ShapeDtypeStruct(mixed.shape, BF), TOKEN],
        compiler_params=params(8),
        cost_estimate=cost(1.5),
        name="latents_out",
    )(mixed, own, near, far, *deps)


def block_mask(head_size, lats):
    rows = GROUP * lats
    cols = GROUP * head_size
    row_head = lax.broadcasted_iota(jnp.int32, (rows, cols), 0) // lats
    col_head = lax.broadcasted_iota(jnp.int32, (rows, cols), 1) // head_size
    return row_head == col_head


def spread_heads(values, mask):
    tiled = jnp.concatenate([values] * GROUP, axis=0)
    return jnp.where(mask, tiled, jnp.zeros_like(tiled))


def gather_heads(full, mask, lats):
    kept = jnp.where(mask, full, 0.0)
    total = kept[:lats]
    for head in range(1, GROUP):
        total = total + kept[head * lats : (head + 1) * lats]
    return total


LANES = 128


def terms(value):
    first = value.astype(BF)
    rest = value - first.astype(F32)
    second = rest.astype(BF)
    return first, second, (rest - second.astype(F32)).astype(BF)


def pick(shape, fn):
    row = lax.broadcasted_iota(jnp.int32, shape, 0)
    col = lax.broadcasted_iota(jnp.int32, shape, 1)
    return jnp.where(fn(row, col), 1.0, 0.0).astype(BF)


def holds(lane, head, figure):
    return (lane < 24 * figure + 24) & (lane >= 24 * figure) & (lane % HEADS == head)


def pack_rows(figures):
    rows = jnp.concatenate([t for f in figures for t in terms(f)], axis=0)
    eye = pick((rows.shape[0], LANES), lambda r, c: r == c)
    return dot(rows, eye, TN).astype(BF)


def pack_cols(figures):
    total = None
    for i, figure in enumerate(figures):
        for k, term in enumerate(terms(figure)):
            at = HEADS * (3 * i + k)
            place = pick((LANES, LANES), lambda r, c: (r < HEADS) & (c == r + at))
            part = dot(term, place, NN)
            total = part if total is None else total + part
    return total.astype(BF)


def widen(packed, figure, inner):
    size = inner // HEADS
    return dot(packed, pick((LANES, inner), lambda r, c: holds(r, c // size, figure)), NN)


def narrow(packed, figure):
    return dot(
        packed, pick((LANES, LANES), lambda r, c: (c < HEADS) & holds(r, c, figure)), NN
    )


def doc_rows(refs, d, lat_rows, cols):
    rows = slice(d * lat_rows, (d + 1) * lat_rows)
    return jnp.concatenate(
        [ref[c, rows, cols] for ref in refs for c in range(ref.shape[0])], axis=0
    )


def doc_spans(doc_ref, micro, docs, slots):
    counts = []
    for d in range(docs):
        total = 0
        for s in range(slots):
            total = total + jnp.where(doc_ref[micro, s] == d, 1, 0)
        counts.append(total)
    first = 0
    spans = []
    for count in counts:
        spans.append((first, count))
        first = first + count
    return spans


def slot_chunk(span, step, slots):
    first, count = span
    low = first + step * CHUNK
    return jnp.minimum(low, slots - CHUNK), low, first + count


def own_rows_of(at, low, high, keys):
    slot = at + lax.broadcasted_iota(jnp.int32, (CHUNK * keys, 1), 0) // keys
    return (slot >= low) & (slot < high)


def steps_of(span):
    return (span[1] + CHUNK - 1) // CHUNK


PAIR = 1


def more_chunks(spans, slots, body):
    counts = [steps_of(span) - 1 for span in spans]
    total = sum(counts)

    def locate(e):
        d, before, end = 0, 0, 0
        for count in counts[:-1]:
            end = end + count
            d = d + jnp.where(e >= end, 1, 0)
            before = jnp.where(e >= end, end, before)
        step = e - before + 1
        first, count = 0, 0
        for i, span in enumerate(spans):
            first = first + jnp.where(d == i, span[0], 0)
            count = count + jnp.where(d == i, span[1], 0)
        at, low, high = slot_chunk((first, count), step, slots)
        return d, step, at, low, jnp.where(e < total, high, low)

    def pair(i, carry):
        body([locate(PAIR * i + k) for k in range(PAIR)])
        return carry

    lax.fori_loop(0, (total + PAIR - 1) // PAIR, pair, 0)


def attend_kernel(deps, doc_ref, q_ref, kv_ref, kvl_ref, *rest):
    keep_ref, send_ref, bd, score, acc, top, tot = rest[deps:]
    chunks, rows, inner = q_ref.shape
    docs, lat_rows = kvl_ref.shape[1:3]
    lats = chunks * lat_rows
    slots, keys = kv_ref.shape[1:3]
    groups = HEADS // GROUP
    span = inner // groups
    micro = pl.program_id(0)
    mask = block_mask(inner // HEADS, lats)
    cols = [slice(g * span, (g + 1) * span) for g in range(groups)]
    vals = [slice(inner + g * span, inner + (g + 1) * span) for g in range(groups)]
    spans = doc_spans(doc_ref, micro, docs, slots)
    tall = CHUNK * keys

    def load(at, part):
        return kv_ref[0, pl.ds(at, CHUNK), :, part].reshape(tall, span)

    for d in range(docs):
        at, low, high = slot_chunk(spans[d], 0, slots)
        bias = jnp.where(own_rows_of(at, low, high, keys), 0.0, FAR)
        bias = jnp.concatenate([bias, jnp.zeros((lat_rows, 1), F32)], axis=0)
        for g in range(groups):
            spread = spread_heads(doc_rows((q_ref,), d, lat_rows, cols[g]), mask)
            bd[d, g] = spread
            key = jnp.concatenate([load(at, cols[g]), kvl_ref[0, d, :, cols[g]]], axis=0)
            val = dot(key, spread, NT) + bias
            score[d, g, 0] = val
            top[d, g] = jnp.max(val, axis=0, keepdims=True)

    def more(parts):
        for k, (d, step, at, low, high) in enumerate(parts):
            bias = jnp.where(own_rows_of(at, low, high, keys), 0.0, FAR)
            for g in range(groups):
                val = dot(load(at, cols[g]), bd[d, g], NT) + bias
                score[d, g, jnp.minimum(step, score.shape[2] - 1), :tall] = val
                top[d, g] = jnp.maximum(top[d, g], jnp.max(val, axis=0, keepdims=True))

    more_chunks(spans, slots, more)
    for d in range(docs):
        at, low, high = slot_chunk(spans[d], 0, slots)
        for g in range(groups):
            expo = jnp.exp(score[d, g, 0] - top[d, g])
            tot[d, g] = jnp.sum(expo, axis=0, keepdims=True)
            val = jnp.concatenate([load(at, vals[g]), kvl_ref[0, d, :, vals[g]]], axis=0)
            acc[d, g] = dot(expo.astype(BF), val, TN)

    def more_values(parts):
        for d, step, at, low, high in parts:
            step = jnp.minimum(step, score.shape[2] - 1)
            own = own_rows_of(at, low, high, keys)
            for g in range(groups):
                expo = jnp.where(own, jnp.exp(score[d, g, step, :tall] - top[d, g]), 0.0)
                tot[d, g] = tot[d, g] + jnp.sum(expo, axis=0, keepdims=True)
                acc[d, g] = acc[d, g] + dot(expo.astype(BF), load(at, vals[g]), TN)

    more_chunks(spans, slots, more_values)
    half = chunks // 2
    for d in range(docs):
        rows_d = slice(d * lat_rows, (d + 1) * lat_rows)

        def by_head(ref):
            return jnp.concatenate(
                [
                    ref[d, g][:, h * lats : (h + 1) * lats]
                    for g in range(groups)
                    for h in range(GROUP)
                ],
                axis=0,
            )

        packed = pack_rows([by_head(top), by_head(tot)])
        outs = [gather_heads(acc[d, g], mask, lats).astype(BF) for g in range(groups)]
        for c in range(chunks):
            ref = keep_ref if c < half else send_ref
            part = slice(c * lat_rows, (c + 1) * lat_rows)
            for g in range(groups):
                ref[c % half, rows_d, cols[g]] = outs[g][part]
            ref[c % half, rows_d, inner:] = packed[part]


def attend_call(doc_ids, queries, kv_med, kv_lat, deps):
    chunks, _, inner = queries.shape
    micro, slots, keys, both = kv_med.shape
    docs, lat_rows = kv_lat.shape[1:3]
    lats = chunks * lat_rows
    rows = docs * lat_rows
    groups = HEADS // GROUP
    span = inner // groups
    wide = GROUP * lats
    half = chunks // 2
    longest = (slots - docs + CHUNK) // CHUNK
    out_spec = pl.BlockSpec((half, rows, inner + LANES), lambda i, ids: (0, i, 0))
    out_shape = jax.ShapeDtypeStruct((half, micro * rows, inner + LANES), BF)
    return hbm_call(
        functools.partial(attend_kernel, len(deps)),
        range(3),
        (),
        grid_spec=pltpu.PrefetchScalarGridSpec(
            num_scalar_prefetch=1,
            grid=(micro,),
            in_specs=[
                pl.BlockSpec((chunks, rows, inner), lambda i, ids: (0, i, 0)),
                pl.BlockSpec((1, slots, keys, both), lambda i, ids: (i, 0, 0, 0)),
                pl.BlockSpec((1, docs, lat_rows, both), lambda i, ids: (i, 0, 0, 0)),
            ]
            + [ANY] * len(deps),
            out_specs=[out_spec, out_spec],
            scratch_shapes=[
                pltpu.VMEM((docs, groups, wide, span), BF),
                pltpu.VMEM((docs, groups, longest, CHUNK * keys + lat_rows, wide), F32),
                pltpu.VMEM((docs, groups, wide, span), F32),
                pltpu.VMEM((docs, groups, 1, wide), F32),
                pltpu.VMEM((docs, groups, 1, wide), F32),
            ],
        ),
        out_shape=[out_shape, out_shape],
        compiler_params=params(40),
        cost_estimate=cost(13),
        name="attend",
    )(doc_ids, queries, kv_med, kv_lat, *deps)


def join_kernel(last, flip, a_ref, b_ref, *rest):
    out_ref = rest[-1]
    inner = a_ref.shape[2] - LANES
    count = a_ref.shape[0]
    for c in range(count):
        first, second = a_ref[c], b_ref[count - 1 - c if flip else c]
        pack_a, pack_b = first[:, inner:], second[:, inner:]
        top_a, top_b = widen(pack_a, 0, inner), widen(pack_b, 0, inner)
        best = jnp.maximum(top_a, top_b)
        fac_a, fac_b = jnp.exp(top_a - best), jnp.exp(top_b - best)
        out = fac_a * first[:, :inner].astype(F32) + fac_b * second[:, :inner].astype(F32)
        if last:
            total = fac_a * widen(pack_a, 1, inner) + fac_b * widen(pack_b, 1, inner)
            out = out / total
        out_ref[c, :, :inner] = out.astype(BF)
        small_a, small_b = narrow(pack_a, 0), narrow(pack_b, 0)
        small = jnp.maximum(small_a, small_b)
        sum_ab = jnp.exp(small_a - small) * narrow(pack_a, 1) + jnp.exp(
            small_b - small
        ) * narrow(pack_b, 1)
        if last:
            lane = lax.broadcasted_iota(jnp.int32, sum_ab.shape, 1)
            lse = jnp.where(lane < HEADS, small + jnp.log(jnp.maximum(sum_ab, 1e-30)), 0.0)
            out_ref[c, :, inner:] = pack_cols([lse])
        else:
            out_ref[c, :, inner:] = pack_cols([small, sum_ab])


def join_call(first, second, last, flip, deps=()):
    count, rows, cols = first.shape
    block = min(rows, 128)
    spec = pl.BlockSpec((count, block, cols), lambda i: (0, i, 0))
    return pl.pallas_call(
        functools.partial(join_kernel, last, flip),
        grid=(rows // block,),
        in_specs=[spec, spec] + [ANY] * len(deps),
        out_specs=spec,
        out_shape=jax.ShapeDtypeStruct(first.shape, BF),
        compiler_params=params(10),
        cost_estimate=cost(3.5),
        name="join_last" if last else "join_first",
    )(first, second, *deps)


def cot_units_kernel(own, far, near, both, wr_ref, units_ref, cot_ref, token_ref):
    token_ref[...] = jnp.zeros_like(token_ref)
    for c, ref in enumerate((own, far, near, both)):
        cot_ref[c] = ref[...]
    for c in range(0, 4, 2):
        rows = own.shape[0]
        pair = cot_ref[c : c + 2].reshape(2 * rows, own.shape[1])
        units_ref[c : c + 2] = dot(pair, wr_ref[...], NT).reshape(2, rows, wr_ref.shape[0])


def cot_units_call(chunks, w_red):
    rows, width = chunks[0].shape
    count = len(chunks)
    return hbm_call(
        cot_units_kernel,
        (0, 4),
        (0, 1),
        (1, 2, 3),
        in_specs=[pl.BlockSpec(memory_space=pltpu.VMEM)] * 5,
        out_shape=[
            jax.ShapeDtypeStruct((count, rows, w_red.shape[0]), F32),
            jax.ShapeDtypeStruct((count, rows, width), BF),
            TOKEN,
        ],
        compiler_params=params(24),
        cost_estimate=cost(6),
        name="cot_units",
    )(*chunks, w_red)


def ff_kernel(
    lat_ref,
    near_ref,
    far_ref,
    units_ref,
    wo_ref,
    we_ref,
    wr_ref,
    gain_ref,
    shift_ref,
    mixed_ref,
    ln_ref,
    act_ref,
    gpre_ref,
    up_own,
    up_keep,
    up_send,
    out_own,
    out_keep,
    out_send,
):
    i = pl.program_id(0)
    half = pl.num_programs(0) // 2
    att = jnp.where(i < half, near_ref[0], far_ref[0])
    mixed = lat_ref[0].astype(F32) + dot(att, wo_ref[...], NN)
    hat, _ = standardize(mixed)
    ln = (hat * gain_ref[...] + shift_ref[...]).astype(BF)
    ln_ref[0] = ln
    pre = dot(ln, we_ref[...], NN)
    cdf = 0.5 + 0.5 * lax.erf(pre * (0.5**0.5))
    slope = cdf + pre * (0.3989422804014327 * jnp.exp(-0.5 * pre * pre))
    act = (pre * cdf).astype(BF)
    act_ref[0] = act
    gpre = (units_ref[0] * slope).astype(BF)
    gpre_ref[0] = gpre
    up = dot(gpre, we_ref[...], NT).astype(BF)
    out = dot(act, wr_ref[...], NN).astype(BF)

    @pl.when(i == 0)
    def _():
        mixed_ref[...] = mixed
        up_own[...] = up
        out_own[...] = out

    @pl.when(i == 1)
    def _():
        up_keep[...] = up
        out_keep[...] = out

    @pl.when(i >= half)
    def _():
        up_send[0] = up
        out_send[0] = out


def ff_call(latents, near, far, cot_units, w_output, w_exp, w_red, gain, shift):
    chunks, rows, width = latents.shape
    inner = w_output.shape[0]
    units = w_exp.shape[1]
    half = chunks // 2

    def chunk(cols):
        return pl.BlockSpec((1, rows, cols), lambda i: (i, 0, 0))

    def first(cols):
        return pl.BlockSpec((1, rows, cols), lambda i: (jnp.minimum(i, half - 1), 0, 0))

    def second(cols):
        return pl.BlockSpec((1, rows, cols), lambda i: (jnp.maximum(i - half, 0), 0, 0))

    def fixed(*shape):
        return pl.BlockSpec(shape, lambda i: (0,) * len(shape))

    def out(count, cols):
        return jax.ShapeDtypeStruct((count, rows, cols), BF)

    return hbm_call(
        ff_kernel,
        (0, 3, 4, 5, 6),
        (0, 1, 2, 3, 4, 7, 8, 9),
        (1, 2),
        grid=(chunks,),
        in_specs=[
            chunk(width),
            first(inner),
            second(inner),
            chunk(units),
            fixed(inner, width),
            fixed(width, units),
            fixed(units, width),
            fixed(1, width),
            fixed(1, width),
        ],
        out_specs=[
            fixed(rows, width),
            chunk(width),
            chunk(units),
            chunk(units),
            fixed(rows, width),
            fixed(rows, width),
            second(width),
            fixed(rows, width),
            fixed(rows, width),
            second(width),
        ],
        out_shape=[
            jax.ShapeDtypeStruct((rows, width), F32),
            out(chunks, width),
            out(chunks, units),
            out(chunks, units),
            jax.ShapeDtypeStruct((rows, width), BF),
            jax.ShapeDtypeStruct((rows, width), BF),
            out(half, width),
            jax.ShapeDtypeStruct((rows, width), BF),
            jax.ShapeDtypeStruct((rows, width), BF),
            out(half, width),
        ],
        compiler_params=params(40),
        cost_estimate=cost(18),
        name="feed_forward",
    )(latents, near, far, cot_units, w_output, w_exp, w_red, gain, shift)


def ff_weights_kernel(ln_ref, gpre_ref, act_ref, cot_ref, *rest):
    out_ref = rest[-1]
    count, rows, width = out_ref.shape
    half = rows // 2
    for part, (left, right) in enumerate(((ln_ref, gpre_ref), (act_ref, cot_ref))):
        product = dot(left[...], right[...], TN).astype(BF)
        out_ref[:, part * half : (part + 1) * half, :] = product.reshape(count, half, width)


def ff_weights_call(ln_ff, grad_pre, hidden_act, cot, imgs, deps):
    tokens, width = ln_ff.shape
    units = grad_pre.shape[1]
    half = units // imgs
    steps = 2
    left = pl.BlockSpec((tokens, width // steps), lambda i: (0, i))
    right = pl.BlockSpec((tokens, width), lambda i: (0, 0))
    return hbm_call(
        ff_weights_kernel,
        range(4),
        (),
        grid=(steps,),
        in_specs=[left, right, left, right] + [ANY] * len(deps),
        out_specs=pl.BlockSpec((imgs // steps, 2 * half, width), lambda i: (i, 0, 0)),
        out_shape=pltpu.HBM((imgs, 2 * half, width), BF),
        compiler_params=params(28),
        cost_estimate=cost(9),
        name="ff_weights",
    )(ln_ff, grad_pre, hidden_act, cot, *deps)


def half_sum_kernel(keep_ref, sent_ref, out_ref, token_ref):
    token_ref[...] = jnp.zeros_like(token_ref)
    out_ref[...] = (keep_ref[...].astype(F32) + sent_ref[1].astype(F32)).astype(BF)


def half_sum(keep, sent):
    return hbm_call(
        half_sum_kernel,
        (0,),
        (),
        (1,),
        in_specs=[pl.BlockSpec(memory_space=pltpu.VMEM)] * 2,
        out_shape=[jax.ShapeDtypeStruct(keep.shape, BF), TOKEN],
        compiler_params=params(6),
        cost_estimate=cost(0.1),
        name="half_sum",
    )(keep, sent)


def mixed_back_kernel(own_ref, near_ref, far_ref, mixed_ref, cot_ref, wo_ref, gain_ref, *rest):
    gm_ref, gb_ref, ga_first, ga_second, dg_ref, ds_ref = rest[-6:]
    up = own_ref[...].astype(F32) + near_ref[0].astype(F32) + far_ref[...].astype(F32)
    hat, inv = standardize(mixed_ref[...])
    back, gains = norm_back(hat, inv, gain_ref[...], up)
    grad = cot_ref[...].astype(F32) + back
    gm_ref[...] = grad
    branch = grad.astype(BF)
    gb_ref[...] = branch
    grad_att = dot(branch, wo_ref[...], NT).astype(BF)
    cut = ga_first.shape[1]
    ga_first[...] = grad_att[:, :cut]
    ga_second[...] = grad_att[:, cut:]
    dg_ref[...] = jnp.sum(gains, axis=0, keepdims=True)
    ds_ref[...] = jnp.sum(up, axis=0, keepdims=True)


def mixed_back_call(own, near, far, mixed, cot, w_output, gain, deps):
    rows, width = mixed.shape
    inner = w_output.shape[0]
    return hbm_call(
        mixed_back_kernel,
        (0, 3, 4, 5),
        (0,),
        (1, 2),
        in_specs=[pl.BlockSpec(memory_space=pltpu.VMEM)] * 7 + [ANY] * len(deps),
        out_shape=[
            jax.ShapeDtypeStruct((rows, width), F32),
            jax.ShapeDtypeStruct((rows, width), BF),
            jax.ShapeDtypeStruct((rows, inner // 2), BF),
            jax.ShapeDtypeStruct((rows, inner // 2), BF),
            jax.ShapeDtypeStruct((1, width), F32),
            jax.ShapeDtypeStruct((1, width), F32),
        ],
        compiler_params=params(20),
        cost_estimate=cost(4),
        name="mixed_back",
    )(own, near, far, mixed, cot, w_output, gain, *deps)


def part_kernel(index_ref, e_ref, r_ref, eo_ref, ro_ref):
    eo_ref[...] = e_ref[...]
    ro_ref[...] = r_ref[...]


def part_call(index, w_expand, w_reduce, imgs, parts):
    width, ff = w_expand.shape
    unit = ff // (imgs * parts)
    return hbm_call(
        part_kernel,
        range(2),
        range(2),
        grid_spec=pltpu.PrefetchScalarGridSpec(
            num_scalar_prefetch=1,
            grid=(imgs,),
            in_specs=[
                pl.BlockSpec((width, unit), lambda i, p: (0, i * parts + p[0])),
                pl.BlockSpec((unit, width), lambda i, p: (i * parts + p[0], 0)),
            ],
            out_specs=[
                pl.BlockSpec((width, unit), lambda i, p: (0, i)),
                pl.BlockSpec((unit, width), lambda i, p: (i, 0)),
            ],
        ),
        out_shape=[
            jax.ShapeDtypeStruct((width, imgs * unit), BF),
            jax.ShapeDtypeStruct((imgs * unit, width), BF),
        ],
        compiler_params=params(6),
        name="weight_part",
    )(index, w_expand, w_reduce)


def attend_back_kernel(
    group,
    deps,
    doc_ref,
    index_ref,
    q_ref,
    go_own,
    go_far,
    go_near,
    go_both,
    att_near,
    att_far,
    lse_near,
    lse_far,
    k_ref,
    v_ref,
    kl_ref,
    vl_ref,
    hat_ref,
    norm_ref,
    vec_in,
    lat_hat_hbm,
    wkv_hbm,
    wq_hbm,
    extra_hbm,
    *rest,
):
    gkv_ref, gkvl_ref, gq_ref, keep_ref, send_ref, vec_ref = rest[deps : deps + 6]
    bdq, bdo, acc, stat, h_med, h_lat, sums, wide_rows = rest[deps + 6 : -6]
    lat_hat_ref, wk_ref, wv_ref, wq_ref, extra_ref, sems = rest[-6:]
    chunks, _, span = q_ref.shape
    docs, lat_rows = kl_ref.shape[1:3]
    lats = chunks * lat_rows
    slots, keys = k_ref.shape[1:3]
    micro = pl.program_id(0)
    mask = block_mask(span // GROUP, lats)
    every = slice(None)
    scale = (span // GROUP) ** (-0.5)
    go_refs = (go_own, go_far, go_near, go_both)
    att_refs, lse_refs = (att_near, att_far), (lse_near, lse_far)

    groups = HEADS // GROUP

    def columns(ref, at):
        return ref.at[:, at * span : (at + 1) * span]

    copies = [
        pltpu.make_async_copy(source, target, sems.at[i])
        for i, (source, target) in enumerate(
            (
                (lat_hat_hbm, lat_hat_ref),
                (columns(wkv_hbm, group), wk_ref),
                (columns(wkv_hbm, groups + group), wv_ref),
                (columns(wq_hbm, group), wq_ref),
                (extra_hbm, extra_ref),
            )
        )
    ]

    @pl.when(micro == 0)
    def _():
        for copy in copies:
            copy.start()

    spans = doc_spans(doc_ref, micro, docs, slots)
    tall = CHUNK * keys

    def pair(key, value, bias, d):
        score = dot(key, bdq[d], NT) + bias
        prob = jnp.exp(score - stat[d, 0:1])
        dprob = dot(value, bdo[d], NT)
        dscore = (prob * (dprob - stat[d, 1:2])).astype(BF)
        grad_key = dot(dscore, bdq[d], NN).astype(BF)
        grad_value = dot(prob.astype(BF), bdo[d], NN).astype(BF)
        grad_query = dot(dscore, key, TN)
        return grad_key, grad_value, grad_query

    def load(ref, at):
        return ref[0, pl.ds(at, CHUNK)].reshape(tall, span)

    def store(at, own, grad_key, grad_value):
        part = pl.ds(pl.multiple_of(at * keys, keys), tall)
        gkv_ref[part, :span] = jnp.where(own, grad_key, gkv_ref[part, :span])
        gkv_ref[part, span:] = jnp.where(own, grad_value, gkv_ref[part, span:])

    sel = pick((HEADS, LANES), lambda r, c: holds(c, r, 0))
    size = span // GROUP
    head_sel = pick((HEADS, span), lambda r, c: c // size == r)

    def row(by_head, at):
        return jnp.concatenate([by_head[at + h : at + h + 1] for h in range(GROUP)], axis=1)

    for d in range(docs):
        out_grad = doc_rows(go_refs, d, lat_rows, every)
        bdq[d] = spread_heads(doc_rows((q_ref,), d, lat_rows, every), mask)
        bdo[d] = spread_heads(out_grad, mask)
        lse = dot(sel, doc_rows(lse_refs, d, lat_rows, every), NT)
        stat[d, 0:1] = row(lse, group * GROUP)
        attended = doc_rows(att_refs, d, lat_rows, every)
        high, low, _ = terms(out_grad.astype(F32) * attended.astype(F32))
        stat[d, 1:2] = row(dot(head_sel, high, NT) + dot(head_sel, low, NT), 0)
    for d in range(docs):
        rows_d = pl.ds((micro * docs + d) * lat_rows, lat_rows)
        at, low, high = slot_chunk(spans[d], 0, slots)
        own = own_rows_of(at, low, high, keys)
        bias = jnp.concatenate([jnp.where(own, 0.0, FAR), jnp.zeros((lat_rows, 1), F32)], axis=0)
        key = jnp.concatenate([load(k_ref, at), kl_ref[0, d]], axis=0)
        value = jnp.concatenate([load(v_ref, at), vl_ref[0, d]], axis=0)
        grad_key, grad_value, grad_query = pair(key, value, bias, d)
        store(at, own, grad_key[:tall], grad_value[:tall])
        gkvl_ref[rows_d, :span] = grad_key[tall:]
        gkvl_ref[rows_d, span:] = grad_value[tall:]
        acc[d] = grad_query

    def more(parts):
        done = []
        for d, step, at, low, high in parts:
            own = own_rows_of(at, low, high, keys)
            bias = jnp.where(own, 0.0, FAR)
            done.append((d, at, own, *pair(load(k_ref, at), load(v_ref, at), bias, d)))
        for d, at, own, grad_key, grad_value, grad_query in done:
            store(at, own, grad_key, grad_value)
            acc[d] = acc[d] + grad_query

    more_chunks(spans, slots, more)
    for d in range(docs):
        full = gather_heads(acc[d], mask, lats).astype(BF)
        for c in range(chunks):
            gq_ref[c, pl.ds(micro * docs * lat_rows + d * lat_rows, lat_rows)] = full[
                c * lat_rows : (c + 1) * lat_rows
            ]
    part = dot(hat_ref[...], gkv_ref[...], TN)
    part_sum = jnp.sum(gkv_ref[...].astype(F32), axis=0, keepdims=True)

    @pl.when(micro == 0)
    def _():
        h_med[...] = part
        sums[0:1, :] = part_sum

    @pl.when(micro > 0)
    def _():
        h_med[...] = h_med[...] + part
        sums[0:1, :] = sums[0:1, :] + part_sum

    @pl.when(micro == pl.num_programs(0) - 1)
    def _():
        width = h_med.shape[0]
        step = 128
        tokens = lat_hat_ref.shape[0] * lat_hat_ref.shape[1]
        for copy in copies:
            copy.wait()
        h_lat[...] = dot(lat_hat_ref[0], gkvl_ref[...], TN)
        sums[1:2, :] = jnp.sum(gkvl_ref[...].astype(F32), axis=0, keepdims=True)
        quer_all = gq_ref[...].reshape(tokens, span)
        h_q = dot(lat_hat_ref[...].reshape(tokens, width), quer_all, TN)
        quer_sum = jnp.sum(quer_all.astype(F32), axis=0, keepdims=True) * scale
        for at in range(0, width, step):
            part = slice(at, at + step)
            norm = norm_ref[:, part].T
            med, lat, quer = h_med[part, :], h_lat[part, :], h_q[part] * scale
            med_sum, lat_sum = sums[0:1, :], sums[1:2, :]
            wide_rows[part, : 2 * span] = (
                norm[:, 0:1] * med
                + norm[:, 1:2] * med_sum
                + norm[:, 2:3] * lat
                + norm[:, 3:4] * lat_sum
            ).astype(BF)
            wide_rows[part, 2 * span :] = (
                norm[:, 2:3] * quer + norm[:, 3:4] * quer_sum
            ).astype(BF)
            wkv = jnp.concatenate([wk_ref[part, :], wv_ref[part, :]], axis=1).astype(F32)
            wq = wq_ref[part, :].astype(F32)

            def total(value):
                return jnp.sum(value, axis=1, keepdims=True)

            vec = jnp.concatenate(
                [
                    total(wkv * med),
                    total(wkv * med_sum),
                    total(wkv * lat) + total(wq * quer),
                    total(wkv * lat_sum) + total(wq * quer_sum),
                    jnp.zeros((step, step - 4), F32),
                ],
                axis=1,
            )
            rows = vec.T[: vec_ref.shape[0]]
            vec_ref[:, part] = rows if group == 0 else vec_in[:, part] + rows
        if len(keep_ref.shape) == 2:
            keep_ref[...] = wide_rows[...]
            return
        imgs, two, height, _ = keep_ref.shape
        share = width // imgs
        tall = share // (2 * two)
        bit = lax.rem(index_ref[0], 2)
        for ref, mine in ((keep_ref, bit), (send_ref, 1 - bit)):
            for i in range(imgs):
                for y in range(two):
                    at = pl.multiple_of(i * share + 2 * y * tall + mine * tall, tall)
                    rows = wide_rows[pl.ds(at, tall), :]
                    ref[i, y, :tall] = rows[:, : 2 * span]
                    ref[i, y, tall : tall + tall // 2, :span] = rows[: tall // 2, 2 * span :]
                    ref[i, y, tall : tall + tall // 2, span:] = rows[tall // 2 :, 2 * span :]
                    start = tall + tall // 2
                    if group == 0:
                        size = extra_ref.shape[0] // (2 * two * imgs)
                        at = pl.multiple_of((i * two + y) * 2 * size + mine * size, size)
                        rows = extra_ref[pl.ds(at, size), :]
                        ref[i, y, start : start + size] = rows[:, : 2 * span]
                        ref[i, y, start + size : start + 2 * size] = rows[:, 2 * span :]
                    else:
                        rows = jnp.zeros((height - start, 2 * span), F32)
                        if y == 0:
                            at = slice(i * share, (i + 1) * share)
                            six = jnp.concatenate([vec_ref[:4, at], extra_ref[:2, at]], axis=0)
                            six = jnp.where(mine == 0, six, 0.0)
                            six = jnp.pad(six, ((0, height - start - 6), (0, 2 * span - share)))
                            rows = six
                        ref[i, y, start:] = rows.astype(BF)


def laid_out(width, imgs, inner):
    share = width // imgs
    return share % 128 == 0 and share <= inner and inner % (64 * imgs) == 0


def attend_back_call(
    group,
    doc_ids,
    queries,
    grad_att,
    att,
    kv_med,
    kv_lat,
    hat_med,
    hat_lat,
    w_keyval,
    w_query,
    norms,
    extra,
    vectors,
    index,
    imgs,
    deps,
):
    chunks, _, inner = queries.shape
    micro, slots, keys, both = kv_med.shape
    docs, lat_rows = kv_lat.shape[1:3]
    lats = chunks * lat_rows
    width = hat_med.shape[1]
    groups = HEADS // GROUP
    span = inner // groups
    wide = GROUP * lats
    rows = slots * keys
    lat_block = docs * lat_rows

    if laid_out(width, imgs, inner):
        tall = width // (imgs * chunks)
        height = tall + tall // 2 + (2 * inner // (imgs * chunks) if group == 0 else 16)
        result = jax.ShapeDtypeStruct((imgs, chunks // 2, height, inner), BF)
    else:
        result = jax.ShapeDtypeStruct((width, 3 * span), BF)
    result_spec = pl.BlockSpec(result.shape, lambda i, ids, p: (0,) * len(result.shape))

    def cols(at, *tail):
        return pl.BlockSpec(
            (1,) + tail, lambda i, ids, p: (i,) + (0,) * (len(tail) - 1) + (at,)
        )

    def tokens(at, size, count=chunks):
        return pl.BlockSpec((count, lat_block, size), lambda i, ids, p: (0, i, at))

    def fixed(at, size):
        return pl.BlockSpec((width, size), lambda i, ids, p: (0, at))

    return hbm_call(
        functools.partial(attend_back_kernel, group, len(deps)),
        range(20),
        (0, 1, 2),
        grid_spec=pltpu.PrefetchScalarGridSpec(
            num_scalar_prefetch=2,
            grid=(micro,),
            in_specs=[
                tokens(group, span),
                *[tokens(0, span, 1)] * 4,
                *[tokens(group, span, 2)] * 2,
                *[tokens(inner // LANES, LANES, 2)] * 2,
                cols(group, slots, keys, span),
                cols(groups + group, slots, keys, span),
                cols(group, docs, lat_rows, span),
                cols(groups + group, docs, lat_rows, span),
                pl.BlockSpec((rows, width), lambda i, ids, p: (i, 0)),
                pl.BlockSpec(norms.shape, lambda i, ids, p: (0, 0)),
                pl.BlockSpec(vectors.shape, lambda i, ids, p: (0, 0)),
                ANY,
                ANY,
                ANY,
                ANY,
            ]
            + [ANY] * len(deps),
            out_specs=[
                pl.BlockSpec((rows, 2 * span), lambda i, ids, p: (i, 0)),
                pl.BlockSpec((micro * lat_block, 2 * span), lambda i, ids, p: (0, 0)),
                pl.BlockSpec((chunks, micro * lat_block, span), lambda i, ids, p: (0, 0, 0)),
                result_spec,
                result_spec,
                pl.BlockSpec(vectors.shape, lambda i, ids, p: (0, 0)),
            ],
            scratch_shapes=[
                pltpu.VMEM((docs, wide, span), BF),
                pltpu.VMEM((docs, wide, span), BF),
                pltpu.VMEM((docs, wide, span), F32),
                pltpu.VMEM((docs, 2, wide), F32),
                pltpu.VMEM((width, 2 * span), F32),
                pltpu.VMEM((width, 2 * span), F32),
                pltpu.VMEM((2, 2 * span), F32),
                pltpu.VMEM((width, 3 * span), BF),
                pltpu.VMEM(hat_lat.shape, BF),
                pltpu.VMEM((width, span), BF),
                pltpu.VMEM((width, span), BF),
                pltpu.VMEM((width, span), BF),
                pltpu.VMEM(extra.shape, extra.dtype),
                pltpu.SemaphoreType.DMA((5,)),
            ],
        ),
        out_shape=[
            jax.ShapeDtypeStruct((micro * rows, 2 * span), BF),
            jax.ShapeDtypeStruct((micro * lat_block, 2 * span), BF),
            jax.ShapeDtypeStruct((chunks, micro * lat_block, span), BF),
            result,
            result,
            jax.ShapeDtypeStruct(vectors.shape, F32),
        ],
        compiler_params=params(48),
        cost_estimate=cost(3),
        name="attend_back",
    )(
        doc_ids,
        index,
        queries,
        *grad_att,
        *att,
        *att,
        kv_med,
        kv_med,
        kv_lat,
        kv_lat,
        hat_med,
        norms,
        vectors,
        hat_lat,
        w_keyval,
        w_query,
        extra,
        *deps,
    )


def media_back_kernel(media_ref, ga_ref, gb_ref, wka_ref, wva_ref, wkb_ref, wvb_ref, gain_ref, *rest):
    out_ref, token_ref = rest[-2:]
    token_ref[...] = jnp.zeros_like(token_ref)
    wa = jnp.concatenate([wka_ref[...], wva_ref[...]], axis=1)
    wb = jnp.concatenate([wkb_ref[...], wvb_ref[...]], axis=1)
    rows = media_ref.shape[0]
    step = min(rows, 256)

    for at in range(0, rows, step):
        part = pl.ds(at, step)
        up = dot(ga_ref[part, :], wa, NT) + dot(gb_ref[part, :], wb, NT)
        hat, inv = standardize(media_ref[part, :].astype(F32))
        back, _ = norm_back(hat, inv, gain_ref[...], up)
        out_ref[part, :] = back.astype(BF)


def key_value_blocks(width, span):
    groups = HEADS // GROUP
    return [
        pl.BlockSpec((width, span), lambda i, at=at: (0, at))
        for g in range(groups)
        for at in (g, groups + g)
    ]


def media_back_call(media, grad_a, grad_b, w_keyval, gain, first, steps, whole, deps):
    rows, width = media.shape
    half = grad_a.shape[1]
    block = 512
    fixed = lambda i: (0, 0)
    moving = lambda i: (first + i, 0)
    extra = tuple(deps) if whole is None else tuple(deps) + (whole,)
    return hbm_call(
        media_back_kernel,
        range(8),
        (0,),
        grid=(steps,),
        in_specs=[
            pl.BlockSpec((block, width), moving),
            pl.BlockSpec((block, half), moving),
            pl.BlockSpec((block, half), moving),
            *key_value_blocks(width, half // 2),
            pl.BlockSpec((1, width), fixed),
        ]
        + [ANY] * len(extra),
        out_specs=[pl.BlockSpec((block, width), moving), pl.BlockSpec(TOKEN.shape, fixed)],
        out_shape=[jax.ShapeDtypeStruct((rows, width), BF), TOKEN],
        input_output_aliases={} if whole is None else {7 + len(extra): 0},
        compiler_params=params(28),
        cost_estimate=cost(2.5 * steps),
        name="media_back",
    )(media, grad_a, grad_b, w_keyval, w_keyval, w_keyval, w_keyval, gain, *extra)


def swap(value, axis, bit):
    size = lax.axis_size(axis)
    return lax.ppermute(value, axis, [(i, i ^ bit) for i in range(size)])


def gather_chunks(own):
    far = swap(own, "patch", 2)
    return own, far, swap(own, "patch", 1), swap(far, "patch", 1)


def gather_patch(own):
    return jnp.stack(gather_chunks(own))


def add(first, second):
    return (first.astype(F32) + second.astype(F32)).astype(BF)


def sum_kernel(ways, terms_in, *refs):
    refs[-1][...] = jnp.zeros_like(refs[-1])
    for k in range(ways):
        value = refs[1 + k][...]
        if terms_in == 2:
            value = (value.astype(F32) + refs[1 + ways + k][...].astype(F32)).astype(BF)
        refs[k - ways - 1][...] = value


def split_sum(first, second, lead, rest, ways, mine, deps):
    count = 1
    for size in lead:
        count *= size
    tail = first.shape[-2:]
    inner = 1
    for size in rest:
        inner *= size
    flat = (count, ways, inner) + tail
    steps = 2 if count % 2 == 0 and first.size * 2 > (1 << 20) else 1
    block = (count // steps, 1, inner) + tail
    outs = [pl.BlockSpec(block, lambda i, m: (i, 0, 0, 0, 0))] * ways
    parts = [
        pl.BlockSpec(block, lambda i, m, k=k: (i, jnp.bitwise_xor(m[0], k), 0, 0, 0))
        for k in range(ways)
    ]
    values = [v.reshape(flat) for v in (first, second) if v is not None]
    *halves, token = pl.pallas_call(
        functools.partial(sum_kernel, ways, len(values)),
        grid_spec=pltpu.PrefetchScalarGridSpec(
            num_scalar_prefetch=1,
            grid=(steps,),
            in_specs=parts * len(values) + [ANY] * len(deps),
            out_specs=outs + [pl.BlockSpec(TOKEN.shape, lambda i, m: (0, 0))],
        ),
        out_shape=[jax.ShapeDtypeStruct((count, 1, inner) + tail, BF)] * ways + [TOKEN],
        compiler_params=params(12),
        cost_estimate=cost(0.3),
        name="split_sum",
    )(mine[None], *[v for v in values for _ in range(ways)], *deps)
    return [h.reshape(lead + rest + tail) for h in halves], token


class Scatter:
    def __init__(self, value, transit, axes, order, scope):
        self.places = [
            (axis, bit)
            for axis in axes
            for bit in reversed(range(lax.axis_size(axis).bit_length() - 1))
            if axis == "img" or any(axis == a and bit in bits for a, bits in order)
        ]
        self.order = list(order)
        self.scope = scope
        self.value, transit = (
            v.reshape((2,) * len(self.places) + v.shape[len(axes) :]) for v in (value, transit)
        )
        self.transit = [transit]

    def step(self, deps=()):
        with jax.named_scope(self.scope):
            if not self.order:
                return ()
            axis, bits = self.order.pop(0)
            place = self.places.index((axis, bits[-1]))
            lead = (2,) * place
            for bit in bits:
                self.places.remove((axis, bit))
            ways = 2 ** len(bits)
            mine = lax.rem(lax.shift_right_logical(lax.axis_index(axis), bits[0]), ways)
            rest = (2,) * (len(self.places) - place)
            (self.value, *send), token = split_sum(
                self.value, self.transit[0], lead, rest, ways, mine, deps
            )
            self.transit = [
                swap(part, axis, (k + 1) << bits[0]) for k, part in enumerate(send)
            ]
            return (token,)


def first_bits():
    return [("img", (bit,)) for bit in range(lax.axis_size("img").bit_length() - 3)]


def last_kernel(index_ref, *refs):
    refs[-1][...] = jnp.zeros_like(refs[-1])
    cut = refs[0].shape[1]
    outs = refs[-1 - refs[0].shape[0] : -1]
    for k, out in enumerate(outs):
        at = jnp.bitwise_xor(index_ref[0], k)
        for part, value, other in ((slice(0, cut), *refs[:2]), (slice(cut, None), *refs[2:4])):
            out[part] = (value[at].astype(F32) + other[at].astype(F32)).astype(BF)


def last_step(first, second, deps):
    count = lax.axis_size("img").bit_length() - 1
    low = max(count - 2, 0)
    ways = 2 ** (count - low)
    values = [
        v.reshape((ways,) + v.shape[-2:])
        for v in (first.value, first.transit[0], second.value, second.transit[0])
    ]
    rows = values[0].shape[1] + values[2].shape[1]
    shape = jax.ShapeDtypeStruct((rows, values[0].shape[2]), BF)
    mine = lax.shift_right_logical(lax.axis_index("img"), low)
    whole = lambda v: pl.BlockSpec(v.shape, lambda i, m: (0,) * len(v.shape))
    own, *send, token = pl.pallas_call(
        last_kernel,
        grid_spec=pltpu.PrefetchScalarGridSpec(
            num_scalar_prefetch=1,
            grid=(1,),
            in_specs=[whole(v) for v in values] + [ANY] * len(deps),
            out_specs=[whole(shape)] * ways + [whole(TOKEN)],
        ),
        out_shape=[shape] * ways + [TOKEN],
        compiler_params=params(6),
        cost_estimate=cost(0.3),
        name="last_sum",
    )(mine[None], *values, *deps)
    sent = [swap(part, "img", (k + 1) << low) for k, part in enumerate(send)]
    return own, sent, token


def reduce_rest(keep, send, scope):
    with jax.named_scope(scope):
        transit = swap(send, "patch", 1)
    return Scatter(keep, transit, ("img", "patch"), [("patch", (1,))] + first_bits(), scope)


def in_order(chunks):
    me = lax.axis_index("patch")
    out = []
    for j in range(4):
        apart = jnp.bitwise_xor(me, j)
        at = 2 * jnp.bitwise_and(apart, 1) + lax.shift_right_logical(apart, 1)
        out.append(lax.dynamic_index_in_dim(chunks, at, 0, keepdims=False))
    return jnp.stack(out)


def place_kernel(index_ref, own, far, near, both, *rest):
    expand_ref, reduce_ref, token_ref = rest[-3:]
    token_ref[...] = jnp.zeros_like(token_ref)
    rows = expand_ref.shape[0]
    parts = 4
    unit = reduce_ref.shape[0] // parts
    blocks = expand_ref.shape[1] // (parts * unit)
    columns = reduce_ref.shape[1]
    step = pl.program_id(0)
    for bits, ref in enumerate((own, near, far, both)):
        part = jnp.bitwise_xor(index_ref[0], bits)
        for k in range(blocks):
            source = pl.ds(pl.multiple_of((step * blocks + k) * unit, unit), unit)
            target = pl.ds(pl.multiple_of((k * parts + part) * unit, unit), unit)
            expand_ref[:, target] = ref[:rows, source].astype(F32)
        source = pl.ds(pl.multiple_of(step * columns, columns), columns)
        target = pl.ds(pl.multiple_of(part * unit, unit), unit)
        reduce_ref[target, :] = ref[rows:, source].astype(F32)


def place_call(index, chunks, rows, imgs, deps):
    both, units = chunks[0].shape
    unit = units // imgs
    parts = len(chunks)
    steps = 2
    return pl.pallas_call(
        place_kernel,
        grid_spec=pltpu.PrefetchScalarGridSpec(
            num_scalar_prefetch=1,
            grid=(steps,),
            in_specs=[pl.BlockSpec((both, units), lambda i, p: (0, 0))] * parts
            + [ANY] * len(deps),
            out_specs=[
                pl.BlockSpec((rows, parts * units // steps), lambda i, p: (0, i)),
                pl.BlockSpec((parts * unit, units // steps), lambda i, p: (0, i)),
                pl.BlockSpec(TOKEN.shape, lambda i, p: (0, 0)),
            ],
        ),
        out_shape=[
            jax.ShapeDtypeStruct((rows, parts * units), F32),
            jax.ShapeDtypeStruct((parts * unit, units), F32),
            TOKEN,
        ],
        compiler_params=params(16),
        cost_estimate=cost(0.1),
        name="place_units",
    )(index, *chunks, *deps)


def local(
    latents,
    media,
    doc_ids,
    w_query,
    w_keyval,
    w_output,
    w_expand,
    w_reduce,
    media_gain,
    media_shift,
    latent_gain,
    latent_shift,
    ff_gain,
    ff_shift,
    out_grad,
):
    micro, docs, lat_rows, width = latents.shape
    slots, keys = media.shape[1:3]
    inner = w_query.shape[1]
    ff = w_expand.shape[1]
    head_size = inner // HEADS
    scale = head_size ** (-0.5)
    parts = lax.axis_size("patch")
    imgs = lax.axis_size("img")
    patch_index = lax.axis_index("patch")
    own_rows = micro * docs * lat_rows
    all_rows = own_rows * parts
    groups = HEADS // GROUP
    span = inner // groups
    unit = ff // (imgs * parts)

    latents_own = latents.reshape(own_rows, width)
    cot_own = out_grad.reshape(own_rows, width)
    media_flat = media.reshape(-1, width)
    with jax.named_scope("gather_latents"):
        latents_far = swap(latents_own, "patch", 2)
        latents_near = swap(latents_own, "patch", 1)

    hat_med, kv_med, token = kv_call(media_flat, media_gain[None], media_shift[None], w_keyval)
    kv_med = kv_med.reshape(micro, slots, keys, 2 * inner)
    if unit % 128 == 0:
        w_exp, w_red = part_call(
            patch_index[None], w_expand, w_reduce, imgs, parts
        )
    else:
        w_exp = lax.dynamic_index_in_dim(
            w_expand.reshape(width, imgs, parts, unit), patch_index, 2, keepdims=False
        ).reshape(width, imgs * unit)
        w_red = lax.dynamic_index_in_dim(
            w_reduce.reshape(imgs, parts, unit, width), patch_index, 1, keepdims=False
        ).reshape(imgs * unit, width)

    (latents_far,) = gate((latents_far,), (token,), pltpu.VMEM)
    with jax.named_scope("gather_latents"):
        latents_both = swap(latents_far, "patch", 1)
    latents_all, hat_all, queries, kv_lat, cot_sent = latent_call(
        (latents_own, latents_far, latents_near, latents_both),
        latent_gain[None],
        latent_shift[None],
        w_query,
        w_keyval,
        cot_own,
        (token,),
    )
    kv_lat = kv_lat.reshape(micro, docs, lat_rows, 2 * inner)
    with jax.named_scope("gather_cotangent"):
        cot_far = swap(cot_sent, "patch", 2)
    keep, send = attend_call(doc_ids, queries, kv_med, kv_lat, ())
    send, cot_far = gate((send, cot_far), (), pltpu.VMEM)
    with jax.named_scope("join_near"):
        near = join_call(keep, swap(send, "patch", 1), False, False)
    with jax.named_scope("gather_cotangent"):
        cot_chunks = (cot_sent, cot_far, swap(cot_sent, "patch", 1), swap(cot_far, "patch", 1))
    cot_units, cot_all, token = cot_units_call(cot_chunks, w_red)
    with jax.named_scope("join_far"):
        att_near = join_call(
            near, swap(near, "patch", 2), True, True, (token,)
        )
        att_far = swap(att_near, "patch", 1)

    mixed, ln_ff, hidden_act, grad_pre, *ff_parts = ff_call(
        latents_all,
        att_near,
        att_far,
        cot_units,
        w_output,
        w_exp,
        w_red,
        ff_gain[None],
        ff_shift[None],
    )
    up_own, up_keep, up_send, out_own, out_keep, out_send = ff_parts
    with jax.named_scope("sum_up"):
        up_sent = swap(up_send, "patch", 1)
        up_near = add(up_keep, up_sent[1])
        up_far = swap(up_near, "patch", 2)

    def flat(value):
        return value.reshape(all_rows, -1)

    ff_grads = ff_weights_call(
        flat(ln_ff), flat(grad_pre), flat(hidden_act), flat(cot_all), imgs, (up_near,)
    )
    (up_far,) = gate((up_far,), (ff_grads,), pltpu.VMEM)
    (ff_grads,) = gate((ff_grads,), (up_far,), pltpu.HBM)
    grad_mixed, grad_branch, att_0, att_1, ff_gain_part, ff_shift_part = mixed_back_call(
        up_own, up_sent, up_far, mixed, cot_sent, w_output, ff_gain[None], ()
    )
    grad_output = dot(att_near[0, :, :inner], grad_branch, TN).astype(BF)
    with jax.named_scope("gather_att"):
        far_0 = swap(att_0, "patch", 2)
        near_0 = swap(att_0, "patch", 1)
        (far_0,) = gate((far_0,), (grad_output,), pltpu.VMEM)
        both_0 = swap(far_0, "patch", 1)
        far_1 = swap(att_1, "patch", 2)
        near_1 = swap(att_1, "patch", 1)
    att = (att_near, att_far)

    with jax.named_scope("sum_ff"):
        ff_own = lax.psum_scatter(ff_grads, "img", scatter_dimension=0, tiled=True)[0]

    zero = jnp.zeros_like(media_gain)
    norms = jnp.stack(
        [media_gain, media_shift, latent_gain, latent_shift, zero, zero, zero, zero]
    )
    ff_vectors = jnp.pad(jnp.concatenate([ff_gain_part, ff_shift_part]), ((0, 6), (0, 0)))
    share = width // imgs
    tall = share // parts
    direct = laid_out(width, imgs, inner)

    def back_call(group, grad_att, extra, vectors, deps):
        gkv, gkv_lat, gq, keep, send, vectors = attend_back_call(
            group,
            doc_ids,
            queries,
            [chunk[None] for chunk in grad_att],
            att,
            kv_med,
            kv_lat,
            hat_med,
            hat_all,
            w_keyval,
            w_query,
            norms,
            extra,
            vectors,
            patch_index[None],
            imgs,
            deps,
        )
        if not direct:

            def split(value):
                size = value.shape[0] // (imgs * parts)
                return value.reshape(imgs, parts // 2, 2, size, value.shape[1])

            rows = split(keep)
            fold = [rows[..., : tall // 2, 2 * span :], rows[..., tall // 2 :, 2 * span :]]
            blocks = [rows[..., : 2 * span], jnp.concatenate(fold, axis=-1)]
            if group == 0:
                blocks += [split(extra)[..., :inner], split(extra)[..., inner:]]
            else:
                six = jnp.concatenate([vectors[:4], extra[:2]]).astype(BF)
                six = jnp.swapaxes(six.reshape(6, imgs, share), 0, 1)
                six = jnp.pad(six, ((0, 0), (0, 10), (0, width - share)))[:, None, None, :, :inner]
                blocks.append(
                    jnp.pad(six, ((0, 0), (0, parts // 2 - 1), (0, 1), (0, 0), (0, 0)))
                )
            blocks = jnp.concatenate(blocks, axis=3)
            bit = lax.rem(patch_index, 2)
            keep = lax.dynamic_index_in_dim(blocks, bit, 2, keepdims=False)
            send = lax.dynamic_index_in_dim(blocks, 1 - bit, 2, keepdims=False)
        return gkv, gkv_lat, gq, keep, send, vectors

    out_keep, out_send = gate((out_keep, out_send), (ff_gain_part,), pltpu.HBM)
    with jax.named_scope("sum_out"):
        out_sent = swap(out_send, "patch", 1)
    gkv_0, gkv_lat_0, gq_0, keep, send, vectors = back_call(
        0, (att_0, far_0, near_0, both_0), grad_output, norms, (ff_vectors,)
    )
    keep, send, out_sent, far_1, near_1 = gate(
        (keep, send, out_sent, far_1, near_1), (), pltpu.VMEM
    )
    with jax.named_scope("gather_att"):
        both_1 = swap(far_1, "patch", 1)
    with jax.named_scope("sum_out"):
        out_far, token = half_sum(out_keep, out_sent)
        out_far = swap(out_far, "patch", 2)
    first = reduce_rest(keep, send, "sum_weights_0")
    gkv_1, gkv_lat_1, gq_1, keep, send, vectors = back_call(
        1, (att_1, far_1, near_1, both_1), ff_vectors, vectors, first.step((token, both_1))
    )
    done = first.step((vectors,))
    keep, send, out_far = gate((keep, send, out_far), done, pltpu.VMEM)
    gq_0, gq_1 = gate((gq_0, gq_1), done, pltpu.HBM)
    second = reduce_rest(keep, send, "sum_weights_1")
    with jax.named_scope("sum_query"):
        gq_keep = jnp.concatenate([gq_0[:2], gq_1[:2]], axis=-1)
        gq_sent = swap(jnp.concatenate([gq_0[2:], gq_1[2:]], axis=-1), "patch", 1)

    def media_piece(at, size, whole, deps):
        return media_back_call(
            media_flat,
            gkv_0,
            gkv_1,
            w_keyval,
            media_gain[None],
            at,
            size,
            whole,
            deps,
        )

    media_grad, *done = media_piece(0, 4, None, second.step())
    latents_out, token = out_call(mixed, out_own, out_sent, out_far, done)
    deps = second.step(done)
    (gq_keep,) = gate((gq_keep,), deps or done, pltpu.VMEM)
    with jax.named_scope("sum_query"):
        gq_near = add(gq_keep, gq_sent)
        gq_far = swap(gq_near[1], "patch", 2)
    (ff_own,) = gate((ff_own,), deps or done, pltpu.HBM)
    with jax.named_scope("gather_ff"):
        ff_far = swap(ff_own, "patch", 2)
    media_grad, *done = media_piece(4, 2, media_grad, (*deps, token))
    while first.order or second.order:
        first.step(done)
        second.step(done)
    with jax.named_scope("sum_weights"):
        own, sent, token = last_step(first, second, done)
    media_grad, *done = media_piece(6, 2, media_grad, (token,))
    (gq_far,) = gate((gq_far,), done, pltpu.VMEM)
    latents_grad, token = latent_back_call(
        scale,
        (
            latents_own,
            grad_mixed,
            gq_near[0],
            gq_far,
            gkv_lat_0,
            gkv_lat_1,
            w_query,
            w_keyval,
            latent_gain[None],
        ),
        done,
    )
    own, ff_far, *sent = gate((own, ff_far, *sent), (token,), pltpu.VMEM)
    with jax.named_scope("gather_ff"):
        ff_chunks = (ff_own, ff_far, swap(ff_own, "patch", 1), swap(ff_far, "patch", 1))
    with jax.named_scope("place_ff"):
        if unit % 128 == 0 and share == unit:
            expand_rows, reduce_rows, placed = place_call(
                patch_index[None], ff_chunks, share, imgs, (token,)
            )
        else:
            placed = token
            ff_rows = in_order(jnp.stack(ff_chunks))
            expand_rows = ff_rows[:, :share].reshape(parts, -1, imgs, unit)
            expand_rows = jnp.transpose(expand_rows, (1, 2, 0, 3)).reshape(-1, ff).astype(F32)
            reduce_rows = ff_rows[:, share:].reshape(-1, width).astype(F32)

    def rows_of(value):
        return value.reshape(-1, value.shape[-1])

    with jax.named_scope("gather_weights"):
        own = own.astype(F32)
        for part in sent:
            own = own + part.astype(F32)
        own = own.astype(BF)
        far = swap(own, "patch", 2)
        near = swap(own, "patch", 1)
        (far,) = gate((far,), (placed,), pltpu.VMEM)
        whole = in_order(jnp.stack([own, far, near, swap(far, "patch", 1)]))
    cut = first.value.shape[-2]
    first, second = whole[:, :cut], whole[:, cut:]
    keyval_rows = [rows_of(first[:, :tall]), rows_of(second[:, :tall])]
    grad_keyval = jnp.concatenate(
        [rows[:, at * span : (at + 1) * span] for at in range(2) for rows in keyval_rows], axis=1
    ).astype(F32)
    end = tall + tall // 2

    def unfold(value):
        return rows_of(jnp.concatenate([value[..., :span], value[..., span:]], axis=1))

    query_rows = jnp.concatenate(
        [unfold(first[:, tall:end]), unfold(second[:, tall:end])], axis=1
    ).astype(F32)
    out_rows = first[:, end:]
    size = out_rows.shape[1] // 2
    out_rows = rows_of(
        jnp.concatenate([out_rows[:, :size], out_rows[:, size:]], axis=2)
    ).astype(F32)
    vectors = second[0, end : end + 6, :share].astype(F32)

    return (
        latents_out.reshape(latents.shape),
        latents_grad.reshape(latents.shape),
        media_grad.reshape(media.shape),
        query_rows,
        grad_keyval,
        out_rows,
        expand_rows,
        reduce_rows,
    ) + tuple(vectors[i] for i in range(6))


def solution(mesh):
    tokens = P(None, "img", "patch", None)
    return jax.shard_map(
        local,
        mesh=mesh,
        in_specs=(tokens, tokens, P(None, "img")) + (P(),) * 11 + (tokens,),
        out_specs=(tokens,) * 3 + (P("img", None),) * 5 + (P("img"),) * 6,
        check_vma=False,
    )
```
